32 devices in a mesh: dp: 8 (over y, x, core), tensor: 4 (over z).
Axes of the slice: x: 2, y: 2, z: 4, core: 2. Of those that a mesh axis runs over, the one named last changes fastest.
Arguments:
- tokens: bfloat16 [24576, 1024], P('dp'), may hold values from -6 to 6
- masked_rows: int32 [24, 153], P('dp'), may hold values from 0 to 1023, as said below
- cotangent: bfloat16 [24, 153, 1024], P('dp'), may hold values from -6 to 6
- norm_gains: float32 [2, 1024], replicated, may hold values from 0.5 to 1.5
- gain_first: float32 [2, 1024], replicated
- gain_second: float32 [2, 1024], replicated, as said below
- owners: int32 [4, 32], P('tensor'), may hold values from 0 to 7, as said below
- master: float32 [4, 64, 128, 1024], P('tensor', 'dp')
- first_moment: float32 [4, 64, 128, 1024], P('tensor', 'dp')
- second_moment: float32 [4, 64, 128, 1024], P('tensor', 'dp'), as said below
Outputs:
- layer_out: bfloat16 [24576, 1024], P('dp')
- input_grad: bfloat16 [24576, 1024], P(('dp', 'tensor'))
- weight_grad: float32 [4, 64, 128, 1024], P('tensor', 'dp')
- weight_first: float32 [4, 64, 128, 1024], P('tensor', 'dp')
- weight_second: float32 [4, 64, 128, 1024], P('tensor', 'dp')
- weight_master: float32 [4, 64, 128, 1024], P('tensor', 'dp')
- weight_low: bfloat16 [4, 64, 128, 1024], P('tensor', 'dp')
- gain_grad: float32 [2, 1024], replicated
- gain_moment: float32 [2, 1024], replicated
- gain_new: float32 [2, 1024], replicated
The draws below stay inside these ranges and needn't reach their ends.
Inputs may be any that keep to these rules, and one draw needn't show every extreme that they name: `masked_rows`: within a window the 153 row numbers are distinct. `owners`: each owner holds at most 8 tiles of one tensor index, and in every row some owner holds exactly 8. `second_moment`: Positive. `gain_second`: Positive.
All inputs are finite; a program needn't handle non-finite values.
Results may differ from the reference program's by a relative error of at most 0.014.
Values may be sent and summed in bfloat16 or wider, within the bound.
A program may use at most 320 MiB of HBM per device.

```python
import math
import jax
import jax.numpy as jnp
from jax import lax

D = 1024
HEADS = 16
HD = 64
FF = 4096
LEN = 1024
TROWS = 128
STEP = 5
NMASK = 153
SEQS = 24
TOKENS = 24576
NTILE = 32
CAP = 8
N_TENSOR = 4


def slot_ranks_drawn(owner_row):
    count_all = owner_row.shape[0]
    tile_order = jnp.arange(count_all, dtype=jnp.int32)
    earlier = (owner_row[:, None] == owner_row[None, :]) & (tile_order[None, :] < tile_order[:, None])
    return jnp.sum(earlier.astype(jnp.int32), axis=1)


def owner_table(key):
    owner_total = 2 * NTILE // CAP

    def one_row(row_key):
        first_key, second_key, third_key = jax.random.split(row_key, 3)
        shuffled = jax.random.permutation(first_key, owner_total).astype(jnp.int32)
        spare = jax.random.permutation(second_key, (owner_total - 1) * CAP)[:NTILE - CAP]
        listed = jnp.concatenate([jnp.full((CAP,), shuffled[0], jnp.int32), shuffled[1 + spare // CAP]])
        return jax.random.permutation(third_key, listed)
    row_keys = jax.random.split(jax.random.fold_in(key, 7), N_TENSOR)
    return jax.vmap(one_row)(row_keys).astype(jnp.int32)


def place_tiles(key, per_tile, fill_value):
    owner_rows = owner_table(key)
    ranks = jax.vmap(slot_ranks_drawn)(owner_rows)
    slot_index = owner_rows * CAP + ranks
    base_scale = jnp.full((N_TENSOR, 2 * NTILE), fill_value, jnp.float32)
    lane_index = jnp.arange(N_TENSOR, dtype=jnp.int32)[:, None]
    return base_scale.at[lane_index, slot_index].set(jnp.broadcast_to(per_tile, (N_TENSOR, NTILE)))


def slot_scales(key):
    masked_total = math.sqrt(NMASK * SEQS)
    token_total = math.sqrt(LEN * SEQS)
    attn_tiles = HEADS * HD // (N_TENSOR * TROWS)
    ffn_tiles = FF // (N_TENSOR * TROWS)
    per_tile = jnp.concatenate([jnp.full((attn_tiles,), masked_total, jnp.float32), jnp.full((attn_tiles,), 0.5 * token_total, jnp.float32), jnp.full((attn_tiles,), token_total, jnp.float32), jnp.full((attn_tiles,), 2.0 * masked_total, jnp.float32), jnp.full((3 * ffn_tiles,), masked_total, jnp.float32)])
    return place_tiles(key, per_tile, masked_total)


def weight_scales(key):
    attn_tiles = HEADS * HD // (N_TENSOR * TROWS)
    ffn_tiles = FF // (N_TENSOR * TROWS)
    in_scale = max(0.04, D ** (-0.5))
    out_scale = max(0.04, (HEADS * HD) ** (-0.5))
    down_scale = max(0.04, FF ** (-0.5))
    per_tile = jnp.concatenate([jnp.full((3 * attn_tiles,), in_scale, jnp.float32), jnp.full((attn_tiles,), out_scale, jnp.float32), jnp.full((2 * ffn_tiles,), in_scale, jnp.float32), jnp.full((ffn_tiles,), down_scale, jnp.float32)])
    return place_tiles(key, per_tile, 0.04)


def gain_scales():
    return jnp.array([1.8 * math.sqrt(LEN * SEQS), 3.6 * math.sqrt(NMASK * SEQS)], jnp.float32)[:, None]


def draw_masked_rows(key, part):
    window_keys = jax.random.split(jax.random.fold_in(key, 5), SEQS)

    def one_window(window_key):
        return jax.random.permutation(window_key, LEN)[:NMASK]
    return jax.vmap(one_window)(window_keys).astype(jnp.int32)


def draw_owners(key, part):
    return owner_table(key)


def draw_master(key, part):
    scales = weight_scales(key)[:, :, None, None]
    noise = jax.random.normal(jax.random.fold_in(key, 61), (N_TENSOR, 2 * NTILE, TROWS, D), jnp.float32)
    return scales * jnp.clip(noise, -6.0, 6.0)


def draw_first_moment(key, part):
    scales = slot_scales(key)[:, :, None, None]
    noise = jax.random.normal(jax.random.fold_in(key, 21), (N_TENSOR, 2 * NTILE, TROWS, D), jnp.float32)
    return scales * noise / 9.0


def draw_second_moment(key, part):
    scales = slot_scales(key)[:, :, None, None]
    spread = jnp.exp(jax.random.uniform(jax.random.fold_in(key, 31), (N_TENSOR, 2 * NTILE, TROWS, D), jnp.float32, 0.0, math.log(4.0)))
    return scales * scales * spread / 19.0


def draw_gain_first(key, part):
    noise = jax.random.normal(jax.random.fold_in(key, 41), (2, D), jnp.float32)
    return gain_scales() * noise / 9.0


def draw_gain_second(key, part):
    scales = gain_scales()
    spread = jnp.exp(jax.random.uniform(jax.random.fold_in(key, 51), (2, D), jnp.float32, 0.0, math.log(4.0)))
    return scales * scales * spread / 19.0


def level_of(rng, extent, cuts, least, largest):
    gain = 1.0
    for axis_at, parts in cuts:
        draws = jax.random.uniform(jax.random.fold_in(jax.random.fold_in(rng, 6), axis_at), (parts,), jnp.float32, least / len(cuts), largest / len(cuts))
        gain = gain * jnp.repeat(jnp.exp(draws), extent[axis_at] // parts).reshape((-1,) + (1,) * (len(extent) - 1 - axis_at))
    return gain


def normal_values(rng, extent, scale, most, pieces=(), held_as=jnp.bfloat16):
    factor_of = level_of(rng, extent, pieces, -0.22, 0.18) if pieces else 1.0
    drawn = jax.random.normal(rng, extent, jnp.float32) * scale * factor_of
    return jnp.minimum(jnp.maximum(drawn, -most), most).astype(held_as)


def setup_inputs(seed: int = 0) -> dict:
    key_list = jax.random.split(jax.random.key(seed), 11)
    return {
        "tokens": normal_values(key_list[0], (TOKENS, D), 1.0, 6.0, ((0, 8),)),
        "masked_rows": draw_masked_rows(jax.random.fold_in(key_list[10], 71), 0),
        "cotangent": normal_values(key_list[2], (SEQS, NMASK, D), 1.0, 6.0, ((0, 8),)),
        "norm_gains": jnp.clip(1.0 + 0.1 * jax.random.normal(key_list[3], (2, D), jnp.float32), 0.5, 1.5),
        "gain_first": draw_gain_first(jax.random.fold_in(key_list[10], 71), 0),
        "gain_second": draw_gain_second(jax.random.fold_in(key_list[10], 71), 0),
        "owners": draw_owners(jax.random.fold_in(key_list[10], 71), 0),
        "master": draw_master(jax.random.fold_in(key_list[10], 71), 0),
        "first_moment": draw_first_moment(jax.random.fold_in(key_list[10], 71), 0),
        "second_moment": draw_second_moment(jax.random.fold_in(key_list[10], 71), 0),
    }


norm_eps = 1e-06
beta_one = 0.9
beta_two = 0.95
adam_eps = 1e-08
weight_rate = 0.05
gain_rate = 0.8
weight_decay = 0.1

@jax.custom_vjp
def low(v):
    return lax.optimization_barrier(v.astype(jnp.bfloat16)).astype(jnp.float32)

@jax.custom_vjp
def low_back(v):
    return v

def low_keep(v):
    return (low(v), None)

def low_pass(kept, grad):
    return (grad,)

def back_keep(v):
    return (v, None)

def back_low(kept, grad):
    return (low(grad),)
low.defvjp(low_keep, low_pass)
low_back.defvjp(back_keep, back_low)

def rotary_tables(length, head_size):
    half_size = head_size // 2
    frequency = jnp.exp(-jnp.log(10000.0) * (2.0 * jnp.arange(half_size, dtype=jnp.float32) / head_size))
    angles = jnp.arange(length, dtype=jnp.float32)[:, None] * frequency[None, :]
    return (jnp.cos(angles), jnp.sin(angles))

def rotate(values, cosine_table, sine_table):
    front_half, back_half = jnp.split(values, 2, axis=-1)
    return jnp.concatenate([front_half * cosine_table - back_half * sine_table, back_half * cosine_table + front_half * sine_table], axis=-1)

def rms_scale(values):
    return lax.rsqrt(lax.optimization_barrier(jnp.mean(values * values, axis=-1, keepdims=True)) + norm_eps)

def slot_ranks(owner_row):
    count_all = owner_row.shape[0]
    tile_order = jnp.arange(count_all, dtype=jnp.int32)
    earlier = (owner_row[:, None] == owner_row[None, :]) & (tile_order[None, :] < tile_order[:, None])
    return lax.optimization_barrier(jnp.sum(earlier.astype(jnp.int32), axis=1))

def unpack(weight_tiles, model_width, attn_local, ffn_local):
    flat_weights = weight_tiles.reshape(-1)
    attn_size = model_width * attn_local
    ffn_size = model_width * ffn_local
    w_query = flat_weights[0:attn_size].reshape(model_width, attn_local)
    w_key = flat_weights[attn_size:2 * attn_size].reshape(model_width, attn_local)
    w_value = flat_weights[2 * attn_size:3 * attn_size].reshape(model_width, attn_local)
    w_out = flat_weights[3 * attn_size:4 * attn_size].reshape(attn_local, model_width)
    base_point = 4 * attn_size
    w_gate = flat_weights[base_point:base_point + ffn_size].reshape(model_width, ffn_local)
    w_up = flat_weights[base_point + ffn_size:base_point + 2 * ffn_size].reshape(model_width, ffn_local)
    w_down = flat_weights[base_point + 2 * ffn_size:base_point + 3 * ffn_size].reshape(ffn_local, model_width)
    return (w_query, w_key, w_value, w_out, w_gate, w_up, w_down)

def full_weights(weight_tiles, attn_local, ffn_local):

    def unpack_lane(lane_tiles):
        return unpack(lane_tiles, D, attn_local, ffn_local)
    w_query, w_key, w_value, w_out, w_gate, w_up, w_down = jax.vmap(unpack_lane)(weight_tiles)

    def side_by_side(stacked):
        return jnp.moveaxis(stacked, 0, 1).reshape(stacked.shape[1], -1)

    def stack_rows(stacked):
        return stacked.reshape(-1, stacked.shape[2])
    return (side_by_side(w_query), side_by_side(w_key), side_by_side(w_value), stack_rows(w_out), side_by_side(w_gate), side_by_side(w_up), stack_rows(w_down))

def matmul(left_side, right_side):
    return jnp.dot(left_side, right_side, precision=lax.Precision.HIGHEST, preferred_element_type=jnp.float32)

def layer_forward(weight_tiles, gains, window_in):
    attn_local = HEADS * HD // N_TENSOR
    ffn_local = FF // N_TENSOR
    w_query, w_key, w_value, w_out, w_gate, w_up, w_down = full_weights(low(weight_tiles), attn_local, ffn_local)
    cosine_table, sine_table = rotary_tables(LEN, HD)
    cosine_table = cosine_table[:, None, :]
    sine_table = sine_table[:, None, :]
    score_scale = HD ** (-0.5)
    normed_a = window_in * rms_scale(window_in)
    hidden_a = low(normed_a * gains[0])
    proj_query = low_back(matmul(hidden_a, w_query)).reshape(LEN, HEADS, HD)
    proj_key = low_back(matmul(hidden_a, w_key)).reshape(LEN, HEADS, HD)
    proj_value = low_back(matmul(hidden_a, w_value)).reshape(LEN, HEADS, HD)
    rot_query = low(rotate(proj_query, cosine_table, sine_table))
    rot_key = low(rotate(proj_key, cosine_table, sine_table))
    values_low = low(proj_value)
    raw_scores = low_back(jnp.einsum('qhd,khd->hqk', rot_query, rot_key, precision=lax.Precision.HIGHEST))
    attention = jax.nn.softmax(raw_scores * score_scale, axis=-1)
    mixed = jnp.einsum('hqk,khd->qhd', low(attention), values_low, precision=lax.Precision.HIGHEST)
    mixed = low(low_back(mixed)).reshape(LEN, HEADS * HD)
    resid = window_in + low_back(matmul(mixed, w_out))
    normed_f = resid * rms_scale(resid)
    hidden_f = low(normed_f * gains[1])
    gate_pre = low_back(matmul(hidden_f, w_gate))
    up_pre = low_back(matmul(hidden_f, w_up))
    activated = low(jax.nn.silu(gate_pre) * up_pre)
    return resid + low_back(matmul(activated, w_down))

def adam_update(grad_now, first_old, second_old, param_old, rate, decay):
    first_new = beta_one * first_old + (1.0 - beta_one) * grad_now
    second_new = beta_two * second_old + (1.0 - beta_two) * grad_now * grad_now
    first_hat = first_new / (1.0 - beta_one ** STEP)
    second_hat = second_new / (1.0 - beta_two ** STEP)
    param_new = param_old - rate * (first_hat / (jnp.sqrt(second_hat) + adam_eps) + decay * param_old)
    return (first_new, second_new, param_new)

def reference(tokens, masked_rows, cotangent, norm_gains, gain_first, gain_second, owners, master, first_moment, second_moment):
    ranks = jax.vmap(slot_ranks)(owners)
    slot_index = (owners * CAP + ranks).astype(jnp.int32)
    lane_index = jnp.arange(N_TENSOR, dtype=jnp.int32)[:, None]
    weight_tiles = master[lane_index, slot_index]
    inputs = tokens.astype(jnp.float32).reshape(SEQS, LEN, D)
    back_rows = cotangent.astype(jnp.float32)

    def one_window(totals, window_items):
        window_in, window_rows, window_back = window_items
        grad_out = jnp.zeros((LEN, D), jnp.float32).at[window_rows].set(window_back)
        result, pullback = jax.vjp(layer_forward, weight_tiles, norm_gains, window_in)
        tile_grad, gains_grad, in_grad = pullback(grad_out)
        return ((totals[0] + tile_grad, totals[1] + gains_grad), (result, in_grad))
    start_totals = (jnp.zeros_like(weight_tiles), jnp.zeros_like(norm_gains))
    (tile_total, gain_total), (results, in_grads) = lax.scan(one_window, start_totals, (inputs, masked_rows, back_rows))
    layer_out = results.reshape(TOKENS, D).astype(jnp.bfloat16)
    input_grad = in_grads.reshape(TOKENS, D).astype(jnp.bfloat16)
    weight_grad = jnp.zeros(master.shape, jnp.float32).at[lane_index, slot_index].set(tile_total)
    slot_used = jnp.zeros(master.shape[:2], jnp.float32).at[lane_index, slot_index].set(1.0)[:, :, None, None]
    first_new, second_new, param_new = adam_update(weight_grad, first_moment, second_moment, master, weight_rate, weight_decay)
    weight_first = first_new * slot_used
    weight_second = second_new * slot_used
    weight_master = param_new * slot_used
    weight_low = weight_master.astype(jnp.bfloat16)
    gain_first_new, gain_moment, gain_new = adam_update(gain_total, gain_first, gain_second, norm_gains, gain_rate, 0.0)
    return (layer_out, input_grad, weight_grad, weight_first, weight_second, weight_master, weight_low, gain_total, gain_moment, gain_new)
```

```python
import functools

import jax
import jax.numpy as jnp
from jax import lax
from jax.experimental import pallas as pl
from jax.experimental.pallas import tpu as pltpu
from jax.sharding import PartitionSpec as P

HEADS = 16
HD = 64
FF = 4096
STEP = 5

norm_eps = 1e-06
beta_one = 0.9
beta_two = 0.95
adam_eps = 1e-08
weight_rate = 0.05
gain_rate = 0.8
weight_decay = 0.1

score_scale = HD ** (-0.5)
f32 = jnp.float32
bf16 = jnp.bfloat16
VMEM_LIMIT = 60 * 1024 * 1024
NT = (((1,), (1,)), ((), ()))
TN = (((0,), (0,)), ((), ()))


def mm(left, right):
    return jnp.dot(left, right, preferred_element_type=f32)


def mm_nt(left, right):
    return lax.dot_general(left, right, NT, preferred_element_type=f32)


def mm_tn(left, right):
    return lax.dot_general(left, right, TN, preferred_element_type=f32)


def params(**kw):
    return pltpu.CompilerParams(vmem_limit_bytes=VMEM_LIMIT, **kw)


def cost(flops, nbytes, transcendentals=0):
    return pl.CostEstimate(
        flops=int(flops), bytes_accessed=int(nbytes), transcendentals=int(transcendentals)
    )


def whole_spec(shape):
    return pl.BlockSpec(shape, lambda *_: (0,) * len(shape))


def rms_scale(values):
    return lax.rsqrt(jnp.mean(values * values, axis=-1, keepdims=True) + norm_eps)


def swap_halves(values):
    width = values.shape[1]
    lane = lax.broadcasted_iota(jnp.int32, values.shape, 1)
    return jnp.where(
        lane % HD < HD // 2,
        pltpu.roll(values, width - HD // 2, 1),
        pltpu.roll(values, HD // 2, 1),
    )


def qkv_kernel(x_ref, gains_ref, w_ref, cos_ref, sin_ref, q_ref, k_ref, v_ref):
    width = q_ref.shape[1]
    x = x_ref[...].astype(f32)
    hidden = (x * rms_scale(x) * gains_ref[0:1, :]).astype(bf16)
    cos, sin = cos_ref[...], sin_ref[...]
    q = mm(hidden, w_ref[:, 0:width])
    q_ref[...] = (q * cos + swap_halves(q) * sin).astype(bf16)
    k = mm(hidden, w_ref[:, width : 2 * width])
    k_ref[...] = (k * cos + swap_halves(k) * sin).astype(bf16)
    v_ref[...] = mm(hidden, w_ref[:, 2 * width : 3 * width]).astype(bf16)


def attend(q, k, v):
    first = lax.broadcasted_iota(jnp.int32, q.shape, 1) < HD
    first_v = lax.broadcasted_iota(jnp.int32, v.shape, 1) < HD
    zero, one = jnp.zeros((), bf16), jnp.ones((), bf16)
    outs = []
    for head in range(2):
        q_head = jnp.where(first if head == 0 else ~first, q, zero)
        v_head = jnp.where(first_v if head == 0 else ~first_v, v, one)
        s = mm_nt(q_head, k)
        s = (s - jnp.max(s, axis=-1, keepdims=True)) * score_scale
        outs.append(mm(jnp.exp(s).astype(bf16), v_head))
    value = jnp.where(first, outs[0], outs[1])
    total = pltpu.roll(jnp.where(first, outs[1], outs[0]), HD, 1)
    return (value / total).astype(bf16)


def attend_kernel(q_ref, k_ref, v_ref, o_ref):
    o_ref[...] = attend(q_ref[...], k_ref[...], v_ref[...])


def attend_masked_kernel(rows_ref, x_ref, q_ref, k_ref, v_ref, o_ref, qm_ref, xm_ref):
    window = x_ref.shape[0]
    count = rows_ref.shape[1]
    pick = (
        lax.broadcasted_iota(jnp.int32, (count, window), 1) == rows_ref[0]
    ).astype(bf16)
    xm_ref[...] = mm(pick, x_ref[...]).astype(bf16)
    qm = mm(pick, q_ref[...]).astype(bf16)
    qm_ref[...] = qm
    for pair in range(q_ref.shape[1] // 128):
        lanes = slice(pair * 128, pair * 128 + 128)
        o_ref[:, lanes] = attend(qm[:, lanes], k_ref[:, lanes], v_ref[:, lanes])


def ffn_masked_kernel(
    parts, xm_ref, cot_ref, gains_ref, wg_ref, wu_ref, wd_ref, *refs
):
    o_refs, wo_refs = refs[:parts], refs[parts : 2 * parts]
    rm_ref, dhf_ref, gg_ref, gu_ref, gd_ref, hf_ref, acc_ref = refs[2 * parts :]
    step = pl.program_id(0)

    @pl.when(step == 0)
    def _():
        r = xm_ref[...].astype(f32)
        for o_ref, wo_ref in zip(o_refs, wo_refs):
            r = r + mm(o_ref[...], wo_ref[...])
        rm_ref[...] = r
        hf_ref[...] = (r * rms_scale(r) * gains_ref[1:2, :]).astype(bf16)
        acc_ref[...] = jnp.zeros_like(acc_ref)

    hf, dy = hf_ref[...], cot_ref[...]
    wg, wu, wd = wg_ref[...], wu_ref[...], wd_ref[...]
    g, u = mm(hf, wg), mm(hf, wu)
    sig = jax.nn.sigmoid(g)
    act = (g * sig * u).astype(bf16)
    gd_ref[...] = mm_tn(act, dy).astype(bf16)
    da = mm_nt(dy, wd)
    dg = (da * u * sig * (1.0 + g * (1.0 - sig))).astype(bf16)
    du = (da * g * sig).astype(bf16)
    gg_ref[...] = mm_tn(hf, dg).astype(bf16)
    gu_ref[...] = mm_tn(hf, du).astype(bf16)
    acc_ref[...] += mm_nt(dg, wg) + mm_nt(du, wu)

    @pl.when(step == pl.num_programs(0) - 1)
    def _():
        dhf_ref[...] = acc_ref[...].astype(bf16)


def ffn_kernel(parts, place_ref, x_ref, gains_ref, wg_ref, wu_ref, wd_ref, *refs):
    o_refs, wo_refs = refs[:parts], refs[parts : 2 * parts]
    part_ref, own_ref, r_ref, hf_ref, acc_ref = refs[2 * parts :]
    step = pl.program_id(0)

    @pl.when(step == 0)
    def _():
        r = x_ref[...].astype(f32)
        for o_ref, wo_ref in zip(o_refs, wo_refs):
            r = r + mm(o_ref[...], wo_ref[...])
        r_ref[...] = r
        hf_ref[...] = (r * rms_scale(r) * gains_ref[1:2, :]).astype(bf16)
        acc_ref[...] = jnp.zeros_like(acc_ref)

    hf = hf_ref[...]
    g, u = mm(hf, wg_ref[...]), mm(hf, wu_ref[...])
    act = (g * jax.nn.sigmoid(g) * u).astype(bf16)
    acc_ref[...] += mm(act, wd_ref[...])

    @pl.when(step == pl.num_programs(0) - 1)
    def _():
        part_ref[...] = acc_ref[...].astype(bf16)
        share = own_ref.shape[0]
        mine = pl.ds(pl.multiple_of(place_ref[0] * share, share), share)
        own_ref[...] = r_ref[mine, :] + acc_ref[mine, :]


def attn_back_kernel(
    rows_ref,
    dhf_ref,
    rm_ref,
    cot_ref,
    gains_ref,
    om_ref,
    qm_ref,
    cosm_ref,
    sinm_ref,
    k_ref,
    v_ref,
    x_ref,
    cos_ref,
    sin_ref,
    wo_ref,
    w_ref,
    drm_ref,
    dha_ref,
    gw_ref,
    go_ref,
    gain_ref,
    gw_acc,
    go_acc,
    gain_acc,
    flow_ref,
):
    step = pl.program_id(0)

    @pl.when(step == 0)
    def _():
        gw_acc[...] = jnp.zeros_like(gw_acc)
        go_acc[...] = jnp.zeros_like(go_acc)
        gain_acc[...] = jnp.zeros_like(gain_acc)

    window, width = k_ref.shape
    count = rm_ref.shape[0]
    r = rm_ref[...]
    sf = rms_scale(r)
    nf = r * sf
    dhf = dhf_ref[...].astype(f32)
    dnf = dhf * gains_ref[1:2, :]
    dr = cot_ref[...].astype(f32) + sf * (
        dnf - nf * jnp.mean(dnf * nf, axis=-1, keepdims=True)
    )
    drm_ref[...] = dr
    gain_acc[1:2, :] += jnp.sum(dhf * nf, axis=0, keepdims=True)
    drb = dr.astype(bf16)
    go_acc[...] += mm_tn(om_ref[...], drb)
    dob = mm_nt(drb, wo_ref[...]).astype(bf16)

    first = lax.broadcasted_iota(jnp.int32, (count, 128), 1) < HD
    zero = jnp.zeros((), bf16)
    drq = []
    for pair in range(width // 128):
        lanes = slice(pair * 128, pair * 128 + 128)
        k, v = k_ref[:, lanes], v_ref[:, lanes]
        qm, do = qm_ref[:, lanes], dob[:, lanes]
        parts = []
        drk = dv = None
        for head in range(2):
            mine = first if head == 0 else ~first
            q_head = jnp.where(mine, qm, zero)
            do_head = jnp.where(mine, do, zero)
            s = mm_nt(k, q_head)
            s = jnp.exp((s - jnp.max(s, axis=0, keepdims=True)) * score_scale)
            att = s / jnp.sum(s, axis=0, keepdims=True)
            dpa = mm_nt(v, do_head)
            ds = att * (dpa - jnp.sum(dpa * att, axis=0, keepdims=True))
            ds = (ds * score_scale).astype(bf16)
            parts.append(mm_tn(ds, k))
            drk_head = mm(ds, q_head)
            dv_head = mm(att.astype(bf16), do_head)
            drk = drk_head if drk is None else drk + drk_head
            dv = dv_head if dv is None else dv + dv_head
        drq.append(jnp.where(first, parts[0], parts[1]))
        dk = drk * cos_ref[:, lanes] - swap_halves(drk) * sin_ref[:, lanes]
        flow_ref[:, width + pair * 128 : width + pair * 128 + 128] = dk.astype(bf16)
        flow_ref[:, 2 * width + pair * 128 : 2 * width + pair * 128 + 128] = dv.astype(
            bf16
        )
    spread = (
        lax.broadcasted_iota(jnp.int32, (window, count), 0) == rows_ref[0]
    ).astype(bf16)
    for pair in range(width // 128):
        lanes = slice(pair * 128, pair * 128 + 128)
        dq = drq[pair] * cosm_ref[:, lanes] - swap_halves(drq[pair]) * sinm_ref[:, lanes]
        flow_ref[:, lanes] = mm(spread, dq.astype(bf16)).astype(bf16)

    flow = flow_ref[...]
    x = x_ref[...].astype(f32)
    na = x * rms_scale(x)
    dha = mm_nt(flow, w_ref[...])
    gain_acc[0:1, :] += jnp.sum(dha * na, axis=0, keepdims=True)
    dha_ref[...] = dha.astype(bf16)
    gw_acc[...] += mm_tn((na * gains_ref[0:1, :]).astype(bf16), flow)

    @pl.when(step == pl.num_programs(0) - 1)
    def _():
        gw_ref[...] = gw_acc[...].astype(bf16)
        go_ref[...] = go_acc[...].astype(bf16)
        gain_ref[...] = gain_acc[...]


def input_grad_kernel(
    place_ref, rows_ref, drm_ref, gains_ref, x_ref, part_ref, up_ref, down_ref, out_ref
):
    block, count = x_ref.shape[0], drm_ref.shape[0]
    base = place_ref[0] * (pl.num_programs(0) * block) + pl.program_id(0) * block
    spread = (
        lax.broadcasted_iota(jnp.int32, (block, count), 0) + base == rows_ref[...]
    ).astype(bf16)
    dr = drm_ref[...]
    high = dr.astype(bf16)
    low = (dr - high.astype(f32)).astype(bf16)
    dr = mm(spread, high) + mm(spread, low)
    x = x_ref[...].astype(f32)
    sa = rms_scale(x)
    na = x * sa
    dha = part_ref[...].astype(f32) + up_ref[...].astype(f32) + down_ref[...].astype(f32)
    dna = dha * gains_ref[0:1, :]
    out = dr + sa * (dna - na * jnp.mean(dna * na, axis=-1, keepdims=True))
    out_ref[...] = out.astype(bf16)


def collect_kernel(slot_ref, first, slots_ref, out_ref, sems):
    count = out_ref.shape[0]

    def copy(index):
        return pltpu.make_async_copy(
            slots_ref.at[slot_ref[first + index]], out_ref.at[index], sems.at[index]
        )

    for index in range(count):
        copy(index).start()
    for index in range(count):
        copy(index).wait()


def exchange(value, axis, bit):
    size = lax.axis_size(axis)
    return lax.ppermute(value, axis, [(i, i ^ bit) for i in range(size)])


def dp_total(value):
    size = lax.axis_size("dp")
    value = value + exchange(value, "dp", 1)
    bits = []
    bit = 2
    while bit < size:
        bits.append(bit)
        bit *= 2
    core = lax.axis_index("dp") % 2
    half = value.shape[0] // 2
    mine = lax.dynamic_slice_in_dim(value, core * half, half, 0)
    cut = half // 2
    low, high = mine[:cut], mine[cut:]
    for bit_low, bit_high in zip(bits, bits[::-1]):
        low = low + exchange(low, "dp", bit_low)
        high = high + exchange(high, "dp", bit_high)
    mine = jnp.concatenate([low, high], axis=0)
    other = exchange(mine, "dp", 1)
    return jnp.where(
        core == 0,
        jnp.concatenate([mine, other], axis=0),
        jnp.concatenate([other, mine], axis=0),
    )


def around(value):
    size = lax.axis_size("tensor")
    return [value] + [
        lax.ppermute(value, "tensor", [(i, (i + k) % size) for i in range(size)])
        for k in range(1, size)
    ]


def chain_sums(value, share):
    size = lax.axis_size("tensor")
    place = lax.axis_index("tensor")
    up = down = None
    for step in range(size - 1):
        index = jnp.minimum(size - 1 - step + place, size - 1)
        send = lax.dynamic_slice_in_dim(value, index * share, share, 0)
        if up is not None:
            send = (send.astype(f32) + up.astype(f32)).astype(bf16)
        up = lax.ppermute(
            send, "tensor", [(i, i + 1) for i in range(min(step, size - 2) + 1)]
        )
        index = jnp.maximum(place - (size - 1 - step), 0)
        send = lax.dynamic_slice_in_dim(value, index * share, share, 0)
        if down is not None:
            send = (send.astype(f32) + down.astype(f32)).astype(bf16)
        down = lax.ppermute(
            send,
            "tensor",
            [(size - 1 - i, size - 2 - i) for i in range(min(step, size - 2) + 1)],
        )
    return up, down


def small_total(value):
    for axis in ("dp", "tensor"):
        bit = 1
        while bit < lax.axis_size(axis):
            value = value + exchange(value, axis, bit)
            bit *= 2
    return value


def slot_ranks(owner_row):
    count_all = owner_row.shape[0]
    tile_order = jnp.arange(count_all, dtype=jnp.int32)
    earlier = (owner_row[:, None] == owner_row[None, :]) & (
        tile_order[None, :] < tile_order[:, None]
    )
    return jnp.sum(earlier.astype(jnp.int32), axis=1)


def adam_update(grad_now, first_old, second_old, param_old, rate, decay):
    first_new = beta_one * first_old + (1.0 - beta_one) * grad_now
    second_new = beta_two * second_old + (1.0 - beta_two) * grad_now * grad_now
    first_hat = first_new / (1.0 - beta_one**STEP)
    second_hat = second_new / (1.0 - beta_two**STEP)
    param_new = param_old - rate * (
        first_hat / (jnp.sqrt(second_hat) + adam_eps) + decay * param_old
    )
    return (first_new, second_new, param_new)


def head_tables(positions, heads):
    frequency = jnp.exp(
        -jnp.log(10000.0) * (2.0 * jnp.arange(HD // 2, dtype=f32) / HD)
    )
    angles = positions.astype(f32)[..., None] * frequency
    cos, sin = jnp.cos(angles), jnp.sin(angles)
    cos = jnp.concatenate([cos, cos], axis=-1)
    sin = jnp.concatenate([-sin, sin], axis=-1)
    reps = (1,) * (cos.ndim - 1) + (heads,)
    return jnp.tile(cos, reps), jnp.tile(sin, reps)


def on_device(
    tokens,
    masked_rows,
    cotangent,
    norm_gains,
    gain_first,
    gain_second,
    owners,
    master,
    first_moment,
    second_moment,
):
    seq_count, mask_count = masked_rows.shape
    total_rows, model = tokens.shape
    window = total_rows // seq_count
    parts = lax.axis_size("tensor")
    place = lax.axis_index("tensor")
    owner_self = lax.axis_index("dp")
    heads = HEADS // parts
    width = heads * HD
    hidden = FF // parts
    capacity, tile_rows = master.shape[1:3]
    tile_size = tile_rows * model
    attn_tiles = 4 * model * width // tile_size
    ffn_tiles = 3 * model * hidden // tile_size
    count = -(-mask_count // 16) * 16
    place_ref = place.astype(jnp.int32).reshape(1)

    owner_row = owners[0]
    slot_rank = slot_ranks(owner_row)
    slot_index = owner_row * capacity + slot_rank
    slot_match = (owner_row[None, :] == owner_self) & (
        slot_rank[None, :] == jnp.arange(capacity, dtype=jnp.int32)[:, None]
    )
    slot_used = jnp.any(slot_match, axis=1)[:, None, None]
    slot_tile = jnp.argmax(slot_match, axis=1)

    low_slots = master[0].astype(bf16)
    held = (owner_row[:attn_tiles] == owner_self)[:, None, None]
    attn_mine = jnp.where(held, low_slots[slot_rank[:attn_tiles]], jnp.zeros((), bf16))
    attn_flat = dp_total(attn_mine).reshape(4, -1)
    w_qkv = jnp.concatenate(
        [attn_flat[i].reshape(model, width) for i in range(3)], axis=1
    )
    w_out = attn_flat[3].reshape(width, model)
    every_slot = lax.all_gather(low_slots, "dp", axis=0, tiled=True)
    ffn_all = pl.pallas_call(
        lambda slot_ref, slots_ref, out_ref, sems: collect_kernel(
            slot_ref, attn_tiles, slots_ref, out_ref, sems
        ),
        out_shape=jax.ShapeDtypeStruct((ffn_tiles, tile_rows, model), bf16),
        grid_spec=pltpu.PrefetchScalarGridSpec(
            num_scalar_prefetch=1,
            grid=(1,),
            in_specs=[pl.BlockSpec(memory_space=pl.ANY)],
            out_specs=pl.BlockSpec(memory_space=pl.ANY),
            scratch_shapes=[pltpu.SemaphoreType.DMA((ffn_tiles,))],
        ),
        compiler_params=params(),
        cost_estimate=cost(0, 2 * ffn_tiles * tile_size * 2),
        name="collect",
    )(slot_index, every_slot)
    ffn_flat = ffn_all.reshape(3, -1)
    w_gate = ffn_flat[0].reshape(model, hidden)
    w_up = ffn_flat[1].reshape(model, hidden)
    w_down = ffn_flat[2].reshape(hidden, model)
    w_outs = around(w_out)

    cos, sin = head_tables(jnp.arange(window), heads)
    rows = jnp.pad(masked_rows, ((0, 0), (0, count - mask_count)), constant_values=-1)
    cos_m, sin_m = head_tables(rows, heads)
    cot = jnp.pad(cotangent, ((0, 0), (0, count - mask_count), (0, 0)))
    cot = cot.reshape(seq_count * count, model)
    cos_m = cos_m.reshape(seq_count * count, width)
    sin_m = sin_m.reshape(seq_count * count, width)

    block = min(512, window)
    per_window = window // block
    row_block = pl.BlockSpec((block, model), lambda i: (i, 0))
    head_block = pl.BlockSpec((block, width), lambda i: (i, 0))
    table_block = pl.BlockSpec((block, width), lambda i: (i % per_window, 0))
    q, k, v = pl.pallas_call(
        qkv_kernel,
        out_shape=[jax.ShapeDtypeStruct((total_rows, width), bf16)] * 3,
        grid=(total_rows // block,),
        in_specs=[
            row_block,
            whole_spec((2, model)),
            whole_spec((model, 3 * width)),
            table_block,
            table_block,
        ],
        out_specs=[head_block] * 3,
        compiler_params=params(),
        cost_estimate=cost(6 * total_rows * model * width, 2 * total_rows * model * 2),
        name="qkv",
    )(tokens, norm_gains, w_qkv, cos, sin)

    win_model = pl.BlockSpec((window, model), lambda i: (i, 0))
    win_head = pl.BlockSpec((window, width), lambda i: (i, 0))
    mask_model = pl.BlockSpec((count, model), lambda i: (i, 0))
    mask_head = pl.BlockSpec((count, width), lambda i: (i, 0))
    o_m, q_m, x_m = pl.pallas_call(
        attend_masked_kernel,
        out_shape=[
            jax.ShapeDtypeStruct((seq_count * count, width), bf16),
            jax.ShapeDtypeStruct((seq_count * count, width), bf16),
            jax.ShapeDtypeStruct((seq_count * count, model), bf16),
        ],
        grid=(seq_count,),
        in_specs=[
            pl.BlockSpec((1, count, 1), lambda i: (i, 0, 0)),
            win_model,
            win_head,
            win_head,
            win_head,
        ],
        out_specs=[mask_head, mask_head, mask_model],
        compiler_params=params(),
        cost_estimate=cost(
            seq_count * count * window * (2 * model + 8 * width), 9e6, seq_count * count * window * heads
        ),
        name="attend_masked",
    )(rows[:, :, None], tokens, q, k, v)
    o_ms = around(o_m)

    q_block = min(256, window)

    def attend_window(w):
        return pl.pallas_call(
            attend_kernel,
            out_shape=jax.ShapeDtypeStruct((window, width), bf16),
            grid=(width // 128, window // q_block),
            in_specs=[
                pl.BlockSpec((q_block, 128), lambda p, i: (w * (window // q_block) + i, p)),
                pl.BlockSpec((window, 128), lambda p, i: (w, p)),
                pl.BlockSpec((window, 128), lambda p, i: (w, p)),
            ],
            out_specs=pl.BlockSpec((q_block, 128), lambda p, i: (i, p)),
            compiler_params=params(),
            cost_estimate=cost(
                16 * window * window * width, 4 * window * width * 2, window * window * heads
            ),
            name="attend",
        )(q, k, v)

    windows_o = [around(attend_window(w)) for w in range(seq_count)]

    mask_rows = seq_count * count
    cols = min(256, hidden)
    col_block = pl.BlockSpec((model, cols), lambda c: (0, c))
    down_block = pl.BlockSpec((cols, model), lambda c: (c, 0))
    r_m, dhf_part, g_gate, g_up, g_down = pl.pallas_call(
        functools.partial(ffn_masked_kernel, parts),
        out_shape=[
            jax.ShapeDtypeStruct((mask_rows, model), f32),
            jax.ShapeDtypeStruct((mask_rows, model), bf16),
            jax.ShapeDtypeStruct((model, hidden), bf16),
            jax.ShapeDtypeStruct((model, hidden), bf16),
            jax.ShapeDtypeStruct((hidden, model), bf16),
        ],
        grid=(hidden // cols,),
        in_specs=[
            whole_spec((mask_rows, model)),
            whole_spec((mask_rows, model)),
            whole_spec((2, model)),
            col_block,
            col_block,
            down_block,
        ]
        + [whole_spec((mask_rows, width))] * parts
        + [whole_spec((width, model))] * parts,
        out_specs=[
            whole_spec((mask_rows, model)),
            whole_spec((mask_rows, model)),
            col_block,
            col_block,
            down_block,
        ],
        scratch_shapes=[
            pltpu.VMEM((mask_rows, model), bf16),
            pltpu.VMEM((mask_rows, model), f32),
        ],
        compiler_params=params(),
        cost_estimate=cost(
            mask_rows * model * (18 * hidden + 2 * model), 20e6, mask_rows * hidden
        ),
        name="ffn_masked",
    )(x_m, cot, norm_gains, w_gate, w_up, w_down, *o_ms, *w_outs)

    share_m = mask_rows // parts
    dhf_mine = lax.dynamic_slice_in_dim(dhf_part, place * share_m, share_m, 0).astype(f32)
    for step in range(1, parts):
        send = lax.dynamic_slice_in_dim(
            dhf_part, lax.rem(place + step, parts) * share_m, share_m, 0
        )
        dhf_mine = dhf_mine + lax.ppermute(
            send, "tensor", [(i, (i + step) % parts) for i in range(parts)]
        ).astype(f32)
    dhf_all = around(dhf_mine.astype(bf16))
    dhf = jnp.zeros((mask_rows, model), bf16)
    for step, piece in enumerate(dhf_all):
        origin = lax.rem(place + parts - step, parts)
        dhf = lax.dynamic_update_slice_in_dim(dhf, piece, origin * share_m, 0)

    def total_tiles(tiles):
        piece = lax.psum_scatter(tiles, "dp", scatter_dimension=0, tiled=True)
        return lax.all_gather(piece, "dp", axis=0, tiled=True)

    ffn_grads = total_tiles(
        jnp.concatenate(
            [g.reshape(-1, model) for g in (g_gate, g_up, g_down)], axis=0
        )
    )

    dr_m, dha, g_qkv, g_out, gains_part = pl.pallas_call(
        attn_back_kernel,
        out_shape=[
            jax.ShapeDtypeStruct((mask_rows, model), f32),
            jax.ShapeDtypeStruct((total_rows, model), bf16),
            jax.ShapeDtypeStruct((model, 3 * width), bf16),
            jax.ShapeDtypeStruct((width, model), bf16),
            jax.ShapeDtypeStruct((2, model), f32),
        ],
        grid=(seq_count,),
        in_specs=[
            pl.BlockSpec((1, 1, count), lambda i: (i, 0, 0)),
            mask_model,
            mask_model,
            mask_model,
            whole_spec((2, model)),
            mask_head,
            mask_head,
            mask_head,
            mask_head,
            win_head,
            win_head,
            win_model,
            whole_spec((window, width)),
            whole_spec((window, width)),
            whole_spec((width, model)),
            whole_spec((model, 3 * width)),
        ],
        out_specs=[
            mask_model,
            win_model,
            whole_spec((model, 3 * width)),
            whole_spec((width, model)),
            whole_spec((2, model)),
        ],
        scratch_shapes=[
            pltpu.VMEM((model, 3 * width), f32),
            pltpu.VMEM((width, model), f32),
            pltpu.VMEM((2, model), f32),
            pltpu.VMEM((window, 3 * width), bf16),
        ],
        compiler_params=params(),
        cost_estimate=cost(
            12 * total_rows * model * width, 30e6, mask_rows * window * heads
        ),
        name="attn_back",
    )(
        rows[:, None, :],
        dhf,
        r_m,
        cot,
        norm_gains,
        o_m,
        q_m,
        cos_m,
        sin_m,
        k,
        v,
        tokens,
        cos,
        sin,
        w_out,
        w_qkv,
    )

    share_rows = total_rows // parts
    dha_up, dha_down = chain_sums(dha, share_rows)
    out_block = share_rows // 3 if share_rows % 3 == 0 else share_rows
    flat_rows = jnp.where(
        rows >= 0, rows + window * jnp.arange(seq_count, dtype=jnp.int32)[:, None], -1
    ).reshape(1, mask_rows)
    blocks = share_rows // out_block
    here = pl.BlockSpec((out_block, model), lambda i, place_ref: (i, 0))
    there = pl.BlockSpec(
        (out_block, model), lambda i, place_ref: (place_ref[0] * blocks + i, 0)
    )
    input_grad = pl.pallas_call(
        input_grad_kernel,
        out_shape=jax.ShapeDtypeStruct((share_rows, model), bf16),
        grid_spec=pltpu.PrefetchScalarGridSpec(
            num_scalar_prefetch=1,
            grid=(blocks,),
            in_specs=[
                whole_spec((1, mask_rows)),
                whole_spec((mask_rows, model)),
                whole_spec((2, model)),
                there,
                there,
                here,
                here,
            ],
            out_specs=here,
        ),
        compiler_params=params(),
        cost_estimate=cost(4 * share_rows * mask_rows * model, 10e6),
        name="input_grad",
    )(place_ref, flat_rows, dr_m, norm_gains, tokens, dha, dha_up, dha_down)

    share = window // parts
    layer_out = jnp.zeros((total_rows, model), bf16)
    for w in range(seq_count):
        part, own = pl.pallas_call(
            functools.partial(ffn_kernel, parts),
            out_shape=[
                jax.ShapeDtypeStruct((window, model), bf16),
                jax.ShapeDtypeStruct((share, model), f32),
            ],
            grid_spec=pltpu.PrefetchScalarGridSpec(
                num_scalar_prefetch=1,
                grid=(hidden // cols,),
                in_specs=[
                    pl.BlockSpec((window, model), lambda c, place_ref, w=w: (w, 0)),
                    whole_spec((2, model)),
                    pl.BlockSpec((model, cols), lambda c, place_ref: (0, c)),
                    pl.BlockSpec((model, cols), lambda c, place_ref: (0, c)),
                    pl.BlockSpec((cols, model), lambda c, place_ref: (c, 0)),
                ]
                + [whole_spec((window, width))] * parts
                + [whole_spec((width, model))] * parts,
                out_specs=[whole_spec((window, model)), whole_spec((share, model))],
                scratch_shapes=[
                    pltpu.VMEM((window, model), f32),
                    pltpu.VMEM((window, model), bf16),
                    pltpu.VMEM((window, model), f32),
                ],
            ),
            compiler_params=params(),
            cost_estimate=cost(
                window * model * (6 * hidden + 2 * model), 16e6, window * hidden
            ),
            name="ffn",
        )(place_ref, tokens, norm_gains, w_gate, w_up, w_down, *windows_o[w], *w_outs)
        up, down = chain_sums(part, share)
        piece = (own + up.astype(f32) + down.astype(f32)).astype(bf16)
        for step, got in enumerate(around(piece)):
            origin = lax.rem(place + parts - step, parts)
            layer_out = lax.dynamic_update_slice_in_dim(
                layer_out, got, w * window + origin * share, 0
            )

    even = jnp.array([[1.0], [1.0 / parts]], f32)
    gain_grad = small_total(gains_part * even)
    _, gain_moment, gain_new = adam_update(
        gain_grad, gain_first, gain_second, norm_gains, gain_rate, 0.0
    )

    attn_grads = total_tiles(
        jnp.concatenate(
            [g_qkv[:, i * width : (i + 1) * width].reshape(-1, model) for i in range(3)]
            + [g_out],
            axis=0,
        )
    )
    tiles = jnp.concatenate([attn_grads, ffn_grads], axis=0).reshape(-1, tile_rows, model)
    reduced = tiles[slot_tile].astype(f32)
    first_new, second_new, param_new = adam_update(
        reduced, first_moment[0], second_moment[0], master[0], weight_rate, weight_decay
    )
    weight_grad = jnp.where(slot_used, reduced, 0.0)
    weight_first = jnp.where(slot_used, first_new, 0.0)
    weight_second = jnp.where(slot_used, second_new, 0.0)
    weight_master = jnp.where(slot_used, param_new, 0.0)
    weight_low = weight_master.astype(bf16)
    return (
        layer_out,
        input_grad,
        weight_grad[None],
        weight_first[None],
        weight_second[None],
        weight_master[None],
        weight_low[None],
        gain_grad,
        gain_moment,
        gain_new,
    )


def solution(mesh):
    return jax.shard_map(
        on_device,
        mesh=mesh,
        in_specs=(
            P("dp", None),
            P("dp", None),
            P("dp", None, None),
            P(),
            P(),
            P(),
            P("tensor", None),
            P("tensor", "dp", None, None),
            P("tensor", "dp", None, None),
            P("tensor", "dp", None, None),
        ),
        out_specs=(
            P("dp", None),
            P(("dp", "tensor"), None),
            P("tensor", "dp", None, None),
            P("tensor", "dp", None, None),
            P("tensor", "dp", None, None),
            P("tensor", "dp", None, None),
            P("tensor", "dp", None, None),
            P(),
            P(),
            P(),
        ),
        check_vma=False,
    )
```

```python
import functools

import jax
import jax.numpy as jnp
from jax import lax
from jax.experimental import pallas as pl
from jax.experimental.pallas import tpu as pltpu
from jax.sharding import PartitionSpec as P

HEADS = 16
HD = 64
FF = 4096
STEP = 5

norm_eps = 1e-06
beta_one = 0.9
beta_two = 0.95
adam_eps = 1e-08
weight_rate = 0.05
gain_rate = 0.8
weight_decay = 0.1

score_scale = HD ** (-0.5)
f32 = jnp.float32
bf16 = jnp.bfloat16
VMEM_LIMIT = 60 * 1024 * 1024
NT = (((1,), (1,)), ((), ()))
TN = (((0,), (0,)), ((), ()))


def mm(left, right):
    return jnp.dot(left, right, preferred_element_type=f32)


def mm_nt(left, right):
    return lax.dot_general(left, right, NT, preferred_element_type=f32)


def mm_tn(left, right):
    return lax.dot_general(left, right, TN, preferred_element_type=f32)


def params(**kw):
    return pltpu.CompilerParams(vmem_limit_bytes=VMEM_LIMIT, **kw)


def cost(flops, nbytes, transcendentals=0):
    return pl.CostEstimate(
        flops=int(flops), bytes_accessed=int(nbytes), transcendentals=int(transcendentals)
    )


def whole_spec(shape):
    return pl.BlockSpec(shape, lambda *_: (0,) * len(shape))


def after(kernel, inputs, count):
    return lambda *refs: kernel(*refs[:inputs], *refs[inputs + count :])


UNREAD = pl.BlockSpec(memory_space=pl.ANY)


def rms_scale(values):
    return lax.rsqrt(jnp.mean(values * values, axis=-1, keepdims=True) + norm_eps)


def swap_halves(values):
    width = values.shape[1]
    lane = lax.broadcasted_iota(jnp.int32, values.shape, 1)
    return jnp.where(
        lane % HD < HD // 2,
        pltpu.roll(values, width - HD // 2, 1),
        pltpu.roll(values, HD // 2, 1),
    )


def cast_kernel(rank_ref, held_ref, slot_ref, tile_ref, low_ref, mine_ref):
    low_ref[...] = slot_ref[...].astype(bf16)
    tile = tile_ref[...].astype(bf16)
    held = held_ref[pl.program_id(0)] > 0
    mine_ref[...] = jnp.where(held, tile, jnp.zeros((), bf16))


def qkv_kernel(
    x_ref, gains_ref, tiles_ref, cos_ref, sin_ref, q_ref, k_ref, v_ref, w_ref, w_wide
):
    width = q_ref.shape[1]
    model = x_ref.shape[1]
    fold = model // width

    @pl.when(pl.program_id(0) == 0)
    def _():
        for block in range(3 * width // 128):
            part, lane = divmod(block * 128, width)
            for piece in range(fold):
                at = piece * width + lane
                w_wide[block, pl.ds(piece, width, stride=fold), :] = tiles_ref[
                    part * width : (part + 1) * width, at : at + 128
                ].astype(f32)
            w_ref[:, block * 128 : (block + 1) * 128] = w_wide[block].astype(bf16)

    x = x_ref[...].astype(f32)
    hidden = (x * rms_scale(x) * gains_ref[0:1, :]).astype(bf16)
    cos, sin = cos_ref[...], sin_ref[...]
    q = mm(hidden, w_ref[:, 0:width])
    q_ref[...] = (q * cos + swap_halves(q) * sin).astype(bf16)
    k = mm(hidden, w_ref[:, width : 2 * width])
    k_ref[...] = (k * cos + swap_halves(k) * sin).astype(bf16)
    v_ref[...] = mm(hidden, w_ref[:, 2 * width : 3 * width]).astype(bf16)


def attend(q, k, v):
    first = lax.broadcasted_iota(jnp.int32, q.shape, 1) < HD
    first_v = lax.broadcasted_iota(jnp.int32, v.shape, 1) < HD
    zero, one = jnp.zeros((), bf16), jnp.ones((), bf16)
    outs = []
    for head in range(2):
        q_head = jnp.where(first if head == 0 else ~first, q, zero)
        v_head = jnp.where(first_v if head == 0 else ~first_v, v, one)
        s = mm_nt(q_head, k)
        s = (s - jnp.max(s, axis=-1, keepdims=True)) * score_scale
        outs.append(mm(jnp.exp(s).astype(bf16), v_head))
    value = jnp.where(first, outs[0], outs[1])
    total = pltpu.roll(jnp.where(first, outs[1], outs[0]), HD, 1)
    return (value / total).astype(bf16)


def attend_kernel(q_ref, k_ref, v_ref, o_ref):
    o_ref[...] = attend(q_ref[...], k_ref[...], v_ref[...])


def attend_masked_kernel(rows_ref, x_ref, q_ref, k_ref, v_ref, o_ref, qm_ref, xm_ref):
    window = x_ref.shape[0]
    count = rows_ref.shape[1]
    pick = (
        lax.broadcasted_iota(jnp.int32, (count, window), 1) == rows_ref[0]
    ).astype(bf16)
    xm_ref[...] = mm(pick, x_ref[...]).astype(bf16)
    qm = mm(pick, q_ref[...]).astype(bf16)
    qm_ref[...] = qm
    for pair in range(q_ref.shape[1] // 128):
        lanes = slice(pair * 128, pair * 128 + 128)
        o_ref[:, lanes] = attend(qm[:, lanes], k_ref[:, lanes], v_ref[:, lanes])


def ffn_masked_kernel(
    parts, xm_ref, cot_ref, gains_ref, wg_ref, wu_ref, wd_ref, *refs
):
    o_refs, wo_refs = refs[:parts], refs[parts : 2 * parts]
    rm_ref, dhf_ref, grad_ref, hf_ref, acc_ref, wide_ref = refs[2 * parts :]
    step = pl.program_id(0)
    width = wg_ref.shape[1]
    cols = pl.ds(pl.multiple_of(step * width, width), width)
    hidden, model = grad_ref.shape[1:]
    fold = model // hidden

    def put(part, grad):
        if fold == 1:
            grad_ref[part, :, cols] = grad.astype(bf16)
            return
        for block in range(width // 128):
            wide_ref[block] = grad[:, block * 128 : (block + 1) * 128]
            for piece in range(fold):
                at = piece * hidden + step * width + block * 128
                at = pl.ds(pl.multiple_of(at, 128), 128)
                grad_ref[part, :, at] = wide_ref[
                    block, pl.ds(piece, hidden, stride=fold), :
                ].astype(bf16)

    @pl.when(step == 0)
    def _():
        r = xm_ref[...].astype(f32)
        for o_ref, wo_ref in zip(o_refs, wo_refs):
            r = r + mm(o_ref[...], wo_ref[...])
        rm_ref[...] = r
        hf_ref[...] = (r * rms_scale(r) * gains_ref[1:2, :]).astype(bf16)
        acc_ref[...] = jnp.zeros_like(acc_ref)

    hf, dy = hf_ref[...], cot_ref[...]
    wg, wu, wd = wg_ref[...], wu_ref[...], wd_ref[...]
    g, u = mm(hf, wg), mm(hf, wu)
    sig = jax.nn.sigmoid(g)
    act = (g * sig * u).astype(bf16)
    grad_ref[2, cols, :] = mm_tn(act, dy).astype(bf16)
    da = mm_nt(dy, wd)
    dg = (da * u * sig * (1.0 + g * (1.0 - sig))).astype(bf16)
    du = (da * g * sig).astype(bf16)
    put(0, mm_tn(hf, dg))
    put(1, mm_tn(hf, du))
    acc_ref[...] += mm_nt(dg, wg) + mm_nt(du, wu)

    @pl.when(step == pl.num_programs(0) - 1)
    def _():
        dhf_ref[...] = acc_ref[...].astype(bf16)


def far_start(place, parts, share):
    return jnp.where(place < parts // 2, share, 0)


def ffn_kernel(parts, place_ref, x_ref, gains_ref, wg_ref, wu_ref, wd_ref, *refs):
    o_refs, wo_refs = refs[:parts], refs[parts : 2 * parts]
    part_ref, ship_ref, own_ref, r_ref, hf_ref, acc_ref = refs[2 * parts :]
    step = pl.program_id(0)

    @pl.when(step == 0)
    def _():
        r = x_ref[...].astype(f32)
        for o_ref, wo_ref in zip(o_refs, wo_refs):
            r = r + mm(o_ref[...], wo_ref[...])
        r_ref[...] = r
        hf_ref[...] = (r * rms_scale(r) * gains_ref[1:2, :]).astype(bf16)
        acc_ref[...] = jnp.zeros_like(acc_ref)

    hf = hf_ref[...]
    g, u = mm(hf, wg_ref[...]), mm(hf, wu_ref[...])
    act = (g * jax.nn.sigmoid(g) * u).astype(bf16)
    acc_ref[...] += mm(act, wd_ref[...])

    @pl.when(step == pl.num_programs(0) - 1)
    def _():
        share = own_ref.shape[0]
        part_ref[...] = acc_ref[...].astype(bf16)
        far = pl.ds(pl.multiple_of(far_start(place_ref[0], parts, share), share), ship_ref.shape[0])
        ship_ref[...] = part_ref[far, :]
        mine = pl.ds(pl.multiple_of(place_ref[0] * share, share), share)
        own_ref[...] = r_ref[mine, :] + acc_ref[mine, :]


def attn_back_kernel(
    rows_ref,
    dhf_ref,
    rm_ref,
    cot_ref,
    gains_ref,
    om_ref,
    qm_ref,
    cosm_ref,
    sinm_ref,
    k_ref,
    v_ref,
    x_ref,
    cos_ref,
    sin_ref,
    wo_ref,
    w_ref,
    drm_ref,
    dha_ref,
    gw_ref,
    gain_ref,
    gw_acc,
    go_acc,
    gain_acc,
    flow_ref,
    gw_wide,
):
    step = pl.program_id(0)

    @pl.when(step == 0)
    def _():
        gw_acc[...] = jnp.zeros_like(gw_acc)
        go_acc[...] = jnp.zeros_like(go_acc)
        gain_acc[...] = jnp.zeros_like(gain_acc)

    window, width = k_ref.shape
    count = rm_ref.shape[0]
    r = rm_ref[...]
    sf = rms_scale(r)
    nf = r * sf
    dhf = dhf_ref[...].astype(f32)
    dnf = dhf * gains_ref[1:2, :]
    dr = cot_ref[...].astype(f32) + sf * (
        dnf - nf * jnp.mean(dnf * nf, axis=-1, keepdims=True)
    )
    drm_ref[...] = dr
    gain_acc[1:2, :] += jnp.sum(dhf * nf, axis=0, keepdims=True)
    drb = dr.astype(bf16)
    go_acc[...] += mm_tn(om_ref[...], drb)
    dob = mm_nt(drb, wo_ref[...]).astype(bf16)

    first = lax.broadcasted_iota(jnp.int32, (count, 128), 1) < HD
    zero = jnp.zeros((), bf16)
    drq = []
    for pair in range(width // 128):
        lanes = slice(pair * 128, pair * 128 + 128)
        k, v = k_ref[:, lanes], v_ref[:, lanes]
        qm, do = qm_ref[:, lanes], dob[:, lanes]
        parts = []
        drk = dv = None
        for head in range(2):
            mine = first if head == 0 else ~first
            q_head = jnp.where(mine, qm, zero)
            do_head = jnp.where(mine, do, zero)
            s = mm_nt(k, q_head)
            s = jnp.exp((s - jnp.max(s, axis=0, keepdims=True)) * score_scale)
            att = s / jnp.sum(s, axis=0, keepdims=True)
            dpa = mm_nt(v, do_head)
            ds = att * (dpa - jnp.sum(dpa * att, axis=0, keepdims=True))
            ds = (ds * score_scale).astype(bf16)
            parts.append(mm_tn(ds, k))
            drk_head = mm(ds, q_head)
            dv_head = mm(att.astype(bf16), do_head)
            drk = drk_head if drk is None else drk + drk_head
            dv = dv_head if dv is None else dv + dv_head
        drq.append(jnp.where(first, parts[0], parts[1]))
        dk = drk * cos_ref[:, lanes] - swap_halves(drk) * sin_ref[:, lanes]
        flow_ref[:, width + pair * 128 : width + pair * 128 + 128] = dk.astype(bf16)
        flow_ref[:, 2 * width + pair * 128 : 2 * width + pair * 128 + 128] = dv.astype(
            bf16
        )
    spread = (
        lax.broadcasted_iota(jnp.int32, (window, count), 0) == rows_ref[0]
    ).astype(bf16)
    for pair in range(width // 128):
        lanes = slice(pair * 128, pair * 128 + 128)
        dq = drq[pair] * cosm_ref[:, lanes] - swap_halves(drq[pair]) * sinm_ref[:, lanes]
        flow_ref[:, lanes] = mm(spread, dq.astype(bf16)).astype(bf16)

    flow = flow_ref[...]
    x = x_ref[...].astype(f32)
    na = x * rms_scale(x)
    dha = mm_nt(flow, w_ref[...])
    gain_acc[0:1, :] += jnp.sum(dha * na, axis=0, keepdims=True)
    cuts, shares, rows = dha_ref.shape[:3]
    for piece in range(window // rows):
        block = step * (window // rows) + piece
        dha_ref[block % cuts, block // cuts] = dha[piece * rows : (piece + 1) * rows].astype(bf16)
    gw_acc[...] += mm_tn((na * gains_ref[0:1, :]).astype(bf16), flow)

    @pl.when(step == pl.num_programs(0) - 1)
    def _():
        fold = gw_acc.shape[0] // width
        for block in range(3 * width // 128):
            part, lane = divmod(block * 128, width)
            gw_wide[block] = gw_acc[:, block * 128 : (block + 1) * 128]
            for piece in range(fold):
                at = piece * width + lane
                gw_ref[part * width : (part + 1) * width, at : at + 128] = gw_wide[
                    block, pl.ds(piece, width, stride=fold), :
                ].astype(bf16)
        gw_ref[3 * width :, :] = go_acc[...].astype(bf16)
        gain_ref[...] = gain_acc[...]


def input_grad_kernel(
    cut, place_ref, rows_ref, drm_ref, gains_ref, x_ref, part_ref, *refs
):
    out_ref = refs[-1]
    block, count = x_ref.shape[0], drm_ref.shape[0]
    base = (place_ref[0] * cut[1] + cut[0]) * block
    spread = (
        lax.broadcasted_iota(jnp.int32, (block, count), 0) + base == rows_ref[...]
    ).astype(bf16)
    dr = drm_ref[...]
    high = dr.astype(bf16)
    low = (dr - high.astype(f32)).astype(bf16)
    dr = mm(spread, high) + mm(spread, low)
    x = x_ref[...].astype(f32)
    sa = rms_scale(x)
    na = x * sa
    dha = part_ref[0, 0].astype(f32)
    for ref in refs[: cut[2]]:
        dha = dha + ref[...].astype(f32)
    dna = dha * gains_ref[0:1, :]
    out = dr + sa * (dna - na * jnp.mean(dna * na, axis=-1, keepdims=True))
    out_ref[...] = out.astype(bf16)


def input_grad_rows(dha, x, dr, gain, spread):
    high = dr.astype(bf16)
    low = (dr - high.astype(f32)).astype(bf16)
    dr = mm(spread, high) + mm(spread, low)
    sa = rms_scale(x)
    na = x * sa
    dna = dha * gain
    return dr + sa * (dna - na * jnp.mean(dna * na, axis=-1, keepdims=True))


def remote(src, dst, send, recv, place):
    return pltpu.make_async_remote_copy(
        src_ref=src,
        dst_ref=dst,
        send_sem=send,
        recv_sem=recv,
        device_id={"tensor": place},
        device_id_type=pl.DeviceIdType.MESH,
    )


def greet_line(place):
    barrier = pltpu.get_barrier_semaphore()
    for k in range(1, 4):
        pl.semaphore_signal(
            barrier,
            inc=1,
            device_id={"tensor": lax.rem(place + k, 4)},
            device_id_type=pl.DeviceIdType.MESH,
        )
    pl.semaphore_wait(barrier, 3)


def rows_ref(ref, index, share, count):
    return ref.at[pl.ds(pl.multiple_of(index * share, share), count * share), :]


def lines_kernel(
    cuts, windows, order, rows_in, drm_ref, gains_ref, x_ref, dha_ref, *refs
):
    part_refs, own_refs = refs[:windows], refs[windows : 2 * windows]
    (
        out_ref,
        grad_ref,
        ra,
        rb,
        rc,
        value,
        own,
        piece,
        x_rows,
        grad,
        a_send,
        a_recv,
        b_send,
        b_recv,
        c_send,
        c_recv,
        g_send,
        g_recv,
        v_sem,
        o_sem,
        x_sem,
        l_sem,
        i_sem,
    ) = refs[2 * windows :]
    place = lax.axis_index("tensor")
    lower = place < 2
    outer = (place == 0) | (place == 3)
    inner = (place == 1) | (place == 2)
    share = rc.shape[1]
    folds = len(order)

    def whole(f):
        kind, index = order[f]
        return part_refs[index] if kind == 0 else dha_ref.at[index]

    def copy_a(f):
        far = rows_ref(whole(f), jnp.where(lower, 1, 0), share, 3)
        return remote(far, ra.at[f], a_send.at[f], a_recv.at[f], jnp.where(lower, 1, 2))

    def copy_b(f):
        src = rows_ref(ra.at[f], jnp.where(lower, 1, 0), share, 2)
        return remote(src, rb.at[f], b_send.at[f], b_recv.at[f], jnp.where(lower, 2, 1))

    def copy_c(f):
        src = rows_ref(rb.at[f], jnp.where(lower, 0, 1), share, 1)
        return remote(src, rc.at[f], c_send.at[f], c_recv.at[f], jnp.where(lower, 0, 3))

    def load(f):
        return pltpu.make_async_copy(whole(f), value.at[f], v_sem.at[f])

    def load_own(w):
        return pltpu.make_async_copy(own_refs[w], own.at[w], o_sem.at[w])

    def copy_g(w, k, origin):
        rows = pl.ds(pl.multiple_of(w * 4 * share + origin * share, share), share)
        return remote(
            piece.at[w],
            out_ref.at[rows, :],
            g_send.at[w, k - 1],
            g_recv.at[w, k - 1],
            lax.rem(place + k, 4),
        )

    def keep(w):
        rows = pl.ds(pl.multiple_of(w * 4 * share + place * share, share), share)
        return pltpu.make_async_copy(piece.at[w], out_ref.at[rows, :], l_sem.at[w])

    def store(c):
        return pltpu.make_async_copy(
            grad.at[c], grad_ref.at[pl.ds(c * share, share), :], i_sem.at[c]
        )

    x_load = pltpu.make_async_copy(
        rows_ref(x_ref, place * cuts, share, cuts), x_rows, x_sem
    )

    for f in range(folds):
        load(f).start()
    for w in range(windows):
        load_own(w).start()
    x_load.start()
    greet_line(place)

    @pl.when(outer)
    def _():
        for f in range(2):
            copy_a(f).start()

    def add_rows(buffer, at, f, index):
        rows = pl.ds(pl.multiple_of(at * share, share), share)
        mine = pl.ds(pl.multiple_of(index * share, share), share)
        total = buffer[f, rows, :].astype(f32) + value[f, mine, :].astype(f32)
        buffer[f, rows, :] = total.astype(bf16)

    def finish(f, terms):
        kind, index = order[f]
        if kind == 0:
            load_own(index).wait()
            total = own[index]
        else:
            mine = pl.ds(pl.multiple_of(place * share, share), share)
            total = value[f, mine, :].astype(f32)
        for term in terms:
            total = total + term.astype(f32)
        if kind == 0:
            piece[index] = total.astype(bf16)
            for k in range(1, 4):
                copy_g(index, k, place).start()
            keep(index).start()
        else:
            first = place * (cuts * share) + index * share
            count = drm_ref.shape[0]
            spread = (
                lax.broadcasted_iota(jnp.int32, (share, count), 0) + first == rows_in[...]
            ).astype(bf16)
            x = x_rows[pl.ds(index * share, share), :].astype(f32)
            grad[index] = input_grad_rows(
                total, x, drm_ref[...], gains_ref[0:1, :], spread
            ).astype(bf16)
            store(index).start()

    for f in range(folds):
        load(f).wait()
    x_load.wait()
    for step in range(folds + 1):

        @pl.when(inner)
        def _():
            if step < folds:
                copy_a(step).wait_recv()
                for n in range(2):
                    add_rows(
                        ra, jnp.where(lower, 1, 0) + n, step, jnp.where(lower, 2, 0) + n
                    )
                copy_b(step).start()
            if step > 0:
                f = step - 1
                copy_b(f).wait_recv()
                add_rows(rb, jnp.where(lower, 0, 1), f, jnp.where(lower, 0, 3))
                copy_c(f).start()

        if step > 0:
            f = step - 1

            @pl.when(outer)
            def _():
                copy_c(f).wait_recv()
                finish(f, [rc[f]])

            @pl.when(inner)
            def _():
                sel_a = pl.ds(pl.multiple_of(jnp.where(lower, 0, 2) * share, share), share)
                sel_b = pl.ds(pl.multiple_of(jnp.where(lower, 1, 0) * share, share), share)
                finish(f, [ra[f, sel_a, :], rb[f, sel_b, :]])

        @pl.when(outer)
        def _():
            if step < folds:
                copy_a(step).wait_send()
            if step + 2 < folds:
                copy_a(step + 2).start()

    @pl.when(inner)
    def _():
        for f in range(folds):
            copy_b(f).wait_send()
            copy_c(f).wait_send()

    for w in range(windows):
        keep(w).wait()
        for k in range(1, 4):
            copy_g(w, k, place).wait_send()
            copy_g(w, k, lax.rem(place + 4 - k, 4)).wait_recv()
    for c in range(cuts):
        store(c).wait()


def place_kernel(place_ref, *refs):
    out_ref = refs[-1]
    parts = lax.axis_size("tensor")
    share = refs[0].shape[0]
    for step in range(parts):
        origin = lax.rem(place_ref[0] + parts - step, parts)
        out_ref[pl.ds(pl.multiple_of(origin * share, share), share), :] = refs[step][...]


def copy_kernel(in_ref, out_ref):
    out_ref[...] = in_ref[...]


def collect_kernel(slot_ref, *refs):
    out_ref = refs[-1]
    for index, ref in enumerate(refs[:-1]):
        out_ref[index] = ref[0]


def exchange(value, axis, bit):
    size = lax.axis_size(axis)
    return lax.ppermute(value, axis, [(i, i ^ bit) for i in range(size)])


def dp_total(value):
    size = lax.axis_size("dp")
    value = value + exchange(value, "dp", 1)
    bits = []
    bit = 2
    while bit < size:
        bits.append(bit)
        bit *= 2
    core = lax.axis_index("dp") % 2
    half = value.shape[0] // 2
    mine = lax.dynamic_slice_in_dim(value, core * half, half, 0)
    cut = half // 2
    low, high = mine[:cut], mine[cut:]
    for bit_low, bit_high in zip(bits, bits[::-1]):
        low = low + exchange(low, "dp", bit_low)
        high = high + exchange(high, "dp", bit_high)
    mine = jnp.concatenate([low, high], axis=0)
    other = exchange(mine, "dp", 1)
    return jnp.where(
        core == 0,
        jnp.concatenate([mine, other], axis=0),
        jnp.concatenate([other, mine], axis=0),
    )


def around(value):
    size = lax.axis_size("tensor")
    return [value] + [
        lax.ppermute(value, "tensor", [(i, (i + k) % size) for i in range(size)])
        for k in range(1, size)
    ]


def rows_at(value, index, share, count):
    return lax.dynamic_slice_in_dim(value, index * share, count * share, 0)


def line_sums(value, ship, share):
    place = lax.axis_index("tensor")
    lower = place < 2
    first = lax.ppermute(ship, "tensor", [(0, 1), (3, 2)])
    send = rows_at(value, jnp.where(lower, 2, 0), share, 2).astype(f32)
    send = send + rows_at(first, jnp.where(lower, 1, 0), share, 2).astype(f32)
    second = lax.ppermute(send.astype(bf16), "tensor", [(1, 2), (2, 1)])
    send = rows_at(value, jnp.where(lower, 0, 3), share, 1).astype(f32)
    send = send + rows_at(second, jnp.where(lower, 0, 1), share, 1).astype(f32)
    third = lax.ppermute(send.astype(bf16), "tensor", [(1, 0), (2, 3)])
    return (
        rows_at(first, jnp.where(lower, 0, 2), share, 1),
        rows_at(second, jnp.where(lower, 1, 0), share, 1),
        third,
    )


def other_sums(value, ship, share):
    if lax.axis_size("tensor") == 4:
        return line_sums(value, ship, share)
    place = lax.axis_index("tensor")
    total = lax.psum_scatter(value, "tensor", scatter_dimension=0, tiled=True)
    own = rows_at(value, place, share, 1).astype(f32)
    return (total.astype(f32) - own,)


def small_total(value):
    for axis in ("dp", "tensor"):
        bit = 1
        while bit < lax.axis_size(axis):
            value = value + exchange(value, axis, bit)
            bit *= 2
    return value


def slot_ranks(owner_row):
    count_all = owner_row.shape[0]
    tile_order = jnp.arange(count_all, dtype=jnp.int32)
    earlier = (owner_row[:, None] == owner_row[None, :]) & (
        tile_order[None, :] < tile_order[:, None]
    )
    return jnp.sum(earlier.astype(jnp.int32), axis=1)


def adam_update(grad_now, first_old, second_old, param_old, rate, decay):
    first_new = beta_one * first_old + (1.0 - beta_one) * grad_now
    second_new = beta_two * second_old + (1.0 - beta_two) * grad_now * grad_now
    first_hat = first_new / (1.0 - beta_one**STEP)
    second_hat = second_new / (1.0 - beta_two**STEP)
    param_new = param_old - rate * (
        first_hat / (jnp.sqrt(second_hat) + adam_eps) + decay * param_old
    )
    return (first_new, second_new, param_new)


def head_tables(positions, heads):
    frequency = jnp.exp(
        -jnp.log(10000.0) * (2.0 * jnp.arange(HD // 2, dtype=f32) / HD)
    )
    angles = positions.astype(f32)[..., None] * frequency
    cos, sin = jnp.cos(angles), jnp.sin(angles)
    cos = jnp.concatenate([cos, cos], axis=-1)
    sin = jnp.concatenate([-sin, sin], axis=-1)
    reps = (1,) * (cos.ndim - 1) + (heads,)
    return jnp.tile(cos, reps), jnp.tile(sin, reps)


def on_device(
    tokens,
    masked_rows,
    cotangent,
    norm_gains,
    gain_first,
    gain_second,
    owners,
    master,
    first_moment,
    second_moment,
):
    seq_count, mask_count = masked_rows.shape
    total_rows, model = tokens.shape
    window = total_rows // seq_count
    parts = lax.axis_size("tensor")
    place = lax.axis_index("tensor")
    owner_self = lax.axis_index("dp")
    heads = HEADS // parts
    width = heads * HD
    hidden = FF // parts
    capacity, tile_rows = master.shape[1:3]
    tile_size = tile_rows * model
    attn_tiles = 4 * model * width // tile_size
    ffn_tiles = 3 * model * hidden // tile_size
    count = -(-mask_count // 16) * 16
    place_ref = place.astype(jnp.int32).reshape(1)

    owner_row = owners[0]
    slot_rank = slot_ranks(owner_row)
    slot_index = owner_row * capacity + slot_rank
    slot_match = (owner_row[None, :] == owner_self) & (
        slot_rank[None, :] == jnp.arange(capacity, dtype=jnp.int32)[:, None]
    )
    slot_used = jnp.any(slot_match, axis=1)[:, None, None]
    slot_tile = jnp.argmax(slot_match, axis=1)

    tile_block = (1, tile_rows, model)
    grid_size = max(capacity, attn_tiles)
    low_slots, attn_mine = pl.pallas_call(
        cast_kernel,
        out_shape=[
            jax.ShapeDtypeStruct((capacity, tile_rows, model), bf16),
            jax.ShapeDtypeStruct((attn_tiles, tile_rows, model), bf16),
        ],
        grid_spec=pltpu.PrefetchScalarGridSpec(
            num_scalar_prefetch=2,
            grid=(grid_size,),
            in_specs=[
                pl.BlockSpec(
                    tile_block, lambda i, rank, held: (jnp.minimum(i, capacity - 1), 0, 0)
                ),
                pl.BlockSpec(
                    tile_block,
                    lambda i, rank, held: (rank[jnp.minimum(i, attn_tiles - 1)], 0, 0),
                ),
            ],
            out_specs=[
                pl.BlockSpec(
                    tile_block, lambda i, rank, held: (jnp.minimum(i, capacity - 1), 0, 0)
                ),
                pl.BlockSpec(
                    tile_block, lambda i, rank, held: (jnp.minimum(i, attn_tiles - 1), 0, 0)
                ),
            ],
        ),
        compiler_params=params(),
        cost_estimate=cost(0, 12 * capacity * tile_size),
        name="cast",
    )(
        slot_rank,
        jnp.pad(
            (owner_row[:attn_tiles] == owner_self).astype(jnp.int32),
            (0, grid_size - attn_tiles),
            mode="edge",
        ),
        master[0],
        master[0],
    )
    attn_flat = dp_total(attn_mine).reshape(4 * width, model)
    w_out = attn_flat[3 * width :]
    every_slot = lax.all_gather(low_slots, "dp", axis=0, tiled=True)
    w_outs = around(w_out)

    cos, sin = head_tables(jnp.arange(window), heads)
    rows = jnp.pad(masked_rows, ((0, 0), (0, count - mask_count)), constant_values=-1)
    cos_m, sin_m = head_tables(rows, heads)
    cot = jnp.pad(cotangent, ((0, 0), (0, count - mask_count), (0, 0)))
    cot = cot.reshape(seq_count * count, model)
    cos_m = cos_m.reshape(seq_count * count, width)
    sin_m = sin_m.reshape(seq_count * count, width)

    block = min(512, window)
    per_window = window // block
    row_block = pl.BlockSpec((block, model), lambda i: (i, 0))
    head_block = pl.BlockSpec((block, width), lambda i: (i, 0))
    table_block = pl.BlockSpec((block, width), lambda i: (i % per_window, 0))
    q, k, v, w_qkv = pl.pallas_call(
        qkv_kernel,
        out_shape=[jax.ShapeDtypeStruct((total_rows, width), bf16)] * 3
        + [jax.ShapeDtypeStruct((model, 3 * width), bf16)],
        grid=(total_rows // block,),
        in_specs=[
            row_block,
            whole_spec((2, model)),
            whole_spec((3 * width, model)),
            table_block,
            table_block,
        ],
        out_specs=[head_block] * 3 + [whole_spec((model, 3 * width))],
        scratch_shapes=[pltpu.VMEM((3 * width // 128, model, 128), f32)],
        compiler_params=params(),
        cost_estimate=cost(6 * total_rows * model * width, 2 * total_rows * model * 2),
        name="qkv",
    )(tokens, norm_gains, attn_flat, cos, sin)

    win_model = pl.BlockSpec((window, model), lambda i: (i, 0))
    win_head = pl.BlockSpec((window, width), lambda i: (i, 0))
    mask_model = pl.BlockSpec((count, model), lambda i: (i, 0))
    mask_head = pl.BlockSpec((count, width), lambda i: (i, 0))
    o_m, q_m, x_m = pl.pallas_call(
        attend_masked_kernel,
        out_shape=[
            jax.ShapeDtypeStruct((seq_count * count, width), bf16),
            jax.ShapeDtypeStruct((seq_count * count, width), bf16),
            jax.ShapeDtypeStruct((seq_count * count, model), bf16),
        ],
        grid=(seq_count,),
        in_specs=[
            pl.BlockSpec((1, count, 1), lambda i: (i, 0, 0)),
            win_model,
            win_head,
            win_head,
            win_head,
        ],
        out_specs=[mask_head, mask_head, mask_model],
        compiler_params=params(),
        cost_estimate=cost(
            seq_count * count * window * (2 * model + 8 * width), 9e6, seq_count * count * window * heads
        ),
        name="attend_masked",
    )(rows[:, :, None], tokens, q, k, v)
    o_ms = around(o_m)

    q_block = min(256, window)

    def attend_window(w, before):
        return pl.pallas_call(
            after(attend_kernel, 3, 1),
            out_shape=jax.ShapeDtypeStruct((window, width), bf16),
            grid=(width // 128, window // q_block),
            in_specs=[
                pl.BlockSpec((q_block, 128), lambda p, i: (w * (window // q_block) + i, p)),
                pl.BlockSpec((window, 128), lambda p, i: (w, p)),
                pl.BlockSpec((window, 128), lambda p, i: (w, p)),
                UNREAD,
            ],
            out_specs=pl.BlockSpec((q_block, 128), lambda p, i: (i, p)),
            compiler_params=params(),
            cost_estimate=cost(
                16 * window * window * width, 4 * window * width * 2, window * window * heads
            ),
            name="attend",
        )(q, k, v, before)

    early = max(seq_count - 1, 1)
    o_own = []
    for w in range(early):
        o_own.append(attend_window(w, o_own[-1] if o_own else o_m))

    group = 4
    ffn_all = pl.pallas_call(
        after(collect_kernel, 1 + group, 1),
        out_shape=jax.ShapeDtypeStruct((ffn_tiles, tile_rows, model), bf16),
        grid_spec=pltpu.PrefetchScalarGridSpec(
            num_scalar_prefetch=1,
            grid=(ffn_tiles // group,),
            in_specs=[
                pl.BlockSpec(
                    tile_block,
                    lambda i, slot, n=n: (slot[attn_tiles + i * group + n], 0, 0),
                )
                for n in range(group)
            ]
            + [UNREAD],
            out_specs=pl.BlockSpec((group, tile_rows, model), lambda i, slot: (i, 0, 0)),
        ),
        compiler_params=params(),
        cost_estimate=cost(0, 4 * ffn_tiles * tile_size),
        name="collect",
    )(slot_index, *[every_slot] * group, o_own[-1])
    ffn_flat = ffn_all.reshape(3, -1)
    w_gate = ffn_flat[0].reshape(model, hidden)
    w_up = ffn_flat[1].reshape(model, hidden)
    w_down = ffn_flat[2].reshape(hidden, model)

    mask_rows = seq_count * count
    cols = min(256, hidden)
    col_block = pl.BlockSpec((model, cols), lambda c: (0, c))
    down_block = pl.BlockSpec((cols, model), lambda c: (c, 0))
    r_m, dhf_part, ffn_grad = pl.pallas_call(
        functools.partial(ffn_masked_kernel, parts),
        out_shape=[
            jax.ShapeDtypeStruct((mask_rows, model), f32),
            jax.ShapeDtypeStruct((mask_rows, model), bf16),
            jax.ShapeDtypeStruct((3, hidden, model), bf16),
        ],
        grid=(hidden // cols,),
        in_specs=[
            whole_spec((mask_rows, model)),
            whole_spec((mask_rows, model)),
            whole_spec((2, model)),
            col_block,
            col_block,
            down_block,
        ]
        + [whole_spec((mask_rows, width))] * parts
        + [whole_spec((width, model))] * parts,
        out_specs=[
            whole_spec((mask_rows, model)),
            whole_spec((mask_rows, model)),
            whole_spec((3, hidden, model)),
        ],
        scratch_shapes=[
            pltpu.VMEM((mask_rows, model), bf16),
            pltpu.VMEM((mask_rows, model), f32),
            pltpu.VMEM((cols // 128, model, 128), f32),
        ],
        compiler_params=params(),
        cost_estimate=cost(
            mask_rows * model * (18 * hidden + 2 * model), 20e6, mask_rows * hidden
        ),
        name="ffn_masked",
    )(x_m, cot, norm_gains, w_gate, w_up, w_down, *o_ms, *w_outs)

    for w in range(early, seq_count):
        o_own.append(attend_window(w, r_m))
    windows_o = [around(o) for o in o_own]

    share_m = mask_rows // parts
    dhf_mine = lax.dynamic_slice_in_dim(dhf_part, place * share_m, share_m, 0).astype(f32)
    for step in range(1, parts):
        send = lax.dynamic_slice_in_dim(
            dhf_part, lax.rem(place + step, parts) * share_m, share_m, 0
        )
        dhf_mine = dhf_mine + lax.ppermute(
            send, "tensor", [(i, (i + step) % parts) for i in range(parts)]
        ).astype(f32)
    dhf_all = around(dhf_mine.astype(bf16))
    dhf = jnp.zeros((mask_rows, model), bf16)
    for step, piece in enumerate(dhf_all):
        origin = lax.rem(place + parts - step, parts)
        dhf = lax.dynamic_update_slice_in_dim(dhf, piece, origin * share_m, 0)

    share = window // parts
    far = share * (parts - 1)
    layer_out = None

    def ffn_window(w, before):
        return pl.pallas_call(
            after(functools.partial(ffn_kernel, parts), 6 + 2 * parts, 1),
            out_shape=[
                jax.ShapeDtypeStruct((window, model), bf16),
                jax.ShapeDtypeStruct((far, model), bf16),
                jax.ShapeDtypeStruct((share, model), f32),
            ],
            grid_spec=pltpu.PrefetchScalarGridSpec(
                num_scalar_prefetch=1,
                grid=(hidden // cols,),
                in_specs=[
                    pl.BlockSpec((window, model), lambda c, place_ref: (w, 0)),
                    whole_spec((2, model)),
                    pl.BlockSpec((model, cols), lambda c, place_ref: (0, c)),
                    pl.BlockSpec((model, cols), lambda c, place_ref: (0, c)),
                    pl.BlockSpec((cols, model), lambda c, place_ref: (c, 0)),
                ]
                + [whole_spec((window, width))] * parts
                + [whole_spec((width, model))] * parts
                + [UNREAD],
                out_specs=[
                    whole_spec((window, model)),
                    whole_spec((far, model)),
                    whole_spec((share, model)),
                ],
                scratch_shapes=[
                    pltpu.VMEM((window, model), f32),
                    pltpu.VMEM((window, model), bf16),
                    pltpu.VMEM((window, model), f32),
                ],
            ),
            compiler_params=params(),
            cost_estimate=cost(
                window * model * (6 * hidden + 2 * model), 16e6, window * hidden
            ),
            name="ffn",
        )(
            place_ref,
            tokens,
            norm_gains,
            w_gate,
            w_up,
            w_down,
            *windows_o[w],
            *w_outs,
            before,
        )

    def place_window(w, part, ship, own):
        terms = other_sums(part, ship, share)
        total = own
        for term in terms:
            total = total + term.astype(f32)
        pieces = around(total.astype(bf16))
        return pl.pallas_call(
            after(place_kernel, 1 + parts, 0 if layer_out is None else 1),
            out_shape=jax.ShapeDtypeStruct((total_rows, model), bf16),
            grid_spec=pltpu.PrefetchScalarGridSpec(
                num_scalar_prefetch=1,
                grid=(1,),
                in_specs=[whole_spec((share, model))] * parts
                + [UNREAD] * (layer_out is not None),
                out_specs=pl.BlockSpec((window, model), lambda i, place_ref: (w, 0)),
            ),
            input_output_aliases={} if layer_out is None else {1 + parts: 0},
            compiler_params=params(),
            cost_estimate=cost(0, 4 * window * model),
            name="place",
        )(place_ref, *pieces, *([] if layer_out is None else [layer_out]))

    parts_out = [ffn_window(0, o_own[-1])]

    share_rows = total_rows // parts
    cuts = seq_count if share_rows % (16 * seq_count) == 0 else 1
    cut_rows = share_rows // cuts
    dr_m, dha, attn_grad, gains_part = pl.pallas_call(
        after(attn_back_kernel, 16, 1),
        out_shape=[
            jax.ShapeDtypeStruct((mask_rows, model), f32),
            jax.ShapeDtypeStruct((cuts, parts, cut_rows, model), bf16),
            jax.ShapeDtypeStruct((4 * width, model), bf16),
            jax.ShapeDtypeStruct((2, model), f32),
        ],
        grid=(seq_count,),
        in_specs=[
            pl.BlockSpec((1, 1, count), lambda i: (i, 0, 0)),
            mask_model,
            mask_model,
            mask_model,
            whole_spec((2, model)),
            mask_head,
            mask_head,
            mask_head,
            mask_head,
            win_head,
            win_head,
            win_model,
            whole_spec((window, width)),
            whole_spec((window, width)),
            whole_spec((width, model)),
            whole_spec((model, 3 * width)),
            UNREAD,
        ],
        out_specs=[
            mask_model,
            whole_spec((cuts, parts, cut_rows, model)),
            whole_spec((4 * width, model)),
            whole_spec((2, model)),
        ],
        scratch_shapes=[
            pltpu.VMEM((model, 3 * width), f32),
            pltpu.VMEM((width, model), f32),
            pltpu.VMEM((2, model), f32),
            pltpu.VMEM((window, 3 * width), bf16),
            pltpu.VMEM((3 * width // 128, model, 128), f32),
        ],
        compiler_params=params(),
        cost_estimate=cost(
            12 * total_rows * model * width, 30e6, mask_rows * window * heads
        ),
        name="attn_back",
    )(
        rows[:, None, :],
        dhf,
        r_m,
        cot,
        norm_gains,
        o_m,
        q_m,
        cos_m,
        sin_m,
        k,
        v,
        tokens,
        cos,
        sin,
        w_out,
        w_qkv,
        parts_out[0][0],
    )

    for w in range(1, seq_count):
        parts_out.append(ffn_window(w, gains_part if w == 1 else parts_out[-1][0]))

    flat_rows = jnp.where(
        rows >= 0, rows + window * jnp.arange(seq_count, dtype=jnp.int32)[:, None], -1
    ).reshape(1, mask_rows)
    if parts == 4 and cut_rows == share:
        order = [(kind, i) for i in range(seq_count) for kind in (0, 1)]
        folds = len(order)
        anywhere = pl.BlockSpec(memory_space=pl.ANY)
        inside = pl.BlockSpec(memory_space=pltpu.VMEM)
        dma = pltpu.SemaphoreType.DMA
        layer_out, input_grad = pl.pallas_call(
            functools.partial(lines_kernel, cuts, seq_count, order),
            out_shape=[
                jax.ShapeDtypeStruct((total_rows, model), bf16),
                jax.ShapeDtypeStruct((share_rows, model), bf16),
            ],
            in_specs=[inside] * 3 + [anywhere] * (2 + 2 * seq_count),
            out_specs=[anywhere] * 2,
            scratch_shapes=[
                pltpu.VMEM((folds, 3 * share, model), bf16),
                pltpu.VMEM((folds, 2 * share, model), bf16),
                pltpu.VMEM((folds, share, model), bf16),
                pltpu.VMEM((folds, window, model), bf16),
                pltpu.VMEM((seq_count, share, model), f32),
                pltpu.VMEM((seq_count, share, model), bf16),
                pltpu.VMEM((share_rows, model), bf16),
                pltpu.VMEM((cuts, share, model), bf16),
                dma((folds,)),
                dma((folds,)),
                dma((folds,)),
                dma((folds,)),
                dma((folds,)),
                dma((folds,)),
                dma((seq_count, 3)),
                dma((seq_count, 3)),
                dma((folds,)),
                dma((seq_count,)),
                dma,
                dma((seq_count,)),
                dma((cuts,)),
            ],
            compiler_params=params(collective_id=1, has_side_effects=True),
            cost_estimate=cost(4 * share_rows * mask_rows * model, 60e6),
            name="lines",
        )(
            flat_rows,
            dr_m,
            norm_gains,
            tokens,
            dha.reshape(cuts, window, model),
            *[outs[0] for outs in parts_out],
            *[outs[2] for outs in parts_out],
        )
    else:
        input_grad = None
        for cut in range(cuts):
            value = dha[cut].reshape(parts * cut_rows, model)
            ship = rows_at(value, jnp.where(place < parts // 2, 1, 0), cut_rows, parts - 1)
            terms = other_sums(value, ship, cut_rows)
            before = [] if input_grad is None else [input_grad]
            input_grad = pl.pallas_call(
                after(
                    functools.partial(input_grad_kernel, (cut, cuts, len(terms))),
                    6 + len(terms),
                    len(before),
                ),
                out_shape=jax.ShapeDtypeStruct((share_rows, model), bf16),
                grid_spec=pltpu.PrefetchScalarGridSpec(
                    num_scalar_prefetch=1,
                    grid=(1,),
                    in_specs=[
                        whole_spec((1, mask_rows)),
                        whole_spec((mask_rows, model)),
                        whole_spec((2, model)),
                        pl.BlockSpec(
                            (cut_rows, model),
                            lambda i, place_ref, cut=cut: (place_ref[0] * cuts + cut, 0),
                        ),
                        pl.BlockSpec(
                            (1, 1, cut_rows, model),
                            lambda i, place_ref, cut=cut: (cut, place_ref[0], 0, 0),
                        ),
                    ]
                    + [whole_spec((cut_rows, model))] * len(terms)
                    + [UNREAD] * len(before),
                    out_specs=pl.BlockSpec((cut_rows, model), lambda i, place_ref, cut=cut: (cut, 0)),
                ),
                input_output_aliases={6 + len(terms): 0} if before else {},
                compiler_params=params(),
                cost_estimate=cost(4 * cut_rows * mask_rows * model, 6e6),
                name="input_grad",
            )(place_ref, flat_rows, dr_m, norm_gains, tokens, dha, *terms, *before)

        for w, outs in enumerate(parts_out):
            layer_out = place_window(w, *outs)

    even = jnp.array([[1.0], [1.0 / parts]], f32)
    gain_grad = small_total(gains_part * even)
    _, gain_moment, gain_new = adam_update(
        gain_grad, gain_first, gain_second, norm_gains, gain_rate, 0.0
    )

    def total_tiles(tiles, before):
        piece = lax.psum_scatter(tiles, "dp", scatter_dimension=0, tiled=True)
        piece = pl.pallas_call(
            after(copy_kernel, 1, 1),
            out_shape=jax.ShapeDtypeStruct(piece.shape, bf16),
            in_specs=[pl.BlockSpec(memory_space=pltpu.VMEM), UNREAD],
            out_specs=pl.BlockSpec(memory_space=pltpu.VMEM),
            compiler_params=params(),
            name="copy",
        )(piece, before)
        return lax.all_gather(piece, "dp", axis=0, tiled=True)

    ffn_grads = total_tiles(ffn_grad.reshape(3 * hidden, model), parts_out[1][0])
    attn_grads = total_tiles(attn_grad, parts_out[-1][0])
    tiles = jnp.concatenate([attn_grads, ffn_grads], axis=0).reshape(-1, tile_rows, model)
    reduced = tiles[slot_tile].astype(f32)
    first_new, second_new, param_new = adam_update(
        reduced, first_moment[0], second_moment[0], master[0], weight_rate, weight_decay
    )
    weight_grad = jnp.where(slot_used, reduced, 0.0)
    weight_first = jnp.where(slot_used, first_new, 0.0)
    weight_second = jnp.where(slot_used, second_new, 0.0)
    weight_master = jnp.where(slot_used, param_new, 0.0)
    weight_low = weight_master.astype(bf16)
    return (
        layer_out,
        input_grad,
        weight_grad[None],
        weight_first[None],
        weight_second[None],
        weight_master[None],
        weight_low[None],
        gain_grad,
        gain_moment,
        gain_new,
    )


def solution(mesh):
    return jax.shard_map(
        on_device,
        mesh=mesh,
        in_specs=(
            P("dp", None),
            P("dp", None),
            P("dp", None, None),
            P(),
            P(),
            P(),
            P("tensor", None),
            P("tensor", "dp", None, None),
            P("tensor", "dp", None, None),
            P("tensor", "dp", None, None),
        ),
        out_specs=(
            P("dp", None),
            P(("dp", "tensor"), None),
            P("tensor", "dp", None, None),
            P("tensor", "dp", None, None),
            P("tensor", "dp", None, None),
            P("tensor", "dp", None, None),
            P("tensor", "dp", None, None),
            P(),
            P(),
            P(),
        ),
        check_vma=False,
    )
```

```python
import functools

import jax
import jax.numpy as jnp
from jax import lax
from jax.experimental import pallas as pl
from jax.experimental.pallas import tpu as pltpu
from jax.sharding import PartitionSpec as P

HEADS = 16
HD = 64
FF = 4096
STEP = 5

norm_eps = 1e-06
beta_one = 0.9
beta_two = 0.95
adam_eps = 1e-08
weight_rate = 0.05
gain_rate = 0.8
weight_decay = 0.1

score_scale = HD ** (-0.5)
f32 = jnp.float32
bf16 = jnp.bfloat16
VMEM_LIMIT = 60 * 1024 * 1024
NT = (((1,), (1,)), ((), ()))
TN = (((0,), (0,)), ((), ()))


def mm(left, right):
    return jnp.dot(left, right, preferred_element_type=f32)


def mm_nt(left, right):
    return lax.dot_general(left, right, NT, preferred_element_type=f32)


def mm_tn(left, right):
    return lax.dot_general(left, right, TN, preferred_element_type=f32)


def params(**kw):
    return pltpu.CompilerParams(vmem_limit_bytes=VMEM_LIMIT, **kw)


def cost(flops, nbytes, transcendentals=0):
    return pl.CostEstimate(
        flops=int(flops), bytes_accessed=int(nbytes), transcendentals=int(transcendentals)
    )


def whole_spec(shape):
    return pl.BlockSpec(shape, lambda *_: (0,) * len(shape))


def after(kernel, inputs, count):
    return lambda *refs: kernel(*refs[:inputs], *refs[inputs + count :])


UNREAD = pl.BlockSpec(memory_space=pl.ANY)


def rms_scale(values):
    return lax.rsqrt(jnp.mean(values * values, axis=-1, keepdims=True) + norm_eps)


def swap_halves(values):
    width = values.shape[1]
    lane = lax.broadcasted_iota(jnp.int32, values.shape, 1)
    return jnp.where(
        lane % HD < HD // 2,
        pltpu.roll(values, width - HD // 2, 1),
        pltpu.roll(values, HD // 2, 1),
    )


def cast_kernel(rank_ref, held_ref, slot_ref, tile_ref, low_ref, mine_ref):
    low_ref[...] = slot_ref[...].astype(bf16)
    tile = tile_ref[...].astype(bf16)
    held = held_ref[pl.program_id(0)] > 0
    mine_ref[...] = jnp.where(held, tile, jnp.zeros((), bf16))


def qkv_kernel(
    x_ref, gains_ref, tiles_ref, cos_ref, sin_ref, q_ref, k_ref, v_ref, w_ref, w_wide
):
    width = q_ref.shape[1]
    model = x_ref.shape[1]
    fold = model // width

    @pl.when(pl.program_id(0) == 0)
    def _():
        for block in range(3 * width // 128):
            part, lane = divmod(block * 128, width)
            for piece in range(fold):
                at = piece * width + lane
                w_wide[block, pl.ds(piece, width, stride=fold), :] = tiles_ref[
                    part * width : (part + 1) * width, at : at + 128
                ].astype(f32)
            w_ref[:, block * 128 : (block + 1) * 128] = w_wide[block].astype(bf16)

    x = x_ref[...].astype(f32)
    hidden = (x * rms_scale(x) * gains_ref[0:1, :]).astype(bf16)
    cos, sin = cos_ref[...], sin_ref[...]
    q = mm(hidden, w_ref[:, 0:width])
    q_ref[...] = (q * cos + swap_halves(q) * sin).astype(bf16)
    k = mm(hidden, w_ref[:, width : 2 * width])
    k_ref[...] = (k * cos + swap_halves(k) * sin).astype(bf16)
    v_ref[...] = mm(hidden, w_ref[:, 2 * width : 3 * width]).astype(bf16)


def attend(q, k, v):
    first = lax.broadcasted_iota(jnp.int32, q.shape, 1) < HD
    first_v = lax.broadcasted_iota(jnp.int32, v.shape, 1) < HD
    zero, one = jnp.zeros((), bf16), jnp.ones((), bf16)
    outs = []
    for head in range(2):
        q_head = jnp.where(first if head == 0 else ~first, q, zero)
        v_head = jnp.where(first_v if head == 0 else ~first_v, v, one)
        s = mm_nt(q_head, k)
        s = (s - jnp.max(s, axis=-1, keepdims=True)) * score_scale
        outs.append(mm(jnp.exp(s).astype(bf16), v_head))
    value = jnp.where(first, outs[0], outs[1])
    total = pltpu.roll(jnp.where(first, outs[1], outs[0]), HD, 1)
    return (value / total).astype(bf16)


def attend_kernel(q_ref, k_ref, v_ref, o_ref):
    o_ref[...] = attend(q_ref[...], k_ref[...], v_ref[...])


def attend_masked_kernel(rows_ref, x_ref, q_ref, k_ref, v_ref, o_ref, qm_ref, xm_ref):
    window = x_ref.shape[0]
    count = rows_ref.shape[1]
    pick = (
        lax.broadcasted_iota(jnp.int32, (count, window), 1) == rows_ref[0]
    ).astype(bf16)
    xm_ref[...] = mm(pick, x_ref[...]).astype(bf16)
    qm = mm(pick, q_ref[...]).astype(bf16)
    qm_ref[...] = qm
    for pair in range(q_ref.shape[1] // 128):
        lanes = slice(pair * 128, pair * 128 + 128)
        o_ref[:, lanes] = attend(qm[:, lanes], k_ref[:, lanes], v_ref[:, lanes])


def ffn_masked_kernel(
    parts, xm_ref, cot_ref, gains_ref, wg_ref, wu_ref, wd_ref, *refs
):
    o_refs, wo_refs = refs[:parts], refs[parts : 2 * parts]
    rm_ref, dhf_ref, grad_ref, hf_ref, acc_ref, wide_ref = refs[2 * parts :]
    step = pl.program_id(0)
    width = wg_ref.shape[1]
    cols = pl.ds(pl.multiple_of(step * width, width), width)
    hidden, model = grad_ref.shape[1:]
    fold = model // hidden

    def put(part, grad):
        if fold == 1:
            grad_ref[part, :, cols] = grad.astype(bf16)
            return
        for block in range(width // 128):
            wide_ref[block] = grad[:, block * 128 : (block + 1) * 128]
            for piece in range(fold):
                at = piece * hidden + step * width + block * 128
                at = pl.ds(pl.multiple_of(at, 128), 128)
                grad_ref[part, :, at] = wide_ref[
                    block, pl.ds(piece, hidden, stride=fold), :
                ].astype(bf16)

    @pl.when(step == 0)
    def _():
        r = xm_ref[...].astype(f32)
        for o_ref, wo_ref in zip(o_refs, wo_refs):
            r = r + mm(o_ref[...], wo_ref[...])
        rm_ref[...] = r
        hf_ref[...] = (r * rms_scale(r) * gains_ref[1:2, :]).astype(bf16)
        acc_ref[...] = jnp.zeros_like(acc_ref)

    hf, dy = hf_ref[...], cot_ref[...]
    wg, wu, wd = wg_ref[...], wu_ref[...], wd_ref[...]
    g, u = mm(hf, wg), mm(hf, wu)
    sig = jax.nn.sigmoid(g)
    act = (g * sig * u).astype(bf16)
    grad_ref[2, cols, :] = mm_tn(act, dy).astype(bf16)
    da = mm_nt(dy, wd)
    dg = (da * u * sig * (1.0 + g * (1.0 - sig))).astype(bf16)
    du = (da * g * sig).astype(bf16)
    put(0, mm_tn(hf, dg))
    put(1, mm_tn(hf, du))
    acc_ref[...] += mm_nt(dg, wg) + mm_nt(du, wu)

    @pl.when(step == pl.num_programs(0) - 1)
    def _():
        dhf_ref[...] = acc_ref[...].astype(bf16)


def ffn_kernel(parts, place_ref, x_ref, gains_ref, wg_ref, wu_ref, wd_ref, *refs):
    o_refs, wo_refs = refs[:parts], refs[parts : 2 * parts]
    part_ref, own_ref, r_ref, hf_ref, acc_ref = refs[2 * parts :]
    step = pl.program_id(0)

    @pl.when(step == 0)
    def _():
        r = x_ref[...].astype(f32)
        for o_ref, wo_ref in zip(o_refs, wo_refs):
            r = r + mm(o_ref[...], wo_ref[...])
        r_ref[...] = r
        hf_ref[...] = (r * rms_scale(r) * gains_ref[1:2, :]).astype(bf16)
        acc_ref[...] = jnp.zeros_like(acc_ref)

    hf = hf_ref[...]
    g, u = mm(hf, wg_ref[...]), mm(hf, wu_ref[...])
    act = (g * jax.nn.sigmoid(g) * u).astype(bf16)
    acc_ref[...] += mm(act, wd_ref[...])

    @pl.when(step == pl.num_programs(0) - 1)
    def _():
        share = own_ref.shape[0]
        part_ref[...] = acc_ref[...].astype(bf16)
        mine = pl.ds(pl.multiple_of(place_ref[0] * share, share), share)
        own_ref[...] = r_ref[mine, :] + acc_ref[mine, :]


def attn_back_kernel(
    rows_ref,
    dhf_ref,
    rm_ref,
    cot_ref,
    gains_ref,
    om_ref,
    qm_ref,
    cosm_ref,
    sinm_ref,
    k_ref,
    v_ref,
    x_ref,
    cos_ref,
    sin_ref,
    wo_ref,
    w_ref,
    drm_ref,
    dha_ref,
    gw_ref,
    gain_ref,
    gw_acc,
    go_acc,
    gain_acc,
    flow_ref,
    gw_wide,
):
    step = pl.program_id(0)

    @pl.when(step == 0)
    def _():
        gw_acc[...] = jnp.zeros_like(gw_acc)
        go_acc[...] = jnp.zeros_like(go_acc)
        gain_acc[...] = jnp.zeros_like(gain_acc)

    window, width = k_ref.shape
    count = rm_ref.shape[0]
    r = rm_ref[...]
    sf = rms_scale(r)
    nf = r * sf
    dhf = dhf_ref[...].astype(f32)
    dnf = dhf * gains_ref[1:2, :]
    dr = cot_ref[...].astype(f32) + sf * (
        dnf - nf * jnp.mean(dnf * nf, axis=-1, keepdims=True)
    )
    drm_ref[...] = dr
    gain_acc[1:2, :] += jnp.sum(dhf * nf, axis=0, keepdims=True)
    drb = dr.astype(bf16)
    go_acc[...] += mm_tn(om_ref[...], drb)
    dob = mm_nt(drb, wo_ref[...]).astype(bf16)

    first = lax.broadcasted_iota(jnp.int32, (count, 128), 1) < HD
    zero = jnp.zeros((), bf16)
    drq = []
    for pair in range(width // 128):
        lanes = slice(pair * 128, pair * 128 + 128)
        k, v = k_ref[:, lanes], v_ref[:, lanes]
        qm, do = qm_ref[:, lanes], dob[:, lanes]
        parts = []
        drk = dv = None
        for head in range(2):
            mine = first if head == 0 else ~first
            q_head = jnp.where(mine, qm, zero)
            do_head = jnp.where(mine, do, zero)
            s = mm_nt(k, q_head)
            s = jnp.exp((s - jnp.max(s, axis=0, keepdims=True)) * score_scale)
            att = s / jnp.sum(s, axis=0, keepdims=True)
            dpa = mm_nt(v, do_head)
            ds = att * (dpa - jnp.sum(dpa * att, axis=0, keepdims=True))
            ds = (ds * score_scale).astype(bf16)
            parts.append(mm_tn(ds, k))
            drk_head = mm(ds, q_head)
            dv_head = mm(att.astype(bf16), do_head)
            drk = drk_head if drk is None else drk + drk_head
            dv = dv_head if dv is None else dv + dv_head
        drq.append(jnp.where(first, parts[0], parts[1]))
        dk = drk * cos_ref[:, lanes] - swap_halves(drk) * sin_ref[:, lanes]
        flow_ref[:, width + pair * 128 : width + pair * 128 + 128] = dk.astype(bf16)
        flow_ref[:, 2 * width + pair * 128 : 2 * width + pair * 128 + 128] = dv.astype(
            bf16
        )
    spread = (
        lax.broadcasted_iota(jnp.int32, (window, count), 0) == rows_ref[0]
    ).astype(bf16)
    for pair in range(width // 128):
        lanes = slice(pair * 128, pair * 128 + 128)
        dq = drq[pair] * cosm_ref[:, lanes] - swap_halves(drq[pair]) * sinm_ref[:, lanes]
        flow_ref[:, lanes] = mm(spread, dq.astype(bf16)).astype(bf16)

    flow = flow_ref[...]
    x = x_ref[...].astype(f32)
    na = x * rms_scale(x)
    dha = mm_nt(flow, w_ref[...])
    gain_acc[0:1, :] += jnp.sum(dha * na, axis=0, keepdims=True)
    cuts, shares, rows = dha_ref.shape[:3]
    for piece in range(window // rows):
        block = step * (window // rows) + piece
        dha_ref[block % cuts, block // cuts] = dha[piece * rows : (piece + 1) * rows].astype(bf16)
    gw_acc[...] += mm_tn((na * gains_ref[0:1, :]).astype(bf16), flow)

    @pl.when(step == pl.num_programs(0) - 1)
    def _():
        fold = gw_acc.shape[0] // width
        for block in range(3 * width // 128):
            part, lane = divmod(block * 128, width)
            gw_wide[block] = gw_acc[:, block * 128 : (block + 1) * 128]
            for piece in range(fold):
                at = piece * width + lane
                gw_ref[part * width : (part + 1) * width, at : at + 128] = gw_wide[
                    block, pl.ds(piece, width, stride=fold), :
                ].astype(bf16)
        gw_ref[3 * width :, :] = go_acc[...].astype(bf16)
        gain_ref[...] = gain_acc[...]


def input_grad_kernel(
    cut, place_ref, rows_ref, drm_ref, gains_ref, x_ref, part_ref, *refs
):
    out_ref = refs[-1]
    block, count = x_ref.shape[0], drm_ref.shape[0]
    base = (place_ref[0] * cut[1] + cut[0]) * block
    spread = (
        lax.broadcasted_iota(jnp.int32, (block, count), 0) + base == rows_ref[...]
    ).astype(bf16)
    dr = drm_ref[...]
    high = dr.astype(bf16)
    low = (dr - high.astype(f32)).astype(bf16)
    dr = mm(spread, high) + mm(spread, low)
    x = x_ref[...].astype(f32)
    sa = rms_scale(x)
    na = x * sa
    dha = part_ref[0, 0].astype(f32)
    for ref in refs[: cut[2]]:
        dha = dha + ref[...].astype(f32)
    dna = dha * gains_ref[0:1, :]
    out = dr + sa * (dna - na * jnp.mean(dna * na, axis=-1, keepdims=True))
    out_ref[...] = out.astype(bf16)


def input_grad_rows(dha, x, dr, gain, spread):
    high = dr.astype(bf16)
    low = (dr - high.astype(f32)).astype(bf16)
    dr = mm(spread, high) + mm(spread, low)
    sa = rms_scale(x)
    na = x * sa
    dna = dha * gain
    return dr + sa * (dna - na * jnp.mean(dna * na, axis=-1, keepdims=True))


def remote(src, dst, send, recv, place):
    return pltpu.make_async_remote_copy(
        src_ref=src,
        dst_ref=dst,
        send_sem=send,
        recv_sem=recv,
        device_id={"tensor": place},
        device_id_type=pl.DeviceIdType.MESH,
    )


def greet_line(place):
    barrier = pltpu.get_barrier_semaphore()
    for k in range(1, 4):
        pl.semaphore_signal(
            barrier,
            inc=1,
            device_id={"tensor": lax.rem(place + k, 4)},
            device_id_type=pl.DeviceIdType.MESH,
        )
    pl.semaphore_wait(barrier, 3)


def rows_ref(ref, index, share, count):
    return ref.at[pl.ds(pl.multiple_of(index * share, share), count * share), :]


def masked_attention_back(qm, do, k, v):
    first = lax.broadcasted_iota(jnp.int32, qm.shape, 1) < HD
    zero = jnp.zeros((), bf16)
    parts = []
    drk = dv = None
    for head in range(2):
        mine = first if head == 0 else ~first
        q_head = jnp.where(mine, qm, zero)
        do_head = jnp.where(mine, do, zero)
        s = mm_nt(k, q_head)
        s = jnp.exp((s - jnp.max(s, axis=0, keepdims=True)) * score_scale)
        att = s / jnp.sum(s, axis=0, keepdims=True)
        dpa = mm_nt(v, do_head)
        ds = att * (dpa - jnp.sum(dpa * att, axis=0, keepdims=True))
        ds = (ds * score_scale).astype(bf16)
        parts.append(mm_tn(ds, k))
        drk_head = mm(ds, q_head)
        dv_head = mm(att.astype(bf16), do_head)
        drk = drk_head if drk is None else drk + drk_head
        dv = dv_head if dv is None else dv + dv_head
    return jnp.where(first, parts[0], parts[1]), drk, dv


def middle_kernel(
    windows,
    rows_in,
    gains_ref,
    xm_ref,
    cot_ref,
    qm_ref,
    cosm_ref,
    sinm_ref,
    cos_ref,
    sin_ref,
    w_ref,
    wg_ref,
    wu_ref,
    wd_ref,
    *refs,
):
    om_refs, wo_refs, oa_refs = refs[0:4], refs[4:8], refs[8:12]
    x_hbm, k_hbm, v_hbm, o_one, o_two = refs[12:17]
    part_out, own_out, ra_out, dha_out, grads_out, drm_ref, gain_ref = refs[17:24]
    (
        r_ref,
        hf_ref,
        acc_ref,
        p_ref,
        own_ref,
        obuf,
        x_ref,
        kv,
        flow_ref,
        gw_acc,
        gw_wide,
        go_acc,
        rm_ref,
        dpart,
        drecv,
        dall,
        o_load,
        x_sem,
        kv_sem,
        grad_sem,
        p_sem,
        dha_sem,
        own_sem,
        a_send,
        a_recv,
        o_send,
        o_recv,
        d_send,
        d_recv,
        e_send,
        e_recv,
    ) = refs[24:]
    place = lax.axis_index("tensor")
    lower = place < 2
    outer = (place == 0) | (place == 3)
    inner = (place == 1) | (place == 2)
    window, model = x_ref.shape
    width = kv.shape[3]
    hidden = wg_ref.shape[1]
    share = own_ref.shape[0]
    count = rm_ref.shape[0] // windows
    masked = rm_ref.shape[0]
    cols = 256
    chunks = hidden // cols

    def hop(g, d, up):
        src, dst = (d - 1, d) if up else ((5 - d) % 4, 4 - d)
        n = 0 if up else 1
        return remote(
            obuf.at[g, src],
            obuf.at[g, dst],
            o_send.at[g, d - 1, n],
            o_recv.at[g, d - 1, n],
            lax.rem(place + (1 if up else 3), 4),
        )

    def sends(d, up):
        if up:
            return (place >= d - 1) & (place <= 2)
        return (place <= 4 - d) & (place >= 1)

    def receives(d, up):
        return place >= d if up else place <= 3 - d

    def hops(g, d):
        for up in (True, False):

            @pl.when(sends(d, up))
            def _():
                hop(g, d, up).start()

    def hops_in(g, d):
        for up in (True, False):

            @pl.when(receives(d, up))
            def _():
                hop(g, d, up).wait_recv()

    def load_o(g):
        return pltpu.make_async_copy((o_one, o_two)[g], obuf.at[g, 0], o_load.at[g])

    def load_x(w):
        return pltpu.make_async_copy(
            x_hbm.at[pl.ds(w * window, window), :], x_ref, x_sem
        )

    def load_kv(w):
        return [
            pltpu.make_async_copy(
                hbm.at[pl.ds(w * window, window), :], kv.at[w % 2, n], kv_sem.at[w % 2, n]
            )
            for n, hbm in enumerate((k_hbm, v_hbm))
        ]

    def store_p(to):
        return pltpu.make_async_copy(p_ref, to, p_sem)

    def store_own(w):
        return pltpu.make_async_copy(own_ref, own_out.at[w], own_sem)

    def copy_a(w):
        far = rows_ref(part_out.at[w], jnp.where(lower, 1, 0), share, 3)
        return remote(far, ra_out.at[w], a_send.at[w], a_recv.at[w], jnp.where(lower, 1, 2))

    def copy_d(k):
        to = lax.rem(place + k, 4)
        return remote(dpart.at[to], drecv.at[k - 1], d_send.at[k - 1], d_recv.at[k - 1], to)

    def copy_e(k, origin):
        to = lax.rem(place + k, 4)
        return remote(dall.at[origin], dall.at[origin], e_send.at[k - 1], e_recv.at[k - 1], to)

    for g in range(2):
        load_o(g).start()
    load_x(0).start()
    for copy in load_kv(0):
        copy.start()
    greet_line(place)
    load_o(0).wait()
    hops(0, 1)

    gain_att, gain_ffn = gains_ref[0:1, :], gains_ref[1:2, :]
    r = xm_ref[...].astype(f32)
    for om_ref, wo_ref in zip(om_refs, wo_refs):
        r = r + mm(om_ref[...], wo_ref[...])
    rm_ref[...] = r
    hf_ref[0:masked, :] = (r * rms_scale(r) * gain_ffn).astype(bf16)

    def grad_copies(c):
        side = (c % 2) * 2 * cols
        base = 4 * width
        at = pl.ds(c * cols, cols)
        below = window - 2 * cols + (c % 2) * cols
        return [
            pltpu.make_async_copy(
                p_ref.at[:, pl.ds(side, cols)],
                grads_out.at[pl.ds(base, model), at],
                grad_sem.at[c % 2, 0],
            ),
            pltpu.make_async_copy(
                p_ref.at[:, pl.ds(side + cols, cols)],
                grads_out.at[pl.ds(base + hidden, model), at],
                grad_sem.at[c % 2, 1],
            ),
            pltpu.make_async_copy(
                hf_ref.at[pl.ds(below, cols), :],
                grads_out.at[pl.ds(base + 2 * hidden + c * cols, cols), :],
                grad_sem.at[c % 2, 2],
            ),
        ]

    def masked_chunk(c):
        if c >= 2:
            for copy in grad_copies(c - 2):
                copy.wait()
        at = slice(c * cols, (c + 1) * cols)
        side = (c % 2) * 2 * cols
        below = window - 2 * cols + (c % 2) * cols
        hf, dy = hf_ref[0:masked, :], cot_ref[...]
        wg, wu, wd = wg_ref[:, at], wu_ref[:, at], wd_ref[at, :]
        g, u = mm(hf, wg), mm(hf, wu)
        sig = jax.nn.sigmoid(g)
        act = (g * sig * u).astype(bf16)
        hf_ref[below : below + cols, :] = mm_tn(act, dy).astype(bf16)
        da = mm_nt(dy, wd)
        dg = (da * u * sig * (1.0 + g * (1.0 - sig))).astype(bf16)
        du = (da * g * sig).astype(bf16)
        p_ref[:, side : side + cols] = mm_tn(hf, dg).astype(bf16)
        p_ref[:, side + cols : side + 2 * cols] = mm_tn(hf, du).astype(bf16)
        part = mm_nt(dg, wg) + mm_nt(du, wu)
        if c == 0:
            acc_ref[0:masked, :] = part
        else:
            acc_ref[0:masked, :] += part
        for copy in grad_copies(c):
            copy.start()

    for c in range(chunks // 2):
        masked_chunk(c)
    hops_in(0, 1)
    hops(0, 2)
    for c in range(chunks // 2, chunks):
        masked_chunk(c)
    block = model // 4
    for n in range(4):
        dpart[n] = acc_ref[0:masked, n * block : (n + 1) * block].astype(bf16)
    for k in range(1, 4):
        copy_d(k).start()
    hops_in(0, 2)
    hops(0, 3)
    load_o(1).wait()
    hops(1, 1)
    for c in range(chunks - 2, chunks):
        for copy in grad_copies(c):
            copy.wait()

    def ffn(w, o_refs, next_x):
        half = window // 2

        def first(n, carry):
            rows = pl.ds(pl.multiple_of(n * half, half), half)
            r = x_ref[rows, :].astype(f32)
            for o, wo in zip(o_refs, wo_refs):
                r = r + mm(o[rows, :], wo[...])
            r_ref[rows, :] = r
            hf_ref[rows, :] = (r * rms_scale(r) * gain_ffn).astype(bf16)
            return carry

        lax.fori_loop(0, 2, first, 0)
        if next_x is not None:
            load_x(next_x).start()
        acc_ref[...] = jnp.zeros_like(acc_ref)

        def chunk(c, carry):
            at = pl.ds(pl.multiple_of(c * cols, cols), cols)
            hf = hf_ref[...]
            g, u = mm(hf, wg_ref[:, at]), mm(hf, wu_ref[:, at])
            act = (g * jax.nn.sigmoid(g) * u).astype(bf16)
            acc_ref[...] += mm(act, wd_ref[at, :])
            return carry

        lax.fori_loop(0, chunks, chunk, 0)
        p_ref[...] = acc_ref[...].astype(bf16)
        store_p(part_out.at[w]).start()
        mine = pl.ds(pl.multiple_of(place * share, share), share)
        own_ref[...] = r_ref[mine, :] + acc_ref[mine, :]
        store_own(w).start()
        store_p(part_out.at[w]).wait()
        store_own(w).wait()

    def inward(w):
        @pl.when(outer)
        def _():
            copy_a(w).start()

    load_x(0).wait()
    ffn(0, oa_refs, 1)
    inward(0)

    for k in range(1, 4):
        copy_d(k).wait_recv()
    total = dpart[place].astype(f32)
    for k in range(3):
        total = total + drecv[k].astype(f32)
    dall[place] = total.astype(bf16)
    for k in range(1, 4):
        copy_e(k, place).start()

    hops_in(0, 3)
    hops_in(1, 1)
    hops(1, 2)
    load_x(1).wait()
    ffn(1, [obuf.at[0, n] for n in range(4)], 0)
    inward(1)
    hops_in(1, 2)
    hops(1, 3)

    for k in range(1, 4):
        copy_e(k, lax.rem(place + 4 - k, 4)).wait_recv()
    gw_acc[...] = jnp.zeros_like(gw_acc)
    go_acc[...] = jnp.zeros_like(go_acc)
    gain_ref[...] = jnp.zeros_like(gain_ref)
    for w in range(windows):
        for copy in load_kv(w):
            copy.wait()
        if w + 1 < windows:
            for copy in load_kv(w + 1):
                copy.start()
        at = slice(w * count, (w + 1) * count)
        r = rm_ref[at, :]
        sf = rms_scale(r)
        nf = r * sf
        dhf = jnp.concatenate([dall[n, at, :] for n in range(4)], axis=1).astype(f32)
        dnf = dhf * gain_ffn
        dr = cot_ref[at, :].astype(f32) + sf * (
            dnf - nf * jnp.mean(dnf * nf, axis=-1, keepdims=True)
        )
        drm_ref[at, :] = dr
        gain_ref[1:2, :] += jnp.sum(dhf * nf, axis=0, keepdims=True)
        drb = dr.astype(bf16)
        go_acc[...] += mm_tn(om_refs[0][at, :], drb)
        dob = mm_nt(drb, wo_refs[0][...]).astype(bf16)
        spread = (
            lax.broadcasted_iota(jnp.int32, (window, count), 0) == rows_in[w]
        ).astype(bf16)
        for pair in range(width // 128):
            lanes = slice(pair * 128, pair * 128 + 128)
            drq, drk, dv = masked_attention_back(
                qm_ref[at, lanes], dob[:, lanes], kv[w % 2, 0, :, lanes], kv[w % 2, 1, :, lanes]
            )
            dk = drk * cos_ref[:, lanes] - swap_halves(drk) * sin_ref[:, lanes]
            dq = drq * cosm_ref[at, lanes] - swap_halves(drq) * sinm_ref[at, lanes]
            first = pair * 128
            flow_ref[:, first : first + 128] = mm(spread, dq.astype(bf16)).astype(bf16)
            flow_ref[:, width + first : width + first + 128] = dk.astype(bf16)
            flow_ref[:, 2 * width + first : 2 * width + first + 128] = dv.astype(bf16)
        load_x(w).wait()
        if w > 0:
            for copy in dha_copies(dha_out, p_ref, dha_sem, w - 1, windows, share):
                copy.wait()

        def back(n, carry):
            rows = pl.ds(pl.multiple_of(n * share, share), share)
            x = x_ref[rows, :].astype(f32)
            na = x * rms_scale(x)
            dha = mm_nt(flow_ref[rows, :], w_ref[...])
            gain_ref[0:1, :] += jnp.sum(dha * na, axis=0, keepdims=True)
            p_ref[rows, :] = dha.astype(bf16)
            hf_ref[rows, :] = (na * gain_att).astype(bf16)
            return carry

        lax.fori_loop(0, window // share, back, 0)
        for copy in dha_copies(dha_out, p_ref, dha_sem, w, windows, share):
            copy.start()
        if w + 1 < windows:
            load_x(w + 1).start()
        gw_acc[...] += mm_tn(hf_ref[...], flow_ref[...])

    for copy in dha_copies(dha_out, p_ref, dha_sem, windows - 1, windows, share):
        copy.wait()
    fold = model // width
    for block in range(3 * width // 128):
        part, lane = divmod(block * 128, width)
        gw_wide[...] = gw_acc[:, block * 128 : (block + 1) * 128]
        for piece in range(fold):
            at = piece * width + lane
            p_ref[part * width : (part + 1) * width, at : at + 128] = gw_wide[
                pl.ds(piece, width, stride=fold), :
            ].astype(bf16)
    p_ref[3 * width :, :] = go_acc[...].astype(bf16)
    store = store_p(grads_out.at[pl.ds(0, 4 * width), :])
    store.start()
    store.wait()

    hops_in(1, 3)
    ffn(2, [obuf.at[1, n] for n in range(4)], None)

    for w in range(2):

        @pl.when(outer)
        def _():
            copy_a(w).wait_send()

        @pl.when(inner)
        def _():
            copy_a(w).wait_recv()

    for k in range(1, 4):
        copy_d(k).wait_send()
        copy_e(k, place).wait_send()
    for g in range(2):
        for d in range(1, 4):
            for up in (True, False):

                @pl.when(sends(d, up))
                def _():
                    hop(g, d, up).wait_send()


def dha_copies(dha_out, p_ref, sem, w, windows, share):
    copies = []
    per = p_ref.shape[0] // share
    for n in range(per):
        block = w * per + n
        copies.append(
            pltpu.make_async_copy(
                p_ref.at[pl.ds(n * share, share), :],
                dha_out.at[block % windows, pl.ds(block // windows * share, share), :],
                sem.at[n],
            )
        )
    return copies


def lines_kernel(
    cuts,
    windows,
    order,
    ready,
    rows_in,
    drm_ref,
    gains_ref,
    x_ref,
    dha_ref,
    part_ref,
    own_in,
    ra_in,
    out_ref,
    grad_ref,
    ra,
    rb,
    rc,
    value,
    own,
    piece,
    x_rows,
    grad,
    a_send,
    a_recv,
    b_send,
    b_recv,
    c_send,
    c_recv,
    g_send,
    g_recv,
    v_sem,
    o_sem,
    r_sem,
    x_sem,
    l_sem,
    i_sem,
):
    place = lax.axis_index("tensor")
    lower = place < 2
    outer = (place == 0) | (place == 3)
    inner = (place == 1) | (place == 2)
    share = rc.shape[1]
    folds = len(order)

    def whole(f):
        kind, index = order[f]
        return part_ref.at[index] if kind == 0 else dha_ref.at[index]

    def copy_a(f):
        far = rows_ref(whole(f), jnp.where(lower, 1, 0), share, 3)
        return remote(far, ra.at[f], a_send.at[f], a_recv.at[f], jnp.where(lower, 1, 2))

    def copy_b(f):
        src = rows_ref(ra.at[f], jnp.where(lower, 1, 0), share, 2)
        return remote(src, rb.at[f], b_send.at[f], b_recv.at[f], jnp.where(lower, 2, 1))

    def copy_c(f):
        src = rows_ref(rb.at[f], jnp.where(lower, 0, 1), share, 1)
        return remote(src, rc.at[f], c_send.at[f], c_recv.at[f], jnp.where(lower, 0, 3))

    def load(f):
        return pltpu.make_async_copy(whole(f), value.at[f], v_sem.at[f])

    def load_own(w):
        return pltpu.make_async_copy(own_in.at[w], own.at[w], o_sem.at[w])

    def load_ra(f):
        return pltpu.make_async_copy(ra_in.at[order[f][1]], ra.at[f], r_sem.at[f])

    def hop(w, d, up, origin):
        rows = pl.ds(pl.multiple_of(w * 4 * share + origin * share, share), share)
        n = 0 if up else 1
        return remote(
            piece.at[w] if d == 1 else out_ref.at[rows, :],
            out_ref.at[rows, :],
            g_send.at[w, d - 1, n],
            g_recv.at[w, d - 1, n],
            lax.rem(place + (1 if up else 3), 4),
        )

    def sends(d, up):
        if up:
            return (place >= d - 1) & (place <= 2)
        return (place <= 4 - d) & (place >= 1)

    def receives(d, up):
        return place >= d if up else place <= 3 - d

    def source(d, up):
        return jnp.clip(place - (d - 1) if up else place + (d - 1), 0, 3)

    def hops(w, d):
        for up in (True, False):

            @pl.when(sends(d, up))
            def _():
                hop(w, d, up, source(d, up)).start()

    def hops_in(w, d):
        for up in (True, False):

            @pl.when(receives(d, up))
            def _():
                hop(w, d, up, source(d + 1, up)).wait_recv()

    def keep(w):
        rows = pl.ds(pl.multiple_of(w * 4 * share + place * share, share), share)
        return pltpu.make_async_copy(piece.at[w], out_ref.at[rows, :], l_sem.at[w])

    def store(c):
        return pltpu.make_async_copy(
            grad.at[c], grad_ref.at[pl.ds(c * share, share), :], i_sem.at[c]
        )

    x_load = pltpu.make_async_copy(
        rows_ref(x_ref, place * cuts, share, cuts), x_rows, x_sem
    )

    for f in range(folds):
        load(f).start()
    for w in range(windows):
        load_own(w).start()
    x_load.start()
    greet_line(place)
    sent = list(range(ready, folds))

    @pl.when(outer)
    def _():
        for f in sent[:2]:
            copy_a(f).start()

    @pl.when(inner)
    def _():
        for f in range(ready):
            load_ra(f).start()

    def add_rows(buffer, at, f, index):
        rows = pl.ds(pl.multiple_of(at * share, share), share)
        mine = pl.ds(pl.multiple_of(index * share, share), share)
        total = buffer[f, rows, :].astype(f32) + value[f, mine, :].astype(f32)
        buffer[f, rows, :] = total.astype(bf16)

    def finish(f, terms):
        kind, index = order[f]
        if kind == 0:
            total = own[index]
        else:
            mine = pl.ds(pl.multiple_of(place * share, share), share)
            total = value[f, mine, :].astype(f32)
        for term in terms:
            total = total + term.astype(f32)
        if kind == 0:
            piece[index] = total.astype(bf16)
        else:
            first = place * (cuts * share) + index * share
            count = drm_ref.shape[0]
            spread = (
                lax.broadcasted_iota(jnp.int32, (share, count), 0) + first == rows_in[...]
            ).astype(bf16)
            x = x_rows[pl.ds(index * share, share), :].astype(f32)
            grad[index] = input_grad_rows(
                total, x, drm_ref[...], gains_ref[0:1, :], spread
            ).astype(bf16)
            store(index).start()

    for f in range(folds):
        load(f).wait()
    for w in range(windows):
        load_own(w).wait()
    x_load.wait()
    moving = {}
    for step in range(folds + 1):
        if step < folds:

            @pl.when(inner)
            def _():
                if step < ready:
                    load_ra(step).wait()
                else:
                    copy_a(step).wait_recv()
                for n in range(2):
                    add_rows(
                        ra, jnp.where(lower, 1, 0) + n, step, jnp.where(lower, 2, 0) + n
                    )
                copy_b(step).start()

        if step > 0:
            f = step - 1

            @pl.when(inner)
            def _():
                copy_b(f).wait_recv()
                add_rows(rb, jnp.where(lower, 0, 1), f, jnp.where(lower, 0, 3))
                copy_c(f).start()
                sel_a = pl.ds(pl.multiple_of(jnp.where(lower, 0, 2) * share, share), share)
                sel_b = pl.ds(pl.multiple_of(jnp.where(lower, 1, 0) * share, share), share)
                finish(f, [ra[f, sel_a, :], rb[f, sel_b, :]])

            @pl.when(outer)
            def _():
                copy_c(f).wait_recv()
                finish(f, [rc[f]])

            for w in list(moving):
                hops_in(w, moving[w])
                if moving[w] == 3:
                    del moving[w]
                else:
                    moving[w] += 1
                    hops(w, moving[w])
            kind, index = order[f]
            if kind == 0:
                hops(index, 1)
                keep(index).start()
                moving[index] = 1

        if ready <= step < folds:

            @pl.when(outer)
            def _():
                copy_a(step).wait_send()
                if step + 2 < folds:
                    copy_a(step + 2).start()

    while moving:
        for w in list(moving):
            hops_in(w, moving[w])
            if moving[w] == 3:
                del moving[w]
            else:
                moving[w] += 1
                hops(w, moving[w])

    @pl.when(inner)
    def _():
        for f in range(folds):
            copy_b(f).wait_send()
            copy_c(f).wait_send()

    for w in range(windows):
        keep(w).wait()
        for d in range(1, 4):
            for up in (True, False):

                @pl.when(sends(d, up))
                def _():
                    hop(w, d, up, source(d, up)).wait_send()

    for c in range(cuts):
        store(c).wait()


def place_kernel(place_ref, *refs):
    out_ref = refs[-1]
    parts = lax.axis_size("tensor")
    share = refs[0].shape[0]
    for step in range(parts):
        origin = lax.rem(place_ref[0] + parts - step, parts)
        out_ref[pl.ds(pl.multiple_of(origin * share, share), share), :] = refs[step][...]


def spread_kernel(tile_ref, used_ref, *refs):
    out_ref = refs[-1]
    step = pl.program_id(0)
    per = len(refs) - 1
    for n in range(per):
        used = used_ref[step * per + n] > 0
        out_ref[n] = jnp.where(used, refs[n][0], jnp.zeros((), bf16))


def copy_kernel(in_ref, out_ref):
    out_ref[...] = in_ref[...]


def collect_kernel(slot_ref, *refs):
    out_ref = refs[-1]
    for index, ref in enumerate(refs[:-1]):
        out_ref[index] = ref[0]


def exchange(value, axis, bit):
    size = lax.axis_size(axis)
    return lax.ppermute(value, axis, [(i, i ^ bit) for i in range(size)])


def dp_total(value):
    size = lax.axis_size("dp")
    value = value + exchange(value, "dp", 1)
    bits = []
    bit = 2
    while bit < size:
        bits.append(bit)
        bit *= 2
    core = lax.axis_index("dp") % 2
    half = value.shape[0] // 2
    mine = lax.dynamic_slice_in_dim(value, core * half, half, 0)
    cut = half // 2
    low, high = mine[:cut], mine[cut:]
    for bit_low, bit_high in zip(bits, bits[::-1]):
        low = low + exchange(low, "dp", bit_low)
        high = high + exchange(high, "dp", bit_high)
    mine = jnp.concatenate([low, high], axis=0)
    other = exchange(mine, "dp", 1)
    return jnp.where(
        core == 0,
        jnp.concatenate([mine, other], axis=0),
        jnp.concatenate([other, mine], axis=0),
    )


def around(value):
    size = lax.axis_size("tensor")
    return [value] + [
        lax.ppermute(value, "tensor", [(i, (i + k) % size) for i in range(size)])
        for k in range(1, size)
    ]


def rows_at(value, index, share, count):
    return lax.dynamic_slice_in_dim(value, index * share, count * share, 0)


def other_sums(value, share):
    place = lax.axis_index("tensor")
    total = lax.psum_scatter(value, "tensor", scatter_dimension=0, tiled=True)
    own = rows_at(value, place, share, 1).astype(f32)
    return (total.astype(f32) - own,)


def small_total(value):
    for axis in ("dp", "tensor"):
        bit = 1
        while bit < lax.axis_size(axis):
            value = value + exchange(value, axis, bit)
            bit *= 2
    return value


def slot_ranks(owner_row):
    count_all = owner_row.shape[0]
    tile_order = jnp.arange(count_all, dtype=jnp.int32)
    earlier = (owner_row[:, None] == owner_row[None, :]) & (
        tile_order[None, :] < tile_order[:, None]
    )
    return jnp.sum(earlier.astype(jnp.int32), axis=1)


def adam_update(grad_now, first_old, second_old, param_old, rate, decay):
    first_new = beta_one * first_old + (1.0 - beta_one) * grad_now
    second_new = beta_two * second_old + (1.0 - beta_two) * grad_now * grad_now
    first_hat = first_new / (1.0 - beta_one**STEP)
    second_hat = second_new / (1.0 - beta_two**STEP)
    param_new = param_old - rate * (
        first_hat / (jnp.sqrt(second_hat) + adam_eps) + decay * param_old
    )
    return (first_new, second_new, param_new)


def head_tables(positions, heads):
    frequency = jnp.exp(
        -jnp.log(10000.0) * (2.0 * jnp.arange(HD // 2, dtype=f32) / HD)
    )
    angles = positions.astype(f32)[..., None] * frequency
    cos, sin = jnp.cos(angles), jnp.sin(angles)
    cos = jnp.concatenate([cos, cos], axis=-1)
    sin = jnp.concatenate([-sin, sin], axis=-1)
    reps = (1,) * (cos.ndim - 1) + (heads,)
    return jnp.tile(cos, reps), jnp.tile(sin, reps)


def on_device(
    tokens,
    masked_rows,
    cotangent,
    norm_gains,
    gain_first,
    gain_second,
    owners,
    master,
    first_moment,
    second_moment,
):
    seq_count, mask_count = masked_rows.shape
    total_rows, model = tokens.shape
    window = total_rows // seq_count
    parts = lax.axis_size("tensor")
    place = lax.axis_index("tensor")
    owner_self = lax.axis_index("dp")
    heads = HEADS // parts
    width = heads * HD
    hidden = FF // parts
    capacity, tile_rows = master.shape[1:3]
    tile_size = tile_rows * model
    attn_tiles = 4 * model * width // tile_size
    ffn_tiles = 3 * model * hidden // tile_size
    count = -(-mask_count // 16) * 16
    place_ref = place.astype(jnp.int32).reshape(1)

    owner_row = owners[0]
    slot_rank = slot_ranks(owner_row)
    slot_index = owner_row * capacity + slot_rank
    slot_match = (owner_row[None, :] == owner_self) & (
        slot_rank[None, :] == jnp.arange(capacity, dtype=jnp.int32)[:, None]
    )
    slot_used = jnp.any(slot_match, axis=1)[:, None, None]
    slot_tile = jnp.argmax(slot_match, axis=1)

    tile_block = (1, tile_rows, model)
    grid_size = max(capacity, attn_tiles)
    low_slots, attn_mine = pl.pallas_call(
        cast_kernel,
        out_shape=[
            jax.ShapeDtypeStruct((capacity, tile_rows, model), bf16),
            jax.ShapeDtypeStruct((attn_tiles, tile_rows, model), bf16),
        ],
        grid_spec=pltpu.PrefetchScalarGridSpec(
            num_scalar_prefetch=2,
            grid=(grid_size,),
            in_specs=[
                pl.BlockSpec(
                    tile_block, lambda i, rank, held: (jnp.minimum(i, capacity - 1), 0, 0)
                ),
                pl.BlockSpec(
                    tile_block,
                    lambda i, rank, held: (rank[jnp.minimum(i, attn_tiles - 1)], 0, 0),
                ),
            ],
            out_specs=[
                pl.BlockSpec(
                    tile_block, lambda i, rank, held: (jnp.minimum(i, capacity - 1), 0, 0)
                ),
                pl.BlockSpec(
                    tile_block, lambda i, rank, held: (jnp.minimum(i, attn_tiles - 1), 0, 0)
                ),
            ],
        ),
        compiler_params=params(),
        cost_estimate=cost(0, 12 * capacity * tile_size),
        name="cast",
    )(
        slot_rank,
        jnp.pad(
            (owner_row[:attn_tiles] == owner_self).astype(jnp.int32),
            (0, grid_size - attn_tiles),
            mode="edge",
        ),
        master[0],
        master[0],
    )
    attn_flat = dp_total(attn_mine).reshape(4 * width, model)
    w_out = attn_flat[3 * width :]
    every_slot = lax.all_gather(low_slots, "dp", axis=0, tiled=True)
    w_outs = around(w_out)

    cos, sin = head_tables(jnp.arange(window), heads)
    rows = jnp.pad(masked_rows, ((0, 0), (0, count - mask_count)), constant_values=-1)
    cos_m, sin_m = head_tables(rows, heads)
    cot = jnp.pad(cotangent, ((0, 0), (0, count - mask_count), (0, 0)))
    cot = cot.reshape(seq_count * count, model)
    cos_m = cos_m.reshape(seq_count * count, width)
    sin_m = sin_m.reshape(seq_count * count, width)

    block = min(512, window)
    per_window = window // block
    row_block = pl.BlockSpec((block, model), lambda i: (i, 0))
    head_block = pl.BlockSpec((block, width), lambda i: (i, 0))
    table_block = pl.BlockSpec((block, width), lambda i: (i % per_window, 0))
    q, k, v, w_qkv = pl.pallas_call(
        qkv_kernel,
        out_shape=[jax.ShapeDtypeStruct((total_rows, width), bf16)] * 3
        + [jax.ShapeDtypeStruct((model, 3 * width), bf16)],
        grid=(total_rows // block,),
        in_specs=[
            row_block,
            whole_spec((2, model)),
            whole_spec((3 * width, model)),
            table_block,
            table_block,
        ],
        out_specs=[head_block] * 3 + [whole_spec((model, 3 * width))],
        scratch_shapes=[pltpu.VMEM((3 * width // 128, model, 128), f32)],
        compiler_params=params(),
        cost_estimate=cost(6 * total_rows * model * width, 2 * total_rows * model * 2),
        name="qkv",
    )(tokens, norm_gains, attn_flat, cos, sin)

    win_model = pl.BlockSpec((window, model), lambda i: (i, 0))
    win_head = pl.BlockSpec((window, width), lambda i: (i, 0))
    mask_model = pl.BlockSpec((count, model), lambda i: (i, 0))
    mask_head = pl.BlockSpec((count, width), lambda i: (i, 0))
    o_m, q_m, x_m = pl.pallas_call(
        attend_masked_kernel,
        out_shape=[
            jax.ShapeDtypeStruct((seq_count * count, width), bf16),
            jax.ShapeDtypeStruct((seq_count * count, width), bf16),
            jax.ShapeDtypeStruct((seq_count * count, model), bf16),
        ],
        grid=(seq_count,),
        in_specs=[
            pl.BlockSpec((1, count, 1), lambda i: (i, 0, 0)),
            win_model,
            win_head,
            win_head,
            win_head,
        ],
        out_specs=[mask_head, mask_head, mask_model],
        compiler_params=params(),
        cost_estimate=cost(
            seq_count * count * window * (2 * model + 8 * width), 9e6, seq_count * count * window * heads
        ),
        name="attend_masked",
    )(rows[:, :, None], tokens, q, k, v)
    o_ms = around(o_m)

    q_block = min(256, window)

    def attend_window(w, before):
        return pl.pallas_call(
            after(attend_kernel, 3, 1),
            out_shape=jax.ShapeDtypeStruct((window, width), bf16),
            grid=(width // 128, window // q_block),
            in_specs=[
                pl.BlockSpec((q_block, 128), lambda p, i: (w * (window // q_block) + i, p)),
                pl.BlockSpec((window, 128), lambda p, i: (w, p)),
                pl.BlockSpec((window, 128), lambda p, i: (w, p)),
                UNREAD,
            ],
            out_specs=pl.BlockSpec((q_block, 128), lambda p, i: (i, p)),
            compiler_params=params(),
            cost_estimate=cost(
                16 * window * window * width, 4 * window * width * 2, window * window * heads
            ),
            name="attend",
        )(q, k, v, before)

    mask_rows = seq_count * count
    share = window // parts
    share_rows = total_rows // parts
    lines = parts == 4 and seq_count == 3 and hidden == model and mask_rows <= window // 2
    early = seq_count if lines else max(seq_count - 1, 1)
    o_own = []
    for w in range(early):
        o_own.append(attend_window(w, o_own[-1] if o_own else o_m))

    group = 4
    ffn_all = pl.pallas_call(
        after(collect_kernel, 1 + group, 1),
        out_shape=jax.ShapeDtypeStruct((ffn_tiles, tile_rows, model), bf16),
        grid_spec=pltpu.PrefetchScalarGridSpec(
            num_scalar_prefetch=1,
            grid=(ffn_tiles // group,),
            in_specs=[
                pl.BlockSpec(
                    tile_block,
                    lambda i, slot, n=n: (slot[attn_tiles + i * group + n], 0, 0),
                )
                for n in range(group)
            ]
            + [UNREAD],
            out_specs=pl.BlockSpec((group, tile_rows, model), lambda i, slot: (i, 0, 0)),
        ),
        compiler_params=params(),
        cost_estimate=cost(0, 4 * ffn_tiles * tile_size),
        name="collect",
    )(slot_index, *[every_slot] * group, o_own[-1])
    ffn_flat = ffn_all.reshape(3, -1)
    w_gate = ffn_flat[0].reshape(model, hidden)
    w_up = ffn_flat[1].reshape(model, hidden)
    w_down = ffn_flat[2].reshape(hidden, model)

    flat_rows = jnp.where(
        rows >= 0, rows + window * jnp.arange(seq_count, dtype=jnp.int32)[:, None], -1
    ).reshape(1, mask_rows)
    if lines:
        anywhere = pl.BlockSpec(memory_space=pl.ANY)
        inside = pl.BlockSpec(memory_space=pltpu.VMEM)
        dma = pltpu.SemaphoreType.DMA
        grad_rows = 4 * width + 3 * hidden
        part, own, first_sums, dha, grads, dr_m, gains_part = pl.pallas_call(
            functools.partial(middle_kernel, seq_count),
            out_shape=[
                jax.ShapeDtypeStruct((seq_count, window, model), bf16),
                jax.ShapeDtypeStruct((seq_count, share, model), f32),
                jax.ShapeDtypeStruct((2, 3 * share, model), bf16),
                jax.ShapeDtypeStruct((seq_count, window, model), bf16),
                jax.ShapeDtypeStruct((grad_rows, model), bf16),
                jax.ShapeDtypeStruct((mask_rows, model), f32),
                jax.ShapeDtypeStruct((2, model), f32),
            ],
            in_specs=[inside] * (13 + 3 * parts) + [anywhere] * 5,
            out_specs=[anywhere] * 5 + [inside] * 2,
            scratch_shapes=[
                pltpu.VMEM((window, model), f32),
                pltpu.VMEM((window, model), bf16),
                pltpu.VMEM((window, model), f32),
                pltpu.VMEM((window, model), bf16),
                pltpu.VMEM((share, model), f32),
                pltpu.VMEM((2, 4, window, width), bf16),
                pltpu.VMEM((window, model), bf16),
                pltpu.VMEM((2, 2, window, width), bf16),
                pltpu.VMEM((window, 3 * width), bf16),
                pltpu.VMEM((model, 3 * width), f32),
                pltpu.VMEM((model, 128), f32),
                pltpu.VMEM((width, model), f32),
                pltpu.VMEM((mask_rows, model), f32),
                pltpu.VMEM((4, mask_rows, model // 4), bf16),
                pltpu.VMEM((3, mask_rows, model // 4), bf16),
                pltpu.VMEM((4, mask_rows, model // 4), bf16),
                dma((2,)),
                dma,
                dma((2, 2)),
                dma((2, 3)),
                dma,
                dma((window // share,)),
                dma,
                dma((2,)),
                dma((2,)),
                dma((2, 3, 2)),
                dma((2, 3, 2)),
                dma((3,)),
                dma((3,)),
                dma((3,)),
                dma((3,)),
            ],
            compiler_params=params(collective_id=1, has_side_effects=True),
            cost_estimate=cost(1e11, 100e6),
            name="middle",
        )(
            rows[:, None, :],
            norm_gains,
            x_m,
            cot,
            q_m,
            cos_m,
            sin_m,
            cos,
            sin,
            w_qkv,
            w_gate,
            w_up,
            w_down,
            *o_ms,
            *w_outs,
            *around(o_own[0]),
            tokens,
            k,
            v,
            o_own[1],
            o_own[2],
        )

        slots = lax.axis_size("dp") * capacity
        slot_hit = slot_index[None, :] == jnp.arange(slots, dtype=jnp.int32)[:, None]
        group = 4
        in_slots = pl.pallas_call(
            spread_kernel,
            out_shape=jax.ShapeDtypeStruct((slots, tile_rows, model), bf16),
            grid_spec=pltpu.PrefetchScalarGridSpec(
                num_scalar_prefetch=2,
                grid=(slots // group,),
                in_specs=[
                    pl.BlockSpec(
                        tile_block, lambda i, tile, used, n=n: (tile[i * group + n], 0, 0)
                    )
                    for n in range(group)
                ],
                out_specs=pl.BlockSpec(
                    (group, tile_rows, model), lambda i, tile, used: (i, 0, 0)
                ),
            ),
            compiler_params=params(),
            cost_estimate=cost(0, 24 * capacity * tile_size),
            name="spread",
        )(
            jnp.argmax(slot_hit, axis=1).astype(jnp.int32),
            jnp.any(slot_hit, axis=1).astype(jnp.int32),
            *[grads.reshape(-1, tile_rows, model)] * group,
        )
        reduced = lax.psum_scatter(in_slots, "dp", scatter_dimension=0, tiled=True).astype(f32)

        order = [(0, 0), (0, 1), (1, 0), (0, 2), (1, 1), (1, 2)]
        folds = len(order)
        layer_out, input_grad = pl.pallas_call(
            after(functools.partial(lines_kernel, seq_count, seq_count, order, 2), 8, 1),
            out_shape=[
                jax.ShapeDtypeStruct((total_rows, model), bf16),
                jax.ShapeDtypeStruct((share_rows, model), bf16),
            ],
            in_specs=[inside] * 3 + [anywhere] * 6,
            out_specs=[anywhere] * 2,
            scratch_shapes=[
                pltpu.VMEM((folds, 3 * share, model), bf16),
                pltpu.VMEM((folds, 2 * share, model), bf16),
                pltpu.VMEM((folds, share, model), bf16),
                pltpu.VMEM((folds, window, model), bf16),
                pltpu.VMEM((seq_count, share, model), f32),
                pltpu.VMEM((seq_count, share, model), bf16),
                pltpu.VMEM((share_rows, model), bf16),
                pltpu.VMEM((seq_count, share, model), bf16),
                dma((folds,)),
                dma((folds,)),
                dma((folds,)),
                dma((folds,)),
                dma((folds,)),
                dma((folds,)),
                dma((seq_count, 3, 2)),
                dma((seq_count, 3, 2)),
                dma((folds,)),
                dma((seq_count,)),
                dma((2,)),
                dma,
                dma((seq_count,)),
                dma((seq_count,)),
            ],
            compiler_params=params(collective_id=2, has_side_effects=True),
            cost_estimate=cost(4 * share_rows * mask_rows * model, 60e6),
            name="lines",
        )(
            flat_rows,
            dr_m,
            norm_gains,
            tokens,
            dha,
            part,
            own,
            first_sums,
            in_slots,
        )
    else:
        cols = min(256, hidden)
        col_block = pl.BlockSpec((model, cols), lambda c: (0, c))
        down_block = pl.BlockSpec((cols, model), lambda c: (c, 0))
        r_m, dhf_part, ffn_grad = pl.pallas_call(
            functools.partial(ffn_masked_kernel, parts),
            out_shape=[
                jax.ShapeDtypeStruct((mask_rows, model), f32),
                jax.ShapeDtypeStruct((mask_rows, model), bf16),
                jax.ShapeDtypeStruct((3, hidden, model), bf16),
            ],
            grid=(hidden // cols,),
            in_specs=[
                whole_spec((mask_rows, model)),
                whole_spec((mask_rows, model)),
                whole_spec((2, model)),
                col_block,
                col_block,
                down_block,
            ]
            + [whole_spec((mask_rows, width))] * parts
            + [whole_spec((width, model))] * parts,
            out_specs=[
                whole_spec((mask_rows, model)),
                whole_spec((mask_rows, model)),
                whole_spec((3, hidden, model)),
            ],
            scratch_shapes=[
                pltpu.VMEM((mask_rows, model), bf16),
                pltpu.VMEM((mask_rows, model), f32),
                pltpu.VMEM((cols // 128, model, 128), f32),
            ],
            compiler_params=params(),
            cost_estimate=cost(
                mask_rows * model * (18 * hidden + 2 * model), 20e6, mask_rows * hidden
            ),
            name="ffn_masked",
        )(x_m, cot, norm_gains, w_gate, w_up, w_down, *o_ms, *w_outs)

        for w in range(early, seq_count):
            o_own.append(attend_window(w, r_m))
        windows_o = [around(o) for o in o_own]

        share_m = mask_rows // parts
        dhf_mine = lax.dynamic_slice_in_dim(dhf_part, place * share_m, share_m, 0).astype(f32)
        for step in range(1, parts):
            send = lax.dynamic_slice_in_dim(
                dhf_part, lax.rem(place + step, parts) * share_m, share_m, 0
            )
            dhf_mine = dhf_mine + lax.ppermute(
                send, "tensor", [(i, (i + step) % parts) for i in range(parts)]
            ).astype(f32)
        dhf_all = around(dhf_mine.astype(bf16))
        dhf = jnp.zeros((mask_rows, model), bf16)
        for step, piece in enumerate(dhf_all):
            origin = lax.rem(place + parts - step, parts)
            dhf = lax.dynamic_update_slice_in_dim(dhf, piece, origin * share_m, 0)

        layer_out = None

        def ffn_window(w, before):
            return pl.pallas_call(
                after(functools.partial(ffn_kernel, parts), 6 + 2 * parts, 1),
                out_shape=[
                    jax.ShapeDtypeStruct((window, model), bf16),
                    jax.ShapeDtypeStruct((share, model), f32),
                ],
                grid_spec=pltpu.PrefetchScalarGridSpec(
                    num_scalar_prefetch=1,
                    grid=(hidden // cols,),
                    in_specs=[
                        pl.BlockSpec((window, model), lambda c, place_ref: (w, 0)),
                        whole_spec((2, model)),
                        pl.BlockSpec((model, cols), lambda c, place_ref: (0, c)),
                        pl.BlockSpec((model, cols), lambda c, place_ref: (0, c)),
                        pl.BlockSpec((cols, model), lambda c, place_ref: (c, 0)),
                    ]
                    + [whole_spec((window, width))] * parts
                    + [whole_spec((width, model))] * parts
                    + [UNREAD],
                    out_specs=[
                        whole_spec((window, model)),
                        whole_spec((share, model)),
                    ],
                    scratch_shapes=[
                        pltpu.VMEM((window, model), f32),
                        pltpu.VMEM((window, model), bf16),
                        pltpu.VMEM((window, model), f32),
                    ],
                ),
                compiler_params=params(),
                cost_estimate=cost(
                    window * model * (6 * hidden + 2 * model), 16e6, window * hidden
                ),
                name="ffn",
            )(
                place_ref,
                tokens,
                norm_gains,
                w_gate,
                w_up,
                w_down,
                *windows_o[w],
                *w_outs,
                before,
            )

        def place_window(w, part, own):
            terms = other_sums(part, share)
            total = own
            for term in terms:
                total = total + term.astype(f32)
            pieces = around(total.astype(bf16))
            return pl.pallas_call(
                after(place_kernel, 1 + parts, 0 if layer_out is None else 1),
                out_shape=jax.ShapeDtypeStruct((total_rows, model), bf16),
                grid_spec=pltpu.PrefetchScalarGridSpec(
                    num_scalar_prefetch=1,
                    grid=(1,),
                    in_specs=[whole_spec((share, model))] * parts
                    + [UNREAD] * (layer_out is not None),
                    out_specs=pl.BlockSpec((window, model), lambda i, place_ref: (w, 0)),
                ),
                input_output_aliases={} if layer_out is None else {1 + parts: 0},
                compiler_params=params(),
                cost_estimate=cost(0, 4 * window * model),
                name="place",
            )(place_ref, *pieces, *([] if layer_out is None else [layer_out]))

        parts_out = [ffn_window(0, o_own[-1])]

        cuts = seq_count if share_rows % (16 * seq_count) == 0 else 1
        cut_rows = share_rows // cuts
        dr_m, dha, attn_grad, gains_part = pl.pallas_call(
            after(attn_back_kernel, 16, 1),
            out_shape=[
                jax.ShapeDtypeStruct((mask_rows, model), f32),
                jax.ShapeDtypeStruct((cuts, parts, cut_rows, model), bf16),
                jax.ShapeDtypeStruct((4 * width, model), bf16),
                jax.ShapeDtypeStruct((2, model), f32),
            ],
            grid=(seq_count,),
            in_specs=[
                pl.BlockSpec((1, 1, count), lambda i: (i, 0, 0)),
                mask_model,
                mask_model,
                mask_model,
                whole_spec((2, model)),
                mask_head,
                mask_head,
                mask_head,
                mask_head,
                win_head,
                win_head,
                win_model,
                whole_spec((window, width)),
                whole_spec((window, width)),
                whole_spec((width, model)),
                whole_spec((model, 3 * width)),
                UNREAD,
            ],
            out_specs=[
                mask_model,
                whole_spec((cuts, parts, cut_rows, model)),
                whole_spec((4 * width, model)),
                whole_spec((2, model)),
            ],
            scratch_shapes=[
                pltpu.VMEM((model, 3 * width), f32),
                pltpu.VMEM((width, model), f32),
                pltpu.VMEM((2, model), f32),
                pltpu.VMEM((window, 3 * width), bf16),
                pltpu.VMEM((3 * width // 128, model, 128), f32),
            ],
            compiler_params=params(),
            cost_estimate=cost(
                12 * total_rows * model * width, 30e6, mask_rows * window * heads
            ),
            name="attn_back",
        )(
            rows[:, None, :],
            dhf,
            r_m,
            cot,
            norm_gains,
            o_m,
            q_m,
            cos_m,
            sin_m,
            k,
            v,
            tokens,
            cos,
            sin,
            w_out,
            w_qkv,
            parts_out[0][0],
        )

        for w in range(1, seq_count):
            parts_out.append(ffn_window(w, gains_part if w == 1 else parts_out[-1][0]))

        input_grad = None
        for cut in range(cuts):
            value = dha[cut].reshape(parts * cut_rows, model)
            terms = other_sums(value, cut_rows)
            before = [] if input_grad is None else [input_grad]
            input_grad = pl.pallas_call(
                after(
                    functools.partial(input_grad_kernel, (cut, cuts, len(terms))),
                    6 + len(terms),
                    len(before),
                ),
                out_shape=jax.ShapeDtypeStruct((share_rows, model), bf16),
                grid_spec=pltpu.PrefetchScalarGridSpec(
                    num_scalar_prefetch=1,
                    grid=(1,),
                    in_specs=[
                        whole_spec((1, mask_rows)),
                        whole_spec((mask_rows, model)),
                        whole_spec((2, model)),
                        pl.BlockSpec(
                            (cut_rows, model),
                            lambda i, place_ref, cut=cut: (place_ref[0] * cuts + cut, 0),
                        ),
                        pl.BlockSpec(
                            (1, 1, cut_rows, model),
                            lambda i, place_ref, cut=cut: (cut, place_ref[0], 0, 0),
                        ),
                    ]
                    + [whole_spec((cut_rows, model))] * len(terms)
                    + [UNREAD] * len(before),
                    out_specs=pl.BlockSpec((cut_rows, model), lambda i, place_ref, cut=cut: (cut, 0)),
                ),
                input_output_aliases={6 + len(terms): 0} if before else {},
                compiler_params=params(),
                cost_estimate=cost(4 * cut_rows * mask_rows * model, 6e6),
                name="input_grad",
            )(place_ref, flat_rows, dr_m, norm_gains, tokens, dha, *terms, *before)

        for w, outs in enumerate(parts_out):
            layer_out = place_window(w, *outs)

        def total_tiles(tiles, before):
            piece = lax.psum_scatter(tiles, "dp", scatter_dimension=0, tiled=True)
            piece = pl.pallas_call(
                after(copy_kernel, 1, 1),
                out_shape=jax.ShapeDtypeStruct(piece.shape, bf16),
                in_specs=[pl.BlockSpec(memory_space=pltpu.VMEM), UNREAD],
                out_specs=pl.BlockSpec(memory_space=pltpu.VMEM),
                compiler_params=params(),
                name="copy",
            )(piece, before)
            return lax.all_gather(piece, "dp", axis=0, tiled=True)

        ffn_grads = total_tiles(ffn_grad.reshape(3 * hidden, model), parts_out[1][0])
        attn_grads = total_tiles(attn_grad, parts_out[-1][0])
        tiles = jnp.concatenate([attn_grads, ffn_grads], axis=0).reshape(-1, tile_rows, model)
        reduced = tiles[slot_tile].astype(f32)

    even = jnp.array([[1.0], [1.0 / parts]], f32)
    gain_grad = small_total(gains_part * even)
    _, gain_moment, gain_new = adam_update(
        gain_grad, gain_first, gain_second, norm_gains, gain_rate, 0.0
    )

    first_new, second_new, param_new = adam_update(
        reduced, first_moment[0], second_moment[0], master[0], weight_rate, weight_decay
    )
    weight_grad = jnp.where(slot_used, reduced, 0.0)
    weight_first = jnp.where(slot_used, first_new, 0.0)
    weight_second = jnp.where(slot_used, second_new, 0.0)
    weight_master = jnp.where(slot_used, param_new, 0.0)
    weight_low = weight_master.astype(bf16)
    return (
        layer_out,
        input_grad,
        weight_grad[None],
        weight_first[None],
        weight_second[None],
        weight_master[None],
        weight_low[None],
        gain_grad,
        gain_moment,
        gain_new,
    )


def solution(mesh):
    return jax.shard_map(
        on_device,
        mesh=mesh,
        in_specs=(
            P("dp", None),
            P("dp", None),
            P("dp", None, None),
            P(),
            P(),
            P(),
            P("tensor", None),
            P("tensor", "dp", None, None),
            P("tensor", "dp", None, None),
            P("tensor", "dp", None, None),
        ),
        out_specs=(
            P("dp", None),
            P(("dp", "tensor"), None),
            P("tensor", "dp", None, None),
            P("tensor", "dp", None, None),
            P("tensor", "dp", None, None),
            P("tensor", "dp", None, None),
            P("tensor", "dp", None, None),
            P(),
            P(),
            P(),
        ),
        check_vma=False,
    )
```

```python
import functools

import jax
import jax.numpy as jnp
import numpy as np
from jax import lax
from jax.experimental import pallas as pl
from jax.experimental.pallas import tpu as pltpu
from jax.sharding import PartitionSpec as P

HEADS = 16
HD = 64
FF = 4096
STEP = 5

norm_eps = 1e-06
beta_one = 0.9
beta_two = 0.95
adam_eps = 1e-08
weight_rate = 0.05
gain_rate = 0.8
weight_decay = 0.1

score_scale = HD ** (-0.5)
f32 = jnp.float32
bf16 = jnp.bfloat16
VMEM_LIMIT = 60 * 1024 * 1024
NT = (((1,), (1,)), ((), ()))
TN = (((0,), (0,)), ((), ()))


def mm(left, right):
    return jnp.dot(left, right, preferred_element_type=f32)


def mm_nt(left, right):
    return lax.dot_general(left, right, NT, preferred_element_type=f32)


def mm_tn(left, right):
    return lax.dot_general(left, right, TN, preferred_element_type=f32)


def params(**kw):
    return pltpu.CompilerParams(vmem_limit_bytes=VMEM_LIMIT, **kw)


def cost(flops, nbytes, transcendentals=0):
    return pl.CostEstimate(
        flops=int(flops), bytes_accessed=int(nbytes), transcendentals=int(transcendentals)
    )


def whole_spec(shape):
    return pl.BlockSpec(shape, lambda *_: (0,) * len(shape))


def after(kernel, inputs, count):
    return lambda *refs: kernel(*refs[:inputs], *refs[inputs + count :])


UNREAD = pl.BlockSpec(memory_space=pl.ANY)


def rms_scale(values):
    return lax.rsqrt(jnp.mean(values * values, axis=-1, keepdims=True) + norm_eps)


def swap_halves(values):
    width = values.shape[1]
    lane = lax.broadcasted_iota(jnp.int32, values.shape, 1)
    return jnp.where(
        lane % HD < HD // 2,
        pltpu.roll(values, width - HD // 2, 1),
        pltpu.roll(values, HD // 2, 1),
    )


def cast_kernel(rank_ref, held_ref, slot_ref, tile_ref, low_ref, mine_ref):
    low_ref[...] = slot_ref[...].astype(bf16)
    tile = tile_ref[...].astype(bf16)
    held = held_ref[pl.program_id(0)] > 0
    mine_ref[...] = jnp.where(held, tile, jnp.zeros((), bf16))


def qkv_kernel(
    x_ref, gains_ref, tiles_ref, cos_ref, sin_ref, q_ref, k_ref, v_ref, w_ref, w_wide
):
    width = q_ref.shape[1]
    model = x_ref.shape[1]
    fold = model // width

    @pl.when(pl.program_id(0) == 0)
    def _():
        for block in range(3 * width // 128):
            part, lane = divmod(block * 128, width)
            for piece in range(fold):
                at = piece * width + lane
                w_wide[block, pl.ds(piece, width, stride=fold), :] = tiles_ref[
                    part * width : (part + 1) * width, at : at + 128
                ].astype(f32)
            w_ref[:, block * 128 : (block + 1) * 128] = w_wide[block].astype(bf16)

    x = x_ref[...].astype(f32)
    hidden = (x * rms_scale(x) * gains_ref[0:1, :]).astype(bf16)
    cos, sin = cos_ref[...], sin_ref[...]
    q = mm(hidden, w_ref[:, 0:width])
    q_ref[...] = (q * cos + swap_halves(q) * sin).astype(bf16)
    k = mm(hidden, w_ref[:, width : 2 * width])
    k_ref[...] = (k * cos + swap_halves(k) * sin).astype(bf16)
    v_ref[...] = mm(hidden, w_ref[:, 2 * width : 3 * width]).astype(bf16)


def attend(q, k, v):
    first = lax.broadcasted_iota(jnp.int32, q.shape, 1) < HD
    first_v = lax.broadcasted_iota(jnp.int32, v.shape, 1) < HD
    zero, one = jnp.zeros((), bf16), jnp.ones((), bf16)
    outs = []
    for head in range(2):
        q_head = jnp.where(first if head == 0 else ~first, q, zero)
        v_head = jnp.where(first_v if head == 0 else ~first_v, v, one)
        s = mm_nt(q_head, k)
        s = (s - jnp.max(s, axis=-1, keepdims=True)) * score_scale
        outs.append(mm(jnp.exp(s).astype(bf16), v_head))
    value = jnp.where(first, outs[0], outs[1])
    total = pltpu.roll(jnp.where(first, outs[1], outs[0]), HD, 1)
    return (value / total).astype(bf16)


def attend_kernel(q_ref, k_ref, v_ref, o_ref):
    o_ref[...] = attend(q_ref[...], k_ref[...], v_ref[...])


def attend_masked_kernel(rows_ref, x_ref, q_ref, k_ref, v_ref, o_ref, qm_ref, xm_ref):
    window = x_ref.shape[0]
    count = rows_ref.shape[1]
    pick = (
        lax.broadcasted_iota(jnp.int32, (count, window), 1) == rows_ref[0]
    ).astype(bf16)
    xm_ref[...] = mm(pick, x_ref[...]).astype(bf16)
    qm = mm(pick, q_ref[...]).astype(bf16)
    qm_ref[...] = qm
    for pair in range(q_ref.shape[1] // 128):
        lanes = slice(pair * 128, pair * 128 + 128)
        o_ref[:, lanes] = attend(qm[:, lanes], k_ref[:, lanes], v_ref[:, lanes])


def ffn_masked_kernel(
    parts, xm_ref, cot_ref, gains_ref, wg_ref, wu_ref, wd_ref, *refs
):
    o_refs, wo_refs = refs[:parts], refs[parts : 2 * parts]
    rm_ref, dhf_ref, grad_ref, hf_ref, acc_ref, wide_ref = refs[2 * parts :]
    step = pl.program_id(0)
    width = wg_ref.shape[1]
    cols = pl.ds(pl.multiple_of(step * width, width), width)
    hidden, model = grad_ref.shape[1:]
    fold = model // hidden

    def put(part, grad):
        if fold == 1:
            grad_ref[part, :, cols] = grad.astype(bf16)
            return
        for block in range(width // 128):
            wide_ref[block] = grad[:, block * 128 : (block + 1) * 128]
            for piece in range(fold):
                at = piece * hidden + step * width + block * 128
                at = pl.ds(pl.multiple_of(at, 128), 128)
                grad_ref[part, :, at] = wide_ref[
                    block, pl.ds(piece, hidden, stride=fold), :
                ].astype(bf16)

    @pl.when(step == 0)
    def _():
        r = xm_ref[...].astype(f32)
        for o_ref, wo_ref in zip(o_refs, wo_refs):
            r = r + mm(o_ref[...], wo_ref[...])
        rm_ref[...] = r
        hf_ref[...] = (r * rms_scale(r) * gains_ref[1:2, :]).astype(bf16)
        acc_ref[...] = jnp.zeros_like(acc_ref)

    hf, dy = hf_ref[...], cot_ref[...]
    wg, wu, wd = wg_ref[...], wu_ref[...], wd_ref[...]
    g, u = mm(hf, wg), mm(hf, wu)
    sig = jax.nn.sigmoid(g)
    act = (g * sig * u).astype(bf16)
    grad_ref[2, cols, :] = mm_tn(act, dy).astype(bf16)
    da = mm_nt(dy, wd)
    dg = (da * u * sig * (1.0 + g * (1.0 - sig))).astype(bf16)
    du = (da * g * sig).astype(bf16)
    put(0, mm_tn(hf, dg))
    put(1, mm_tn(hf, du))
    acc_ref[...] += mm_nt(dg, wg) + mm_nt(du, wu)

    @pl.when(step == pl.num_programs(0) - 1)
    def _():
        dhf_ref[...] = acc_ref[...].astype(bf16)


def ffn_kernel(parts, place_ref, x_ref, gains_ref, wg_ref, wu_ref, wd_ref, *refs):
    o_refs, wo_refs = refs[:parts], refs[parts : 2 * parts]
    part_ref, own_ref, r_ref, hf_ref, acc_ref = refs[2 * parts :]
    step = pl.program_id(0)

    @pl.when(step == 0)
    def _():
        r = x_ref[...].astype(f32)
        for o_ref, wo_ref in zip(o_refs, wo_refs):
            r = r + mm(o_ref[...], wo_ref[...])
        r_ref[...] = r
        hf_ref[...] = (r * rms_scale(r) * gains_ref[1:2, :]).astype(bf16)
        acc_ref[...] = jnp.zeros_like(acc_ref)

    hf = hf_ref[...]
    g, u = mm(hf, wg_ref[...]), mm(hf, wu_ref[...])
    act = (g * jax.nn.sigmoid(g) * u).astype(bf16)
    acc_ref[...] += mm(act, wd_ref[...])

    @pl.when(step == pl.num_programs(0) - 1)
    def _():
        share = own_ref.shape[0]
        part_ref[...] = acc_ref[...].astype(bf16)
        mine = pl.ds(pl.multiple_of(place_ref[0] * share, share), share)
        own_ref[...] = r_ref[mine, :] + acc_ref[mine, :]


def attn_back_kernel(
    rows_ref,
    dhf_ref,
    rm_ref,
    cot_ref,
    gains_ref,
    om_ref,
    qm_ref,
    cosm_ref,
    sinm_ref,
    k_ref,
    v_ref,
    x_ref,
    cos_ref,
    sin_ref,
    wo_ref,
    w_ref,
    drm_ref,
    dha_ref,
    gw_ref,
    gain_ref,
    gw_acc,
    go_acc,
    gain_acc,
    flow_ref,
    gw_wide,
):
    step = pl.program_id(0)

    @pl.when(step == 0)
    def _():
        gw_acc[...] = jnp.zeros_like(gw_acc)
        go_acc[...] = jnp.zeros_like(go_acc)
        gain_acc[...] = jnp.zeros_like(gain_acc)

    window, width = k_ref.shape
    count = rm_ref.shape[0]
    r = rm_ref[...]
    sf = rms_scale(r)
    nf = r * sf
    dhf = dhf_ref[...].astype(f32)
    dnf = dhf * gains_ref[1:2, :]
    dr = cot_ref[...].astype(f32) + sf * (
        dnf - nf * jnp.mean(dnf * nf, axis=-1, keepdims=True)
    )
    drm_ref[...] = dr
    gain_acc[1:2, :] += jnp.sum(dhf * nf, axis=0, keepdims=True)
    drb = dr.astype(bf16)
    go_acc[...] += mm_tn(om_ref[...], drb)
    dob = mm_nt(drb, wo_ref[...]).astype(bf16)

    first = lax.broadcasted_iota(jnp.int32, (count, 128), 1) < HD
    zero = jnp.zeros((), bf16)
    drq = []
    for pair in range(width // 128):
        lanes = slice(pair * 128, pair * 128 + 128)
        k, v = k_ref[:, lanes], v_ref[:, lanes]
        qm, do = qm_ref[:, lanes], dob[:, lanes]
        parts = []
        drk = dv = None
        for head in range(2):
            mine = first if head == 0 else ~first
            q_head = jnp.where(mine, qm, zero)
            do_head = jnp.where(mine, do, zero)
            s = mm_nt(k, q_head)
            s = jnp.exp((s - jnp.max(s, axis=0, keepdims=True)) * score_scale)
            att = s / jnp.sum(s, axis=0, keepdims=True)
            dpa = mm_nt(v, do_head)
            ds = att * (dpa - jnp.sum(dpa * att, axis=0, keepdims=True))
            ds = (ds * score_scale).astype(bf16)
            parts.append(mm_tn(ds, k))
            drk_head = mm(ds, q_head)
            dv_head = mm(att.astype(bf16), do_head)
            drk = drk_head if drk is None else drk + drk_head
            dv = dv_head if dv is None else dv + dv_head
        drq.append(jnp.where(first, parts[0], parts[1]))
        dk = drk * cos_ref[:, lanes] - swap_halves(drk) * sin_ref[:, lanes]
        flow_ref[:, width + pair * 128 : width + pair * 128 + 128] = dk.astype(bf16)
        flow_ref[:, 2 * width + pair * 128 : 2 * width + pair * 128 + 128] = dv.astype(
            bf16
        )
    spread = (
        lax.broadcasted_iota(jnp.int32, (window, count), 0) == rows_ref[0]
    ).astype(bf16)
    for pair in range(width // 128):
        lanes = slice(pair * 128, pair * 128 + 128)
        dq = drq[pair] * cosm_ref[:, lanes] - swap_halves(drq[pair]) * sinm_ref[:, lanes]
        flow_ref[:, lanes] = mm(spread, dq.astype(bf16)).astype(bf16)

    flow = flow_ref[...]
    x = x_ref[...].astype(f32)
    na = x * rms_scale(x)
    dha = mm_nt(flow, w_ref[...])
    gain_acc[0:1, :] += jnp.sum(dha * na, axis=0, keepdims=True)
    cuts, shares, rows = dha_ref.shape[:3]
    for piece in range(window // rows):
        block = step * (window // rows) + piece
        dha_ref[block % cuts, block // cuts] = dha[piece * rows : (piece + 1) * rows].astype(bf16)
    gw_acc[...] += mm_tn((na * gains_ref[0:1, :]).astype(bf16), flow)

    @pl.when(step == pl.num_programs(0) - 1)
    def _():
        fold = gw_acc.shape[0] // width
        for block in range(3 * width // 128):
            part, lane = divmod(block * 128, width)
            gw_wide[block] = gw_acc[:, block * 128 : (block + 1) * 128]
            for piece in range(fold):
                at = piece * width + lane
                gw_ref[part * width : (part + 1) * width, at : at + 128] = gw_wide[
                    block, pl.ds(piece, width, stride=fold), :
                ].astype(bf16)
        gw_ref[3 * width :, :] = go_acc[...].astype(bf16)
        gain_ref[...] = gain_acc[...]


def input_grad_kernel(
    cut, place_ref, rows_ref, drm_ref, gains_ref, x_ref, part_ref, *refs
):
    out_ref = refs[-1]
    block, count = x_ref.shape[0], drm_ref.shape[0]
    base = (place_ref[0] * cut[1] + cut[0]) * block
    spread = (
        lax.broadcasted_iota(jnp.int32, (block, count), 0) + base == rows_ref[...]
    ).astype(bf16)
    dr = drm_ref[...]
    high = dr.astype(bf16)
    low = (dr - high.astype(f32)).astype(bf16)
    dr = mm(spread, high) + mm(spread, low)
    x = x_ref[...].astype(f32)
    sa = rms_scale(x)
    na = x * sa
    dha = part_ref[0, 0].astype(f32)
    for ref in refs[: cut[2]]:
        dha = dha + ref[...].astype(f32)
    dna = dha * gains_ref[0:1, :]
    out = dr + sa * (dna - na * jnp.mean(dna * na, axis=-1, keepdims=True))
    out_ref[...] = out.astype(bf16)


def input_grad_rows(dha, x, dr, gain, spread):
    high = dr.astype(bf16)
    low = (dr - high.astype(f32)).astype(bf16)
    dr = mm(spread, high) + mm(spread, low)
    sa = rms_scale(x)
    na = x * sa
    dna = dha * gain
    return dr + sa * (dna - na * jnp.mean(dna * na, axis=-1, keepdims=True))


def remote(src, dst, send, recv, place):
    return pltpu.make_async_remote_copy(
        src_ref=src,
        dst_ref=dst,
        send_sem=send,
        recv_sem=recv,
        device_id={"tensor": place},
        device_id_type=pl.DeviceIdType.MESH,
    )


def greet_line(place, others=()):
    barrier = pltpu.get_barrier_semaphore()
    for axis, other in others:
        pl.semaphore_signal(
            barrier,
            inc=1,
            device_id={axis: other},
            device_id_type=pl.DeviceIdType.MESH,
        )
    for k in range(1, 4):
        pl.semaphore_signal(
            barrier,
            inc=1,
            device_id={"tensor": lax.rem(place + k, 4)},
            device_id_type=pl.DeviceIdType.MESH,
        )
    pl.semaphore_wait(barrier, 3 + len(others))


def sends(place, d, up):
    if up:
        return (place >= d - 1) & (place <= 2)
    return (place <= 4 - d) & (place >= 1)


def receives(place, d, up):
    return place >= d if up else place <= 3 - d


def each_way(place, d, rule, act):
    for up in (True, False):

        @pl.when(rule(place, d, up))
        def _():
            act(up)


def rows_ref(ref, index, share, count):
    return ref.at[pl.ds(pl.multiple_of(index * share, share), count * share), :]


def weights_kernel(
    rank_ref,
    held_ref,
    master_ref,
    low_ref,
    out_ref,
    mine,
    got,
    work,
    trade,
    h_send,
    h_recv,
    t_send,
    t_recv,
    f_send,
    f_recv,
    f_keep,
):
    me = lax.axis_index("dp")
    core = lax.rem(me, 2)
    tiles = mine.shape[0]
    half = tiles // 2

    def pair(bit):
        return me + bit - 2 * bit * lax.rem(me // bit, 2)

    def to(src, dst, send, recv, bit):
        return pltpu.make_async_remote_copy(
            src_ref=src,
            dst_ref=dst,
            send_sem=send,
            recv_sem=recv,
            device_id={"dp": pair(bit)},
            device_id_type=pl.DeviceIdType.MESH,
        )

    def share(first):
        return pl.ds(first * half, half)

    swap = to(mine.at[share(1 - core)], got, h_send, h_recv, 1)

    def move(stage, t):
        bit = (2, 4)[(stage + t // (half // 2)) % 2]
        return to(
            work.at[stage, t],
            trade.at[stage, t],
            t_send.at[stage, t],
            t_recv.at[stage, t],
            bit,
        )

    def final(t):
        return to(work.at[2, t], out_ref.at[core * half + t], f_send.at[t], f_recv.at[t], 1)

    def final_in(t):
        at = out_ref.at[(1 - core) * half + t]
        return to(at, at, f_send.at[t], f_recv.at[t], 1)

    def keep(t):
        return pltpu.make_async_copy(
            work.at[2, t], out_ref.at[core * half + t], f_keep.at[t]
        )

    barrier = pltpu.get_barrier_semaphore()
    for bit in (1, 2, 4):
        pl.semaphore_signal(
            barrier, inc=1, device_id={"dp": pair(bit)}, device_id_type=pl.DeviceIdType.MESH
        )
    for t in range(tiles):
        tile = master_ref[rank_ref[t]].astype(bf16)
        mine[t] = jnp.where(held_ref[t] > 0, tile, jnp.zeros((), bf16))
    pl.semaphore_wait(barrier, 3)
    swap.start()
    for n in range(low_ref.shape[0]):
        low_ref[n] = master_ref[n].astype(bf16)
    swap.wait_recv()
    turns = [t + n for t in range(half // 2) for n in (0, half // 2)]
    for t in turns:
        work[0, t] = mine[core * half + t] + got[t]
        move(0, t).start()
    for stage in (1, 2):
        for t in turns:
            move(stage - 1, t).wait_recv()
            work[stage, t] = work[stage - 1, t] + trade[stage - 1, t]
            if stage == 1:
                move(1, t).start()
            else:
                final(t).start()
                keep(t).start()
    for t in range(half):
        final_in(t).wait_recv()
    swap.wait_send()
    for t in range(half):
        keep(t).wait()
        final(t).wait_send()
        for stage in range(2):
            move(stage, t).wait_send()


def attend_all_kernel(
    windows,
    rows_in,
    gains_ref,
    tiles_ref,
    cos_ref,
    sin_ref,
    x_hbm,
    tiles_hbm,
    om_out,
    oa_out,
    ob_out,
    oc_out,
    wo_out,
    qm_ref,
    xm_ref,
    cosm_ref,
    sinm_ref,
    k_ref,
    v_ref,
    w_ref,
    q_ref,
    w_wide,
    om_own,
    o_own,
    x_ref,
    x_sem,
    own_sem,
    keep_sem,
    m_send,
    m_recv,
    o_send,
    o_recv,
    w_send,
    w_recv,
    c_send,
    c_recv,
):
    place = lax.axis_index("tensor")
    window = x_ref.shape[1]
    width = q_ref.shape[1]
    count = rows_in.shape[1]
    q_block = 256

    def load_x(w):
        return pltpu.make_async_copy(
            x_hbm.at[pl.ds(w * window, window), :], x_ref.at[w % 2], x_sem.at[w % 2]
        )

    def hop(kind, d, up):
        own, out, send, recv = (
            (om_own, om_out, m_send, m_recv) if kind == 0 else (o_own.at[0], oa_out, o_send, o_recv)
        )
        src, dst = (d - 1, d) if up else ((5 - d) % 4, 4 - d)
        n = 0 if up else 1
        return remote(
            own if d == 1 else out.at[src],
            out.at[dst],
            send.at[d - 1, n],
            recv.at[d - 1, n],
            lax.rem(place + (1 if up else 3), 4),
        )

    me = lax.axis_index("dp")
    core = lax.rem(me, 2)
    half = width // 2

    def half_of(ref, first):
        return ref.at[pl.ds(pl.multiple_of(first + core * half, half), half), :]

    def hop_w(d, up):
        src, dst = (d - 1, d) if up else ((5 - d) % 4, 4 - d)
        n = 0 if up else 1
        return remote(
            half_of(tiles_hbm, 3 * width) if d == 1 else half_of(wo_out.at[src - 1], 0),
            half_of(wo_out.at[dst - 1], 0),
            w_send.at[d - 1, n],
            w_recv.at[d - 1, n],
            lax.rem(place + (1 if up else 3), 4),
        )

    sibling = me + 1 - 2 * core

    def copy_w(n):
        return pltpu.make_async_remote_copy(
            src_ref=half_of(wo_out.at[n], 0),
            dst_ref=half_of(wo_out.at[n], 0),
            send_sem=c_send.at[n],
            recv_sem=c_recv.at[n],
            device_id={"dp": sibling},
            device_id_type=pl.DeviceIdType.MESH,
        )

    def copy_w_in(n):
        rows = pl.ds(pl.multiple_of((1 - core) * half, half), half)
        return pltpu.make_async_remote_copy(
            src_ref=wo_out.at[n].at[rows, :],
            dst_ref=wo_out.at[n].at[rows, :],
            send_sem=c_send.at[n],
            recv_sem=c_recv.at[n],
            device_id={"dp": sibling},
            device_id_type=pl.DeviceIdType.MESH,
        )

    def any_hop(kind, d, up):
        return hop_w(d, up) if kind == 2 else hop(kind, d, up)

    def hops(kind, d):
        each_way(place, d, sends, lambda up: any_hop(kind, d, up).start())

    def hops_in(kind, d):
        each_way(place, d, receives, lambda up: any_hop(kind, d, up).wait_recv())

    def store(w):
        to = (oa_out.at[0], ob_out, oc_out)[w]
        return pltpu.make_async_copy(o_own.at[w], to, own_sem.at[w])

    def attend_rows(w, first, last):
        for pair in range(width // 128):
            lanes = slice(pair * 128, pair * 128 + 128)
            keys = slice(w * window, (w + 1) * window)

            def block(i, carry):
                rows = pl.ds(pl.multiple_of(w * window + i * q_block, q_block), q_block)
                into = pl.ds(pl.multiple_of(i * q_block, q_block), q_block)
                o_own[w, into, lanes] = attend(
                    q_ref[rows, lanes], k_ref[keys, lanes], v_ref[keys, lanes]
                )
                return carry

            lax.fori_loop(first, last, block, 0)

    def picked(pick, table):
        high = table.astype(bf16)
        low = (table - high.astype(f32)).astype(bf16)
        return mm(pick, high) + mm(pick, low)

    def project(w):
        rows = window // 2

        def block(n, carry):
            here = pl.ds(pl.multiple_of(n * rows, rows), rows)
            at = pl.ds(pl.multiple_of(w * window + n * rows, rows), rows)
            x = x_ref[w % 2, here, :].astype(f32)
            hidden = (x * rms_scale(x) * gains_ref[0:1, :]).astype(bf16)
            cos, sin = cos_ref[here, :], sin_ref[here, :]
            q = mm(hidden, w_ref[:, 0:width])
            q_ref[at, :] = (q * cos + swap_halves(q) * sin).astype(bf16)
            k = mm(hidden, w_ref[:, width : 2 * width])
            k_ref[at, :] = (k * cos + swap_halves(k) * sin).astype(bf16)
            v_ref[at, :] = mm(hidden, w_ref[:, 2 * width : 3 * width]).astype(bf16)
            return carry

        load_x(w).wait()
        lax.fori_loop(0, 2, block, 0)
        at = slice(w * count, (w + 1) * count)
        pick = (
            lax.broadcasted_iota(jnp.int32, (count, window), 1) == rows_in[w]
        ).astype(bf16)
        xm_ref[at, :] = mm(pick, x_ref[w % 2]).astype(bf16)
        if w + 2 < windows:
            load_x(w + 2).start()
        cosm_ref[at, :] = picked(pick, cos_ref[...])
        sinm_ref[at, :] = picked(pick, sin_ref[...])
        qm_ref[at, :] = mm(pick, q_ref[w * window : (w + 1) * window, :]).astype(bf16)

    for w in range(2):
        load_x(w).start()
    greet_line(place, [("dp", sibling)])
    blocks = window // q_block
    hops(2, 1)
    fold = tiles_ref.shape[1] // width
    for block in range(3 * width // 128):
        part, lane = divmod(block * 128, width)
        for piece in range(fold):
            at = piece * width + lane
            w_wide[block, pl.ds(piece, width, stride=fold), :] = tiles_ref[
                part * width : (part + 1) * width, at : at + 128
            ].astype(f32)
        w_ref[:, block * 128 : (block + 1) * 128] = w_wide[block].astype(bf16)
    project(0)
    hops_in(2, 1)
    hops(2, 2)
    attend_rows(0, 0, blocks)
    hops(1, 1)
    store(0).start()
    hops_in(2, 2)
    hops(2, 3)
    project(1)
    project(2)
    hops_in(1, 1)
    hops(1, 2)
    for w in range(windows):
        keys = slice(w * window, (w + 1) * window)
        at = slice(w * count, (w + 1) * count)
        for pair in range(width // 128):
            lanes = slice(pair * 128, pair * 128 + 128)
            om_own[at, lanes] = attend(
                qm_ref[at, lanes], k_ref[keys, lanes], v_ref[keys, lanes]
            )
    hops(0, 1)
    keep = pltpu.make_async_copy(om_own, om_out.at[0], keep_sem)
    keep.start()
    attend_rows(1, 0, blocks // 2)
    hops_in(0, 1)
    hops(0, 2)
    attend_rows(1, blocks // 2, blocks)
    store(1).start()
    hops_in(0, 2)
    hops(0, 3)
    hops_in(1, 2)
    hops(1, 3)
    attend_rows(2, 0, blocks)
    store(2).start()
    hops_in(2, 3)
    for n in range(3):
        copy_w(n).start()
    keep.wait()
    for w in range(windows):
        store(w).wait()
    for kind in range(2):
        hops_in(kind, 3)
    for kind in range(3):
        for d in range(1, 4):
            each_way(place, d, sends, lambda up: any_hop(kind, d, up).wait_send())
    for n in range(3):
        copy_w(n).wait_send()
        copy_w_in(n).wait_recv()


def masked_attention_back(qm, do, k, v):
    first = lax.broadcasted_iota(jnp.int32, qm.shape, 1) < HD
    zero = jnp.zeros((), bf16)
    parts = []
    drk = dv = None
    for head in range(2):
        mine = first if head == 0 else ~first
        q_head = jnp.where(mine, qm, zero)
        do_head = jnp.where(mine, do, zero)
        s = mm_nt(k, q_head)
        s = jnp.exp((s - jnp.max(s, axis=0, keepdims=True)) * score_scale)
        att = s / jnp.sum(s, axis=0, keepdims=True)
        dpa = mm_nt(v, do_head)
        ds = att * (dpa - jnp.sum(dpa * att, axis=0, keepdims=True))
        ds = (ds * score_scale).astype(bf16)
        parts.append(mm_tn(ds, k))
        drk_head = mm(ds, q_head)
        dv_head = mm(att.astype(bf16), do_head)
        drk = drk_head if drk is None else drk + drk_head
        dv = dv_head if dv is None else dv + dv_head
    return jnp.where(first, parts[0], parts[1]), drk, dv


def middle_kernel(
    windows,
    rows_in,
    gains_ref,
    xm_ref,
    cot_ref,
    qm_ref,
    cosm_ref,
    sinm_ref,
    cos_ref,
    sin_ref,
    w_ref,
    ffn_ref,
    om_ref,
    oa_ref,
    wo_ref,
    wo_far,
    *refs,
):
    wg_ref, wu_ref, wd_ref = (ffn_ref.at[n] for n in range(3))
    om_refs, oa_refs = ([ref.at[n] for n in range(4)] for ref in (om_ref, oa_ref))
    wo_refs = [wo_ref] + [wo_far.at[n] for n in range(3)]
    x_hbm, k_hbm, v_hbm, o_one, o_two = refs[0:5]
    part_out, own_out, ra_out, rb_out, dha_out, grads_out, drm_ref, gain_ref = refs[5:13]
    (
        r_ref,
        hf_ref,
        acc_ref,
        p_ref,
        own_ref,
        obuf,
        x_ref,
        kv,
        flow_ref,
        gw_acc,
        gw_wide,
        go_acc,
        rm_ref,
        dpart,
        drecv,
        dall,
        bsum,
        b_load,
        b_send,
        b_recv,
        o_load,
        x_sem,
        kv_sem,
        grad_sem,
        p_sem,
        dha_sem,
        own_sem,
        a_send,
        a_recv,
        o_send,
        o_recv,
        d_send,
        d_recv,
        e_send,
        e_recv,
    ) = refs[13:]
    place = lax.axis_index("tensor")
    lower = place < 2
    outer = (place == 0) | (place == 3)
    inner = (place == 1) | (place == 2)
    window, model = x_ref.shape
    width = kv.shape[3]
    hidden = ffn_ref.shape[2]
    share = own_ref.shape[0]
    count = rm_ref.shape[0] // windows
    masked = rm_ref.shape[0]
    cols = 256
    chunks = hidden // cols

    def hop(g, d, up):
        src, dst = (d - 1, d) if up else ((5 - d) % 4, 4 - d)
        n = 0 if up else 1
        return remote(
            obuf.at[g, src],
            obuf.at[g, dst],
            o_send.at[g, d - 1, n],
            o_recv.at[g, d - 1, n],
            lax.rem(place + (1 if up else 3), 4),
        )

    def hops(g, d):
        each_way(place, d, sends, lambda up: hop(g, d, up).start())

    def hops_in(g, d):
        each_way(place, d, receives, lambda up: hop(g, d, up).wait_recv())

    def load_o(g):
        return pltpu.make_async_copy((o_one, o_two)[g], obuf.at[g, 0], o_load.at[g])

    def load_x(w):
        return pltpu.make_async_copy(
            x_hbm.at[pl.ds(w * window, window), :], x_ref, x_sem
        )

    def load_kv(w):
        return [
            pltpu.make_async_copy(
                hbm.at[pl.ds(w * window, window), :], kv.at[w % 2, n], kv_sem.at[w % 2, n]
            )
            for n, hbm in enumerate((k_hbm, v_hbm))
        ]

    def store_p(to):
        return pltpu.make_async_copy(p_ref, to, p_sem)

    def store_own(w):
        return pltpu.make_async_copy(own_ref, own_out.at[w], own_sem)

    def copy_a(w):
        far = rows_ref(part_out.at[w], jnp.where(lower, 1, 0), share, 3)
        return remote(far, ra_out.at[w], a_send.at[w], a_recv.at[w], jnp.where(lower, 1, 2))

    def copy_d(k):
        to = lax.rem(place + k, 4)
        return remote(dpart.at[to], drecv.at[k - 1], d_send.at[k - 1], d_recv.at[k - 1], to)

    def copy_e(k, origin):
        to = lax.rem(place + k, 4)
        return remote(dall.at[origin], dall.at[origin], e_send.at[k - 1], e_recv.at[k - 1], to)

    for g in range(2):
        load_o(g).start()
    load_x(0).start()
    for copy in load_kv(0):
        copy.start()
    greet_line(place)
    load_o(0).wait()
    hops(0, 1)
    gain_att, gain_ffn = gains_ref[0:1, :], gains_ref[1:2, :]

    def grad_copies(c):
        side = (c % 2) * 2 * cols
        base = 4 * width
        at = pl.ds(c * cols, cols)
        below = window - 2 * cols + (c % 2) * cols
        return [
            pltpu.make_async_copy(
                p_ref.at[:, pl.ds(side, cols)],
                grads_out.at[pl.ds(base, model), at],
                grad_sem.at[c % 2, 0],
            ),
            pltpu.make_async_copy(
                p_ref.at[:, pl.ds(side + cols, cols)],
                grads_out.at[pl.ds(base + hidden, model), at],
                grad_sem.at[c % 2, 1],
            ),
            pltpu.make_async_copy(
                hf_ref.at[pl.ds(below, cols), :],
                grads_out.at[pl.ds(base + 2 * hidden + c * cols, cols), :],
                grad_sem.at[c % 2, 2],
            ),
        ]

    def masked_chunk(c):
        if c >= 2:
            for copy in grad_copies(c - 2):
                copy.wait()
        at = slice(c * cols, (c + 1) * cols)
        side = (c % 2) * 2 * cols
        below = window - 2 * cols + (c % 2) * cols
        hf, dy = hf_ref[0:masked, :], cot_ref[...]
        wg, wu, wd = wg_ref[:, at], wu_ref[:, at], wd_ref[at, :]
        g, u = mm(hf, wg), mm(hf, wu)
        sig = jax.nn.sigmoid(g)
        act = (g * sig * u).astype(bf16)
        hf_ref[below : below + cols, :] = mm_tn(act, dy).astype(bf16)
        da = mm_nt(dy, wd)
        dg = (da * u * sig * (1.0 + g * (1.0 - sig))).astype(bf16)
        du = (da * g * sig).astype(bf16)
        p_ref[:, side : side + cols] = mm_tn(hf, dg).astype(bf16)
        p_ref[:, side + cols : side + 2 * cols] = mm_tn(hf, du).astype(bf16)
        part = mm_nt(dg, wg) + mm_nt(du, wu)
        if c == 0:
            acc_ref[0:masked, :] = part
        else:
            acc_ref[0:masked, :] += part
        for copy in grad_copies(c):
            copy.start()

    def ffn(w, o_refs, next_x, between=None):
        half = window // 2

        def first(n, carry):
            rows = pl.ds(pl.multiple_of(n * half, half), half)
            r = x_ref[rows, :].astype(f32)
            for o, wo in zip(o_refs, wo_refs):
                r = r + mm(o[rows, :], wo[...])
            r_ref[rows, :] = r
            hf_ref[rows, :] = (r * rms_scale(r) * gain_ffn).astype(bf16)
            return carry

        lax.fori_loop(0, 2, first, 0)
        if next_x is not None:
            load_x(next_x).start()
        acc_ref[...] = jnp.zeros_like(acc_ref)

        def chunk(c, carry):
            at = pl.ds(pl.multiple_of(c * cols, cols), cols)
            hf = hf_ref[...]
            g, u = mm(hf, wg_ref[:, at]), mm(hf, wu_ref[:, at])
            act = (g * jax.nn.sigmoid(g) * u).astype(bf16)
            acc_ref[...] += mm(act, wd_ref[at, :])
            return carry

        if between is None:
            lax.fori_loop(0, chunks, chunk, 0)
        else:
            lax.fori_loop(0, chunks - 1, chunk, 0)
            between()
            lax.fori_loop(chunks - 1, chunks, chunk, 0)
        p_ref[...] = acc_ref[...].astype(bf16)
        store_p(part_out.at[w]).start()
        mine = pl.ds(pl.multiple_of(place * share, share), share)
        own_ref[...] = r_ref[mine, :] + acc_ref[mine, :]
        store_own(w).start()
        store_p(part_out.at[w]).wait()
        store_own(w).wait()

    def inward(w):
        @pl.when(outer)
        def _():
            copy_a(w).start()

    def sum_dhf():
        for k in range(1, 4):
            copy_d(k).wait_recv()
        total = dpart[place].astype(f32)
        for k in range(3):
            total = total + drecv[k].astype(f32)
        dall[place] = total.astype(bf16)
        for k in range(1, 4):
            copy_e(k, place).start()

    r = xm_ref[...].astype(f32)
    for om, wo in zip(om_refs, wo_refs):
        r = r + mm(om[...], wo[...])
    rm_ref[...] = r
    hf_ref[0:masked, :] = (r * rms_scale(r) * gain_ffn).astype(bf16)
    for c in range(chunks // 2):
        masked_chunk(c)
    hops_in(0, 1)
    hops(0, 2)
    for c in range(chunks // 2, chunks):
        masked_chunk(c)
    block = model // 4
    for n in range(4):
        dpart[n] = acc_ref[0:masked, n * block : (n + 1) * block].astype(bf16)
    for k in range(1, 4):
        copy_d(k).start()
    hops_in(0, 2)
    hops(0, 3)
    for c in range(chunks - 2, chunks):
        for copy in grad_copies(c):
            copy.wait()

    load_o(1).wait()
    load_x(0).wait()
    ffn(0, oa_refs, 1)
    inward(0)
    hops_in(0, 3)
    hops(1, 1)
    load_x(1).wait()

    def meanwhile():
        sum_dhf()
        hops_in(1, 1)
        hops(1, 2)

    ffn(1, [obuf.at[0, n] for n in range(4)], 2, meanwhile)
    inward(1)
    hops_in(1, 2)
    hops(1, 3)
    hops_in(1, 3)
    load_x(2).wait()
    ffn(2, [obuf.at[1, n] for n in range(4)], 0)
    inward(2)

    def copy_b(w):
        return remote(
            bsum.at[w], rb_out.at[w], b_send.at[w], b_recv.at[w], jnp.where(lower, 2, 1)
        )

    def exchange_rows(w):
        @pl.when(inner)
        def _():
            copy_a(w).wait_recv()
            rows = rows_ref(ra_out.at[w], jnp.where(lower, 1, 0), share, 2)
            mine = rows_ref(part_out.at[w], jnp.where(lower, 2, 0), share, 2)
            got = pltpu.make_async_copy(rows, bsum.at[w], b_load.at[0])
            add = pltpu.make_async_copy(mine, hf_ref.at[pl.ds(0, 2 * share), :], b_load.at[1])
            got.start()
            add.start()
            got.wait()
            add.wait()
            total = bsum[w].astype(f32) + hf_ref[0 : 2 * share, :].astype(f32)
            bsum[w] = total.astype(bf16)
            copy_b(w).start()

    exchange_rows(0)

    for k in range(1, 4):
        copy_e(k, lax.rem(place + 4 - k, 4)).wait_recv()
    gw_acc[...] = jnp.zeros_like(gw_acc)
    go_acc[...] = jnp.zeros_like(go_acc)
    gain_ref[...] = jnp.zeros_like(gain_ref)
    def back_window(w, next_x):
        for copy in load_kv(w):
            copy.wait()
        if w + 1 < windows:
            for copy in load_kv(w + 1):
                copy.start()
        at = slice(w * count, (w + 1) * count)
        r = rm_ref[at, :]
        sf = rms_scale(r)
        nf = r * sf
        dhf = jnp.concatenate([dall[n, at, :] for n in range(4)], axis=1).astype(f32)
        dnf = dhf * gain_ffn
        dr = cot_ref[at, :].astype(f32) + sf * (
            dnf - nf * jnp.mean(dnf * nf, axis=-1, keepdims=True)
        )
        drm_ref[at, :] = dr
        gain_ref[1:2, :] += jnp.sum(dhf * nf, axis=0, keepdims=True)
        drb = dr.astype(bf16)
        go_acc[...] += mm_tn(om_refs[0][at, :], drb)
        dob = mm_nt(drb, wo_refs[0][...]).astype(bf16)
        spread = (
            lax.broadcasted_iota(jnp.int32, (window, count), 0) == rows_in[w]
        ).astype(bf16)
        for pair in range(width // 128):
            lanes = slice(pair * 128, pair * 128 + 128)
            drq, drk, dv = masked_attention_back(
                qm_ref[at, lanes], dob[:, lanes], kv[w % 2, 0, :, lanes], kv[w % 2, 1, :, lanes]
            )
            dk = drk * cos_ref[:, lanes] - swap_halves(drk) * sin_ref[:, lanes]
            dq = drq * cosm_ref[at, lanes] - swap_halves(drq) * sinm_ref[at, lanes]
            first = pair * 128
            flow_ref[:, first : first + 128] = mm(spread, dq.astype(bf16)).astype(bf16)
            flow_ref[:, width + first : width + first + 128] = dk.astype(bf16)
            flow_ref[:, 2 * width + first : 2 * width + first + 128] = dv.astype(bf16)
        load_x(w).wait()

        def back(n, carry):
            rows = pl.ds(pl.multiple_of(n * share, share), share)
            x = x_ref[rows, :].astype(f32)
            na = x * rms_scale(x)
            dha = mm_nt(flow_ref[rows, :], w_ref[...])
            gain_ref[0:1, :] += jnp.sum(dha * na, axis=0, keepdims=True)
            p_ref[rows, :] = dha.astype(bf16)
            hf_ref[rows, :] = (na * gain_att).astype(bf16)
            return carry

        lax.fori_loop(0, window // share, back, 0)
        for copy in dha_copies(dha_out, p_ref, dha_sem, w, windows, share):
            copy.start()
        if next_x is not None:
            load_x(next_x).start()
        gw_acc[...] += mm_tn(hf_ref[...], flow_ref[...])

    def dha_stored(w):
        for copy in dha_copies(dha_out, p_ref, dha_sem, w, windows, share):
            copy.wait()

    back_window(0, 1)
    dha_stored(0)
    back_window(1, 2)
    dha_stored(1)
    exchange_rows(1)
    back_window(2, None)
    dha_stored(2)
    fold = model // width
    for block in range(3 * width // 128):
        part, lane = divmod(block * 128, width)
        gw_wide[...] = gw_acc[:, block * 128 : (block + 1) * 128]
        for piece in range(fold):
            at = piece * width + lane
            p_ref[part * width : (part + 1) * width, at : at + 128] = gw_wide[
                pl.ds(piece, width, stride=fold), :
            ].astype(bf16)
    p_ref[3 * width :, :] = go_acc[...].astype(bf16)
    store = store_p(grads_out.at[pl.ds(0, 4 * width), :])
    store.start()
    store.wait()

    for w in range(windows):

        @pl.when(outer)
        def _():
            copy_a(w).wait_send()

    @pl.when(inner)
    def _():
        copy_a(2).wait_recv()
        for w in range(2):
            copy_b(w).wait_send()
            copy_b(w).wait_recv()

    for k in range(1, 4):
        copy_d(k).wait_send()
        copy_e(k, place).wait_send()
    for g in range(2):
        for d in range(1, 4):
            each_way(place, d, sends, lambda up: hop(g, d, up).wait_send())


def dha_copies(dha_out, p_ref, sem, w, windows, share):
    copies = []
    per = p_ref.shape[0] // share
    for n in range(per):
        block = w * per + n
        copies.append(
            pltpu.make_async_copy(
                p_ref.at[pl.ds(n * share, share), :],
                dha_out.at[block % windows, pl.ds(block // windows * share, share), :],
                sem.at[n],
            )
        )
    return copies


def lines_kernel(
    cuts,
    windows,
    order,
    ready,
    traded,
    rows_in,
    drm_ref,
    gains_ref,
    x_ref,
    dha_ref,
    part_ref,
    own_in,
    ra_in,
    rb_in,
    gain_in,
    out_ref,
    grad_ref,
    gain_ref,
    ra,
    rb,
    rc,
    value,
    own,
    piece,
    x_rows,
    grad,
    gain_sum,
    gain_got,
    s_send,
    s_recv,
    a_send,
    a_recv,
    b_send,
    b_recv,
    c_send,
    c_recv,
    g_send,
    g_recv,
    v_sem,
    o_sem,
    r_sem,
    t_sem,
    x_sem,
    l_sem,
    i_sem,
):
    place = lax.axis_index("tensor")
    lower = place < 2
    outer = (place == 0) | (place == 3)
    inner = (place == 1) | (place == 2)
    share = rc.shape[1]
    folds = len(order)

    def whole(f):
        kind, index = order[f]
        return part_ref.at[index] if kind == 0 else dha_ref.at[index]

    def copy_a(f):
        far = rows_ref(whole(f), jnp.where(lower, 1, 0), share, 3)
        return remote(far, ra.at[f], a_send.at[f], a_recv.at[f], jnp.where(lower, 1, 2))

    def copy_b(f):
        src = rows_ref(ra.at[f], jnp.where(lower, 1, 0), share, 2)
        return remote(src, rb.at[f], b_send.at[f], b_recv.at[f], jnp.where(lower, 2, 1))

    def copy_c(f):
        src = rows_ref(rb.at[f], jnp.where(lower, 0, 1), share, 1)
        return remote(src, rc.at[f], c_send.at[f], c_recv.at[f], jnp.where(lower, 0, 3))

    def load(f):
        return pltpu.make_async_copy(whole(f), value.at[f], v_sem.at[f])

    def load_own(w):
        return pltpu.make_async_copy(own_in.at[w], own.at[w], o_sem.at[w])

    def load_ra(f):
        return pltpu.make_async_copy(ra_in.at[order[f][1]], ra.at[f], r_sem.at[f])

    def load_rb(f):
        return pltpu.make_async_copy(rb_in.at[order[f][1]], rb.at[f], t_sem.at[f])

    def hop(w, d, up, origin):
        rows = pl.ds(pl.multiple_of(w * 4 * share + origin * share, share), share)
        n = 0 if up else 1
        return remote(
            piece.at[w] if d == 1 else out_ref.at[rows, :],
            out_ref.at[rows, :],
            g_send.at[w, d - 1, n],
            g_recv.at[w, d - 1, n],
            lax.rem(place + (1 if up else 3), 4),
        )

    def source(d, up):
        return jnp.clip(place - (d - 1) if up else place + (d - 1), 0, 3)

    def hops(w, d):
        each_way(place, d, sends, lambda up: hop(w, d, up, source(d, up)).start())

    def hops_in(w, d):
        each_way(
            place, d, receives, lambda up: hop(w, d, up, source(d + 1, up)).wait_recv()
        )

    def keep(w):
        rows = pl.ds(pl.multiple_of(w * 4 * share + place * share, share), share)
        return pltpu.make_async_copy(piece.at[w], out_ref.at[rows, :], l_sem.at[w])

    def store(c):
        return pltpu.make_async_copy(
            grad.at[c], grad_ref.at[pl.ds(c * share, share), :], i_sem.at[c]
        )

    x_load = pltpu.make_async_copy(
        rows_ref(x_ref, place * cuts, share, cuts), x_rows, x_sem
    )

    for f in range(folds):
        load(f).start()
    for w in range(windows):
        load_own(w).start()
    x_load.start()

    pairs = []
    for axis in ("dp", "tensor"):
        index, bit = lax.axis_index(axis), 1
        while bit < lax.axis_size(axis):
            pairs.append((axis, index + bit - 2 * bit * lax.rem(index // bit, 2)))
            bit *= 2

    def copy_s(t):
        axis, other = pairs[t]
        return pltpu.make_async_remote_copy(
            src_ref=gain_sum.at[t],
            dst_ref=gain_got.at[t],
            send_sem=s_send.at[t],
            recv_sem=s_recv.at[t],
            device_id={axis: other},
            device_id_type=pl.DeviceIdType.MESH,
        )

    def next_pair(t):
        if t > 0:
            copy_s(t - 1).wait_recv()
            gain_sum[t] = gain_sum[t - 1] + gain_got[t - 1]
        if t < len(pairs):
            copy_s(t).start()

    greet_line(place, [pair for pair in pairs if pair[0] == "dp"])
    gain_sum[0] = jnp.zeros(gain_sum.shape[1:], f32)
    gain_sum[0, 0:2, :] = gain_in[...]
    sent = list(range(ready, folds))

    @pl.when(outer)
    def _():
        for f in sent[:2]:
            copy_a(f).start()

    @pl.when(inner)
    def _():
        for f in range(ready):
            load_ra(f).start()
        for f in range(traded):
            load_rb(f).start()

    def add_rows(buffer, at, f, index):
        rows = pl.ds(pl.multiple_of(at * share, share), share)
        mine = pl.ds(pl.multiple_of(index * share, share), share)
        total = buffer[f, rows, :].astype(f32) + value[f, mine, :].astype(f32)
        buffer[f, rows, :] = total.astype(bf16)

    def finish(f, terms):
        kind, index = order[f]
        if kind == 0:
            total = own[index]
        else:
            mine = pl.ds(pl.multiple_of(place * share, share), share)
            total = value[f, mine, :].astype(f32)
        for term in terms:
            total = total + term.astype(f32)
        if kind == 0:
            piece[index] = total.astype(bf16)
        else:
            first = place * (cuts * share) + index * share
            count = drm_ref.shape[0]
            spread = (
                lax.broadcasted_iota(jnp.int32, (share, count), 0) + first == rows_in[...]
            ).astype(bf16)
            x = x_rows[pl.ds(index * share, share), :].astype(f32)
            grad[index] = input_grad_rows(
                total, x, drm_ref[...], gains_ref[0:1, :], spread
            ).astype(bf16)
            store(index).start()

    for f in range(folds):
        load(f).wait()
    for w in range(windows):
        load_own(w).wait()
    x_load.wait()
    moving = {}
    turn = 0
    for step in range(folds + 1):
        if turn <= len(pairs):
            next_pair(turn)
            turn += 1
        if step < folds:

            @pl.when(inner)
            def _():
                if step < ready:
                    load_ra(step).wait()
                else:
                    copy_a(step).wait_recv()
                if step >= traded:
                    for n in range(2):
                        add_rows(
                            ra,
                            jnp.where(lower, 1, 0) + n,
                            step,
                            jnp.where(lower, 2, 0) + n,
                        )
                    copy_b(step).start()

        if step > 0:
            f = step - 1

            @pl.when(inner)
            def _():
                if f < traded:
                    load_rb(f).wait()
                else:
                    copy_b(f).wait_recv()
                add_rows(rb, jnp.where(lower, 0, 1), f, jnp.where(lower, 0, 3))
                copy_c(f).start()
                sel_a = pl.ds(pl.multiple_of(jnp.where(lower, 0, 2) * share, share), share)
                sel_b = pl.ds(pl.multiple_of(jnp.where(lower, 1, 0) * share, share), share)
                finish(f, [ra[f, sel_a, :], rb[f, sel_b, :]])

            @pl.when(outer)
            def _():
                copy_c(f).wait_recv()
                finish(f, [rc[f]])

            for w in list(moving):
                hops_in(w, moving[w])
                if moving[w] == 3:
                    del moving[w]
                else:
                    moving[w] += 1
                    hops(w, moving[w])
            kind, index = order[f]
            if kind == 0:
                hops(index, 1)
                keep(index).start()
                moving[index] = 1

        if ready <= step < folds:

            @pl.when(outer)
            def _():
                copy_a(step).wait_send()
                if step + 2 < folds:
                    copy_a(step + 2).start()

    while turn <= len(pairs):
        next_pair(turn)
        turn += 1
    gain_ref[...] = gain_sum[len(pairs), 0:2, :]
    for t in range(len(pairs)):
        copy_s(t).wait_send()
    while moving:
        for w in list(moving):
            hops_in(w, moving[w])
            if moving[w] == 3:
                del moving[w]
            else:
                moving[w] += 1
                hops(w, moving[w])

    @pl.when(inner)
    def _():
        for f in range(folds):
            if f >= traded:
                copy_b(f).wait_send()
            copy_c(f).wait_send()

    for w in range(windows):
        keep(w).wait()
        for d in range(1, 4):
            each_way(
                place, d, sends, lambda up: hop(w, d, up, source(d, up)).wait_send()
            )

    for c in range(cuts):
        store(c).wait()


def place_kernel(place_ref, *refs):
    out_ref = refs[-1]
    parts = lax.axis_size("tensor")
    share = refs[0].shape[0]
    for step in range(parts):
        origin = lax.rem(place_ref[0] + parts - step, parts)
        out_ref[pl.ds(pl.multiple_of(origin * share, share), share), :] = refs[step][...]


def spread_kernel(tile_ref, used_ref, *refs):
    out_ref = refs[-1]
    step = pl.program_id(0)
    per = len(refs) - 1
    for n in range(per):
        used = used_ref[step * per + n] > 0

        @pl.when(used)
        def _():
            out_ref[n] = refs[n][0]

        @pl.when(jnp.logical_not(used))
        def _():
            out_ref[n] = jnp.zeros(out_ref.shape[1:], bf16)


def copy_kernel(in_ref, out_ref):
    out_ref[...] = in_ref[...]


def collect_kernel(slot_ref, *refs):
    out_ref = refs[-1]
    for index, ref in enumerate(refs[:-1]):
        out_ref[index] = ref[0]


def exchange(value, axis, bit):
    size = lax.axis_size(axis)
    return lax.ppermute(value, axis, [(i, i ^ bit) for i in range(size)])


def dp_total(value):
    size = lax.axis_size("dp")
    value = value + exchange(value, "dp", 1)
    bits = []
    bit = 2
    while bit < size:
        bits.append(bit)
        bit *= 2
    core = lax.axis_index("dp") % 2
    half = value.shape[0] // 2
    mine = lax.dynamic_slice_in_dim(value, core * half, half, 0)
    cut = half // 2
    low, high = mine[:cut], mine[cut:]
    for bit_low, bit_high in zip(bits, bits[::-1]):
        low = low + exchange(low, "dp", bit_low)
        high = high + exchange(high, "dp", bit_high)
    mine = jnp.concatenate([low, high], axis=0)
    other = exchange(mine, "dp", 1)
    return jnp.where(
        core == 0,
        jnp.concatenate([mine, other], axis=0),
        jnp.concatenate([other, mine], axis=0),
    )


def around(value):
    size = lax.axis_size("tensor")
    return [value] + [
        lax.ppermute(value, "tensor", [(i, (i + k) % size) for i in range(size)])
        for k in range(1, size)
    ]


def rows_at(value, index, share, count):
    return lax.dynamic_slice_in_dim(value, index * share, count * share, 0)


def other_sums(value, share):
    place = lax.axis_index("tensor")
    total = lax.psum_scatter(value, "tensor", scatter_dimension=0, tiled=True)
    own = rows_at(value, place, share, 1).astype(f32)
    return (total.astype(f32) - own,)


def small_total(value):
    for axis in ("dp", "tensor"):
        bit = 1
        while bit < lax.axis_size(axis):
            value = value + exchange(value, axis, bit)
            bit *= 2
    return value


def slot_ranks(owner_row):
    count_all = owner_row.shape[0]
    tile_order = jnp.arange(count_all, dtype=jnp.int32)
    earlier = (owner_row[:, None] == owner_row[None, :]) & (
        tile_order[None, :] < tile_order[:, None]
    )
    return jnp.sum(earlier.astype(jnp.int32), axis=1)


def adam_update(grad_now, first_old, second_old, param_old, rate, decay):
    first_new = beta_one * first_old + (1.0 - beta_one) * grad_now
    second_new = beta_two * second_old + (1.0 - beta_two) * grad_now * grad_now
    first_hat = first_new / (1.0 - beta_one**STEP)
    second_hat = second_new / (1.0 - beta_two**STEP)
    param_new = param_old - rate * (
        first_hat / (jnp.sqrt(second_hat) + adam_eps) + decay * param_old
    )
    return (first_new, second_new, param_new)


def head_tables(positions, heads, lib):
    frequency = lib.exp(
        -lib.log(lib.float32(10000.0))
        * (2.0 * lib.arange(HD // 2, dtype=lib.float32) / HD).astype(lib.float32)
    )
    angles = positions.astype(lib.float32)[..., None] * frequency
    cos, sin = lib.cos(angles), lib.sin(angles)
    cos = lib.concatenate([cos, cos], axis=-1)
    sin = lib.concatenate([-sin, sin], axis=-1)
    reps = (1,) * (cos.ndim - 1) + (heads,)
    return lib.tile(cos, reps), lib.tile(sin, reps)


def on_device(
    tokens,
    masked_rows,
    cotangent,
    norm_gains,
    gain_first,
    gain_second,
    owners,
    master,
    first_moment,
    second_moment,
):
    seq_count, mask_count = masked_rows.shape
    total_rows, model = tokens.shape
    window = total_rows // seq_count
    parts = lax.axis_size("tensor")
    place = lax.axis_index("tensor")
    owner_self = lax.axis_index("dp")
    heads = HEADS // parts
    width = heads * HD
    hidden = FF // parts
    capacity, tile_rows = master.shape[1:3]
    tile_size = tile_rows * model
    attn_tiles = 4 * model * width // tile_size
    ffn_tiles = 3 * model * hidden // tile_size
    count = -(-mask_count // 16) * 16
    place_ref = place.astype(jnp.int32).reshape(1)

    owner_row = owners[0]
    slot_rank = slot_ranks(owner_row)
    slot_index = owner_row * capacity + slot_rank
    slot_match = (owner_row[None, :] == owner_self) & (
        slot_rank[None, :] == jnp.arange(capacity, dtype=jnp.int32)[:, None]
    )
    slot_used = jnp.any(slot_match, axis=1)[:, None, None]
    slot_tile = jnp.argmax(slot_match, axis=1)

    mask_rows = seq_count * count
    share = window // parts
    share_rows = total_rows // parts
    dp_size = lax.axis_size("dp")
    lines = dp_size == 8 and attn_tiles == 8 and parts == 4 and seq_count == 3 and hidden == model and mask_rows <= window // 2
    anywhere = pl.BlockSpec(memory_space=pl.ANY)
    inside = pl.BlockSpec(memory_space=pltpu.VMEM)
    dma = pltpu.SemaphoreType.DMA

    tile_block = (1, tile_rows, model)
    if lines:
        small = pl.BlockSpec(memory_space=pltpu.SMEM)
        half_tiles = attn_tiles // 2
        low_slots, attn_sums = pl.pallas_call(
            weights_kernel,
            out_shape=[
                jax.ShapeDtypeStruct((capacity, tile_rows, model), bf16),
                jax.ShapeDtypeStruct((attn_tiles, tile_rows, model), bf16),
            ],
            in_specs=[small, small, inside],
            out_specs=[inside, anywhere],
            scratch_shapes=[
                pltpu.VMEM((attn_tiles, tile_rows, model), bf16),
                pltpu.VMEM((half_tiles, tile_rows, model), bf16),
                pltpu.VMEM((3, half_tiles, tile_rows, model), bf16),
                pltpu.VMEM((2, half_tiles, tile_rows, model), bf16),
                dma,
                dma,
                dma((2, half_tiles)),
                dma((2, half_tiles)),
                dma((half_tiles,)),
                dma((half_tiles,)),
                dma((half_tiles,)),
            ],
            compiler_params=params(collective_id=4, has_side_effects=True),
            cost_estimate=cost(0, 12e6),
            name="weights",
        )(
            slot_rank[:attn_tiles],
            (owner_row[:attn_tiles] == owner_self).astype(jnp.int32),
            master[0],
        )
        attn_flat = attn_sums.reshape(4 * width, model)
    else:
        grid_size = max(capacity, attn_tiles)
        low_slots, attn_mine = pl.pallas_call(
            cast_kernel,
            out_shape=[
                jax.ShapeDtypeStruct((capacity, tile_rows, model), bf16),
                jax.ShapeDtypeStruct((attn_tiles, tile_rows, model), bf16),
            ],
            grid_spec=pltpu.PrefetchScalarGridSpec(
                num_scalar_prefetch=2,
                grid=(grid_size,),
                in_specs=[
                    pl.BlockSpec(
                        tile_block, lambda i, rank, held: (jnp.minimum(i, capacity - 1), 0, 0)
                    ),
                    pl.BlockSpec(
                        tile_block,
                        lambda i, rank, held: (rank[jnp.minimum(i, attn_tiles - 1)], 0, 0),
                    ),
                ],
                out_specs=[
                    pl.BlockSpec(
                        tile_block, lambda i, rank, held: (jnp.minimum(i, capacity - 1), 0, 0)
                    ),
                    pl.BlockSpec(
                        tile_block, lambda i, rank, held: (jnp.minimum(i, attn_tiles - 1), 0, 0)
                    ),
                ],
            ),
            compiler_params=params(),
            cost_estimate=cost(0, 12 * capacity * tile_size),
            name="cast",
        )(
            slot_rank,
            jnp.pad(
                (owner_row[:attn_tiles] == owner_self).astype(jnp.int32),
                (0, grid_size - attn_tiles),
                mode="edge",
            ),
            master[0],
            master[0],
        )
        attn_flat = dp_total(attn_mine).reshape(4 * width, model)
    w_out = attn_flat[3 * width :]
    every_slot = lax.all_gather(low_slots, "dp", axis=0, tiled=True)

    cos, sin = map(jnp.asarray, head_tables(np.arange(window), heads, np))
    rows = jnp.pad(masked_rows, ((0, 0), (0, count - mask_count)), constant_values=-1)
    cot = jnp.pad(cotangent, ((0, 0), (0, count - mask_count), (0, 0)))
    cot = cot.reshape(seq_count * count, model)

    win_model = pl.BlockSpec((window, model), lambda i: (i, 0))
    win_head = pl.BlockSpec((window, width), lambda i: (i, 0))
    mask_model = pl.BlockSpec((count, model), lambda i: (i, 0))
    mask_head = pl.BlockSpec((count, width), lambda i: (i, 0))
    if lines:
        (
            o_m,
            o_first,
            o_second,
            o_third,
            w_far,
            q_m,
            x_m,
            cos_m,
            sin_m,
            k,
            v,
            w_qkv,
        ) = pl.pallas_call(
            functools.partial(attend_all_kernel, seq_count),
            out_shape=[
                jax.ShapeDtypeStruct((4, mask_rows, width), bf16),
                jax.ShapeDtypeStruct((4, window, width), bf16),
                jax.ShapeDtypeStruct((window, width), bf16),
                jax.ShapeDtypeStruct((window, width), bf16),
                jax.ShapeDtypeStruct((3, width, model), bf16),
                jax.ShapeDtypeStruct((mask_rows, width), bf16),
                jax.ShapeDtypeStruct((mask_rows, model), bf16),
                jax.ShapeDtypeStruct((mask_rows, width), f32),
                jax.ShapeDtypeStruct((mask_rows, width), f32),
                jax.ShapeDtypeStruct((total_rows, width), bf16),
                jax.ShapeDtypeStruct((total_rows, width), bf16),
                jax.ShapeDtypeStruct((model, 3 * width), bf16),
            ],
            in_specs=[inside] * 5 + [anywhere] * 2,
            out_specs=[anywhere] * 5 + [inside] * 7,
            scratch_shapes=[
                pltpu.VMEM((total_rows, width), bf16),
                pltpu.VMEM((3 * width // 128, model, 128), f32),
                pltpu.VMEM((mask_rows, width), bf16),
                pltpu.VMEM((seq_count, window, width), bf16),
                pltpu.VMEM((2, window, model), bf16),
                dma((2,)),
                dma((seq_count,)),
                dma,
                dma((3, 2)),
                dma((3, 2)),
                dma((3, 2)),
                dma((3, 2)),
                dma((3, 2)),
                dma((3, 2)),
                dma((3,)),
                dma((3,)),
            ],
            compiler_params=params(collective_id=3, has_side_effects=True),
            cost_estimate=cost(4e10, 20e6),
            name="attend_all",
        )(rows[:, :, None], norm_gains, attn_flat, cos, sin, tokens, attn_flat)
        before_tiles = o_third
    else:
        block = min(512, window)
        per_window = window // block
        row_block = pl.BlockSpec((block, model), lambda i: (i, 0))
        head_block = pl.BlockSpec((block, width), lambda i: (i, 0))
        table_block = pl.BlockSpec((block, width), lambda i: (i % per_window, 0))
        q, k, v, w_qkv = pl.pallas_call(
            qkv_kernel,
            out_shape=[jax.ShapeDtypeStruct((total_rows, width), bf16)] * 3
            + [jax.ShapeDtypeStruct((model, 3 * width), bf16)],
            grid=(total_rows // block,),
            in_specs=[
                row_block,
                whole_spec((2, model)),
                whole_spec((3 * width, model)),
                table_block,
                table_block,
            ],
            out_specs=[head_block] * 3 + [whole_spec((model, 3 * width))],
            scratch_shapes=[pltpu.VMEM((3 * width // 128, model, 128), f32)],
            compiler_params=params(),
            cost_estimate=cost(6 * total_rows * model * width, 2 * total_rows * model * 2),
            name="qkv",
        )(tokens, norm_gains, attn_flat, cos, sin)

        o_m, q_m, x_m = pl.pallas_call(
            attend_masked_kernel,
            out_shape=[
                jax.ShapeDtypeStruct((seq_count * count, width), bf16),
                jax.ShapeDtypeStruct((seq_count * count, width), bf16),
                jax.ShapeDtypeStruct((seq_count * count, model), bf16),
            ],
            grid=(seq_count,),
            in_specs=[
                pl.BlockSpec((1, count, 1), lambda i: (i, 0, 0)),
                win_model,
                win_head,
                win_head,
                win_head,
            ],
            out_specs=[mask_head, mask_head, mask_model],
            compiler_params=params(),
            cost_estimate=cost(
                seq_count * count * window * (2 * model + 8 * width), 9e6, seq_count * count * window * heads
            ),
            name="attend_masked",
        )(rows[:, :, None], tokens, q, k, v)
        o_ms = around(o_m)

        q_block = min(256, window)

        def attend_window(w, before):
            return pl.pallas_call(
                after(attend_kernel, 3, 1),
                out_shape=jax.ShapeDtypeStruct((window, width), bf16),
                grid=(width // 128, window // q_block),
                in_specs=[
                    pl.BlockSpec((q_block, 128), lambda p, i: (w * (window // q_block) + i, p)),
                    pl.BlockSpec((window, 128), lambda p, i: (w, p)),
                    pl.BlockSpec((window, 128), lambda p, i: (w, p)),
                    UNREAD,
                ],
                out_specs=pl.BlockSpec((q_block, 128), lambda p, i: (i, p)),
                compiler_params=params(),
                cost_estimate=cost(
                    16 * window * window * width, 4 * window * width * 2, window * window * heads
                ),
                name="attend",
            )(q, k, v, before)

        early = max(seq_count - 1, 1)
        o_own = []
        for w in range(early):
            o_own.append(attend_window(w, o_own[-1] if o_own else o_m))
        before_tiles = o_own[-1]
        cos_m, sin_m = (
            table.reshape(mask_rows, width) for table in head_tables(rows, heads, jnp)
        )

    group = 4
    ffn_all = pl.pallas_call(
        after(collect_kernel, 1 + group, 1),
        out_shape=jax.ShapeDtypeStruct((ffn_tiles, tile_rows, model), bf16),
        grid_spec=pltpu.PrefetchScalarGridSpec(
            num_scalar_prefetch=1,
            grid=(ffn_tiles // group,),
            in_specs=[
                pl.BlockSpec(
                    tile_block,
                    lambda i, slot, n=n: (slot[attn_tiles + i * group + n], 0, 0),
                )
                for n in range(group)
            ]
            + [UNREAD],
            out_specs=pl.BlockSpec((group, tile_rows, model), lambda i, slot: (i, 0, 0)),
        ),
        compiler_params=params(),
        cost_estimate=cost(0, 4 * ffn_tiles * tile_size),
        name="collect",
    )(slot_index, *[every_slot] * group, before_tiles)
    even = jnp.array([[1.0], [1.0 / parts]], f32)
    flat_rows = jnp.where(
        rows >= 0, rows + window * jnp.arange(seq_count, dtype=jnp.int32)[:, None], -1
    ).reshape(1, mask_rows)
    if lines:
        grad_rows = 4 * width + 3 * hidden
        part, own, first_sums, second_sums, dha, grads, dr_m, gains_part = pl.pallas_call(
            functools.partial(middle_kernel, seq_count),
            out_shape=[
                jax.ShapeDtypeStruct((seq_count, window, model), bf16),
                jax.ShapeDtypeStruct((seq_count, share, model), f32),
                jax.ShapeDtypeStruct((seq_count, 3 * share, model), bf16),
                jax.ShapeDtypeStruct((2, 2 * share, model), bf16),
                jax.ShapeDtypeStruct((seq_count, window, model), bf16),
                jax.ShapeDtypeStruct((grad_rows, model), bf16),
                jax.ShapeDtypeStruct((mask_rows, model), f32),
                jax.ShapeDtypeStruct((2, model), f32),
            ],
            in_specs=[inside] * 15 + [anywhere] * 5,
            out_specs=[anywhere] * 6 + [inside] * 2,
            scratch_shapes=[
                pltpu.VMEM((window, model), f32),
                pltpu.VMEM((window, model), bf16),
                pltpu.VMEM((window, model), f32),
                pltpu.VMEM((window, model), bf16),
                pltpu.VMEM((share, model), f32),
                pltpu.VMEM((2, 4, window, width), bf16),
                pltpu.VMEM((window, model), bf16),
                pltpu.VMEM((2, 2, window, width), bf16),
                pltpu.VMEM((window, 3 * width), bf16),
                pltpu.VMEM((model, 3 * width), f32),
                pltpu.VMEM((model, 128), f32),
                pltpu.VMEM((width, model), f32),
                pltpu.VMEM((mask_rows, model), f32),
                pltpu.VMEM((4, mask_rows, model // 4), bf16),
                pltpu.VMEM((3, mask_rows, model // 4), bf16),
                pltpu.VMEM((4, mask_rows, model // 4), bf16),
                pltpu.VMEM((2, 2 * share, model), bf16),
                dma((2,)),
                dma((2,)),
                dma((2,)),
                dma((2,)),
                dma,
                dma((2, 2)),
                dma((2, 3)),
                dma,
                dma((window // share,)),
                dma,
                dma((seq_count,)),
                dma((seq_count,)),
                dma((2, 3, 2)),
                dma((2, 3, 2)),
                dma((3,)),
                dma((3,)),
                dma((3,)),
                dma((3,)),
            ],
            compiler_params=params(collective_id=1, has_side_effects=True),
            cost_estimate=cost(1e11, 100e6),
            name="middle",
        )(
            rows[:, None, :],
            norm_gains,
            x_m,
            cot,
            q_m,
            cos_m,
            sin_m,
            cos,
            sin,
            w_qkv,
            ffn_all.reshape(3, model, hidden),
            o_m,
            o_first,
            w_out,
            w_far,
            tokens,
            k,
            v,
            o_second,
            o_third,
        )

        group = 8
        slots = lax.axis_size("dp") * capacity
        slot_hit = slot_index[None, :] == jnp.arange(slots, dtype=jnp.int32)[:, None]
        used = jnp.any(slot_hit, axis=1).astype(jnp.int32)
        tile_count = slot_index.shape[0]
        held_at = jnp.arange(slots, dtype=jnp.int32) // group * tile_count
        held_at = held_at + jnp.argmax(slot_hit, axis=1).astype(jnp.int32)
        held_at = jnp.where(used > 0, held_at, 0).reshape(-1, group)
        from_tile = lax.rem(lax.cummax(held_at, axis=0), tile_count).reshape(-1)
        in_slots = pl.pallas_call(
            spread_kernel,
            out_shape=jax.ShapeDtypeStruct((slots, tile_rows, model), bf16),
            grid_spec=pltpu.PrefetchScalarGridSpec(
                num_scalar_prefetch=2,
                grid=(slots // group,),
                in_specs=[
                    pl.BlockSpec(
                        tile_block, lambda i, tile, used, n=n: (tile[i * group + n], 0, 0)
                    )
                    for n in range(group)
                ],
                out_specs=pl.BlockSpec(
                    (group, tile_rows, model), lambda i, tile, used: (i, 0, 0)
                ),
            ),
            compiler_params=params(),
            cost_estimate=cost(0, 24 * capacity * tile_size),
            name="spread",
        )(
            from_tile,
            used,
            *[grads.reshape(-1, tile_rows, model)] * group,
        )
        reduced = lax.psum_scatter(in_slots, "dp", scatter_dimension=0, tiled=True).astype(f32)

        order = [(kind, i) for kind in (0, 1) for i in range(seq_count)]
        folds = len(order)
        pair_count = (lax.axis_size("dp") * parts).bit_length() - 1
        layer_out, input_grad, gain_grad = pl.pallas_call(
            after(functools.partial(lines_kernel, seq_count, seq_count, order, seq_count, 2), 10, 1),
            out_shape=[
                jax.ShapeDtypeStruct((total_rows, model), bf16),
                jax.ShapeDtypeStruct((share_rows, model), bf16),
                jax.ShapeDtypeStruct((2, model), f32),
            ],
            in_specs=[inside] * 3 + [anywhere] * 6 + [inside, anywhere],
            out_specs=[anywhere] * 2 + [inside],
            scratch_shapes=[
                pltpu.VMEM((folds, 3 * share, model), bf16),
                pltpu.VMEM((folds, 2 * share, model), bf16),
                pltpu.VMEM((folds, share, model), bf16),
                pltpu.VMEM((folds, window, model), bf16),
                pltpu.VMEM((seq_count, share, model), f32),
                pltpu.VMEM((seq_count, share, model), bf16),
                pltpu.VMEM((share_rows, model), bf16),
                pltpu.VMEM((seq_count, share, model), bf16),
                pltpu.VMEM((pair_count + 1, 8, model), f32),
                pltpu.VMEM((pair_count, 8, model), f32),
                dma((pair_count,)),
                dma((pair_count,)),
                dma((folds,)),
                dma((folds,)),
                dma((folds,)),
                dma((folds,)),
                dma((folds,)),
                dma((folds,)),
                dma((seq_count, 3, 2)),
                dma((seq_count, 3, 2)),
                dma((folds,)),
                dma((seq_count,)),
                dma((seq_count,)),
                dma((2,)),
                dma,
                dma((seq_count,)),
                dma((seq_count,)),
            ],
            compiler_params=params(collective_id=2, has_side_effects=True),
            cost_estimate=cost(4 * share_rows * mask_rows * model, 60e6),
            name="lines",
        )(
            flat_rows,
            dr_m,
            norm_gains,
            tokens,
            dha,
            part,
            own,
            first_sums,
            second_sums,
            gains_part * even,
            in_slots,
        )
    else:
        w_outs = around(w_out)
        ffn_flat = ffn_all.reshape(3, -1)
        w_gate = ffn_flat[0].reshape(model, hidden)
        w_up = ffn_flat[1].reshape(model, hidden)
        w_down = ffn_flat[2].reshape(hidden, model)
        cols = min(256, hidden)
        col_block = pl.BlockSpec((model, cols), lambda c: (0, c))
        down_block = pl.BlockSpec((cols, model), lambda c: (c, 0))
        r_m, dhf_part, ffn_grad = pl.pallas_call(
            functools.partial(ffn_masked_kernel, parts),
            out_shape=[
                jax.ShapeDtypeStruct((mask_rows, model), f32),
                jax.ShapeDtypeStruct((mask_rows, model), bf16),
                jax.ShapeDtypeStruct((3, hidden, model), bf16),
            ],
            grid=(hidden // cols,),
            in_specs=[
                whole_spec((mask_rows, model)),
                whole_spec((mask_rows, model)),
                whole_spec((2, model)),
                col_block,
                col_block,
                down_block,
            ]
            + [whole_spec((mask_rows, width))] * parts
            + [whole_spec((width, model))] * parts,
            out_specs=[
                whole_spec((mask_rows, model)),
                whole_spec((mask_rows, model)),
                whole_spec((3, hidden, model)),
            ],
            scratch_shapes=[
                pltpu.VMEM((mask_rows, model), bf16),
                pltpu.VMEM((mask_rows, model), f32),
                pltpu.VMEM((cols // 128, model, 128), f32),
            ],
            compiler_params=params(),
            cost_estimate=cost(
                mask_rows * model * (18 * hidden + 2 * model), 20e6, mask_rows * hidden
            ),
            name="ffn_masked",
        )(x_m, cot, norm_gains, w_gate, w_up, w_down, *o_ms, *w_outs)

        for w in range(early, seq_count):
            o_own.append(attend_window(w, r_m))
        windows_o = [around(o) for o in o_own]

        share_m = mask_rows // parts
        dhf_mine = lax.dynamic_slice_in_dim(dhf_part, place * share_m, share_m, 0).astype(f32)
        for step in range(1, parts):
            send = lax.dynamic_slice_in_dim(
                dhf_part, lax.rem(place + step, parts) * share_m, share_m, 0
            )
            dhf_mine = dhf_mine + lax.ppermute(
                send, "tensor", [(i, (i + step) % parts) for i in range(parts)]
            ).astype(f32)
        dhf_all = around(dhf_mine.astype(bf16))
        dhf = jnp.zeros((mask_rows, model), bf16)
        for step, piece in enumerate(dhf_all):
            origin = lax.rem(place + parts - step, parts)
            dhf = lax.dynamic_update_slice_in_dim(dhf, piece, origin * share_m, 0)

        layer_out = None

        def ffn_window(w, before):
            return pl.pallas_call(
                after(functools.partial(ffn_kernel, parts), 6 + 2 * parts, 1),
                out_shape=[
                    jax.ShapeDtypeStruct((window, model), bf16),
                    jax.ShapeDtypeStruct((share, model), f32),
                ],
                grid_spec=pltpu.PrefetchScalarGridSpec(
                    num_scalar_prefetch=1,
                    grid=(hidden // cols,),
                    in_specs=[
                        pl.BlockSpec((window, model), lambda c, place_ref: (w, 0)),
                        whole_spec((2, model)),
                        pl.BlockSpec((model, cols), lambda c, place_ref: (0, c)),
                        pl.BlockSpec((model, cols), lambda c, place_ref: (0, c)),
                        pl.BlockSpec((cols, model), lambda c, place_ref: (c, 0)),
                    ]
                    + [whole_spec((window, width))] * parts
                    + [whole_spec((width, model))] * parts
                    + [UNREAD],
                    out_specs=[
                        whole_spec((window, model)),
                        whole_spec((share, model)),
                    ],
                    scratch_shapes=[
                        pltpu.VMEM((window, model), f32),
                        pltpu.VMEM((window, model), bf16),
                        pltpu.VMEM((window, model), f32),
                    ],
                ),
                compiler_params=params(),
                cost_estimate=cost(
                    window * model * (6 * hidden + 2 * model), 16e6, window * hidden
                ),
                name="ffn",
            )(
                place_ref,
                tokens,
                norm_gains,
                w_gate,
                w_up,
                w_down,
                *windows_o[w],
                *w_outs,
                before,
            )

        def place_window(w, part, own):
            terms = other_sums(part, share)
            total = own
            for term in terms:
                total = total + term.astype(f32)
            pieces = around(total.astype(bf16))
            return pl.pallas_call(
                after(place_kernel, 1 + parts, 0 if layer_out is None else 1),
                out_shape=jax.ShapeDtypeStruct((total_rows, model), bf16),
                grid_spec=pltpu.PrefetchScalarGridSpec(
                    num_scalar_prefetch=1,
                    grid=(1,),
                    in_specs=[whole_spec((share, model))] * parts
                    + [UNREAD] * (layer_out is not None),
                    out_specs=pl.BlockSpec((window, model), lambda i, place_ref: (w, 0)),
                ),
                input_output_aliases={} if layer_out is None else {1 + parts: 0},
                compiler_params=params(),
                cost_estimate=cost(0, 4 * window * model),
                name="place",
            )(place_ref, *pieces, *([] if layer_out is None else [layer_out]))

        parts_out = [ffn_window(0, o_own[-1])]

        cuts = seq_count if share_rows % (16 * seq_count) == 0 else 1
        cut_rows = share_rows // cuts
        dr_m, dha, attn_grad, gains_part = pl.pallas_call(
            after(attn_back_kernel, 16, 1),
            out_shape=[
                jax.ShapeDtypeStruct((mask_rows, model), f32),
                jax.ShapeDtypeStruct((cuts, parts, cut_rows, model), bf16),
                jax.ShapeDtypeStruct((4 * width, model), bf16),
                jax.ShapeDtypeStruct((2, model), f32),
            ],
            grid=(seq_count,),
            in_specs=[
                pl.BlockSpec((1, 1, count), lambda i: (i, 0, 0)),
                mask_model,
                mask_model,
                mask_model,
                whole_spec((2, model)),
                mask_head,
                mask_head,
                mask_head,
                mask_head,
                win_head,
                win_head,
                win_model,
                whole_spec((window, width)),
                whole_spec((window, width)),
                whole_spec((width, model)),
                whole_spec((model, 3 * width)),
                UNREAD,
            ],
            out_specs=[
                mask_model,
                whole_spec((cuts, parts, cut_rows, model)),
                whole_spec((4 * width, model)),
                whole_spec((2, model)),
            ],
            scratch_shapes=[
                pltpu.VMEM((model, 3 * width), f32),
                pltpu.VMEM((width, model), f32),
                pltpu.VMEM((2, model), f32),
                pltpu.VMEM((window, 3 * width), bf16),
                pltpu.VMEM((3 * width // 128, model, 128), f32),
            ],
            compiler_params=params(),
            cost_estimate=cost(
                12 * total_rows * model * width, 30e6, mask_rows * window * heads
            ),
            name="attn_back",
        )(
            rows[:, None, :],
            dhf,
            r_m,
            cot,
            norm_gains,
            o_m,
            q_m,
            cos_m,
            sin_m,
            k,
            v,
            tokens,
            cos,
            sin,
            w_out,
            w_qkv,
            parts_out[0][0],
        )

        for w in range(1, seq_count):
            parts_out.append(ffn_window(w, gains_part if w == 1 else parts_out[-1][0]))

        input_grad = None
        for cut in range(cuts):
            value = dha[cut].reshape(parts * cut_rows, model)
            terms = other_sums(value, cut_rows)
            before = [] if input_grad is None else [input_grad]
            input_grad = pl.pallas_call(
                after(
                    functools.partial(input_grad_kernel, (cut, cuts, len(terms))),
                    6 + len(terms),
                    len(before),
                ),
                out_shape=jax.ShapeDtypeStruct((share_rows, model), bf16),
                grid_spec=pltpu.PrefetchScalarGridSpec(
                    num_scalar_prefetch=1,
                    grid=(1,),
                    in_specs=[
                        whole_spec((1, mask_rows)),
                        whole_spec((mask_rows, model)),
                        whole_spec((2, model)),
                        pl.BlockSpec(
                            (cut_rows, model),
                            lambda i, place_ref, cut=cut: (place_ref[0] * cuts + cut, 0),
                        ),
                        pl.BlockSpec(
                            (1, 1, cut_rows, model),
                            lambda i, place_ref, cut=cut: (cut, place_ref[0], 0, 0),
                        ),
                    ]
                    + [whole_spec((cut_rows, model))] * len(terms)
                    + [UNREAD] * len(before),
                    out_specs=pl.BlockSpec((cut_rows, model), lambda i, place_ref, cut=cut: (cut, 0)),
                ),
                input_output_aliases={6 + len(terms): 0} if before else {},
                compiler_params=params(),
                cost_estimate=cost(4 * cut_rows * mask_rows * model, 6e6),
                name="input_grad",
            )(place_ref, flat_rows, dr_m, norm_gains, tokens, dha, *terms, *before)

        for w, outs in enumerate(parts_out):
            layer_out = place_window(w, *outs)

        gain_grad = small_total(gains_part * even)

        def total_tiles(tiles, before):
            piece = lax.psum_scatter(tiles, "dp", scatter_dimension=0, tiled=True)
            piece = pl.pallas_call(
                after(copy_kernel, 1, 1),
                out_shape=jax.ShapeDtypeStruct(piece.shape, bf16),
                in_specs=[pl.BlockSpec(memory_space=pltpu.VMEM), UNREAD],
                out_specs=pl.BlockSpec(memory_space=pltpu.VMEM),
                compiler_params=params(),
                name="copy",
            )(piece, before)
            return lax.all_gather(piece, "dp", axis=0, tiled=True)

        ffn_grads = total_tiles(ffn_grad.reshape(3 * hidden, model), parts_out[1][0])
        attn_grads = total_tiles(attn_grad, parts_out[-1][0])
        tiles = jnp.concatenate([attn_grads, ffn_grads], axis=0).reshape(-1, tile_rows, model)
        reduced = tiles[slot_tile].astype(f32)

    _, gain_moment, gain_new = adam_update(
        gain_grad, gain_first, gain_second, norm_gains, gain_rate, 0.0
    )

    first_new, second_new, param_new = adam_update(
        reduced, first_moment[0], second_moment[0], master[0], weight_rate, weight_decay
    )
    weight_grad = jnp.where(slot_used, reduced, 0.0)
    weight_first = jnp.where(slot_used, first_new, 0.0)
    weight_second = jnp.where(slot_used, second_new, 0.0)
    weight_master = jnp.where(slot_used, param_new, 0.0)
    weight_low = weight_master.astype(bf16)
    return (
        layer_out,
        input_grad,
        weight_grad[None],
        weight_first[None],
        weight_second[None],
        weight_master[None],
        weight_low[None],
        gain_grad,
        gain_moment,
        gain_new,
    )


def solution(mesh):
    return jax.shard_map(
        on_device,
        mesh=mesh,
        in_specs=(
            P("dp", None),
            P("dp", None),
            P("dp", None, None),
            P(),
            P(),
            P(),
            P("tensor", None),
            P("tensor", "dp", None, None),
            P("tensor", "dp", None, None),
            P("tensor", "dp", None, None),
        ),
        out_specs=(
            P("dp", None),
            P(("dp", "tensor"), None),
            P("tensor", "dp", None, None),
            P("tensor", "dp", None, None),
            P("tensor", "dp", None, None),
            P("tensor", "dp", None, None),
            P("tensor", "dp", None, None),
            P(),
            P(),
            P(),
        ),
        check_vma=False,
    )
```

```python
import functools

import jax
import jax.numpy as jnp
import numpy as np
from jax import lax
from jax.experimental import pallas as pl
from jax.experimental.pallas import tpu as pltpu
from jax.sharding import PartitionSpec as P

HEADS = 16
HD = 64
FF = 4096
STEP = 5

norm_eps = 1e-06
beta_one = 0.9
beta_two = 0.95
adam_eps = 1e-08
weight_rate = 0.05
gain_rate = 0.8
weight_decay = 0.1

score_scale = HD ** (-0.5)
f32 = jnp.float32
bf16 = jnp.bfloat16
VMEM_LIMIT = 60 * 1024 * 1024
NT = (((1,), (1,)), ((), ()))
TN = (((0,), (0,)), ((), ()))


def mm(left, right):
    return jnp.dot(left, right, preferred_element_type=f32)


def mm_nt(left, right):
    return lax.dot_general(left, right, NT, preferred_element_type=f32)


def mm_tn(left, right):
    return lax.dot_general(left, right, TN, preferred_element_type=f32)


def params(**kw):
    return pltpu.CompilerParams(vmem_limit_bytes=VMEM_LIMIT, **kw)


def cost(flops, nbytes, transcendentals=0):
    return pl.CostEstimate(
        flops=int(flops), bytes_accessed=int(nbytes), transcendentals=int(transcendentals)
    )


def whole_spec(shape):
    return pl.BlockSpec(shape, lambda *_: (0,) * len(shape))


def after(kernel, inputs, count):
    return lambda *refs: kernel(*refs[:inputs], *refs[inputs + count :])


UNREAD = pl.BlockSpec(memory_space=pl.ANY)


def rms_scale(values):
    return lax.rsqrt(jnp.mean(values * values, axis=-1, keepdims=True) + norm_eps)


def swap_halves(values):
    width = values.shape[1]
    lane = lax.broadcasted_iota(jnp.int32, values.shape, 1)
    return jnp.where(
        lane % HD < HD // 2,
        pltpu.roll(values, width - HD // 2, 1),
        pltpu.roll(values, HD // 2, 1),
    )


def cast_kernel(rank_ref, held_ref, slot_ref, tile_ref, low_ref, mine_ref):
    low_ref[...] = slot_ref[...].astype(bf16)
    tile = tile_ref[...].astype(bf16)
    held = held_ref[pl.program_id(0)] > 0
    mine_ref[...] = jnp.where(held, tile, jnp.zeros((), bf16))


def qkv_kernel(
    x_ref, gains_ref, tiles_ref, cos_ref, sin_ref, q_ref, k_ref, v_ref, w_ref, w_wide
):
    width = q_ref.shape[1]
    model = x_ref.shape[1]
    fold = model // width

    @pl.when(pl.program_id(0) == 0)
    def _():
        for block in range(3 * width // 128):
            part, lane = divmod(block * 128, width)
            for piece in range(fold):
                at = piece * width + lane
                w_wide[block, pl.ds(piece, width, stride=fold), :] = tiles_ref[
                    part * width : (part + 1) * width, at : at + 128
                ].astype(f32)
            w_ref[:, block * 128 : (block + 1) * 128] = w_wide[block].astype(bf16)

    x = x_ref[...].astype(f32)
    hidden = (x * rms_scale(x) * gains_ref[0:1, :]).astype(bf16)
    cos, sin = cos_ref[...], sin_ref[...]
    q = mm(hidden, w_ref[:, 0:width])
    q_ref[...] = (q * cos + swap_halves(q) * sin).astype(bf16)
    k = mm(hidden, w_ref[:, width : 2 * width])
    k_ref[...] = (k * cos + swap_halves(k) * sin).astype(bf16)
    v_ref[...] = mm(hidden, w_ref[:, 2 * width : 3 * width]).astype(bf16)


def attend(q, k, v):
    first = lax.broadcasted_iota(jnp.int32, q.shape, 1) < HD
    first_v = lax.broadcasted_iota(jnp.int32, v.shape, 1) < HD
    zero, one = jnp.zeros((), bf16), jnp.ones((), bf16)
    outs = []
    for head in range(2):
        q_head = jnp.where(first if head == 0 else ~first, q, zero)
        v_head = jnp.where(first_v if head == 0 else ~first_v, v, one)
        s = mm_nt(q_head, k)
        s = (s - jnp.max(s, axis=-1, keepdims=True)) * score_scale
        outs.append(mm(jnp.exp(s).astype(bf16), v_head))
    value = jnp.where(first, outs[0], outs[1])
    total = pltpu.roll(jnp.where(first, outs[1], outs[0]), HD, 1)
    return (value / total).astype(bf16)


def attend_kernel(q_ref, k_ref, v_ref, o_ref):
    o_ref[...] = attend(q_ref[...], k_ref[...], v_ref[...])


def attend_masked_kernel(rows_ref, x_ref, q_ref, k_ref, v_ref, o_ref, qm_ref, xm_ref):
    window = x_ref.shape[0]
    count = rows_ref.shape[1]
    pick = (
        lax.broadcasted_iota(jnp.int32, (count, window), 1) == rows_ref[0]
    ).astype(bf16)
    xm_ref[...] = mm(pick, x_ref[...]).astype(bf16)
    qm = mm(pick, q_ref[...]).astype(bf16)
    qm_ref[...] = qm
    for pair in range(q_ref.shape[1] // 128):
        lanes = slice(pair * 128, pair * 128 + 128)
        o_ref[:, lanes] = attend(qm[:, lanes], k_ref[:, lanes], v_ref[:, lanes])


def ffn_masked_kernel(
    parts, xm_ref, cot_ref, gains_ref, wg_ref, wu_ref, wd_ref, *refs
):
    o_refs, wo_refs = refs[:parts], refs[parts : 2 * parts]
    rm_ref, dhf_ref, grad_ref, hf_ref, acc_ref, wide_ref = refs[2 * parts :]
    step = pl.program_id(0)
    width = wg_ref.shape[1]
    cols = pl.ds(pl.multiple_of(step * width, width), width)
    hidden, model = grad_ref.shape[1:]
    fold = model // hidden

    def put(part, grad):
        if fold == 1:
            grad_ref[part, :, cols] = grad.astype(bf16)
            return
        for block in range(width // 128):
            wide_ref[block] = grad[:, block * 128 : (block + 1) * 128]
            for piece in range(fold):
                at = piece * hidden + step * width + block * 128
                at = pl.ds(pl.multiple_of(at, 128), 128)
                grad_ref[part, :, at] = wide_ref[
                    block, pl.ds(piece, hidden, stride=fold), :
                ].astype(bf16)

    @pl.when(step == 0)
    def _():
        r = xm_ref[...].astype(f32)
        for o_ref, wo_ref in zip(o_refs, wo_refs):
            r = r + mm(o_ref[...], wo_ref[...])
        rm_ref[...] = r
        hf_ref[...] = (r * rms_scale(r) * gains_ref[1:2, :]).astype(bf16)
        acc_ref[...] = jnp.zeros_like(acc_ref)

    hf, dy = hf_ref[...], cot_ref[...]
    wg, wu, wd = wg_ref[...], wu_ref[...], wd_ref[...]
    g, u = mm(hf, wg), mm(hf, wu)
    sig = jax.nn.sigmoid(g)
    act = (g * sig * u).astype(bf16)
    grad_ref[2, cols, :] = mm_tn(act, dy).astype(bf16)
    da = mm_nt(dy, wd)
    dg = (da * u * sig * (1.0 + g * (1.0 - sig))).astype(bf16)
    du = (da * g * sig).astype(bf16)
    put(0, mm_tn(hf, dg))
    put(1, mm_tn(hf, du))
    acc_ref[...] += mm_nt(dg, wg) + mm_nt(du, wu)

    @pl.when(step == pl.num_programs(0) - 1)
    def _():
        dhf_ref[...] = acc_ref[...].astype(bf16)


def ffn_kernel(parts, place_ref, x_ref, gains_ref, wg_ref, wu_ref, wd_ref, *refs):
    o_refs, wo_refs = refs[:parts], refs[parts : 2 * parts]
    part_ref, own_ref, r_ref, hf_ref, acc_ref = refs[2 * parts :]
    step = pl.program_id(0)

    @pl.when(step == 0)
    def _():
        r = x_ref[...].astype(f32)
        for o_ref, wo_ref in zip(o_refs, wo_refs):
            r = r + mm(o_ref[...], wo_ref[...])
        r_ref[...] = r
        hf_ref[...] = (r * rms_scale(r) * gains_ref[1:2, :]).astype(bf16)
        acc_ref[...] = jnp.zeros_like(acc_ref)

    hf = hf_ref[...]
    g, u = mm(hf, wg_ref[...]), mm(hf, wu_ref[...])
    act = (g * jax.nn.sigmoid(g) * u).astype(bf16)
    acc_ref[...] += mm(act, wd_ref[...])

    @pl.when(step == pl.num_programs(0) - 1)
    def _():
        share = own_ref.shape[0]
        part_ref[...] = acc_ref[...].astype(bf16)
        mine = pl.ds(pl.multiple_of(place_ref[0] * share, share), share)
        own_ref[...] = r_ref[mine, :] + acc_ref[mine, :]


def attn_back_kernel(
    rows_ref,
    dhf_ref,
    rm_ref,
    cot_ref,
    gains_ref,
    om_ref,
    qm_ref,
    cosm_ref,
    sinm_ref,
    k_ref,
    v_ref,
    x_ref,
    cos_ref,
    sin_ref,
    wo_ref,
    w_ref,
    drm_ref,
    dha_ref,
    gw_ref,
    gain_ref,
    gw_acc,
    go_acc,
    gain_acc,
    flow_ref,
    gw_wide,
):
    step = pl.program_id(0)

    @pl.when(step == 0)
    def _():
        gw_acc[...] = jnp.zeros_like(gw_acc)
        go_acc[...] = jnp.zeros_like(go_acc)
        gain_acc[...] = jnp.zeros_like(gain_acc)

    window, width = k_ref.shape
    count = rm_ref.shape[0]
    r = rm_ref[...]
    sf = rms_scale(r)
    nf = r * sf
    dhf = dhf_ref[...].astype(f32)
    dnf = dhf * gains_ref[1:2, :]
    dr = cot_ref[...].astype(f32) + sf * (
        dnf - nf * jnp.mean(dnf * nf, axis=-1, keepdims=True)
    )
    drm_ref[...] = dr
    gain_acc[1:2, :] += jnp.sum(dhf * nf, axis=0, keepdims=True)
    drb = dr.astype(bf16)
    go_acc[...] += mm_tn(om_ref[...], drb)
    dob = mm_nt(drb, wo_ref[...]).astype(bf16)

    first = lax.broadcasted_iota(jnp.int32, (count, 128), 1) < HD
    zero = jnp.zeros((), bf16)
    drq = []
    for pair in range(width // 128):
        lanes = slice(pair * 128, pair * 128 + 128)
        k, v = k_ref[:, lanes], v_ref[:, lanes]
        qm, do = qm_ref[:, lanes], dob[:, lanes]
        parts = []
        drk = dv = None
        for head in range(2):
            mine = first if head == 0 else ~first
            q_head = jnp.where(mine, qm, zero)
            do_head = jnp.where(mine, do, zero)
            s = mm_nt(k, q_head)
            s = jnp.exp((s - jnp.max(s, axis=0, keepdims=True)) * score_scale)
            att = s / jnp.sum(s, axis=0, keepdims=True)
            dpa = mm_nt(v, do_head)
            ds = att * (dpa - jnp.sum(dpa * att, axis=0, keepdims=True))
            ds = (ds * score_scale).astype(bf16)
            parts.append(mm_tn(ds, k))
            drk_head = mm(ds, q_head)
            dv_head = mm(att.astype(bf16), do_head)
            drk = drk_head if drk is None else drk + drk_head
            dv = dv_head if dv is None else dv + dv_head
        drq.append(jnp.where(first, parts[0], parts[1]))
        dk = drk * cos_ref[:, lanes] - swap_halves(drk) * sin_ref[:, lanes]
        flow_ref[:, width + pair * 128 : width + pair * 128 + 128] = dk.astype(bf16)
        flow_ref[:, 2 * width + pair * 128 : 2 * width + pair * 128 + 128] = dv.astype(
            bf16
        )
    spread = (
        lax.broadcasted_iota(jnp.int32, (window, count), 0) == rows_ref[0]
    ).astype(bf16)
    for pair in range(width // 128):
        lanes = slice(pair * 128, pair * 128 + 128)
        dq = drq[pair] * cosm_ref[:, lanes] - swap_halves(drq[pair]) * sinm_ref[:, lanes]
        flow_ref[:, lanes] = mm(spread, dq.astype(bf16)).astype(bf16)

    flow = flow_ref[...]
    x = x_ref[...].astype(f32)
    na = x * rms_scale(x)
    dha = mm_nt(flow, w_ref[...])
    gain_acc[0:1, :] += jnp.sum(dha * na, axis=0, keepdims=True)
    cuts, shares, rows = dha_ref.shape[:3]
    for piece in range(window // rows):
        block = step * (window // rows) + piece
        dha_ref[block % cuts, block // cuts] = dha[piece * rows : (piece + 1) * rows].astype(bf16)
    gw_acc[...] += mm_tn((na * gains_ref[0:1, :]).astype(bf16), flow)

    @pl.when(step == pl.num_programs(0) - 1)
    def _():
        fold = gw_acc.shape[0] // width
        for block in range(3 * width // 128):
            part, lane = divmod(block * 128, width)
            gw_wide[block] = gw_acc[:, block * 128 : (block + 1) * 128]
            for piece in range(fold):
                at = piece * width + lane
                gw_ref[part * width : (part + 1) * width, at : at + 128] = gw_wide[
                    block, pl.ds(piece, width, stride=fold), :
                ].astype(bf16)
        gw_ref[3 * width :, :] = go_acc[...].astype(bf16)
        gain_ref[...] = gain_acc[...]


def input_grad_kernel(
    cut, place_ref, rows_ref, drm_ref, gains_ref, x_ref, part_ref, *refs
):
    out_ref = refs[-1]
    block, count = x_ref.shape[0], drm_ref.shape[0]
    base = (place_ref[0] * cut[1] + cut[0]) * block
    spread = (
        lax.broadcasted_iota(jnp.int32, (block, count), 0) + base == rows_ref[...]
    ).astype(bf16)
    dr = drm_ref[...]
    high = dr.astype(bf16)
    low = (dr - high.astype(f32)).astype(bf16)
    dr = mm(spread, high) + mm(spread, low)
    x = x_ref[...].astype(f32)
    sa = rms_scale(x)
    na = x * sa
    dha = part_ref[0, 0].astype(f32)
    for ref in refs[: cut[2]]:
        dha = dha + ref[...].astype(f32)
    dna = dha * gains_ref[0:1, :]
    out = dr + sa * (dna - na * jnp.mean(dna * na, axis=-1, keepdims=True))
    out_ref[...] = out.astype(bf16)


def input_grad_rows(dha, x, dr, gain, spread):
    high = dr.astype(bf16)
    low = (dr - high.astype(f32)).astype(bf16)
    dr = mm(spread, high) + mm(spread, low)
    sa = rms_scale(x)
    na = x * sa
    dna = dha * gain
    return dr + sa * (dna - na * jnp.mean(dna * na, axis=-1, keepdims=True))


def remote(src, dst, send, recv, place):
    return pltpu.make_async_remote_copy(
        src_ref=src,
        dst_ref=dst,
        send_sem=send,
        recv_sem=recv,
        device_id={"tensor": place},
        device_id_type=pl.DeviceIdType.MESH,
    )


def greet_line(place, others=()):
    barrier = pltpu.get_barrier_semaphore()
    for axis, other in others:
        pl.semaphore_signal(
            barrier,
            inc=1,
            device_id={axis: other},
            device_id_type=pl.DeviceIdType.MESH,
        )
    for k in range(1, 4):
        pl.semaphore_signal(
            barrier,
            inc=1,
            device_id={"tensor": lax.rem(place + k, 4)},
            device_id_type=pl.DeviceIdType.MESH,
        )
    pl.semaphore_wait(barrier, 3 + len(others))


def sends(place, d, up):
    if up:
        return (place >= d - 1) & (place <= 2)
    return (place <= 4 - d) & (place >= 1)


def receives(place, d, up):
    return place >= d if up else place <= 3 - d


def each_way(place, d, rule, act):
    for up in (True, False):

        @pl.when(rule(place, d, up))
        def _():
            act(up)


def rows_ref(ref, index, share, count):
    return ref.at[pl.ds(pl.multiple_of(index * share, share), count * share), :]


def weights_kernel(
    rank_ref,
    held_ref,
    master_ref,
    low_ref,
    out_ref,
    mine,
    got,
    work,
    trade,
    h_send,
    h_recv,
    t_send,
    t_recv,
    f_send,
    f_recv,
    f_keep,
):
    me = lax.axis_index("dp")
    core = lax.rem(me, 2)
    tiles = mine.shape[0]
    half = tiles // 2

    def pair(bit):
        return me + bit - 2 * bit * lax.rem(me // bit, 2)

    def to(src, dst, send, recv, bit):
        return pltpu.make_async_remote_copy(
            src_ref=src,
            dst_ref=dst,
            send_sem=send,
            recv_sem=recv,
            device_id={"dp": pair(bit)},
            device_id_type=pl.DeviceIdType.MESH,
        )

    def share(first):
        return pl.ds(first * half, half)

    swap = to(mine.at[share(1 - core)], got, h_send, h_recv, 1)

    def move(stage, t):
        bit = (2, 4)[(stage + t // (half // 2)) % 2]
        return to(
            work.at[stage, t],
            trade.at[stage, t],
            t_send.at[stage, t],
            t_recv.at[stage, t],
            bit,
        )

    def final(t):
        return to(work.at[2, t], out_ref.at[core * half + t], f_send.at[t], f_recv.at[t], 1)

    def final_in(t):
        at = out_ref.at[(1 - core) * half + t]
        return to(at, at, f_send.at[t], f_recv.at[t], 1)

    def keep(t):
        return pltpu.make_async_copy(
            work.at[2, t], out_ref.at[core * half + t], f_keep.at[t]
        )

    barrier = pltpu.get_barrier_semaphore()
    for bit in (1, 2, 4):
        pl.semaphore_signal(
            barrier, inc=1, device_id={"dp": pair(bit)}, device_id_type=pl.DeviceIdType.MESH
        )
    for t in range(tiles):
        tile = master_ref[rank_ref[t]].astype(bf16)
        mine[t] = jnp.where(held_ref[t] > 0, tile, jnp.zeros((), bf16))
    pl.semaphore_wait(barrier, 3)
    swap.start()
    for n in range(low_ref.shape[0]):
        low_ref[n] = master_ref[n].astype(bf16)
    swap.wait_recv()
    turns = [t + n for t in range(half // 2) for n in (0, half // 2)]
    for t in turns:
        work[0, t] = mine[core * half + t] + got[t]
        move(0, t).start()
    for stage in (1, 2):
        for t in turns:
            move(stage - 1, t).wait_recv()
            work[stage, t] = work[stage - 1, t] + trade[stage - 1, t]
            if stage == 1:
                move(1, t).start()
            else:
                final(t).start()
                keep(t).start()
    for t in range(half):
        final_in(t).wait_recv()
    swap.wait_send()
    for t in range(half):
        keep(t).wait()
        final(t).wait_send()
        for stage in range(2):
            move(stage, t).wait_send()


def attend_all_kernel(
    windows,
    rows_in,
    gains_ref,
    tiles_ref,
    cos_ref,
    sin_ref,
    x_hbm,
    tiles_hbm,
    om_out,
    oa_out,
    ob_out,
    oc_out,
    wo_out,
    qm_ref,
    xm_ref,
    cosm_ref,
    sinm_ref,
    k_ref,
    v_ref,
    w_ref,
    q_ref,
    w_wide,
    om_own,
    o_own,
    x_ref,
    x_sem,
    own_sem,
    keep_sem,
    m_send,
    m_recv,
    o_send,
    o_recv,
    w_send,
    w_recv,
    c_send,
    c_recv,
):
    place = lax.axis_index("tensor")
    window = x_ref.shape[1]
    width = q_ref.shape[1]
    count = rows_in.shape[1]
    q_block = 256

    def load_x(w):
        return pltpu.make_async_copy(
            x_hbm.at[pl.ds(w * window, window), :], x_ref.at[w % 2], x_sem.at[w % 2]
        )

    def hop(kind, d, up):
        own, out, send, recv = (
            (om_own, om_out, m_send, m_recv) if kind == 0 else (o_own.at[0], oa_out, o_send, o_recv)
        )
        src, dst = (d - 1, d) if up else ((5 - d) % 4, 4 - d)
        n = 0 if up else 1
        return remote(
            own if d == 1 else out.at[src],
            out.at[dst],
            send.at[d - 1, n],
            recv.at[d - 1, n],
            lax.rem(place + (1 if up else 3), 4),
        )

    me = lax.axis_index("dp")
    core = lax.rem(me, 2)
    half = width // 2

    def half_of(ref, first):
        return ref.at[pl.ds(pl.multiple_of(first + core * half, half), half), :]

    def hop_w(d, up):
        src, dst = (d - 1, d) if up else ((5 - d) % 4, 4 - d)
        n = 0 if up else 1
        return remote(
            half_of(tiles_hbm, 3 * width) if d == 1 else half_of(wo_out.at[src - 1], 0),
            half_of(wo_out.at[dst - 1], 0),
            w_send.at[d - 1, n],
            w_recv.at[d - 1, n],
            lax.rem(place + (1 if up else 3), 4),
        )

    sibling = me + 1 - 2 * core

    def copy_w(n):
        return pltpu.make_async_remote_copy(
            src_ref=half_of(wo_out.at[n], 0),
            dst_ref=half_of(wo_out.at[n], 0),
            send_sem=c_send.at[n],
            recv_sem=c_recv.at[n],
            device_id={"dp": sibling},
            device_id_type=pl.DeviceIdType.MESH,
        )

    def copy_w_in(n):
        rows = pl.ds(pl.multiple_of((1 - core) * half, half), half)
        return pltpu.make_async_remote_copy(
            src_ref=wo_out.at[n].at[rows, :],
            dst_ref=wo_out.at[n].at[rows, :],
            send_sem=c_send.at[n],
            recv_sem=c_recv.at[n],
            device_id={"dp": sibling},
            device_id_type=pl.DeviceIdType.MESH,
        )

    def any_hop(kind, d, up):
        return hop_w(d, up) if kind == 2 else hop(kind, d, up)

    def hops(kind, d):
        each_way(place, d, sends, lambda up: any_hop(kind, d, up).start())

    def hops_in(kind, d):
        each_way(place, d, receives, lambda up: any_hop(kind, d, up).wait_recv())

    def store(w):
        to = (oa_out.at[0], ob_out, oc_out)[w]
        return pltpu.make_async_copy(o_own.at[w], to, own_sem.at[w])

    def attend_rows(w, first, last):
        for pair in range(width // 128):
            lanes = slice(pair * 128, pair * 128 + 128)
            keys = slice(w * window, (w + 1) * window)

            def block(i, carry):
                rows = pl.ds(pl.multiple_of(w * window + i * q_block, q_block), q_block)
                into = pl.ds(pl.multiple_of(i * q_block, q_block), q_block)
                o_own[w, into, lanes] = attend(
                    q_ref[rows, lanes], k_ref[keys, lanes], v_ref[keys, lanes]
                )
                return carry

            lax.fori_loop(first, last, block, 0)

    def picked(pick, table):
        high = table.astype(bf16)
        low = (table - high.astype(f32)).astype(bf16)
        return mm(pick, high) + mm(pick, low)

    def project(w):
        rows = window // 2

        def block(n, carry):
            here = pl.ds(pl.multiple_of(n * rows, rows), rows)
            at = pl.ds(pl.multiple_of(w * window + n * rows, rows), rows)
            x = x_ref[w % 2, here, :].astype(f32)
            hidden = (x * rms_scale(x) * gains_ref[0:1, :]).astype(bf16)
            cos, sin = cos_ref[here, :], sin_ref[here, :]
            q = mm(hidden, w_ref[:, 0:width])
            q_ref[at, :] = (q * cos + swap_halves(q) * sin).astype(bf16)
            k = mm(hidden, w_ref[:, width : 2 * width])
            k_ref[at, :] = (k * cos + swap_halves(k) * sin).astype(bf16)
            v_ref[at, :] = mm(hidden, w_ref[:, 2 * width : 3 * width]).astype(bf16)
            return carry

        load_x(w).wait()
        lax.fori_loop(0, 2, block, 0)
        at = slice(w * count, (w + 1) * count)
        pick = (
            lax.broadcasted_iota(jnp.int32, (count, window), 1) == rows_in[w]
        ).astype(bf16)
        xm_ref[at, :] = mm(pick, x_ref[w % 2]).astype(bf16)
        if w + 2 < windows:
            load_x(w + 2).start()
        cosm_ref[at, :] = picked(pick, cos_ref[...])
        sinm_ref[at, :] = picked(pick, sin_ref[...])
        qm_ref[at, :] = mm(pick, q_ref[w * window : (w + 1) * window, :]).astype(bf16)

    for w in range(2):
        load_x(w).start()
    greet_line(place, [("dp", sibling)])
    blocks = window // q_block
    hops(2, 1)
    fold = tiles_ref.shape[1] // width
    for block in range(3 * width // 128):
        part, lane = divmod(block * 128, width)
        for piece in range(fold):
            at = piece * width + lane
            w_wide[block, pl.ds(piece, width, stride=fold), :] = tiles_ref[
                part * width : (part + 1) * width, at : at + 128
            ].astype(f32)
        w_ref[:, block * 128 : (block + 1) * 128] = w_wide[block].astype(bf16)
    project(0)
    hops_in(2, 1)
    hops(2, 2)
    attend_rows(0, 0, blocks)
    hops(1, 1)
    store(0).start()
    hops_in(2, 2)
    hops(2, 3)
    project(1)
    project(2)
    hops_in(1, 1)
    hops(1, 2)
    for w in range(windows):
        keys = slice(w * window, (w + 1) * window)
        at = slice(w * count, (w + 1) * count)
        for pair in range(width // 128):
            lanes = slice(pair * 128, pair * 128 + 128)
            om_own[at, lanes] = attend(
                qm_ref[at, lanes], k_ref[keys, lanes], v_ref[keys, lanes]
            )
    hops(0, 1)
    keep = pltpu.make_async_copy(om_own, om_out.at[0], keep_sem)
    keep.start()
    attend_rows(1, 0, blocks // 2)
    hops_in(0, 1)
    hops(0, 2)
    attend_rows(1, blocks // 2, blocks)
    store(1).start()
    hops_in(0, 2)
    hops(0, 3)
    hops_in(1, 2)
    hops(1, 3)
    attend_rows(2, 0, blocks)
    store(2).start()
    hops_in(2, 3)
    for n in range(3):
        copy_w(n).start()
    keep.wait()
    for w in range(windows):
        store(w).wait()
    for kind in range(2):
        hops_in(kind, 3)
    for kind in range(3):
        for d in range(1, 4):
            each_way(place, d, sends, lambda up: any_hop(kind, d, up).wait_send())
    for n in range(3):
        copy_w(n).wait_send()
        copy_w_in(n).wait_recv()


def masked_attention_back(qm, do, k, v):
    first = lax.broadcasted_iota(jnp.int32, qm.shape, 1) < HD
    zero = jnp.zeros((), bf16)
    parts = []
    drk = dv = None
    for head in range(2):
        mine = first if head == 0 else ~first
        q_head = jnp.where(mine, qm, zero)
        do_head = jnp.where(mine, do, zero)
        s = mm_nt(k, q_head)
        s = jnp.exp((s - jnp.max(s, axis=0, keepdims=True)) * score_scale)
        att = s / jnp.sum(s, axis=0, keepdims=True)
        dpa = mm_nt(v, do_head)
        ds = att * (dpa - jnp.sum(dpa * att, axis=0, keepdims=True))
        ds = (ds * score_scale).astype(bf16)
        parts.append(mm_tn(ds, k))
        drk_head = mm(ds, q_head)
        dv_head = mm(att.astype(bf16), do_head)
        drk = drk_head if drk is None else drk + drk_head
        dv = dv_head if dv is None else dv + dv_head
    return jnp.where(first, parts[0], parts[1]), drk, dv


def middle_kernel(
    windows,
    rows_in,
    gains_ref,
    xm_ref,
    cot_ref,
    qm_ref,
    cosm_ref,
    sinm_ref,
    cos_ref,
    sin_ref,
    w_ref,
    ffn_ref,
    om_ref,
    oa_ref,
    wo_ref,
    wo_far,
    *refs,
):
    wg_ref, wu_ref, wd_ref = (ffn_ref.at[n] for n in range(3))
    om_refs, oa_refs = ([ref.at[n] for n in range(4)] for ref in (om_ref, oa_ref))
    wo_refs = [wo_ref] + [wo_far.at[n] for n in range(3)]
    x_hbm, k_hbm, v_hbm, o_one, o_two = refs[0:5]
    part_out, own_out, ra_out, rb_out, dha_out, grads_out, drm_ref, gain_ref = refs[5:13]
    (
        r_ref,
        hf_ref,
        acc_ref,
        p_ref,
        own_ref,
        obuf,
        x_ref,
        kv,
        flow_ref,
        gw_acc,
        gw_wide,
        go_acc,
        rm_ref,
        dpart,
        drecv,
        dall,
        bsum,
        b_load,
        b_send,
        b_recv,
        o_load,
        x_sem,
        kv_sem,
        grad_sem,
        p_sem,
        dha_sem,
        own_sem,
        a_send,
        a_recv,
        o_send,
        o_recv,
        d_send,
        d_recv,
        e_send,
        e_recv,
    ) = refs[13:]
    place = lax.axis_index("tensor")
    lower = place < 2
    outer = (place == 0) | (place == 3)
    inner = (place == 1) | (place == 2)
    window, model = x_ref.shape
    width = kv.shape[3]
    hidden = ffn_ref.shape[2]
    share = own_ref.shape[0]
    count = rm_ref.shape[0] // windows
    masked = rm_ref.shape[0]
    cols = 256
    chunks = hidden // cols

    def hop(g, d, up):
        src, dst = (d - 1, d) if up else ((5 - d) % 4, 4 - d)
        n = 0 if up else 1
        return remote(
            obuf.at[g, src],
            obuf.at[g, dst],
            o_send.at[g, d - 1, n],
            o_recv.at[g, d - 1, n],
            lax.rem(place + (1 if up else 3), 4),
        )

    def hops(g, d):
        each_way(place, d, sends, lambda up: hop(g, d, up).start())

    def hops_in(g, d):
        each_way(place, d, receives, lambda up: hop(g, d, up).wait_recv())

    def load_o(g):
        return pltpu.make_async_copy((o_one, o_two)[g], obuf.at[g, 0], o_load.at[g])

    def load_x(w):
        return pltpu.make_async_copy(
            x_hbm.at[pl.ds(w * window, window), :], x_ref, x_sem
        )

    def load_kv(w):
        return [
            pltpu.make_async_copy(
                hbm.at[pl.ds(w * window, window), :], kv.at[w % 2, n], kv_sem.at[w % 2, n]
            )
            for n, hbm in enumerate((k_hbm, v_hbm))
        ]

    def store_p(to):
        return pltpu.make_async_copy(p_ref, to, p_sem)

    def store_own(w):
        return pltpu.make_async_copy(own_ref, own_out.at[w], own_sem)

    def copy_a(w):
        far = rows_ref(part_out.at[w], jnp.where(lower, 1, 0), share, 3)
        return remote(far, ra_out.at[w], a_send.at[w], a_recv.at[w], jnp.where(lower, 1, 2))

    def copy_d(k):
        to = lax.rem(place + k, 4)
        return remote(dpart.at[to], drecv.at[k - 1], d_send.at[k - 1], d_recv.at[k - 1], to)

    def copy_e(k, origin):
        to = lax.rem(place + k, 4)
        return remote(dall.at[origin], dall.at[origin], e_send.at[k - 1], e_recv.at[k - 1], to)

    for g in range(2):
        load_o(g).start()
    load_x(0).start()
    for copy in load_kv(0):
        copy.start()
    greet_line(place)
    load_o(0).wait()
    hops(0, 1)
    gain_att, gain_ffn = gains_ref[0:1, :], gains_ref[1:2, :]

    def grad_copies(c):
        side = (c % 2) * 2 * cols
        base = 4 * width
        at = pl.ds(c * cols, cols)
        below = window - 2 * cols + (c % 2) * cols
        return [
            pltpu.make_async_copy(
                p_ref.at[:, pl.ds(side, cols)],
                grads_out.at[pl.ds(base, model), at],
                grad_sem.at[c % 2, 0],
            ),
            pltpu.make_async_copy(
                p_ref.at[:, pl.ds(side + cols, cols)],
                grads_out.at[pl.ds(base + hidden, model), at],
                grad_sem.at[c % 2, 1],
            ),
            pltpu.make_async_copy(
                hf_ref.at[pl.ds(below, cols), :],
                grads_out.at[pl.ds(base + 2 * hidden + c * cols, cols), :],
                grad_sem.at[c % 2, 2],
            ),
        ]

    def masked_chunk(c):
        if c >= 2:
            for copy in grad_copies(c - 2):
                copy.wait()
        at = slice(c * cols, (c + 1) * cols)
        side = (c % 2) * 2 * cols
        below = window - 2 * cols + (c % 2) * cols
        hf, dy = hf_ref[0:masked, :], cot_ref[...]
        wg, wu, wd = wg_ref[:, at], wu_ref[:, at], wd_ref[at, :]
        g, u = mm(hf, wg), mm(hf, wu)
        sig = jax.nn.sigmoid(g)
        act = (g * sig * u).astype(bf16)
        hf_ref[below : below + cols, :] = mm_tn(act, dy).astype(bf16)
        da = mm_nt(dy, wd)
        dg = (da * u * sig * (1.0 + g * (1.0 - sig))).astype(bf16)
        du = (da * g * sig).astype(bf16)
        p_ref[:, side : side + cols] = mm_tn(hf, dg).astype(bf16)
        p_ref[:, side + cols : side + 2 * cols] = mm_tn(hf, du).astype(bf16)
        part = mm_nt(dg, wg) + mm_nt(du, wu)
        if c == 0:
            acc_ref[0:masked, :] = part
        else:
            acc_ref[0:masked, :] += part
        for copy in grad_copies(c):
            copy.start()

    def ffn(w, o_refs, next_x, between=None):
        half = window // 2

        def first(n, carry):
            rows = pl.ds(pl.multiple_of(n * half, half), half)
            r = x_ref[rows, :].astype(f32)
            for o, wo in zip(o_refs, wo_refs):
                r = r + mm(o[rows, :], wo[...])
            r_ref[rows, :] = r
            hf_ref[rows, :] = (r * rms_scale(r) * gain_ffn).astype(bf16)
            return carry

        lax.fori_loop(0, 2, first, 0)
        if next_x is not None:
            load_x(next_x).start()
        acc_ref[...] = jnp.zeros_like(acc_ref)

        def chunk(c, carry):
            at = pl.ds(pl.multiple_of(c * cols, cols), cols)
            hf = hf_ref[...]
            g, u = mm(hf, wg_ref[:, at]), mm(hf, wu_ref[:, at])
            act = (g * jax.nn.sigmoid(g) * u).astype(bf16)
            acc_ref[...] += mm(act, wd_ref[at, :])
            return carry

        if between is None:
            lax.fori_loop(0, chunks, chunk, 0)
        else:
            lax.fori_loop(0, chunks - 1, chunk, 0)
            between()
            lax.fori_loop(chunks - 1, chunks, chunk, 0)
        p_ref[...] = acc_ref[...].astype(bf16)
        store_p(part_out.at[w]).start()
        mine = pl.ds(pl.multiple_of(place * share, share), share)
        own_ref[...] = r_ref[mine, :] + acc_ref[mine, :]
        store_own(w).start()
        store_p(part_out.at[w]).wait()
        store_own(w).wait()

    def inward(w):
        @pl.when(outer)
        def _():
            copy_a(w).start()

    def sum_dhf():
        for k in range(1, 4):
            copy_d(k).wait_recv()
        total = dpart[place].astype(f32)
        for k in range(3):
            total = total + drecv[k].astype(f32)
        dall[place] = total.astype(bf16)
        for k in range(1, 4):
            copy_e(k, place).start()

    r = xm_ref[...].astype(f32)
    for om, wo in zip(om_refs, wo_refs):
        r = r + mm(om[...], wo[...])
    rm_ref[...] = r
    hf_ref[0:masked, :] = (r * rms_scale(r) * gain_ffn).astype(bf16)
    for c in range(chunks // 2):
        masked_chunk(c)
    hops_in(0, 1)
    hops(0, 2)
    for c in range(chunks // 2, chunks):
        masked_chunk(c)
    block = model // 4
    for n in range(4):
        dpart[n] = acc_ref[0:masked, n * block : (n + 1) * block].astype(bf16)
    for k in range(1, 4):
        copy_d(k).start()
    hops_in(0, 2)
    hops(0, 3)
    for c in range(chunks - 2, chunks):
        for copy in grad_copies(c):
            copy.wait()

    load_o(1).wait()
    load_x(0).wait()
    ffn(0, oa_refs, 1)
    hops_in(0, 3)
    hops(1, 1)
    load_x(1).wait()

    def meanwhile():
        sum_dhf()
        inward(0)

    ffn(1, [obuf.at[0, n] for n in range(4)], 0, meanwhile)
    inward(1)
    hops_in(1, 1)
    hops(1, 2)
    hops_in(1, 2)
    hops(1, 3)

    def copy_b(w):
        return remote(
            bsum.at[w], rb_out.at[w], b_send.at[w], b_recv.at[w], jnp.where(lower, 2, 1)
        )

    def exchange_rows(w):
        @pl.when(inner)
        def _():
            copy_a(w).wait_recv()
            rows = rows_ref(ra_out.at[w], jnp.where(lower, 1, 0), share, 2)
            mine = rows_ref(part_out.at[w], jnp.where(lower, 2, 0), share, 2)
            got = pltpu.make_async_copy(rows, bsum.at[w], b_load.at[0])
            add = pltpu.make_async_copy(mine, hf_ref.at[pl.ds(0, 2 * share), :], b_load.at[1])
            got.start()
            add.start()
            got.wait()
            add.wait()
            total = bsum[w].astype(f32) + hf_ref[0 : 2 * share, :].astype(f32)
            bsum[w] = total.astype(bf16)
            copy_b(w).start()

    for k in range(1, 4):
        copy_e(k, lax.rem(place + 4 - k, 4)).wait_recv()
    gw_acc[...] = jnp.zeros_like(gw_acc)
    go_acc[...] = jnp.zeros_like(go_acc)
    gain_ref[...] = jnp.zeros_like(gain_ref)
    def back_window(w, next_x):
        for copy in load_kv(w):
            copy.wait()
        if w + 1 < windows:
            for copy in load_kv(w + 1):
                copy.start()
        at = slice(w * count, (w + 1) * count)
        r = rm_ref[at, :]
        sf = rms_scale(r)
        nf = r * sf
        dhf = jnp.concatenate([dall[n, at, :] for n in range(4)], axis=1).astype(f32)
        dnf = dhf * gain_ffn
        dr = cot_ref[at, :].astype(f32) + sf * (
            dnf - nf * jnp.mean(dnf * nf, axis=-1, keepdims=True)
        )
        drm_ref[at, :] = dr
        gain_ref[1:2, :] += jnp.sum(dhf * nf, axis=0, keepdims=True)
        drb = dr.astype(bf16)
        go_acc[...] += mm_tn(om_refs[0][at, :], drb)
        dob = mm_nt(drb, wo_refs[0][...]).astype(bf16)
        spread = (
            lax.broadcasted_iota(jnp.int32, (window, count), 0) == rows_in[w]
        ).astype(bf16)
        for pair in range(width // 128):
            lanes = slice(pair * 128, pair * 128 + 128)
            drq, drk, dv = masked_attention_back(
                qm_ref[at, lanes], dob[:, lanes], kv[w % 2, 0, :, lanes], kv[w % 2, 1, :, lanes]
            )
            dk = drk * cos_ref[:, lanes] - swap_halves(drk) * sin_ref[:, lanes]
            dq = drq * cosm_ref[at, lanes] - swap_halves(drq) * sinm_ref[at, lanes]
            first = pair * 128
            flow_ref[:, first : first + 128] = mm(spread, dq.astype(bf16)).astype(bf16)
            flow_ref[:, width + first : width + first + 128] = dk.astype(bf16)
            flow_ref[:, 2 * width + first : 2 * width + first + 128] = dv.astype(bf16)
        load_x(w).wait()

        def back(n, carry):
            rows = pl.ds(pl.multiple_of(n * share, share), share)
            x = x_ref[rows, :].astype(f32)
            na = x * rms_scale(x)
            dha = mm_nt(flow_ref[rows, :], w_ref[...])
            gain_ref[0:1, :] += jnp.sum(dha * na, axis=0, keepdims=True)
            p_ref[rows, :] = dha.astype(bf16)
            hf_ref[rows, :] = (na * gain_att).astype(bf16)
            return carry

        lax.fori_loop(0, window // share, back, 0)
        for copy in dha_copies(dha_out, p_ref, dha_sem, w, windows, share):
            copy.start()
        if next_x is not None:
            load_x(next_x).start()
        gw_acc[...] += mm_tn(hf_ref[...], flow_ref[...])

    def dha_stored(w):
        for copy in dha_copies(dha_out, p_ref, dha_sem, w, windows, share):
            copy.wait()

    back_window(0, 1)
    dha_stored(0)
    back_window(1, 2)
    dha_stored(1)
    exchange_rows(0)
    back_window(2, None)
    dha_stored(2)
    hops_in(1, 3)
    ffn(2, [obuf.at[1, n] for n in range(4)], None)
    fold = model // width
    for block in range(3 * width // 128):
        part, lane = divmod(block * 128, width)
        gw_wide[...] = gw_acc[:, block * 128 : (block + 1) * 128]
        for piece in range(fold):
            at = piece * width + lane
            p_ref[part * width : (part + 1) * width, at : at + 128] = gw_wide[
                pl.ds(piece, width, stride=fold), :
            ].astype(bf16)
    p_ref[3 * width :, :] = go_acc[...].astype(bf16)
    store = store_p(grads_out.at[pl.ds(0, 4 * width), :])
    store.start()
    store.wait()

    @pl.when(outer)
    def _():
        for w in range(2):
            copy_a(w).wait_send()

    @pl.when(inner)
    def _():
        copy_a(1).wait_recv()
        copy_b(0).wait_send()
        copy_b(0).wait_recv()

    for k in range(1, 4):
        copy_d(k).wait_send()
        copy_e(k, place).wait_send()
    for g in range(2):
        for d in range(1, 4):
            each_way(place, d, sends, lambda up: hop(g, d, up).wait_send())


def dha_copies(dha_out, p_ref, sem, w, windows, share):
    copies = []
    per = p_ref.shape[0] // share
    for n in range(per):
        block = w * per + n
        copies.append(
            pltpu.make_async_copy(
                p_ref.at[pl.ds(n * share, share), :],
                dha_out.at[block % windows, pl.ds(block // windows * share, share), :],
                sem.at[n],
            )
        )
    return copies


def lines_kernel(
    cuts,
    windows,
    order,
    ready,
    traded,
    rows_in,
    drm_ref,
    gains_ref,
    x_ref,
    dha_ref,
    part_ref,
    own_in,
    ra_in,
    rb_in,
    gain_in,
    out_ref,
    grad_ref,
    gain_ref,
    ra,
    rb,
    rc,
    value,
    own,
    piece,
    x_rows,
    grad,
    gain_sum,
    gain_got,
    s_send,
    s_recv,
    a_send,
    a_recv,
    b_send,
    b_recv,
    c_send,
    c_recv,
    g_send,
    g_recv,
    v_sem,
    o_sem,
    r_sem,
    t_sem,
    x_sem,
    l_sem,
    i_sem,
):
    place = lax.axis_index("tensor")
    lower = place < 2
    outer = (place == 0) | (place == 3)
    inner = (place == 1) | (place == 2)
    share = rc.shape[1]
    folds = len(order)
    next_in = jnp.where(lower, 1, 2)
    inner_far = 3 - place
    outer_near = jnp.where(lower, 0, 3)
    outer_far = 3 - outer_near

    def block(ref, index):
        return rows_ref(ref, index, share, 1)

    def whole(f):
        kind, index = order[f]
        return part_ref.at[index] if kind == 0 else dha_ref.at[index]

    def copy_a(f, i):
        return remote(
            block(whole(f), jnp.where(lower, 3 - i, i)),
            block(ra.at[f], jnp.where(lower, 2 - i, i)),
            a_send.at[f, i],
            a_recv.at[f, i],
            next_in,
        )

    def copy_b(f, i):
        return remote(
            block(ra.at[f], jnp.where(lower, 2 - i, i)),
            block(rb.at[f], jnp.where(lower, 1 - i, i)),
            b_send.at[f, i],
            b_recv.at[f, i],
            jnp.where(lower, 2, 1),
        )

    def copy_c(f):
        src = block(rb.at[f], jnp.where(lower, 0, 1))
        return remote(src, rc.at[f], c_send.at[f], c_recv.at[f], outer_near)

    def load(f):
        return pltpu.make_async_copy(whole(f), value.at[f], v_sem.at[f])

    def load_own(w):
        return pltpu.make_async_copy(own_in.at[w], own.at[w], o_sem.at[w])

    def load_ra(f):
        return pltpu.make_async_copy(ra_in.at[order[f][1]], ra.at[f], r_sem.at[f])

    def load_rb(f):
        return pltpu.make_async_copy(rb_in.at[order[f][1]], rb.at[f], t_sem.at[f])

    def rows_of(w, origin):
        return pl.ds(pl.multiple_of((w * 4 + origin) * share, share), share)

    def pass_on(w, origin, way, n, target):
        rows = rows_of(w, origin)
        return remote(
            piece.at[w] if way < 2 else out_ref.at[rows, :],
            out_ref.at[rows, :],
            g_send.at[w, way],
            g_recv.at[w, n],
            target,
        )

    def got(w, n):
        origin = (
            jnp.where(outer, next_in, inner_far),
            jnp.where(outer, 3 - next_in, outer_near),
            jnp.where(outer, 3 - place, outer_far),
        )[n]
        rows = rows_of(w, origin)
        return remote(
            out_ref.at[rows, :], out_ref.at[rows, :], g_send.at[w, 0], g_recv.at[w, n], inner_far
        )

    def keep(w):
        return pltpu.make_async_copy(
            piece.at[w], out_ref.at[rows_of(w, place), :], l_sem.at[w]
        )

    def store(c):
        return pltpu.make_async_copy(
            grad.at[c], grad_ref.at[pl.ds(c * share, share), :], i_sem.at[c]
        )

    x_load = pltpu.make_async_copy(
        rows_ref(x_ref, place * cuts, share, cuts), x_rows, x_sem
    )

    for w in range(windows):
        load(w).start()
        load_own(w).start()
    for f in range(windows, folds):
        load(f).start()
    x_load.start()

    pairs = []
    for axis in ("dp", "tensor"):
        index, bit = lax.axis_index(axis), 1
        while bit < lax.axis_size(axis):
            pairs.append((axis, index + bit - 2 * bit * lax.rem(index // bit, 2)))
            bit *= 2

    def copy_s(t):
        axis, other = pairs[t]
        return pltpu.make_async_remote_copy(
            src_ref=gain_sum.at[t],
            dst_ref=gain_got.at[t],
            send_sem=s_send.at[t],
            recv_sem=s_recv.at[t],
            device_id={axis: other},
            device_id_type=pl.DeviceIdType.MESH,
        )

    def next_pair(t):
        if t > 0:
            copy_s(t - 1).wait_recv()
            gain_sum[t] = gain_sum[t - 1] + gain_got[t - 1]
        if t < len(pairs):
            copy_s(t).start()

    gain_sum[0] = jnp.zeros(gain_sum.shape[1:], f32)
    gain_sum[0, 0:2, :] = gain_in[...]

    def rows_at_(index):
        return pl.ds(pl.multiple_of(index * share, share), share)

    def finish(f, terms):
        kind, index = order[f]
        if kind == 0:
            load_own(index).wait()
            total = own[index]
        else:
            total = value[f, rows_at_(place), :].astype(f32)
        for term in terms:
            total = total + term.astype(f32)
        if kind == 0:
            piece[index] = total.astype(bf16)
            keep(index).start()
        else:
            first = place * (cuts * share) + index * share
            count = drm_ref.shape[0]
            spread = (
                lax.broadcasted_iota(jnp.int32, (share, count), 0) + first == rows_in[...]
            ).astype(bf16)
            x = x_rows[pl.ds(index * share, share), :].astype(f32)
            grad[index] = input_grad_rows(
                total, x, drm_ref[...], gains_ref[0:1, :], spread
            ).astype(bf16)
            store(index).start()

    greet_line(place, [pair for pair in pairs if pair[0] == "dp"])

    @pl.when(outer)
    def _():
        chunks = [(f, i) for f in range(ready, folds) for i in range(3)]

        def step(n):
            copy_a(*chunks[n]).wait_send()
            if n + 2 < len(chunks):
                copy_a(*chunks[n + 2]).start()

        def total(f):
            copy_c(f).wait_recv()
            if order[f][0] == 1:
                load(f).wait()
            finish(f, [rc[f]])
            if order[f][0] == 0:
                pass_on(f, place, 0, 1, next_in).start()

        for n in range(2):
            copy_a(*chunks[n]).start()
        next_pair(0)
        total(0)
        step(0)
        step(1)
        next_pair(1)
        total(1)
        step(2)
        step(3)
        step(4)
        next_pair(2)
        total(2)
        next_pair(3)
        step(5)
        step(6)
        x_load.wait()
        total(3)
        next_pair(4)
        for n in range(7, 12):
            step(n)
        total(4)
        next_pair(5)
        total(5)
        for w in range(windows):
            load(w).wait()
            pass_on(w, place, 0, 1, next_in).wait_send()
            for n in range(3):
                got(w, n).wait_recv()

    @pl.when(inner)
    def _():
        for f in range(ready):
            load_ra(f).start()
        for f in range(traded):
            load_rb(f).start()

        def give_b(f):
            load(f).wait()
            if f < ready:
                load_ra(f).wait()
            for i in range(2):
                if f >= ready:
                    copy_a(f, i).wait_recv()
                to = rows_at_(jnp.where(lower, 2 - i, i))
                mine = value[f, rows_at_(jnp.where(lower, 3 - i, i)), :]
                ra[f, to, :] = (ra[f, to, :].astype(f32) + mine.astype(f32)).astype(bf16)
                copy_b(f, i).start()

        def total(f):
            if f < traded:
                load(f).wait()
                load_ra(f).wait()
                load_rb(f).wait()
            else:
                came(f, 0)
            to = rows_at_(jnp.where(lower, 0, 1))
            mine = value[f, rows_at_(outer_near), :]
            rb[f, to, :] = (rb[f, to, :].astype(f32) + mine.astype(f32)).astype(bf16)
            copy_c(f).start()
            if f >= traded:
                came(f, 1)
            if f >= ready:
                copy_a(f, 2).wait_recv()
            near = rows_at_(jnp.where(lower, 0, 2))
            other = rows_at_(jnp.where(lower, 1, 0))
            finish(f, [ra[f, near, :], rb[f, other, :]])
            if order[f][0] == 0:
                pass_on(f, place, 0, 0, inner_far).start()
                pass_on(f, place, 1, 0, outer_near).start()

        def came(f, i):
            to = block(rb.at[f], jnp.where(lower, i, 1 - i))
            remote(to, to, b_send.at[f, i], b_recv.at[f, i], inner_far).wait_recv()

        def from_far_inner(w):
            got(w, 0).wait_recv()
            pass_on(w, inner_far, 2, 1, outer_near).start()

        def from_outer(w):
            got(w, 1).wait_recv()
            pass_on(w, outer_near, 3, 2, inner_far).start()

        def from_far_outer(w):
            got(w, 2).wait_recv()
            pass_on(w, outer_far, 4, 2, outer_near).start()

        next_pair(0)
        total(0)
        give_b(1)
        next_pair(1)
        from_far_inner(0)
        total(1)
        next_pair(2)
        give_b(2)
        from_outer(0)
        from_far_inner(1)
        total(2)
        next_pair(3)
        from_far_outer(0)
        from_outer(1)
        give_b(3)
        from_far_inner(2)
        from_far_outer(1)
        x_load.wait()
        total(3)
        next_pair(4)
        from_outer(2)
        give_b(4)
        from_far_outer(2)
        total(4)
        give_b(5)
        total(5)
        next_pair(5)
        for f in range(folds):
            copy_c(f).wait_send()
            for i in range(2):
                if f >= traded:
                    copy_b(f, i).wait_send()
        for w in range(windows):
            pass_on(w, place, 0, 0, inner_far).wait_send()
            pass_on(w, place, 1, 0, outer_near).wait_send()
            pass_on(w, inner_far, 2, 1, outer_near).wait_send()
            pass_on(w, outer_near, 3, 2, inner_far).wait_send()
            pass_on(w, outer_far, 4, 2, outer_near).wait_send()

    gain_ref[...] = gain_sum[len(pairs), 0:2, :]
    for t in range(len(pairs)):
        copy_s(t).wait_send()
    for w in range(windows):
        keep(w).wait()
    for c in range(cuts):
        store(c).wait()


def place_kernel(place_ref, *refs):
    out_ref = refs[-1]
    parts = lax.axis_size("tensor")
    share = refs[0].shape[0]
    for step in range(parts):
        origin = lax.rem(place_ref[0] + parts - step, parts)
        out_ref[pl.ds(pl.multiple_of(origin * share, share), share), :] = refs[step][...]


def spread_kernel(tile_ref, used_ref, *refs):
    out_ref = refs[-1]
    step = pl.program_id(0)
    per = len(refs) - 1
    for n in range(per):
        used = used_ref[step * per + n] > 0

        @pl.when(used)
        def _():
            out_ref[n] = refs[n][0]

        @pl.when(jnp.logical_not(used))
        def _():
            out_ref[n] = jnp.zeros(out_ref.shape[1:], bf16)


def copy_kernel(in_ref, out_ref):
    out_ref[...] = in_ref[...]


def collect_kernel(slot_ref, *refs):
    out_ref = refs[-1]
    for index, ref in enumerate(refs[:-1]):
        out_ref[index] = ref[0]


def exchange(value, axis, bit):
    size = lax.axis_size(axis)
    return lax.ppermute(value, axis, [(i, i ^ bit) for i in range(size)])


def dp_total(value):
    size = lax.axis_size("dp")
    value = value + exchange(value, "dp", 1)
    bits = []
    bit = 2
    while bit < size:
        bits.append(bit)
        bit *= 2
    core = lax.axis_index("dp") % 2
    half = value.shape[0] // 2
    mine = lax.dynamic_slice_in_dim(value, core * half, half, 0)
    cut = half // 2
    low, high = mine[:cut], mine[cut:]
    for bit_low, bit_high in zip(bits, bits[::-1]):
        low = low + exchange(low, "dp", bit_low)
        high = high + exchange(high, "dp", bit_high)
    mine = jnp.concatenate([low, high], axis=0)
    other = exchange(mine, "dp", 1)
    return jnp.where(
        core == 0,
        jnp.concatenate([mine, other], axis=0),
        jnp.concatenate([other, mine], axis=0),
    )


def around(value):
    size = lax.axis_size("tensor")
    return [value] + [
        lax.ppermute(value, "tensor", [(i, (i + k) % size) for i in range(size)])
        for k in range(1, size)
    ]


def rows_at(value, index, share, count):
    return lax.dynamic_slice_in_dim(value, index * share, count * share, 0)


def other_sums(value, share):
    place = lax.axis_index("tensor")
    total = lax.psum_scatter(value, "tensor", scatter_dimension=0, tiled=True)
    own = rows_at(value, place, share, 1).astype(f32)
    return (total.astype(f32) - own,)


def small_total(value):
    for axis in ("dp", "tensor"):
        bit = 1
        while bit < lax.axis_size(axis):
            value = value + exchange(value, axis, bit)
            bit *= 2
    return value


def slot_ranks(owner_row):
    count_all = owner_row.shape[0]
    tile_order = jnp.arange(count_all, dtype=jnp.int32)
    earlier = (owner_row[:, None] == owner_row[None, :]) & (
        tile_order[None, :] < tile_order[:, None]
    )
    return jnp.sum(earlier.astype(jnp.int32), axis=1)


def adam_update(grad_now, first_old, second_old, param_old, rate, decay):
    first_new = beta_one * first_old + (1.0 - beta_one) * grad_now
    second_new = beta_two * second_old + (1.0 - beta_two) * grad_now * grad_now
    first_hat = first_new / (1.0 - beta_one**STEP)
    second_hat = second_new / (1.0 - beta_two**STEP)
    param_new = param_old - rate * (
        first_hat / (jnp.sqrt(second_hat) + adam_eps) + decay * param_old
    )
    return (first_new, second_new, param_new)


def head_tables(positions, heads, lib):
    frequency = lib.exp(
        -lib.log(lib.float32(10000.0))
        * (2.0 * lib.arange(HD // 2, dtype=lib.float32) / HD).astype(lib.float32)
    )
    angles = positions.astype(lib.float32)[..., None] * frequency
    cos, sin = lib.cos(angles), lib.sin(angles)
    cos = lib.concatenate([cos, cos], axis=-1)
    sin = lib.concatenate([-sin, sin], axis=-1)
    reps = (1,) * (cos.ndim - 1) + (heads,)
    return lib.tile(cos, reps), lib.tile(sin, reps)


def on_device(
    tokens,
    masked_rows,
    cotangent,
    norm_gains,
    gain_first,
    gain_second,
    owners,
    master,
    first_moment,
    second_moment,
):
    seq_count, mask_count = masked_rows.shape
    total_rows, model = tokens.shape
    window = total_rows // seq_count
    parts = lax.axis_size("tensor")
    place = lax.axis_index("tensor")
    owner_self = lax.axis_index("dp")
    heads = HEADS // parts
    width = heads * HD
    hidden = FF // parts
    capacity, tile_rows = master.shape[1:3]
    tile_size = tile_rows * model
    attn_tiles = 4 * model * width // tile_size
    ffn_tiles = 3 * model * hidden // tile_size
    count = -(-mask_count // 16) * 16
    place_ref = place.astype(jnp.int32).reshape(1)

    owner_row = owners[0]
    slot_rank = slot_ranks(owner_row)
    slot_index = owner_row * capacity + slot_rank
    slot_match = (owner_row[None, :] == owner_self) & (
        slot_rank[None, :] == jnp.arange(capacity, dtype=jnp.int32)[:, None]
    )
    slot_used = jnp.any(slot_match, axis=1)[:, None, None]
    slot_tile = jnp.argmax(slot_match, axis=1)

    mask_rows = seq_count * count
    share = window // parts
    share_rows = total_rows // parts
    dp_size = lax.axis_size("dp")
    lines = dp_size == 8 and attn_tiles == 8 and parts == 4 and seq_count == 3 and hidden == model and mask_rows <= window // 2
    anywhere = pl.BlockSpec(memory_space=pl.ANY)
    inside = pl.BlockSpec(memory_space=pltpu.VMEM)
    dma = pltpu.SemaphoreType.DMA

    tile_block = (1, tile_rows, model)
    if lines:
        small = pl.BlockSpec(memory_space=pltpu.SMEM)
        half_tiles = attn_tiles // 2
        low_slots, attn_sums = pl.pallas_call(
            weights_kernel,
            out_shape=[
                jax.ShapeDtypeStruct((capacity, tile_rows, model), bf16),
                jax.ShapeDtypeStruct((attn_tiles, tile_rows, model), bf16),
            ],
            in_specs=[small, small, inside],
            out_specs=[inside, anywhere],
            scratch_shapes=[
                pltpu.VMEM((attn_tiles, tile_rows, model), bf16),
                pltpu.VMEM((half_tiles, tile_rows, model), bf16),
                pltpu.VMEM((3, half_tiles, tile_rows, model), bf16),
                pltpu.VMEM((2, half_tiles, tile_rows, model), bf16),
                dma,
                dma,
                dma((2, half_tiles)),
                dma((2, half_tiles)),
                dma((half_tiles,)),
                dma((half_tiles,)),
                dma((half_tiles,)),
            ],
            compiler_params=params(collective_id=4, has_side_effects=True),
            cost_estimate=cost(0, 12e6),
            name="weights",
        )(
            slot_rank[:attn_tiles],
            (owner_row[:attn_tiles] == owner_self).astype(jnp.int32),
            master[0],
        )
        attn_flat = attn_sums.reshape(4 * width, model)
    else:
        grid_size = max(capacity, attn_tiles)
        low_slots, attn_mine = pl.pallas_call(
            cast_kernel,
            out_shape=[
                jax.ShapeDtypeStruct((capacity, tile_rows, model), bf16),
                jax.ShapeDtypeStruct((attn_tiles, tile_rows, model), bf16),
            ],
            grid_spec=pltpu.PrefetchScalarGridSpec(
                num_scalar_prefetch=2,
                grid=(grid_size,),
                in_specs=[
                    pl.BlockSpec(
                        tile_block, lambda i, rank, held: (jnp.minimum(i, capacity - 1), 0, 0)
                    ),
                    pl.BlockSpec(
                        tile_block,
                        lambda i, rank, held: (rank[jnp.minimum(i, attn_tiles - 1)], 0, 0),
                    ),
                ],
                out_specs=[
                    pl.BlockSpec(
                        tile_block, lambda i, rank, held: (jnp.minimum(i, capacity - 1), 0, 0)
                    ),
                    pl.BlockSpec(
                        tile_block, lambda i, rank, held: (jnp.minimum(i, attn_tiles - 1), 0, 0)
                    ),
                ],
            ),
            compiler_params=params(),
            cost_estimate=cost(0, 12 * capacity * tile_size),
            name="cast",
        )(
            slot_rank,
            jnp.pad(
                (owner_row[:attn_tiles] == owner_self).astype(jnp.int32),
                (0, grid_size - attn_tiles),
                mode="edge",
            ),
            master[0],
            master[0],
        )
        attn_flat = dp_total(attn_mine).reshape(4 * width, model)
    w_out = attn_flat[3 * width :]
    every_slot = lax.all_gather(low_slots, "dp", axis=0, tiled=True)

    cos, sin = map(jnp.asarray, head_tables(np.arange(window), heads, np))
    rows = jnp.pad(masked_rows, ((0, 0), (0, count - mask_count)), constant_values=-1)
    cot = jnp.pad(cotangent, ((0, 0), (0, count - mask_count), (0, 0)))
    cot = cot.reshape(seq_count * count, model)

    win_model = pl.BlockSpec((window, model), lambda i: (i, 0))
    win_head = pl.BlockSpec((window, width), lambda i: (i, 0))
    mask_model = pl.BlockSpec((count, model), lambda i: (i, 0))
    mask_head = pl.BlockSpec((count, width), lambda i: (i, 0))
    if lines:
        (
            o_m,
            o_first,
            o_second,
            o_third,
            w_far,
            q_m,
            x_m,
            cos_m,
            sin_m,
            k,
            v,
            w_qkv,
        ) = pl.pallas_call(
            functools.partial(attend_all_kernel, seq_count),
            out_shape=[
                jax.ShapeDtypeStruct((4, mask_rows, width), bf16),
                jax.ShapeDtypeStruct((4, window, width), bf16),
                jax.ShapeDtypeStruct((window, width), bf16),
                jax.ShapeDtypeStruct((window, width), bf16),
                jax.ShapeDtypeStruct((3, width, model), bf16),
                jax.ShapeDtypeStruct((mask_rows, width), bf16),
                jax.ShapeDtypeStruct((mask_rows, model), bf16),
                jax.ShapeDtypeStruct((mask_rows, width), f32),
                jax.ShapeDtypeStruct((mask_rows, width), f32),
                jax.ShapeDtypeStruct((total_rows, width), bf16),
                jax.ShapeDtypeStruct((total_rows, width), bf16),
                jax.ShapeDtypeStruct((model, 3 * width), bf16),
            ],
            in_specs=[inside] * 5 + [anywhere] * 2,
            out_specs=[anywhere] * 5 + [inside] * 7,
            scratch_shapes=[
                pltpu.VMEM((total_rows, width), bf16),
                pltpu.VMEM((3 * width // 128, model, 128), f32),
                pltpu.VMEM((mask_rows, width), bf16),
                pltpu.VMEM((seq_count, window, width), bf16),
                pltpu.VMEM((2, window, model), bf16),
                dma((2,)),
                dma((seq_count,)),
                dma,
                dma((3, 2)),
                dma((3, 2)),
                dma((3, 2)),
                dma((3, 2)),
                dma((3, 2)),
                dma((3, 2)),
                dma((3,)),
                dma((3,)),
            ],
            compiler_params=params(collective_id=3, has_side_effects=True),
            cost_estimate=cost(4e10, 20e6),
            name="attend_all",
        )(rows[:, :, None], norm_gains, attn_flat, cos, sin, tokens, attn_flat)
        before_tiles = o_third
    else:
        block = min(512, window)
        per_window = window // block
        row_block = pl.BlockSpec((block, model), lambda i: (i, 0))
        head_block = pl.BlockSpec((block, width), lambda i: (i, 0))
        table_block = pl.BlockSpec((block, width), lambda i: (i % per_window, 0))
        q, k, v, w_qkv = pl.pallas_call(
            qkv_kernel,
            out_shape=[jax.ShapeDtypeStruct((total_rows, width), bf16)] * 3
            + [jax.ShapeDtypeStruct((model, 3 * width), bf16)],
            grid=(total_rows // block,),
            in_specs=[
                row_block,
                whole_spec((2, model)),
                whole_spec((3 * width, model)),
                table_block,
                table_block,
            ],
            out_specs=[head_block] * 3 + [whole_spec((model, 3 * width))],
            scratch_shapes=[pltpu.VMEM((3 * width // 128, model, 128), f32)],
            compiler_params=params(),
            cost_estimate=cost(6 * total_rows * model * width, 2 * total_rows * model * 2),
            name="qkv",
        )(tokens, norm_gains, attn_flat, cos, sin)

        o_m, q_m, x_m = pl.pallas_call(
            attend_masked_kernel,
            out_shape=[
                jax.ShapeDtypeStruct((seq_count * count, width), bf16),
                jax.ShapeDtypeStruct((seq_count * count, width), bf16),
                jax.ShapeDtypeStruct((seq_count * count, model), bf16),
            ],
            grid=(seq_count,),
            in_specs=[
                pl.BlockSpec((1, count, 1), lambda i: (i, 0, 0)),
                win_model,
                win_head,
                win_head,
                win_head,
            ],
            out_specs=[mask_head, mask_head, mask_model],
            compiler_params=params(),
            cost_estimate=cost(
                seq_count * count * window * (2 * model + 8 * width), 9e6, seq_count * count * window * heads
            ),
            name="attend_masked",
        )(rows[:, :, None], tokens, q, k, v)
        o_ms = around(o_m)

        q_block = min(256, window)

        def attend_window(w, before):
            return pl.pallas_call(
                after(attend_kernel, 3, 1),
                out_shape=jax.ShapeDtypeStruct((window, width), bf16),
                grid=(width // 128, window // q_block),
                in_specs=[
                    pl.BlockSpec((q_block, 128), lambda p, i: (w * (window // q_block) + i, p)),
                    pl.BlockSpec((window, 128), lambda p, i: (w, p)),
                    pl.BlockSpec((window, 128), lambda p, i: (w, p)),
                    UNREAD,
                ],
                out_specs=pl.BlockSpec((q_block, 128), lambda p, i: (i, p)),
                compiler_params=params(),
                cost_estimate=cost(
                    16 * window * window * width, 4 * window * width * 2, window * window * heads
                ),
                name="attend",
            )(q, k, v, before)

        early = max(seq_count - 1, 1)
        o_own = []
        for w in range(early):
            o_own.append(attend_window(w, o_own[-1] if o_own else o_m))
        before_tiles = o_own[-1]
        cos_m, sin_m = (
            table.reshape(mask_rows, width) for table in head_tables(rows, heads, jnp)
        )

    group = 4
    ffn_all = pl.pallas_call(
        after(collect_kernel, 1 + group, 1),
        out_shape=jax.ShapeDtypeStruct((ffn_tiles, tile_rows, model), bf16),
        grid_spec=pltpu.PrefetchScalarGridSpec(
            num_scalar_prefetch=1,
            grid=(ffn_tiles // group,),
            in_specs=[
                pl.BlockSpec(
                    tile_block,
                    lambda i, slot, n=n: (slot[attn_tiles + i * group + n], 0, 0),
                )
                for n in range(group)
            ]
            + [UNREAD],
            out_specs=pl.BlockSpec((group, tile_rows, model), lambda i, slot: (i, 0, 0)),
        ),
        compiler_params=params(),
        cost_estimate=cost(0, 4 * ffn_tiles * tile_size),
        name="collect",
    )(slot_index, *[every_slot] * group, before_tiles)
    even = jnp.array([[1.0], [1.0 / parts]], f32)
    flat_rows = jnp.where(
        rows >= 0, rows + window * jnp.arange(seq_count, dtype=jnp.int32)[:, None], -1
    ).reshape(1, mask_rows)
    if lines:
        grad_rows = 4 * width + 3 * hidden
        part, own, first_sums, second_sums, dha, grads, dr_m, gains_part = pl.pallas_call(
            functools.partial(middle_kernel, seq_count),
            out_shape=[
                jax.ShapeDtypeStruct((seq_count, window, model), bf16),
                jax.ShapeDtypeStruct((seq_count, share, model), f32),
                jax.ShapeDtypeStruct((2, 3 * share, model), bf16),
                jax.ShapeDtypeStruct((1, 2 * share, model), bf16),
                jax.ShapeDtypeStruct((seq_count, window, model), bf16),
                jax.ShapeDtypeStruct((grad_rows, model), bf16),
                jax.ShapeDtypeStruct((mask_rows, model), f32),
                jax.ShapeDtypeStruct((2, model), f32),
            ],
            in_specs=[inside] * 15 + [anywhere] * 5,
            out_specs=[anywhere] * 6 + [inside] * 2,
            scratch_shapes=[
                pltpu.VMEM((window, model), f32),
                pltpu.VMEM((window, model), bf16),
                pltpu.VMEM((window, model), f32),
                pltpu.VMEM((window, model), bf16),
                pltpu.VMEM((share, model), f32),
                pltpu.VMEM((2, 4, window, width), bf16),
                pltpu.VMEM((window, model), bf16),
                pltpu.VMEM((2, 2, window, width), bf16),
                pltpu.VMEM((window, 3 * width), bf16),
                pltpu.VMEM((model, 3 * width), f32),
                pltpu.VMEM((model, 128), f32),
                pltpu.VMEM((width, model), f32),
                pltpu.VMEM((mask_rows, model), f32),
                pltpu.VMEM((4, mask_rows, model // 4), bf16),
                pltpu.VMEM((3, mask_rows, model // 4), bf16),
                pltpu.VMEM((4, mask_rows, model // 4), bf16),
                pltpu.VMEM((1, 2 * share, model), bf16),
                dma((2,)),
                dma((1,)),
                dma((1,)),
                dma((2,)),
                dma,
                dma((2, 2)),
                dma((2, 3)),
                dma,
                dma((window // share,)),
                dma,
                dma((2,)),
                dma((2,)),
                dma((2, 3, 2)),
                dma((2, 3, 2)),
                dma((3,)),
                dma((3,)),
                dma((3,)),
                dma((3,)),
            ],
            compiler_params=params(collective_id=1, has_side_effects=True),
            cost_estimate=cost(1e11, 100e6),
            name="middle",
        )(
            rows[:, None, :],
            norm_gains,
            x_m,
            cot,
            q_m,
            cos_m,
            sin_m,
            cos,
            sin,
            w_qkv,
            ffn_all.reshape(3, model, hidden),
            o_m,
            o_first,
            w_out,
            w_far,
            tokens,
            k,
            v,
            o_second,
            o_third,
        )

        group = 8
        slots = lax.axis_size("dp") * capacity
        slot_hit = slot_index[None, :] == jnp.arange(slots, dtype=jnp.int32)[:, None]
        used = jnp.any(slot_hit, axis=1).astype(jnp.int32)
        tile_count = slot_index.shape[0]
        held_at = jnp.arange(slots, dtype=jnp.int32) // group * tile_count
        held_at = held_at + jnp.argmax(slot_hit, axis=1).astype(jnp.int32)
        held_at = jnp.where(used > 0, held_at, 0).reshape(-1, group)
        from_tile = lax.rem(lax.cummax(held_at, axis=0), tile_count).reshape(-1)
        in_slots = pl.pallas_call(
            spread_kernel,
            out_shape=jax.ShapeDtypeStruct((slots, tile_rows, model), bf16),
            grid_spec=pltpu.PrefetchScalarGridSpec(
                num_scalar_prefetch=2,
                grid=(slots // group,),
                in_specs=[
                    pl.BlockSpec(
                        tile_block, lambda i, tile, used, n=n: (tile[i * group + n], 0, 0)
                    )
                    for n in range(group)
                ],
                out_specs=pl.BlockSpec(
                    (group, tile_rows, model), lambda i, tile, used: (i, 0, 0)
                ),
            ),
            compiler_params=params(),
            cost_estimate=cost(0, 24 * capacity * tile_size),
            name="spread",
        )(
            from_tile,
            used,
            *[grads.reshape(-1, tile_rows, model)] * group,
        )
        reduced = lax.psum_scatter(in_slots, "dp", scatter_dimension=0, tiled=True).astype(f32)

        order = [(kind, i) for kind in (0, 1) for i in range(seq_count)]
        folds = len(order)
        pair_count = (lax.axis_size("dp") * parts).bit_length() - 1
        layer_out, input_grad, gain_grad = pl.pallas_call(
            after(functools.partial(lines_kernel, seq_count, seq_count, order, 2, 1), 10, 1),
            out_shape=[
                jax.ShapeDtypeStruct((total_rows, model), bf16),
                jax.ShapeDtypeStruct((share_rows, model), bf16),
                jax.ShapeDtypeStruct((2, model), f32),
            ],
            in_specs=[inside] * 3 + [anywhere] * 6 + [inside, anywhere],
            out_specs=[anywhere] * 2 + [inside],
            scratch_shapes=[
                pltpu.VMEM((folds, 3 * share, model), bf16),
                pltpu.VMEM((folds, 2 * share, model), bf16),
                pltpu.VMEM((folds, share, model), bf16),
                pltpu.VMEM((folds, window, model), bf16),
                pltpu.VMEM((seq_count, share, model), f32),
                pltpu.VMEM((seq_count, share, model), bf16),
                pltpu.VMEM((share_rows, model), bf16),
                pltpu.VMEM((seq_count, share, model), bf16),
                pltpu.VMEM((pair_count + 1, 8, model), f32),
                pltpu.VMEM((pair_count, 8, model), f32),
                dma((pair_count,)),
                dma((pair_count,)),
                dma((folds, 3)),
                dma((folds, 3)),
                dma((folds, 2)),
                dma((folds, 2)),
                dma((folds,)),
                dma((folds,)),
                dma((seq_count, 5)),
                dma((seq_count, 3)),
                dma((folds,)),
                dma((seq_count,)),
                dma((2,)),
                dma((1,)),
                dma,
                dma((seq_count,)),
                dma((seq_count,)),
            ],
            compiler_params=params(collective_id=2, has_side_effects=True),
            cost_estimate=cost(4 * share_rows * mask_rows * model, 60e6),
            name="lines",
        )(
            flat_rows,
            dr_m,
            norm_gains,
            tokens,
            dha,
            part,
            own,
            first_sums,
            second_sums,
            gains_part * even,
            in_slots,
        )
    else:
        w_outs = around(w_out)
        ffn_flat = ffn_all.reshape(3, -1)
        w_gate = ffn_flat[0].reshape(model, hidden)
        w_up = ffn_flat[1].reshape(model, hidden)
        w_down = ffn_flat[2].reshape(hidden, model)
        cols = min(256, hidden)
        col_block = pl.BlockSpec((model, cols), lambda c: (0, c))
        down_block = pl.BlockSpec((cols, model), lambda c: (c, 0))
        r_m, dhf_part, ffn_grad = pl.pallas_call(
            functools.partial(ffn_masked_kernel, parts),
            out_shape=[
                jax.ShapeDtypeStruct((mask_rows, model), f32),
                jax.ShapeDtypeStruct((mask_rows, model), bf16),
                jax.ShapeDtypeStruct((3, hidden, model), bf16),
            ],
            grid=(hidden // cols,),
            in_specs=[
                whole_spec((mask_rows, model)),
                whole_spec((mask_rows, model)),
                whole_spec((2, model)),
                col_block,
                col_block,
                down_block,
            ]
            + [whole_spec((mask_rows, width))] * parts
            + [whole_spec((width, model))] * parts,
            out_specs=[
                whole_spec((mask_rows, model)),
                whole_spec((mask_rows, model)),
                whole_spec((3, hidden, model)),
            ],
            scratch_shapes=[
                pltpu.VMEM((mask_rows, model), bf16),
                pltpu.VMEM((mask_rows, model), f32),
                pltpu.VMEM((cols // 128, model, 128), f32),
            ],
            compiler_params=params(),
            cost_estimate=cost(
                mask_rows * model * (18 * hidden + 2 * model), 20e6, mask_rows * hidden
            ),
            name="ffn_masked",
        )(x_m, cot, norm_gains, w_gate, w_up, w_down, *o_ms, *w_outs)

        for w in range(early, seq_count):
            o_own.append(attend_window(w, r_m))
        windows_o = [around(o) for o in o_own]

        share_m = mask_rows // parts
        dhf_mine = lax.dynamic_slice_in_dim(dhf_part, place * share_m, share_m, 0).astype(f32)
        for step in range(1, parts):
            send = lax.dynamic_slice_in_dim(
                dhf_part, lax.rem(place + step, parts) * share_m, share_m, 0
            )
            dhf_mine = dhf_mine + lax.ppermute(
                send, "tensor", [(i, (i + step) % parts) for i in range(parts)]
            ).astype(f32)
        dhf_all = around(dhf_mine.astype(bf16))
        dhf = jnp.zeros((mask_rows, model), bf16)
        for step, piece in enumerate(dhf_all):
            origin = lax.rem(place + parts - step, parts)
            dhf = lax.dynamic_update_slice_in_dim(dhf, piece, origin * share_m, 0)

        layer_out = None

        def ffn_window(w, before):
            return pl.pallas_call(
                after(functools.partial(ffn_kernel, parts), 6 + 2 * parts, 1),
                out_shape=[
                    jax.ShapeDtypeStruct((window, model), bf16),
                    jax.ShapeDtypeStruct((share, model), f32),
                ],
                grid_spec=pltpu.PrefetchScalarGridSpec(
                    num_scalar_prefetch=1,
                    grid=(hidden // cols,),
                    in_specs=[
                        pl.BlockSpec((window, model), lambda c, place_ref: (w, 0)),
                        whole_spec((2, model)),
                        pl.BlockSpec((model, cols), lambda c, place_ref: (0, c)),
                        pl.BlockSpec((model, cols), lambda c, place_ref: (0, c)),
                        pl.BlockSpec((cols, model), lambda c, place_ref: (c, 0)),
                    ]
                    + [whole_spec((window, width))] * parts
                    + [whole_spec((width, model))] * parts
                    + [UNREAD],
                    out_specs=[
                        whole_spec((window, model)),
                        whole_spec((share, model)),
                    ],
                    scratch_shapes=[
                        pltpu.VMEM((window, model), f32),
                        pltpu.VMEM((window, model), bf16),
                        pltpu.VMEM((window, model), f32),
                    ],
                ),
                compiler_params=params(),
                cost_estimate=cost(
                    window * model * (6 * hidden + 2 * model), 16e6, window * hidden
                ),
                name="ffn",
            )(
                place_ref,
                tokens,
                norm_gains,
                w_gate,
                w_up,
                w_down,
                *windows_o[w],
                *w_outs,
                before,
            )

        def place_window(w, part, own):
            terms = other_sums(part, share)
            total = own
            for term in terms:
                total = total + term.astype(f32)
            pieces = around(total.astype(bf16))
            return pl.pallas_call(
                after(place_kernel, 1 + parts, 0 if layer_out is None else 1),
                out_shape=jax.ShapeDtypeStruct((total_rows, model), bf16),
                grid_spec=pltpu.PrefetchScalarGridSpec(
                    num_scalar_prefetch=1,
                    grid=(1,),
                    in_specs=[whole_spec((share, model))] * parts
                    + [UNREAD] * (layer_out is not None),
                    out_specs=pl.BlockSpec((window, model), lambda i, place_ref: (w, 0)),
                ),
                input_output_aliases={} if layer_out is None else {1 + parts: 0},
                compiler_params=params(),
                cost_estimate=cost(0, 4 * window * model),
                name="place",
            )(place_ref, *pieces, *([] if layer_out is None else [layer_out]))

        parts_out = [ffn_window(0, o_own[-1])]

        cuts = seq_count if share_rows % (16 * seq_count) == 0 else 1
        cut_rows = share_rows // cuts
        dr_m, dha, attn_grad, gains_part = pl.pallas_call(
            after(attn_back_kernel, 16, 1),
            out_shape=[
                jax.ShapeDtypeStruct((mask_rows, model), f32),
                jax.ShapeDtypeStruct((cuts, parts, cut_rows, model), bf16),
                jax.ShapeDtypeStruct((4 * width, model), bf16),
                jax.ShapeDtypeStruct((2, model), f32),
            ],
            grid=(seq_count,),
            in_specs=[
                pl.BlockSpec((1, 1, count), lambda i: (i, 0, 0)),
                mask_model,
                mask_model,
                mask_model,
                whole_spec((2, model)),
                mask_head,
                mask_head,
                mask_head,
                mask_head,
                win_head,
                win_head,
                win_model,
                whole_spec((window, width)),
                whole_spec((window, width)),
                whole_spec((width, model)),
                whole_spec((model, 3 * width)),
                UNREAD,
            ],
            out_specs=[
                mask_model,
                whole_spec((cuts, parts, cut_rows, model)),
                whole_spec((4 * width, model)),
                whole_spec((2, model)),
            ],
            scratch_shapes=[
                pltpu.VMEM((model, 3 * width), f32),
                pltpu.VMEM((width, model), f32),
                pltpu.VMEM((2, model), f32),
                pltpu.VMEM((window, 3 * width), bf16),
                pltpu.VMEM((3 * width // 128, model, 128), f32),
            ],
            compiler_params=params(),
            cost_estimate=cost(
                12 * total_rows * model * width, 30e6, mask_rows * window * heads
            ),
            name="attn_back",
        )(
            rows[:, None, :],
            dhf,
            r_m,
            cot,
            norm_gains,
            o_m,
            q_m,
            cos_m,
            sin_m,
            k,
            v,
            tokens,
            cos,
            sin,
            w_out,
            w_qkv,
            parts_out[0][0],
        )

        for w in range(1, seq_count):
            parts_out.append(ffn_window(w, gains_part if w == 1 else parts_out[-1][0]))

        input_grad = None
        for cut in range(cuts):
            value = dha[cut].reshape(parts * cut_rows, model)
            terms = other_sums(value, cut_rows)
            before = [] if input_grad is None else [input_grad]
            input_grad = pl.pallas_call(
                after(
                    functools.partial(input_grad_kernel, (cut, cuts, len(terms))),
                    6 + len(terms),
                    len(before),
                ),
                out_shape=jax.ShapeDtypeStruct((share_rows, model), bf16),
                grid_spec=pltpu.PrefetchScalarGridSpec(
                    num_scalar_prefetch=1,
                    grid=(1,),
                    in_specs=[
                        whole_spec((1, mask_rows)),
                        whole_spec((mask_rows, model)),
                        whole_spec((2, model)),
                        pl.BlockSpec(
                            (cut_rows, model),
                            lambda i, place_ref, cut=cut: (place_ref[0] * cuts + cut, 0),
                        ),
                        pl.BlockSpec(
                            (1, 1, cut_rows, model),
                            lambda i, place_ref, cut=cut: (cut, place_ref[0], 0, 0),
                        ),
                    ]
                    + [whole_spec((cut_rows, model))] * len(terms)
                    + [UNREAD] * len(before),
                    out_specs=pl.BlockSpec((cut_rows, model), lambda i, place_ref, cut=cut: (cut, 0)),
                ),
                input_output_aliases={6 + len(terms): 0} if before else {},
                compiler_params=params(),
                cost_estimate=cost(4 * cut_rows * mask_rows * model, 6e6),
                name="input_grad",
            )(place_ref, flat_rows, dr_m, norm_gains, tokens, dha, *terms, *before)

        for w, outs in enumerate(parts_out):
            layer_out = place_window(w, *outs)

        gain_grad = small_total(gains_part * even)

        def total_tiles(tiles, before):
            piece = lax.psum_scatter(tiles, "dp", scatter_dimension=0, tiled=True)
            piece = pl.pallas_call(
                after(copy_kernel, 1, 1),
                out_shape=jax.ShapeDtypeStruct(piece.shape, bf16),
                in_specs=[pl.BlockSpec(memory_space=pltpu.VMEM), UNREAD],
                out_specs=pl.BlockSpec(memory_space=pltpu.VMEM),
                compiler_params=params(),
                name="copy",
            )(piece, before)
            return lax.all_gather(piece, "dp", axis=0, tiled=True)

        ffn_grads = total_tiles(ffn_grad.reshape(3 * hidden, model), parts_out[1][0])
        attn_grads = total_tiles(attn_grad, parts_out[-1][0])
        tiles = jnp.concatenate([attn_grads, ffn_grads], axis=0).reshape(-1, tile_rows, model)
        reduced = tiles[slot_tile].astype(f32)

    _, gain_moment, gain_new = adam_update(
        gain_grad, gain_first, gain_second, norm_gains, gain_rate, 0.0
    )

    first_new, second_new, param_new = adam_update(
        reduced, first_moment[0], second_moment[0], master[0], weight_rate, weight_decay
    )
    weight_grad = jnp.where(slot_used, reduced, 0.0)
    weight_first = jnp.where(slot_used, first_new, 0.0)
    weight_second = jnp.where(slot_used, second_new, 0.0)
    weight_master = jnp.where(slot_used, param_new, 0.0)
    weight_low = weight_master.astype(bf16)
    return (
        layer_out,
        input_grad,
        weight_grad[None],
        weight_first[None],
        weight_second[None],
        weight_master[None],
        weight_low[None],
        gain_grad,
        gain_moment,
        gain_new,
    )


def solution(mesh):
    return jax.shard_map(
        on_device,
        mesh=mesh,
        in_specs=(
            P("dp", None),
            P("dp", None),
            P("dp", None, None),
            P(),
            P(),
            P(),
            P("tensor", None),
            P("tensor", "dp", None, None),
            P("tensor", "dp", None, None),
            P("tensor", "dp", None, None),
        ),
        out_specs=(
            P("dp", None),
            P(("dp", "tensor"), None),
            P("tensor", "dp", None, None),
            P("tensor", "dp", None, None),
            P("tensor", "dp", None, None),
            P("tensor", "dp", None, None),
            P("tensor", "dp", None, None),
            P(),
            P(),
            P(),
        ),
        check_vma=False,
    )
```

```python
import functools

import jax
import jax.numpy as jnp
import numpy as np
from jax import lax
from jax.experimental import pallas as pl
from jax.experimental.pallas import tpu as pltpu
from jax.sharding import PartitionSpec as P

HEADS = 16
HD = 64
FF = 4096
STEP = 5

norm_eps = 1e-06
beta_one = 0.9
beta_two = 0.95
adam_eps = 1e-08
weight_rate = 0.05
gain_rate = 0.8
weight_decay = 0.1

score_scale = HD ** (-0.5)
f32 = jnp.float32
bf16 = jnp.bfloat16
VMEM_LIMIT = 60 * 1024 * 1024
NT = (((1,), (1,)), ((), ()))
TN = (((0,), (0,)), ((), ()))


def mm(left, right):
    return jnp.dot(left, right, preferred_element_type=f32)


def mm_nt(left, right):
    return lax.dot_general(left, right, NT, preferred_element_type=f32)


def mm_tn(left, right):
    return lax.dot_general(left, right, TN, preferred_element_type=f32)


def params(**kw):
    return pltpu.CompilerParams(vmem_limit_bytes=VMEM_LIMIT, **kw)


def cost(flops, nbytes, transcendentals=0):
    return pl.CostEstimate(
        flops=int(flops), bytes_accessed=int(nbytes), transcendentals=int(transcendentals)
    )


def whole_spec(shape):
    return pl.BlockSpec(shape, lambda *_: (0,) * len(shape))


def after(kernel, inputs, count):
    return lambda *refs: kernel(*refs[:inputs], *refs[inputs + count :])


UNREAD = pl.BlockSpec(memory_space=pl.ANY)


def rms_scale(values):
    return lax.rsqrt(jnp.mean(values * values, axis=-1, keepdims=True) + norm_eps)


def swap_halves(values):
    width = values.shape[1]
    lane = lax.broadcasted_iota(jnp.int32, values.shape, 1)
    return jnp.where(
        lane % HD < HD // 2,
        pltpu.roll(values, width - HD // 2, 1),
        pltpu.roll(values, HD // 2, 1),
    )


def cast_kernel(rank_ref, held_ref, slot_ref, tile_ref, low_ref, mine_ref):
    low_ref[...] = slot_ref[...].astype(bf16)
    tile = tile_ref[...].astype(bf16)
    held = held_ref[pl.program_id(0)] > 0
    mine_ref[...] = jnp.where(held, tile, jnp.zeros((), bf16))


def qkv_kernel(
    x_ref, gains_ref, tiles_ref, cos_ref, sin_ref, q_ref, k_ref, v_ref, w_ref, w_wide
):
    width = q_ref.shape[1]
    model = x_ref.shape[1]
    fold = model // width

    @pl.when(pl.program_id(0) == 0)
    def _():
        for block in range(3 * width // 128):
            part, lane = divmod(block * 128, width)
            for piece in range(fold):
                at = piece * width + lane
                w_wide[block, pl.ds(piece, width, stride=fold), :] = tiles_ref[
                    part * width : (part + 1) * width, at : at + 128
                ].astype(f32)
            w_ref[:, block * 128 : (block + 1) * 128] = w_wide[block].astype(bf16)

    x = x_ref[...].astype(f32)
    hidden = (x * rms_scale(x) * gains_ref[0:1, :]).astype(bf16)
    cos, sin = cos_ref[...], sin_ref[...]
    q = mm(hidden, w_ref[:, 0:width])
    q_ref[...] = (q * cos + swap_halves(q) * sin).astype(bf16)
    k = mm(hidden, w_ref[:, width : 2 * width])
    k_ref[...] = (k * cos + swap_halves(k) * sin).astype(bf16)
    v_ref[...] = mm(hidden, w_ref[:, 2 * width : 3 * width]).astype(bf16)


def attend(q, k, v):
    first = lax.broadcasted_iota(jnp.int32, q.shape, 1) < HD
    first_v = lax.broadcasted_iota(jnp.int32, v.shape, 1) < HD
    zero, one = jnp.zeros((), bf16), jnp.ones((), bf16)
    outs = []
    for head in range(2):
        q_head = jnp.where(first if head == 0 else ~first, q, zero)
        v_head = jnp.where(first_v if head == 0 else ~first_v, v, one)
        s = mm_nt(q_head, k)
        s = (s - jnp.max(s, axis=-1, keepdims=True)) * score_scale
        outs.append(mm(jnp.exp(s).astype(bf16), v_head))
    value = jnp.where(first, outs[0], outs[1])
    total = pltpu.roll(jnp.where(first, outs[1], outs[0]), HD, 1)
    return (value / total).astype(bf16)


def attend_kernel(q_ref, k_ref, v_ref, o_ref):
    o_ref[...] = attend(q_ref[...], k_ref[...], v_ref[...])


def attend_masked_kernel(rows_ref, x_ref, q_ref, k_ref, v_ref, o_ref, qm_ref, xm_ref):
    window = x_ref.shape[0]
    count = rows_ref.shape[1]
    pick = (
        lax.broadcasted_iota(jnp.int32, (count, window), 1) == rows_ref[0]
    ).astype(bf16)
    xm_ref[...] = mm(pick, x_ref[...]).astype(bf16)
    qm = mm(pick, q_ref[...]).astype(bf16)
    qm_ref[...] = qm
    for pair in range(q_ref.shape[1] // 128):
        lanes = slice(pair * 128, pair * 128 + 128)
        o_ref[:, lanes] = attend(qm[:, lanes], k_ref[:, lanes], v_ref[:, lanes])


def ffn_masked_kernel(
    parts, xm_ref, cot_ref, gains_ref, wg_ref, wu_ref, wd_ref, *refs
):
    o_refs, wo_refs = refs[:parts], refs[parts : 2 * parts]
    rm_ref, dhf_ref, grad_ref, hf_ref, acc_ref, wide_ref = refs[2 * parts :]
    step = pl.program_id(0)
    width = wg_ref.shape[1]
    cols = pl.ds(pl.multiple_of(step * width, width), width)
    hidden, model = grad_ref.shape[1:]
    fold = model // hidden

    def put(part, grad):
        if fold == 1:
            grad_ref[part, :, cols] = grad.astype(bf16)
            return
        for block in range(width // 128):
            wide_ref[block] = grad[:, block * 128 : (block + 1) * 128]
            for piece in range(fold):
                at = piece * hidden + step * width + block * 128
                at = pl.ds(pl.multiple_of(at, 128), 128)
                grad_ref[part, :, at] = wide_ref[
                    block, pl.ds(piece, hidden, stride=fold), :
                ].astype(bf16)

    @pl.when(step == 0)
    def _():
        r = xm_ref[...].astype(f32)
        for o_ref, wo_ref in zip(o_refs, wo_refs):
            r = r + mm(o_ref[...], wo_ref[...])
        rm_ref[...] = r
        hf_ref[...] = (r * rms_scale(r) * gains_ref[1:2, :]).astype(bf16)
        acc_ref[...] = jnp.zeros_like(acc_ref)

    hf, dy = hf_ref[...], cot_ref[...]
    wg, wu, wd = wg_ref[...], wu_ref[...], wd_ref[...]
    g, u = mm(hf, wg), mm(hf, wu)
    sig = jax.nn.sigmoid(g)
    act = (g * sig * u).astype(bf16)
    grad_ref[2, cols, :] = mm_tn(act, dy).astype(bf16)
    da = mm_nt(dy, wd)
    dg = (da * u * sig * (1.0 + g * (1.0 - sig))).astype(bf16)
    du = (da * g * sig).astype(bf16)
    put(0, mm_tn(hf, dg))
    put(1, mm_tn(hf, du))
    acc_ref[...] += mm_nt(dg, wg) + mm_nt(du, wu)

    @pl.when(step == pl.num_programs(0) - 1)
    def _():
        dhf_ref[...] = acc_ref[...].astype(bf16)


def ffn_kernel(parts, place_ref, x_ref, gains_ref, wg_ref, wu_ref, wd_ref, *refs):
    o_refs, wo_refs = refs[:parts], refs[parts : 2 * parts]
    part_ref, own_ref, r_ref, hf_ref, acc_ref = refs[2 * parts :]
    step = pl.program_id(0)

    @pl.when(step == 0)
    def _():
        r = x_ref[...].astype(f32)
        for o_ref, wo_ref in zip(o_refs, wo_refs):
            r = r + mm(o_ref[...], wo_ref[...])
        r_ref[...] = r
        hf_ref[...] = (r * rms_scale(r) * gains_ref[1:2, :]).astype(bf16)
        acc_ref[...] = jnp.zeros_like(acc_ref)

    hf = hf_ref[...]
    g, u = mm(hf, wg_ref[...]), mm(hf, wu_ref[...])
    act = (g * jax.nn.sigmoid(g) * u).astype(bf16)
    acc_ref[...] += mm(act, wd_ref[...])

    @pl.when(step == pl.num_programs(0) - 1)
    def _():
        share = own_ref.shape[0]
        part_ref[...] = acc_ref[...].astype(bf16)
        mine = pl.ds(pl.multiple_of(place_ref[0] * share, share), share)
        own_ref[...] = r_ref[mine, :] + acc_ref[mine, :]


def attn_back_kernel(
    rows_ref,
    dhf_ref,
    rm_ref,
    cot_ref,
    gains_ref,
    om_ref,
    qm_ref,
    cosm_ref,
    sinm_ref,
    k_ref,
    v_ref,
    x_ref,
    cos_ref,
    sin_ref,
    wo_ref,
    w_ref,
    drm_ref,
    dha_ref,
    gw_ref,
    gain_ref,
    gw_acc,
    go_acc,
    gain_acc,
    flow_ref,
    gw_wide,
):
    step = pl.program_id(0)

    @pl.when(step == 0)
    def _():
        gw_acc[...] = jnp.zeros_like(gw_acc)
        go_acc[...] = jnp.zeros_like(go_acc)
        gain_acc[...] = jnp.zeros_like(gain_acc)

    window, width = k_ref.shape
    count = rm_ref.shape[0]
    r = rm_ref[...]
    sf = rms_scale(r)
    nf = r * sf
    dhf = dhf_ref[...].astype(f32)
    dnf = dhf * gains_ref[1:2, :]
    dr = cot_ref[...].astype(f32) + sf * (
        dnf - nf * jnp.mean(dnf * nf, axis=-1, keepdims=True)
    )
    drm_ref[...] = dr
    gain_acc[1:2, :] += jnp.sum(dhf * nf, axis=0, keepdims=True)
    drb = dr.astype(bf16)
    go_acc[...] += mm_tn(om_ref[...], drb)
    dob = mm_nt(drb, wo_ref[...]).astype(bf16)

    first = lax.broadcasted_iota(jnp.int32, (count, 128), 1) < HD
    zero = jnp.zeros((), bf16)
    drq = []
    for pair in range(width // 128):
        lanes = slice(pair * 128, pair * 128 + 128)
        k, v = k_ref[:, lanes], v_ref[:, lanes]
        qm, do = qm_ref[:, lanes], dob[:, lanes]
        parts = []
        drk = dv = None
        for head in range(2):
            mine = first if head == 0 else ~first
            q_head = jnp.where(mine, qm, zero)
            do_head = jnp.where(mine, do, zero)
            s = mm_nt(k, q_head)
            s = jnp.exp((s - jnp.max(s, axis=0, keepdims=True)) * score_scale)
            att = s / jnp.sum(s, axis=0, keepdims=True)
            dpa = mm_nt(v, do_head)
            ds = att * (dpa - jnp.sum(dpa * att, axis=0, keepdims=True))
            ds = (ds * score_scale).astype(bf16)
            parts.append(mm_tn(ds, k))
            drk_head = mm(ds, q_head)
            dv_head = mm(att.astype(bf16), do_head)
            drk = drk_head if drk is None else drk + drk_head
            dv = dv_head if dv is None else dv + dv_head
        drq.append(jnp.where(first, parts[0], parts[1]))
        dk = drk * cos_ref[:, lanes] - swap_halves(drk) * sin_ref[:, lanes]
        flow_ref[:, width + pair * 128 : width + pair * 128 + 128] = dk.astype(bf16)
        flow_ref[:, 2 * width + pair * 128 : 2 * width + pair * 128 + 128] = dv.astype(
            bf16
        )
    spread = (
        lax.broadcasted_iota(jnp.int32, (window, count), 0) == rows_ref[0]
    ).astype(bf16)
    for pair in range(width // 128):
        lanes = slice(pair * 128, pair * 128 + 128)
        dq = drq[pair] * cosm_ref[:, lanes] - swap_halves(drq[pair]) * sinm_ref[:, lanes]
        flow_ref[:, lanes] = mm(spread, dq.astype(bf16)).astype(bf16)

    flow = flow_ref[...]
    x = x_ref[...].astype(f32)
    na = x * rms_scale(x)
    dha = mm_nt(flow, w_ref[...])
    gain_acc[0:1, :] += jnp.sum(dha * na, axis=0, keepdims=True)
    cuts, shares, rows = dha_ref.shape[:3]
    for piece in range(window // rows):
        block = step * (window // rows) + piece
        dha_ref[block % cuts, block // cuts] = dha[piece * rows : (piece + 1) * rows].astype(bf16)
    gw_acc[...] += mm_tn((na * gains_ref[0:1, :]).astype(bf16), flow)

    @pl.when(step == pl.num_programs(0) - 1)
    def _():
        fold = gw_acc.shape[0] // width
        for block in range(3 * width // 128):
            part, lane = divmod(block * 128, width)
            gw_wide[block] = gw_acc[:, block * 128 : (block + 1) * 128]
            for piece in range(fold):
                at = piece * width + lane
                gw_ref[part * width : (part + 1) * width, at : at + 128] = gw_wide[
                    block, pl.ds(piece, width, stride=fold), :
                ].astype(bf16)
        gw_ref[3 * width :, :] = go_acc[...].astype(bf16)
        gain_ref[...] = gain_acc[...]


def input_grad_kernel(
    cut, place_ref, rows_ref, drm_ref, gains_ref, x_ref, part_ref, *refs
):
    out_ref = refs[-1]
    block, count = x_ref.shape[0], drm_ref.shape[0]
    base = (place_ref[0] * cut[1] + cut[0]) * block
    spread = (
        lax.broadcasted_iota(jnp.int32, (block, count), 0) + base == rows_ref[...]
    ).astype(bf16)
    dr = drm_ref[...]
    high = dr.astype(bf16)
    low = (dr - high.astype(f32)).astype(bf16)
    dr = mm(spread, high) + mm(spread, low)
    x = x_ref[...].astype(f32)
    sa = rms_scale(x)
    na = x * sa
    dha = part_ref[0, 0].astype(f32)
    for ref in refs[: cut[2]]:
        dha = dha + ref[...].astype(f32)
    dna = dha * gains_ref[0:1, :]
    out = dr + sa * (dna - na * jnp.mean(dna * na, axis=-1, keepdims=True))
    out_ref[...] = out.astype(bf16)


def input_grad_rows(dha, x, dr, gain, spread):
    high = dr.astype(bf16)
    low = (dr - high.astype(f32)).astype(bf16)
    dr = mm(spread, high) + mm(spread, low)
    sa = rms_scale(x)
    na = x * sa
    dna = dha * gain
    return dr + sa * (dna - na * jnp.mean(dna * na, axis=-1, keepdims=True))


def remote(src, dst, send, recv, place):
    return pltpu.make_async_remote_copy(
        src_ref=src,
        dst_ref=dst,
        send_sem=send,
        recv_sem=recv,
        device_id={"tensor": place},
        device_id_type=pl.DeviceIdType.MESH,
    )


def greet_line(place, others=()):
    barrier = pltpu.get_barrier_semaphore()
    for axis, other in others:
        pl.semaphore_signal(
            barrier,
            inc=1,
            device_id={axis: other},
            device_id_type=pl.DeviceIdType.MESH,
        )
    for k in range(1, 4):
        pl.semaphore_signal(
            barrier,
            inc=1,
            device_id={"tensor": lax.rem(place + k, 4)},
            device_id_type=pl.DeviceIdType.MESH,
        )
    pl.semaphore_wait(barrier, 3 + len(others))


def sends(place, d, up):
    if up:
        return (place >= d - 1) & (place <= 2)
    return (place <= 4 - d) & (place >= 1)


def receives(place, d, up):
    return place >= d if up else place <= 3 - d


def each_way(place, d, rule, act):
    for up in (True, False):

        @pl.when(rule(place, d, up))
        def _():
            act(up)


def rows_ref(ref, index, share, count):
    return ref.at[pl.ds(pl.multiple_of(index * share, share), count * share), :]


def weights_kernel(
    rank_ref,
    held_ref,
    master_ref,
    low_ref,
    out_ref,
    mine,
    got,
    work,
    trade,
    h_send,
    h_recv,
    t_send,
    t_recv,
    f_send,
    f_recv,
    f_keep,
):
    me = lax.axis_index("dp")
    core = lax.rem(me, 2)
    tiles = mine.shape[0]
    half = tiles // 2

    def pair(bit):
        return me + bit - 2 * bit * lax.rem(me // bit, 2)

    def to(src, dst, send, recv, bit):
        return pltpu.make_async_remote_copy(
            src_ref=src,
            dst_ref=dst,
            send_sem=send,
            recv_sem=recv,
            device_id={"dp": pair(bit)},
            device_id_type=pl.DeviceIdType.MESH,
        )

    def share(first):
        return pl.ds(first * half, half)

    swap = to(mine.at[share(1 - core)], got, h_send, h_recv, 1)

    def move(stage, t):
        bit = (2, 4)[(stage + t // (half // 2)) % 2]
        return to(
            work.at[stage, t],
            trade.at[stage, t],
            t_send.at[stage, t],
            t_recv.at[stage, t],
            bit,
        )

    def final(t):
        return to(work.at[2, t], out_ref.at[core * half + t], f_send.at[t], f_recv.at[t], 1)

    def final_in(t):
        at = out_ref.at[(1 - core) * half + t]
        return to(at, at, f_send.at[t], f_recv.at[t], 1)

    def keep(t):
        return pltpu.make_async_copy(
            work.at[2, t], out_ref.at[core * half + t], f_keep.at[t]
        )

    barrier = pltpu.get_barrier_semaphore()
    for bit in (1, 2, 4):
        pl.semaphore_signal(
            barrier, inc=1, device_id={"dp": pair(bit)}, device_id_type=pl.DeviceIdType.MESH
        )
    for t in range(tiles):
        tile = master_ref[rank_ref[t]].astype(bf16)
        mine[t] = jnp.where(held_ref[t] > 0, tile, jnp.zeros((), bf16))
    pl.semaphore_wait(barrier, 3)
    swap.start()
    for n in range(low_ref.shape[0]):
        low_ref[n] = master_ref[n].astype(bf16)
    swap.wait_recv()
    turns = [t + n for t in range(half // 2) for n in (0, half // 2)]
    for t in turns:
        work[0, t] = mine[core * half + t] + got[t]
        move(0, t).start()
    for stage in (1, 2):
        for t in turns:
            move(stage - 1, t).wait_recv()
            work[stage, t] = work[stage - 1, t] + trade[stage - 1, t]
            if stage == 1:
                move(1, t).start()
            else:
                final(t).start()
                keep(t).start()
    for t in range(half):
        final_in(t).wait_recv()
    swap.wait_send()
    for t in range(half):
        keep(t).wait()
        final(t).wait_send()
        for stage in range(2):
            move(stage, t).wait_send()


def attend_all_kernel(
    windows,
    rows_in,
    gains_ref,
    tiles_ref,
    cos_ref,
    sin_ref,
    x_hbm,
    tiles_hbm,
    om_out,
    oa_out,
    ob_out,
    oc_out,
    wo_out,
    qm_ref,
    xm_ref,
    cosm_ref,
    sinm_ref,
    k_ref,
    v_ref,
    w_ref,
    q_ref,
    w_wide,
    om_own,
    o_own,
    x_ref,
    x_sem,
    own_sem,
    keep_sem,
    m_send,
    m_recv,
    o_send,
    o_recv,
    w_send,
    w_recv,
    c_send,
    c_recv,
):
    place = lax.axis_index("tensor")
    window = x_ref.shape[1]
    width = q_ref.shape[1]
    count = rows_in.shape[1]
    q_block = 256

    def load_x(w):
        return pltpu.make_async_copy(
            x_hbm.at[pl.ds(w * window, window), :], x_ref.at[w % 2], x_sem.at[w % 2]
        )

    def hop(kind, d, up):
        own, out, send, recv = (
            (om_own, om_out, m_send, m_recv) if kind == 0 else (o_own.at[0], oa_out, o_send, o_recv)
        )
        src, dst = (d - 1, d) if up else ((5 - d) % 4, 4 - d)
        n = 0 if up else 1
        return remote(
            own if d == 1 else out.at[src],
            out.at[dst],
            send.at[d - 1, n],
            recv.at[d - 1, n],
            lax.rem(place + (1 if up else 3), 4),
        )

    me = lax.axis_index("dp")
    core = lax.rem(me, 2)
    half = width // 2

    def half_of(ref, first):
        return ref.at[pl.ds(pl.multiple_of(first + core * half, half), half), :]

    def hop_w(d, up):
        src, dst = (d - 1, d) if up else ((5 - d) % 4, 4 - d)
        n = 0 if up else 1
        return remote(
            half_of(tiles_hbm, 3 * width) if d == 1 else half_of(wo_out.at[src - 1], 0),
            half_of(wo_out.at[dst - 1], 0),
            w_send.at[d - 1, n],
            w_recv.at[d - 1, n],
            lax.rem(place + (1 if up else 3), 4),
        )

    sibling = me + 1 - 2 * core

    def copy_w(n):
        return pltpu.make_async_remote_copy(
            src_ref=half_of(wo_out.at[n], 0),
            dst_ref=half_of(wo_out.at[n], 0),
            send_sem=c_send.at[n],
            recv_sem=c_recv.at[n],
            device_id={"dp": sibling},
            device_id_type=pl.DeviceIdType.MESH,
        )

    def copy_w_in(n):
        rows = pl.ds(pl.multiple_of((1 - core) * half, half), half)
        return pltpu.make_async_remote_copy(
            src_ref=wo_out.at[n].at[rows, :],
            dst_ref=wo_out.at[n].at[rows, :],
            send_sem=c_send.at[n],
            recv_sem=c_recv.at[n],
            device_id={"dp": sibling},
            device_id_type=pl.DeviceIdType.MESH,
        )

    def any_hop(kind, d, up):
        return hop_w(d, up) if kind == 2 else hop(kind, d, up)

    def hops(kind, d):
        each_way(place, d, sends, lambda up: any_hop(kind, d, up).start())

    def hops_in(kind, d):
        each_way(place, d, receives, lambda up: any_hop(kind, d, up).wait_recv())

    def store(w):
        to = (oa_out.at[0], ob_out, oc_out)[w]
        return pltpu.make_async_copy(o_own.at[w], to, own_sem.at[w])

    def attend_rows(w, first, last):
        for pair in range(width // 128):
            lanes = slice(pair * 128, pair * 128 + 128)
            keys = slice(w * window, (w + 1) * window)

            def block(i, carry):
                rows = pl.ds(pl.multiple_of(w * window + i * q_block, q_block), q_block)
                into = pl.ds(pl.multiple_of(i * q_block, q_block), q_block)
                o_own[w, into, lanes] = attend(
                    q_ref[rows, lanes], k_ref[keys, lanes], v_ref[keys, lanes]
                )
                return carry

            lax.fori_loop(first, last, block, 0)

    def picked(pick, table):
        high = table.astype(bf16)
        low = (table - high.astype(f32)).astype(bf16)
        return mm(pick, high) + mm(pick, low)

    def project(w):
        rows = window // 2

        def block(n, carry):
            here = pl.ds(pl.multiple_of(n * rows, rows), rows)
            at = pl.ds(pl.multiple_of(w * window + n * rows, rows), rows)
            x = x_ref[w % 2, here, :].astype(f32)
            hidden = (x * rms_scale(x) * gains_ref[0:1, :]).astype(bf16)
            cos, sin = cos_ref[here, :], sin_ref[here, :]
            q = mm(hidden, w_ref[:, 0:width])
            q_ref[at, :] = (q * cos + swap_halves(q) * sin).astype(bf16)
            k = mm(hidden, w_ref[:, width : 2 * width])
            k_ref[at, :] = (k * cos + swap_halves(k) * sin).astype(bf16)
            v_ref[at, :] = mm(hidden, w_ref[:, 2 * width : 3 * width]).astype(bf16)
            return carry

        load_x(w).wait()
        lax.fori_loop(0, 2, block, 0)
        at = slice(w * count, (w + 1) * count)
        pick = (
            lax.broadcasted_iota(jnp.int32, (count, window), 1) == rows_in[w]
        ).astype(bf16)
        xm_ref[at, :] = mm(pick, x_ref[w % 2]).astype(bf16)
        if w + 2 < windows:
            load_x(w + 2).start()
        cosm_ref[at, :] = picked(pick, cos_ref[...])
        sinm_ref[at, :] = picked(pick, sin_ref[...])
        qm_ref[at, :] = mm(pick, q_ref[w * window : (w + 1) * window, :]).astype(bf16)

    for w in range(2):
        load_x(w).start()
    greet_line(place, [("dp", sibling)])
    blocks = window // q_block
    hops(2, 1)
    fold = tiles_ref.shape[1] // width
    for block in range(3 * width // 128):
        part, lane = divmod(block * 128, width)
        for piece in range(fold):
            at = piece * width + lane
            w_wide[block, pl.ds(piece, width, stride=fold), :] = tiles_ref[
                part * width : (part + 1) * width, at : at + 128
            ].astype(f32)
        w_ref[:, block * 128 : (block + 1) * 128] = w_wide[block].astype(bf16)
    project(0)
    hops_in(2, 1)
    hops(2, 2)
    attend_rows(0, 0, blocks)
    hops(1, 1)
    store(0).start()
    hops_in(2, 2)
    hops(2, 3)
    project(1)
    project(2)
    hops_in(1, 1)
    hops(1, 2)
    for w in range(windows):
        keys = slice(w * window, (w + 1) * window)
        at = slice(w * count, (w + 1) * count)
        for pair in range(width // 128):
            lanes = slice(pair * 128, pair * 128 + 128)
            om_own[at, lanes] = attend(
                qm_ref[at, lanes], k_ref[keys, lanes], v_ref[keys, lanes]
            )
    hops(0, 1)
    keep = pltpu.make_async_copy(om_own, om_out.at[0], keep_sem)
    keep.start()
    attend_rows(1, 0, blocks // 2)
    hops_in(0, 1)
    hops(0, 2)
    attend_rows(1, blocks // 2, blocks)
    store(1).start()
    hops_in(0, 2)
    hops(0, 3)
    hops_in(1, 2)
    hops(1, 3)
    attend_rows(2, 0, blocks)
    store(2).start()
    hops_in(2, 3)
    for n in range(3):
        copy_w(n).start()
    keep.wait()
    for w in range(windows):
        store(w).wait()
    for kind in range(2):
        hops_in(kind, 3)
    for kind in range(3):
        for d in range(1, 4):
            each_way(place, d, sends, lambda up: any_hop(kind, d, up).wait_send())
    for n in range(3):
        copy_w(n).wait_send()
        copy_w_in(n).wait_recv()


def masked_attention_back(qm, do, k, v):
    first = lax.broadcasted_iota(jnp.int32, qm.shape, 1) < HD
    zero = jnp.zeros((), bf16)
    parts = []
    drk = dv = None
    for head in range(2):
        mine = first if head == 0 else ~first
        q_head = jnp.where(mine, qm, zero)
        do_head = jnp.where(mine, do, zero)
        s = mm_nt(k, q_head)
        s = jnp.exp((s - jnp.max(s, axis=0, keepdims=True)) * score_scale)
        att = s / jnp.sum(s, axis=0, keepdims=True)
        dpa = mm_nt(v, do_head)
        ds = att * (dpa - jnp.sum(dpa * att, axis=0, keepdims=True))
        ds = (ds * score_scale).astype(bf16)
        parts.append(mm_tn(ds, k))
        drk_head = mm(ds, q_head)
        dv_head = mm(att.astype(bf16), do_head)
        drk = drk_head if drk is None else drk + drk_head
        dv = dv_head if dv is None else dv + dv_head
    return jnp.where(first, parts[0], parts[1]), drk, dv


def middle_kernel(
    windows,
    rows_in,
    gains_ref,
    xm_ref,
    cot_ref,
    qm_ref,
    cosm_ref,
    sinm_ref,
    cos_ref,
    sin_ref,
    w_ref,
    ffn_ref,
    om_ref,
    oa_ref,
    wo_ref,
    wo_far,
    *refs,
):
    wg_ref, wu_ref, wd_ref = (ffn_ref.at[n] for n in range(3))
    om_refs, oa_refs = ([ref.at[n] for n in range(4)] for ref in (om_ref, oa_ref))
    wo_refs = [wo_ref] + [wo_far.at[n] for n in range(3)]
    x_hbm, k_hbm, v_hbm, o_one, o_two = refs[0:5]
    part_out, own_out, ra_out, rb_out, dha_out, grads_out, drm_ref, gain_ref = refs[5:13]
    (
        r_ref,
        hf_ref,
        acc_ref,
        p_ref,
        own_ref,
        obuf,
        x_ref,
        kv,
        flow_ref,
        gw_acc,
        gw_wide,
        go_acc,
        rm_ref,
        dpart,
        drecv,
        dall,
        bsum,
        b_load,
        b_send,
        b_recv,
        o_load,
        x_sem,
        kv_sem,
        grad_sem,
        p_sem,
        dha_sem,
        own_sem,
        a_send,
        a_recv,
        o_send,
        o_recv,
        d_send,
        d_recv,
        e_send,
        e_recv,
    ) = refs[13:]
    place = lax.axis_index("tensor")
    lower = place < 2
    outer = (place == 0) | (place == 3)
    inner = (place == 1) | (place == 2)
    window, model = x_ref.shape
    width = kv.shape[3]
    hidden = ffn_ref.shape[2]
    share = own_ref.shape[0]
    count = rm_ref.shape[0] // windows
    masked = rm_ref.shape[0]
    cols = 256
    chunks = hidden // cols

    def hop(g, d, up):
        src, dst = (d - 1, d) if up else ((5 - d) % 4, 4 - d)
        n = 0 if up else 1
        return remote(
            obuf.at[g, src],
            obuf.at[g, dst],
            o_send.at[g, d - 1, n],
            o_recv.at[g, d - 1, n],
            lax.rem(place + (1 if up else 3), 4),
        )

    def hops(g, d):
        each_way(place, d, sends, lambda up: hop(g, d, up).start())

    def hops_in(g, d):
        each_way(place, d, receives, lambda up: hop(g, d, up).wait_recv())

    def load_o(g):
        return pltpu.make_async_copy((o_one, o_two)[g], obuf.at[g, 0], o_load.at[g])

    def load_x(w):
        return pltpu.make_async_copy(
            x_hbm.at[pl.ds(w * window, window), :], x_ref, x_sem
        )

    def load_kv(w):
        return [
            pltpu.make_async_copy(
                hbm.at[pl.ds(w * window, window), :], kv.at[w % 2, n], kv_sem.at[w % 2, n]
            )
            for n, hbm in enumerate((k_hbm, v_hbm))
        ]

    def store_p(to):
        return pltpu.make_async_copy(p_ref, to, p_sem)

    def store_own(w):
        return pltpu.make_async_copy(own_ref, own_out.at[w], own_sem)

    def copy_a(w, i):
        return remote(
            rows_ref(part_out.at[w], jnp.where(lower, 3 - i, i), share, 1),
            rows_ref(ra_out.at[w], jnp.where(lower, 2 - i, i), share, 1),
            a_send.at[w, i],
            a_recv.at[w, i],
            jnp.where(lower, 1, 2),
        )

    def copy_d(k):
        to = lax.rem(place + k, 4)
        return remote(dpart.at[to], drecv.at[k - 1], d_send.at[k - 1], d_recv.at[k - 1], to)

    def copy_e(k, origin):
        to = lax.rem(place + k, 4)
        return remote(dall.at[origin], dall.at[origin], e_send.at[k - 1], e_recv.at[k - 1], to)

    for g in range(2):
        load_o(g).start()
    load_x(0).start()
    for copy in load_kv(0):
        copy.start()
    greet_line(place)
    load_o(0).wait()
    hops(0, 1)
    gain_att, gain_ffn = gains_ref[0:1, :], gains_ref[1:2, :]

    def grad_copies(c):
        side = (c % 2) * 2 * cols
        base = 4 * width
        at = pl.ds(c * cols, cols)
        below = window - 2 * cols + (c % 2) * cols
        return [
            pltpu.make_async_copy(
                p_ref.at[:, pl.ds(side, cols)],
                grads_out.at[pl.ds(base, model), at],
                grad_sem.at[c % 2, 0],
            ),
            pltpu.make_async_copy(
                p_ref.at[:, pl.ds(side + cols, cols)],
                grads_out.at[pl.ds(base + hidden, model), at],
                grad_sem.at[c % 2, 1],
            ),
            pltpu.make_async_copy(
                hf_ref.at[pl.ds(below, cols), :],
                grads_out.at[pl.ds(base + 2 * hidden + c * cols, cols), :],
                grad_sem.at[c % 2, 2],
            ),
        ]

    def masked_chunk(c):
        if c >= 2:
            for copy in grad_copies(c - 2):
                copy.wait()
        at = slice(c * cols, (c + 1) * cols)
        side = (c % 2) * 2 * cols
        below = window - 2 * cols + (c % 2) * cols
        hf, dy = hf_ref[0:masked, :], cot_ref[...]
        wg, wu, wd = wg_ref[:, at], wu_ref[:, at], wd_ref[at, :]
        g, u = mm(hf, wg), mm(hf, wu)
        sig = jax.nn.sigmoid(g)
        act = (g * sig * u).astype(bf16)
        hf_ref[below : below + cols, :] = mm_tn(act, dy).astype(bf16)
        da = mm_nt(dy, wd)
        dg = (da * u * sig * (1.0 + g * (1.0 - sig))).astype(bf16)
        du = (da * g * sig).astype(bf16)
        p_ref[:, side : side + cols] = mm_tn(hf, dg).astype(bf16)
        p_ref[:, side + cols : side + 2 * cols] = mm_tn(hf, du).astype(bf16)
        part = mm_nt(dg, wg) + mm_nt(du, wu)
        if c == 0:
            acc_ref[0:masked, :] = part
        else:
            acc_ref[0:masked, :] += part
        for copy in grad_copies(c):
            copy.start()

    def ffn(w, o_refs, next_x, between=None):
        half = window // 2

        def first(n, carry):
            rows = pl.ds(pl.multiple_of(n * half, half), half)
            r = x_ref[rows, :].astype(f32)
            for o, wo in zip(o_refs, wo_refs):
                r = r + mm(o[rows, :], wo[...])
            r_ref[rows, :] = r
            hf_ref[rows, :] = (r * rms_scale(r) * gain_ffn).astype(bf16)
            return carry

        lax.fori_loop(0, 2, first, 0)
        if next_x is not None:
            load_x(next_x).start()
        acc_ref[...] = jnp.zeros_like(acc_ref)

        def chunk(c, carry):
            at = pl.ds(pl.multiple_of(c * cols, cols), cols)
            hf = hf_ref[...]
            g, u = mm(hf, wg_ref[:, at]), mm(hf, wu_ref[:, at])
            act = (g * jax.nn.sigmoid(g) * u).astype(bf16)
            acc_ref[...] += mm(act, wd_ref[at, :])
            return carry

        if between is None:
            lax.fori_loop(0, chunks, chunk, 0)
        else:
            lax.fori_loop(0, chunks - 1, chunk, 0)
            between()
            lax.fori_loop(chunks - 1, chunks, chunk, 0)
        p_ref[...] = acc_ref[...].astype(bf16)
        store_p(part_out.at[w]).start()
        mine = pl.ds(pl.multiple_of(place * share, share), share)
        own_ref[...] = r_ref[mine, :] + acc_ref[mine, :]
        store_own(w).start()
        store_p(part_out.at[w]).wait()
        store_own(w).wait()

    def inward(w, blocks):
        @pl.when(outer)
        def _():
            for i in blocks:
                copy_a(w, i).start()

    def sum_dhf():
        for k in range(1, 4):
            copy_d(k).wait_recv()
        total = dpart[place].astype(f32)
        for k in range(3):
            total = total + drecv[k].astype(f32)
        dall[place] = total.astype(bf16)
        for k in range(1, 4):
            copy_e(k, place).start()

    r = xm_ref[...].astype(f32)
    for om, wo in zip(om_refs, wo_refs):
        r = r + mm(om[...], wo[...])
    rm_ref[...] = r
    hf_ref[0:masked, :] = (r * rms_scale(r) * gain_ffn).astype(bf16)
    for c in range(chunks // 2):
        masked_chunk(c)
    hops_in(0, 1)
    hops(0, 2)
    for c in range(chunks // 2, chunks):
        masked_chunk(c)
    block = model // 4
    for n in range(4):
        dpart[n] = acc_ref[0:masked, n * block : (n + 1) * block].astype(bf16)
    for k in range(1, 4):
        copy_d(k).start()
    hops_in(0, 2)
    hops(0, 3)
    for c in range(chunks - 2, chunks):
        for copy in grad_copies(c):
            copy.wait()

    load_o(1).wait()
    load_x(0).wait()
    ffn(0, oa_refs, 1)
    inward(0, (0,))
    hops_in(0, 3)
    hops(1, 1)
    load_x(1).wait()

    def meanwhile():
        sum_dhf()
        inward(0, (1, 2))

    ffn(1, [obuf.at[0, n] for n in range(4)], 0, meanwhile)
    inward(1, (0, 1, 2))
    hops_in(1, 1)
    hops(1, 2)
    hops_in(1, 2)
    hops(1, 3)

    def copy_b(w):
        return remote(
            bsum.at[w], rb_out.at[w], b_send.at[w], b_recv.at[w], jnp.where(lower, 2, 1)
        )

    def exchange_rows(w):
        @pl.when(inner)
        def _():
            for i in range(3):
                copy_a(w, i).wait_recv()
            rows = rows_ref(ra_out.at[w], jnp.where(lower, 1, 0), share, 2)
            mine = rows_ref(part_out.at[w], jnp.where(lower, 2, 0), share, 2)
            got = pltpu.make_async_copy(rows, bsum.at[w], b_load.at[0])
            add = pltpu.make_async_copy(mine, hf_ref.at[pl.ds(0, 2 * share), :], b_load.at[1])
            got.start()
            add.start()
            got.wait()
            add.wait()
            total = bsum[w].astype(f32) + hf_ref[0 : 2 * share, :].astype(f32)
            bsum[w] = total.astype(bf16)
            copy_b(w).start()

    for k in range(1, 4):
        copy_e(k, lax.rem(place + 4 - k, 4)).wait_recv()
    gw_acc[...] = jnp.zeros_like(gw_acc)
    go_acc[...] = jnp.zeros_like(go_acc)
    gain_ref[...] = jnp.zeros_like(gain_ref)
    def back_window(w, next_x):
        for copy in load_kv(w):
            copy.wait()
        if w + 1 < windows:
            for copy in load_kv(w + 1):
                copy.start()
        at = slice(w * count, (w + 1) * count)
        r = rm_ref[at, :]
        sf = rms_scale(r)
        nf = r * sf
        dhf = jnp.concatenate([dall[n, at, :] for n in range(4)], axis=1).astype(f32)
        dnf = dhf * gain_ffn
        dr = cot_ref[at, :].astype(f32) + sf * (
            dnf - nf * jnp.mean(dnf * nf, axis=-1, keepdims=True)
        )
        drm_ref[at, :] = dr
        gain_ref[1:2, :] += jnp.sum(dhf * nf, axis=0, keepdims=True)
        drb = dr.astype(bf16)
        go_acc[...] += mm_tn(om_refs[0][at, :], drb)
        dob = mm_nt(drb, wo_refs[0][...]).astype(bf16)
        spread = (
            lax.broadcasted_iota(jnp.int32, (window, count), 0) == rows_in[w]
        ).astype(bf16)
        for pair in range(width // 128):
            lanes = slice(pair * 128, pair * 128 + 128)
            drq, drk, dv = masked_attention_back(
                qm_ref[at, lanes], dob[:, lanes], kv[w % 2, 0, :, lanes], kv[w % 2, 1, :, lanes]
            )
            dk = drk * cos_ref[:, lanes] - swap_halves(drk) * sin_ref[:, lanes]
            dq = drq * cosm_ref[at, lanes] - swap_halves(drq) * sinm_ref[at, lanes]
            first = pair * 128
            flow_ref[:, first : first + 128] = mm(spread, dq.astype(bf16)).astype(bf16)
            flow_ref[:, width + first : width + first + 128] = dk.astype(bf16)
            flow_ref[:, 2 * width + first : 2 * width + first + 128] = dv.astype(bf16)
        load_x(w).wait()

        def back(n, carry):
            rows = pl.ds(pl.multiple_of(n * share, share), share)
            x = x_ref[rows, :].astype(f32)
            na = x * rms_scale(x)
            dha = mm_nt(flow_ref[rows, :], w_ref[...])
            gain_ref[0:1, :] += jnp.sum(dha * na, axis=0, keepdims=True)
            p_ref[rows, :] = dha.astype(bf16)
            hf_ref[rows, :] = (na * gain_att).astype(bf16)
            return carry

        lax.fori_loop(0, window // share, back, 0)
        for copy in dha_copies(dha_out, p_ref, dha_sem, w, windows, share):
            copy.start()
        if next_x is not None:
            load_x(next_x).start()
        gw_acc[...] += mm_tn(hf_ref[...], flow_ref[...])

    def dha_stored(w):
        for copy in dha_copies(dha_out, p_ref, dha_sem, w, windows, share):
            copy.wait()

    back_window(0, 1)
    dha_stored(0)
    back_window(1, 2)
    dha_stored(1)
    exchange_rows(0)
    back_window(2, None)
    dha_stored(2)
    hops_in(1, 3)
    ffn(2, [obuf.at[1, n] for n in range(4)], None)
    fold = model // width
    for block in range(3 * width // 128):
        part, lane = divmod(block * 128, width)
        gw_wide[...] = gw_acc[:, block * 128 : (block + 1) * 128]
        for piece in range(fold):
            at = piece * width + lane
            p_ref[part * width : (part + 1) * width, at : at + 128] = gw_wide[
                pl.ds(piece, width, stride=fold), :
            ].astype(bf16)
    p_ref[3 * width :, :] = go_acc[...].astype(bf16)
    store = store_p(grads_out.at[pl.ds(0, 4 * width), :])
    store.start()
    store.wait()

    @pl.when(outer)
    def _():
        for w in range(2):
            for i in range(3):
                copy_a(w, i).wait_send()

    @pl.when(inner)
    def _():
        for i in range(3):
            copy_a(1, i).wait_recv()
        copy_b(0).wait_send()
        copy_b(0).wait_recv()

    for k in range(1, 4):
        copy_d(k).wait_send()
        copy_e(k, place).wait_send()
    for g in range(2):
        for d in range(1, 4):
            each_way(place, d, sends, lambda up: hop(g, d, up).wait_send())


def dha_copies(dha_out, p_ref, sem, w, windows, share):
    copies = []
    per = p_ref.shape[0] // share
    for n in range(per):
        block = w * per + n
        copies.append(
            pltpu.make_async_copy(
                p_ref.at[pl.ds(n * share, share), :],
                dha_out.at[block % windows, pl.ds(block // windows * share, share), :],
                sem.at[n],
            )
        )
    return copies


def lines_kernel(
    cuts,
    windows,
    order,
    ready,
    traded,
    rows_in,
    drm_ref,
    gains_ref,
    x_ref,
    dha_ref,
    part_ref,
    own_in,
    ra_in,
    rb_in,
    gain_in,
    out_ref,
    grad_ref,
    gain_ref,
    ra,
    rb,
    rc,
    value,
    own,
    piece,
    x_rows,
    grad,
    gain_sum,
    gain_got,
    s_send,
    s_recv,
    a_send,
    a_recv,
    b_send,
    b_recv,
    c_send,
    c_recv,
    g_send,
    g_recv,
    v_sem,
    o_sem,
    r_sem,
    t_sem,
    x_sem,
    l_sem,
    i_sem,
):
    place = lax.axis_index("tensor")
    lower = place < 2
    outer = (place == 0) | (place == 3)
    inner = (place == 1) | (place == 2)
    share = rc.shape[1]
    folds = len(order)
    next_in = jnp.where(lower, 1, 2)
    inner_far = 3 - place
    outer_near = jnp.where(lower, 0, 3)
    outer_far = 3 - outer_near

    def block(ref, index):
        return rows_ref(ref, index, share, 1)

    def whole(f):
        kind, index = order[f]
        return part_ref.at[index] if kind == 0 else dha_ref.at[index]

    def copy_a(f, i):
        return remote(
            block(whole(f), jnp.where(lower, 3 - i, i)),
            block(ra.at[f], jnp.where(lower, 2 - i, i)),
            a_send.at[f, i],
            a_recv.at[f, i],
            next_in,
        )

    def copy_b(f, i):
        return remote(
            block(ra.at[f], jnp.where(lower, 2 - i, i)),
            block(rb.at[f], jnp.where(lower, 1 - i, i)),
            b_send.at[f, i],
            b_recv.at[f, i],
            jnp.where(lower, 2, 1),
        )

    def copy_c(f):
        src = block(rb.at[f], jnp.where(lower, 0, 1))
        return remote(src, rc.at[f], c_send.at[f], c_recv.at[f], outer_near)

    def load(f):
        return pltpu.make_async_copy(whole(f), value.at[f], v_sem.at[f])

    def load_own(w):
        return pltpu.make_async_copy(own_in.at[w], own.at[w], o_sem.at[w])

    def load_ra(f):
        return pltpu.make_async_copy(ra_in.at[order[f][1]], ra.at[f], r_sem.at[f])

    def load_rb(f):
        return pltpu.make_async_copy(rb_in.at[order[f][1]], rb.at[f], t_sem.at[f])

    def rows_of(w, origin):
        return pl.ds(pl.multiple_of((w * 4 + origin) * share, share), share)

    def pass_on(w, origin, way, n, target):
        rows = rows_of(w, origin)
        return remote(
            piece.at[w] if way < 2 else out_ref.at[rows, :],
            out_ref.at[rows, :],
            g_send.at[w, way],
            g_recv.at[w, n],
            target,
        )

    def got(w, n):
        origin = (
            jnp.where(outer, next_in, inner_far),
            jnp.where(outer, 3 - next_in, outer_near),
            jnp.where(outer, 3 - place, outer_far),
        )[n]
        rows = rows_of(w, origin)
        return remote(
            out_ref.at[rows, :], out_ref.at[rows, :], g_send.at[w, 0], g_recv.at[w, n], inner_far
        )

    def keep(w):
        return pltpu.make_async_copy(
            piece.at[w], out_ref.at[rows_of(w, place), :], l_sem.at[w]
        )

    def store(c):
        return pltpu.make_async_copy(
            grad.at[c], grad_ref.at[pl.ds(c * share, share), :], i_sem.at[c]
        )

    x_load = pltpu.make_async_copy(
        rows_ref(x_ref, place * cuts, share, cuts), x_rows, x_sem
    )

    for w in range(windows):
        load(w).start()
        load_own(w).start()
    for f in range(windows, folds):
        load(f).start()
    x_load.start()

    pairs = []
    for axis in ("dp", "tensor"):
        index, bit = lax.axis_index(axis), 1
        while bit < lax.axis_size(axis):
            pairs.append((axis, index + bit - 2 * bit * lax.rem(index // bit, 2)))
            bit *= 2

    def copy_s(t):
        axis, other = pairs[t]
        return pltpu.make_async_remote_copy(
            src_ref=gain_sum.at[t],
            dst_ref=gain_got.at[t],
            send_sem=s_send.at[t],
            recv_sem=s_recv.at[t],
            device_id={axis: other},
            device_id_type=pl.DeviceIdType.MESH,
        )

    def next_pair(t):
        if t > 0:
            copy_s(t - 1).wait_recv()
            gain_sum[t] = gain_sum[t - 1] + gain_got[t - 1]
        if t < len(pairs):
            copy_s(t).start()

    gain_sum[0] = jnp.zeros(gain_sum.shape[1:], f32)
    gain_sum[0, 0:2, :] = gain_in[...]

    def rows_at_(index):
        return pl.ds(pl.multiple_of(index * share, share), share)

    def finish(f, terms):
        kind, index = order[f]
        if kind == 0:
            load_own(index).wait()
            total = own[index]
        else:
            total = value[f, rows_at_(place), :].astype(f32)
        for term in terms:
            total = total + term.astype(f32)
        if kind == 0:
            piece[index] = total.astype(bf16)
            keep(index).start()
        else:
            first = place * (cuts * share) + index * share
            count = drm_ref.shape[0]
            spread = (
                lax.broadcasted_iota(jnp.int32, (share, count), 0) + first == rows_in[...]
            ).astype(bf16)
            x = x_rows[pl.ds(index * share, share), :].astype(f32)
            grad[index] = input_grad_rows(
                total, x, drm_ref[...], gains_ref[0:1, :], spread
            ).astype(bf16)
            store(index).start()

    greet_line(place, [pair for pair in pairs if pair[0] == "dp"])

    @pl.when(outer)
    def _():
        chunks = [(f, i) for f in range(ready, folds) for i in range(3)]

        def step(n):
            copy_a(*chunks[n]).wait_send()
            if n + 2 < len(chunks):
                copy_a(*chunks[n + 2]).start()

        def total(f):
            copy_c(f).wait_recv()
            if order[f][0] == 1:
                load(f).wait()
            finish(f, [rc[f]])
            if order[f][0] == 0:
                pass_on(f, place, 0, 1, next_in).start()

        for n in range(2):
            copy_a(*chunks[n]).start()
        next_pair(0)
        total(0)
        step(0)
        step(1)
        next_pair(1)
        total(1)
        step(2)
        step(3)
        step(4)
        next_pair(2)
        total(2)
        next_pair(3)
        step(5)
        step(6)
        x_load.wait()
        total(3)
        next_pair(4)
        for n in range(7, 12):
            step(n)
        total(4)
        next_pair(5)
        total(5)
        for w in range(windows):
            load(w).wait()
            pass_on(w, place, 0, 1, next_in).wait_send()
            for n in range(3):
                got(w, n).wait_recv()

    @pl.when(inner)
    def _():
        for f in range(ready):
            load_ra(f).start()
        for f in range(traded):
            load_rb(f).start()

        def give_b(f):
            load(f).wait()
            if f < ready:
                load_ra(f).wait()
            for i in range(2):
                if f >= ready:
                    copy_a(f, i).wait_recv()
                to = rows_at_(jnp.where(lower, 2 - i, i))
                mine = value[f, rows_at_(jnp.where(lower, 3 - i, i)), :]
                ra[f, to, :] = (ra[f, to, :].astype(f32) + mine.astype(f32)).astype(bf16)
                copy_b(f, i).start()

        def total(f):
            if f < traded:
                load(f).wait()
                load_ra(f).wait()
                load_rb(f).wait()
            else:
                came(f, 0)
            to = rows_at_(jnp.where(lower, 0, 1))
            mine = value[f, rows_at_(outer_near), :]
            rb[f, to, :] = (rb[f, to, :].astype(f32) + mine.astype(f32)).astype(bf16)
            copy_c(f).start()
            if f >= traded:
                came(f, 1)
            if f >= ready:
                copy_a(f, 2).wait_recv()
            near = rows_at_(jnp.where(lower, 0, 2))
            other = rows_at_(jnp.where(lower, 1, 0))
            finish(f, [ra[f, near, :], rb[f, other, :]])
            if order[f][0] == 0:
                pass_on(f, place, 0, 0, inner_far).start()
                pass_on(f, place, 1, 0, outer_near).start()

        def came(f, i):
            to = block(rb.at[f], jnp.where(lower, i, 1 - i))
            remote(to, to, b_send.at[f, i], b_recv.at[f, i], inner_far).wait_recv()

        def from_far_inner(w):
            got(w, 0).wait_recv()
            pass_on(w, inner_far, 2, 1, outer_near).start()

        def from_outer(w):
            got(w, 1).wait_recv()
            pass_on(w, outer_near, 3, 2, inner_far).start()

        def from_far_outer(w):
            got(w, 2).wait_recv()
            pass_on(w, outer_far, 4, 2, outer_near).start()

        next_pair(0)
        total(0)
        give_b(1)
        next_pair(1)
        from_far_inner(0)
        total(1)
        next_pair(2)
        give_b(2)
        from_outer(0)
        from_far_inner(1)
        total(2)
        next_pair(3)
        from_far_outer(0)
        from_outer(1)
        give_b(3)
        from_far_inner(2)
        from_far_outer(1)
        x_load.wait()
        total(3)
        next_pair(4)
        from_outer(2)
        give_b(4)
        from_far_outer(2)
        total(4)
        give_b(5)
        total(5)
        next_pair(5)
        for f in range(folds):
            copy_c(f).wait_send()
            for i in range(2):
                if f >= traded:
                    copy_b(f, i).wait_send()
        for w in range(windows):
            pass_on(w, place, 0, 0, inner_far).wait_send()
            pass_on(w, place, 1, 0, outer_near).wait_send()
            pass_on(w, inner_far, 2, 1, outer_near).wait_send()
            pass_on(w, outer_near, 3, 2, inner_far).wait_send()
            pass_on(w, outer_far, 4, 2, outer_near).wait_send()

    gain_ref[...] = gain_sum[len(pairs), 0:2, :]
    for t in range(len(pairs)):
        copy_s(t).wait_send()
    for w in range(windows):
        keep(w).wait()
    for c in range(cuts):
        store(c).wait()


def place_kernel(place_ref, *refs):
    out_ref = refs[-1]
    parts = lax.axis_size("tensor")
    share = refs[0].shape[0]
    for step in range(parts):
        origin = lax.rem(place_ref[0] + parts - step, parts)
        out_ref[pl.ds(pl.multiple_of(origin * share, share), share), :] = refs[step][...]


def spread_kernel(tile_ref, used_ref, *refs):
    out_ref = refs[-1]
    step = pl.program_id(0)
    per = len(refs) - 1
    for n in range(per):
        used = used_ref[step * per + n] > 0

        @pl.when(used)
        def _():
            out_ref[n] = refs[n][0]

        @pl.when(jnp.logical_not(used))
        def _():
            out_ref[n] = jnp.zeros(out_ref.shape[1:], bf16)


def copy_kernel(in_ref, out_ref):
    out_ref[...] = in_ref[...]


def collect_kernel(slot_ref, *refs):
    out_ref = refs[-1]
    for index, ref in enumerate(refs[:-1]):
        out_ref[index] = ref[0]


def exchange(value, axis, bit):
    size = lax.axis_size(axis)
    return lax.ppermute(value, axis, [(i, i ^ bit) for i in range(size)])


def dp_total(value):
    size = lax.axis_size("dp")
    value = value + exchange(value, "dp", 1)
    bits = []
    bit = 2
    while bit < size:
        bits.append(bit)
        bit *= 2
    core = lax.axis_index("dp") % 2
    half = value.shape[0] // 2
    mine = lax.dynamic_slice_in_dim(value, core * half, half, 0)
    cut = half // 2
    low, high = mine[:cut], mine[cut:]
    for bit_low, bit_high in zip(bits, bits[::-1]):
        low = low + exchange(low, "dp", bit_low)
        high = high + exchange(high, "dp", bit_high)
    mine = jnp.concatenate([low, high], axis=0)
    other = exchange(mine, "dp", 1)
    return jnp.where(
        core == 0,
        jnp.concatenate([mine, other], axis=0),
        jnp.concatenate([other, mine], axis=0),
    )


def around(value):
    size = lax.axis_size("tensor")
    return [value] + [
        lax.ppermute(value, "tensor", [(i, (i + k) % size) for i in range(size)])
        for k in range(1, size)
    ]


def rows_at(value, index, share, count):
    return lax.dynamic_slice_in_dim(value, index * share, count * share, 0)


def other_sums(value, share):
    place = lax.axis_index("tensor")
    total = lax.psum_scatter(value, "tensor", scatter_dimension=0, tiled=True)
    own = rows_at(value, place, share, 1).astype(f32)
    return (total.astype(f32) - own,)


def small_total(value):
    for axis in ("dp", "tensor"):
        bit = 1
        while bit < lax.axis_size(axis):
            value = value + exchange(value, axis, bit)
            bit *= 2
    return value


def slot_ranks(owner_row):
    count_all = owner_row.shape[0]
    tile_order = jnp.arange(count_all, dtype=jnp.int32)
    earlier = (owner_row[:, None] == owner_row[None, :]) & (
        tile_order[None, :] < tile_order[:, None]
    )
    return jnp.sum(earlier.astype(jnp.int32), axis=1)


def adam_update(grad_now, first_old, second_old, param_old, rate, decay):
    first_new = beta_one * first_old + (1.0 - beta_one) * grad_now
    second_new = beta_two * second_old + (1.0 - beta_two) * grad_now * grad_now
    first_hat = first_new / (1.0 - beta_one**STEP)
    second_hat = second_new / (1.0 - beta_two**STEP)
    param_new = param_old - rate * (
        first_hat / (jnp.sqrt(second_hat) + adam_eps) + decay * param_old
    )
    return (first_new, second_new, param_new)


def head_tables(positions, heads, lib):
    frequency = lib.exp(
        -lib.log(lib.float32(10000.0))
        * (2.0 * lib.arange(HD // 2, dtype=lib.float32) / HD).astype(lib.float32)
    )
    angles = positions.astype(lib.float32)[..., None] * frequency
    cos, sin = lib.cos(angles), lib.sin(angles)
    cos = lib.concatenate([cos, cos], axis=-1)
    sin = lib.concatenate([-sin, sin], axis=-1)
    reps = (1,) * (cos.ndim - 1) + (heads,)
    return lib.tile(cos, reps), lib.tile(sin, reps)


def on_device(
    tokens,
    masked_rows,
    cotangent,
    norm_gains,
    gain_first,
    gain_second,
    owners,
    master,
    first_moment,
    second_moment,
):
    seq_count, mask_count = masked_rows.shape
    total_rows, model = tokens.shape
    window = total_rows // seq_count
    parts = lax.axis_size("tensor")
    place = lax.axis_index("tensor")
    owner_self = lax.axis_index("dp")
    heads = HEADS // parts
    width = heads * HD
    hidden = FF // parts
    capacity, tile_rows = master.shape[1:3]
    tile_size = tile_rows * model
    attn_tiles = 4 * model * width // tile_size
    ffn_tiles = 3 * model * hidden // tile_size
    count = -(-mask_count // 16) * 16
    place_ref = place.astype(jnp.int32).reshape(1)

    owner_row = owners[0]
    slot_rank = slot_ranks(owner_row)
    slot_index = owner_row * capacity + slot_rank
    slot_match = (owner_row[None, :] == owner_self) & (
        slot_rank[None, :] == jnp.arange(capacity, dtype=jnp.int32)[:, None]
    )
    slot_used = jnp.any(slot_match, axis=1)[:, None, None]
    slot_tile = jnp.argmax(slot_match, axis=1)

    mask_rows = seq_count * count
    share = window // parts
    share_rows = total_rows // parts
    dp_size = lax.axis_size("dp")
    lines = dp_size == 8 and attn_tiles == 8 and parts == 4 and seq_count == 3 and hidden == model and mask_rows <= window // 2
    anywhere = pl.BlockSpec(memory_space=pl.ANY)
    inside = pl.BlockSpec(memory_space=pltpu.VMEM)
    dma = pltpu.SemaphoreType.DMA

    tile_block = (1, tile_rows, model)
    if lines:
        small = pl.BlockSpec(memory_space=pltpu.SMEM)
        half_tiles = attn_tiles // 2
        low_slots, attn_sums = pl.pallas_call(
            weights_kernel,
            out_shape=[
                jax.ShapeDtypeStruct((capacity, tile_rows, model), bf16),
                jax.ShapeDtypeStruct((attn_tiles, tile_rows, model), bf16),
            ],
            in_specs=[small, small, inside],
            out_specs=[inside, anywhere],
            scratch_shapes=[
                pltpu.VMEM((attn_tiles, tile_rows, model), bf16),
                pltpu.VMEM((half_tiles, tile_rows, model), bf16),
                pltpu.VMEM((3, half_tiles, tile_rows, model), bf16),
                pltpu.VMEM((2, half_tiles, tile_rows, model), bf16),
                dma,
                dma,
                dma((2, half_tiles)),
                dma((2, half_tiles)),
                dma((half_tiles,)),
                dma((half_tiles,)),
                dma((half_tiles,)),
            ],
            compiler_params=params(collective_id=4, has_side_effects=True),
            cost_estimate=cost(0, 12e6),
            name="weights",
        )(
            slot_rank[:attn_tiles],
            (owner_row[:attn_tiles] == owner_self).astype(jnp.int32),
            master[0],
        )
        attn_flat = attn_sums.reshape(4 * width, model)
    else:
        grid_size = max(capacity, attn_tiles)
        low_slots, attn_mine = pl.pallas_call(
            cast_kernel,
            out_shape=[
                jax.ShapeDtypeStruct((capacity, tile_rows, model), bf16),
                jax.ShapeDtypeStruct((attn_tiles, tile_rows, model), bf16),
            ],
            grid_spec=pltpu.PrefetchScalarGridSpec(
                num_scalar_prefetch=2,
                grid=(grid_size,),
                in_specs=[
                    pl.BlockSpec(
                        tile_block, lambda i, rank, held: (jnp.minimum(i, capacity - 1), 0, 0)
                    ),
                    pl.BlockSpec(
                        tile_block,
                        lambda i, rank, held: (rank[jnp.minimum(i, attn_tiles - 1)], 0, 0),
                    ),
                ],
                out_specs=[
                    pl.BlockSpec(
                        tile_block, lambda i, rank, held: (jnp.minimum(i, capacity - 1), 0, 0)
                    ),
                    pl.BlockSpec(
                        tile_block, lambda i, rank, held: (jnp.minimum(i, attn_tiles - 1), 0, 0)
                    ),
                ],
            ),
            compiler_params=params(),
            cost_estimate=cost(0, 12 * capacity * tile_size),
            name="cast",
        )(
            slot_rank,
            jnp.pad(
                (owner_row[:attn_tiles] == owner_self).astype(jnp.int32),
                (0, grid_size - attn_tiles),
                mode="edge",
            ),
            master[0],
            master[0],
        )
        attn_flat = dp_total(attn_mine).reshape(4 * width, model)
    w_out = attn_flat[3 * width :]
    every_slot = lax.all_gather(low_slots, "dp", axis=0, tiled=True)

    cos, sin = map(jnp.asarray, head_tables(np.arange(window), heads, np))
    rows = jnp.pad(masked_rows, ((0, 0), (0, count - mask_count)), constant_values=-1)
    cot = jnp.pad(cotangent, ((0, 0), (0, count - mask_count), (0, 0)))
    cot = cot.reshape(seq_count * count, model)

    win_model = pl.BlockSpec((window, model), lambda i: (i, 0))
    win_head = pl.BlockSpec((window, width), lambda i: (i, 0))
    mask_model = pl.BlockSpec((count, model), lambda i: (i, 0))
    mask_head = pl.BlockSpec((count, width), lambda i: (i, 0))
    if lines:
        (
            o_m,
            o_first,
            o_second,
            o_third,
            w_far,
            q_m,
            x_m,
            cos_m,
            sin_m,
            k,
            v,
            w_qkv,
        ) = pl.pallas_call(
            functools.partial(attend_all_kernel, seq_count),
            out_shape=[
                jax.ShapeDtypeStruct((4, mask_rows, width), bf16),
                jax.ShapeDtypeStruct((4, window, width), bf16),
                jax.ShapeDtypeStruct((window, width), bf16),
                jax.ShapeDtypeStruct((window, width), bf16),
                jax.ShapeDtypeStruct((3, width, model), bf16),
                jax.ShapeDtypeStruct((mask_rows, width), bf16),
                jax.ShapeDtypeStruct((mask_rows, model), bf16),
                jax.ShapeDtypeStruct((mask_rows, width), f32),
                jax.ShapeDtypeStruct((mask_rows, width), f32),
                jax.ShapeDtypeStruct((total_rows, width), bf16),
                jax.ShapeDtypeStruct((total_rows, width), bf16),
                jax.ShapeDtypeStruct((model, 3 * width), bf16),
            ],
            in_specs=[inside] * 5 + [anywhere] * 2,
            out_specs=[anywhere] * 5 + [inside] * 7,
            scratch_shapes=[
                pltpu.VMEM((total_rows, width), bf16),
                pltpu.VMEM((3 * width // 128, model, 128), f32),
                pltpu.VMEM((mask_rows, width), bf16),
                pltpu.VMEM((seq_count, window, width), bf16),
                pltpu.VMEM((2, window, model), bf16),
                dma((2,)),
                dma((seq_count,)),
                dma,
                dma((3, 2)),
                dma((3, 2)),
                dma((3, 2)),
                dma((3, 2)),
                dma((3, 2)),
                dma((3, 2)),
                dma((3,)),
                dma((3,)),
            ],
            compiler_params=params(collective_id=3, has_side_effects=True),
            cost_estimate=cost(4e10, 20e6),
            name="attend_all",
        )(rows[:, :, None], norm_gains, attn_flat, cos, sin, tokens, attn_flat)
        before_tiles = o_third
    else:
        block = min(512, window)
        per_window = window // block
        row_block = pl.BlockSpec((block, model), lambda i: (i, 0))
        head_block = pl.BlockSpec((block, width), lambda i: (i, 0))
        table_block = pl.BlockSpec((block, width), lambda i: (i % per_window, 0))
        q, k, v, w_qkv = pl.pallas_call(
            qkv_kernel,
            out_shape=[jax.ShapeDtypeStruct((total_rows, width), bf16)] * 3
            + [jax.ShapeDtypeStruct((model, 3 * width), bf16)],
            grid=(total_rows // block,),
            in_specs=[
                row_block,
                whole_spec((2, model)),
                whole_spec((3 * width, model)),
                table_block,
                table_block,
            ],
            out_specs=[head_block] * 3 + [whole_spec((model, 3 * width))],
            scratch_shapes=[pltpu.VMEM((3 * width // 128, model, 128), f32)],
            compiler_params=params(),
            cost_estimate=cost(6 * total_rows * model * width, 2 * total_rows * model * 2),
            name="qkv",
        )(tokens, norm_gains, attn_flat, cos, sin)

        o_m, q_m, x_m = pl.pallas_call(
            attend_masked_kernel,
            out_shape=[
                jax.ShapeDtypeStruct((seq_count * count, width), bf16),
                jax.ShapeDtypeStruct((seq_count * count, width), bf16),
                jax.ShapeDtypeStruct((seq_count * count, model), bf16),
            ],
            grid=(seq_count,),
            in_specs=[
                pl.BlockSpec((1, count, 1), lambda i: (i, 0, 0)),
                win_model,
                win_head,
                win_head,
                win_head,
            ],
            out_specs=[mask_head, mask_head, mask_model],
            compiler_params=params(),
            cost_estimate=cost(
                seq_count * count * window * (2 * model + 8 * width), 9e6, seq_count * count * window * heads
            ),
            name="attend_masked",
        )(rows[:, :, None], tokens, q, k, v)
        o_ms = around(o_m)

        q_block = min(256, window)

        def attend_window(w, before):
            return pl.pallas_call(
                after(attend_kernel, 3, 1),
                out_shape=jax.ShapeDtypeStruct((window, width), bf16),
                grid=(width // 128, window // q_block),
                in_specs=[
                    pl.BlockSpec((q_block, 128), lambda p, i: (w * (window // q_block) + i, p)),
                    pl.BlockSpec((window, 128), lambda p, i: (w, p)),
                    pl.BlockSpec((window, 128), lambda p, i: (w, p)),
                    UNREAD,
                ],
                out_specs=pl.BlockSpec((q_block, 128), lambda p, i: (i, p)),
                compiler_params=params(),
                cost_estimate=cost(
                    16 * window * window * width, 4 * window * width * 2, window * window * heads
                ),
                name="attend",
            )(q, k, v, before)

        early = max(seq_count - 1, 1)
        o_own = []
        for w in range(early):
            o_own.append(attend_window(w, o_own[-1] if o_own else o_m))
        before_tiles = o_own[-1]
        cos_m, sin_m = (
            table.reshape(mask_rows, width) for table in head_tables(rows, heads, jnp)
        )

    group = 4
    ffn_all = pl.pallas_call(
        after(collect_kernel, 1 + group, 1),
        out_shape=jax.ShapeDtypeStruct((ffn_tiles, tile_rows, model), bf16),
        grid_spec=pltpu.PrefetchScalarGridSpec(
            num_scalar_prefetch=1,
            grid=(ffn_tiles // group,),
            in_specs=[
                pl.BlockSpec(
                    tile_block,
                    lambda i, slot, n=n: (slot[attn_tiles + i * group + n], 0, 0),
                )
                for n in range(group)
            ]
            + [UNREAD],
            out_specs=pl.BlockSpec((group, tile_rows, model), lambda i, slot: (i, 0, 0)),
        ),
        compiler_params=params(),
        cost_estimate=cost(0, 4 * ffn_tiles * tile_size),
        name="collect",
    )(slot_index, *[every_slot] * group, before_tiles)
    even = jnp.array([[1.0], [1.0 / parts]], f32)
    flat_rows = jnp.where(
        rows >= 0, rows + window * jnp.arange(seq_count, dtype=jnp.int32)[:, None], -1
    ).reshape(1, mask_rows)
    if lines:
        grad_rows = 4 * width + 3 * hidden
        part, own, first_sums, second_sums, dha, grads, dr_m, gains_part = pl.pallas_call(
            functools.partial(middle_kernel, seq_count),
            out_shape=[
                jax.ShapeDtypeStruct((seq_count, window, model), bf16),
                jax.ShapeDtypeStruct((seq_count, share, model), f32),
                jax.ShapeDtypeStruct((2, 3 * share, model), bf16),
                jax.ShapeDtypeStruct((1, 2 * share, model), bf16),
                jax.ShapeDtypeStruct((seq_count, window, model), bf16),
                jax.ShapeDtypeStruct((grad_rows, model), bf16),
                jax.ShapeDtypeStruct((mask_rows, model), f32),
                jax.ShapeDtypeStruct((2, model), f32),
            ],
            in_specs=[inside] * 15 + [anywhere] * 5,
            out_specs=[anywhere] * 6 + [inside] * 2,
            scratch_shapes=[
                pltpu.VMEM((window, model), f32),
                pltpu.VMEM((window, model), bf16),
                pltpu.VMEM((window, model), f32),
                pltpu.VMEM((window, model), bf16),
                pltpu.VMEM((share, model), f32),
                pltpu.VMEM((2, 4, window, width), bf16),
                pltpu.VMEM((window, model), bf16),
                pltpu.VMEM((2, 2, window, width), bf16),
                pltpu.VMEM((window, 3 * width), bf16),
                pltpu.VMEM((model, 3 * width), f32),
                pltpu.VMEM((model, 128), f32),
                pltpu.VMEM((width, model), f32),
                pltpu.VMEM((mask_rows, model), f32),
                pltpu.VMEM((4, mask_rows, model // 4), bf16),
                pltpu.VMEM((3, mask_rows, model // 4), bf16),
                pltpu.VMEM((4, mask_rows, model // 4), bf16),
                pltpu.VMEM((1, 2 * share, model), bf16),
                dma((2,)),
                dma((1,)),
                dma((1,)),
                dma((2,)),
                dma,
                dma((2, 2)),
                dma((2, 3)),
                dma,
                dma((window // share,)),
                dma,
                dma((2, 3)),
                dma((2, 3)),
                dma((2, 3, 2)),
                dma((2, 3, 2)),
                dma((3,)),
                dma((3,)),
                dma((3,)),
                dma((3,)),
            ],
            compiler_params=params(collective_id=1, has_side_effects=True),
            cost_estimate=cost(1e11, 100e6),
            name="middle",
        )(
            rows[:, None, :],
            norm_gains,
            x_m,
            cot,
            q_m,
            cos_m,
            sin_m,
            cos,
            sin,
            w_qkv,
            ffn_all.reshape(3, model, hidden),
            o_m,
            o_first,
            w_out,
            w_far,
            tokens,
            k,
            v,
            o_second,
            o_third,
        )

        group = 8
        slots = lax.axis_size("dp") * capacity
        slot_hit = slot_index[None, :] == jnp.arange(slots, dtype=jnp.int32)[:, None]
        used = jnp.any(slot_hit, axis=1).astype(jnp.int32)
        tile_count = slot_index.shape[0]
        held_at = jnp.arange(slots, dtype=jnp.int32) // group * tile_count
        held_at = held_at + jnp.argmax(slot_hit, axis=1).astype(jnp.int32)
        held_at = jnp.where(used > 0, held_at, 0).reshape(-1, group)
        from_tile = lax.rem(lax.cummax(held_at, axis=0), tile_count).reshape(-1)
        in_slots = pl.pallas_call(
            spread_kernel,
            out_shape=jax.ShapeDtypeStruct((slots, tile_rows, model), bf16),
            grid_spec=pltpu.PrefetchScalarGridSpec(
                num_scalar_prefetch=2,
                grid=(slots // group,),
                in_specs=[
                    pl.BlockSpec(
                        tile_block, lambda i, tile, used, n=n: (tile[i * group + n], 0, 0)
                    )
                    for n in range(group)
                ],
                out_specs=pl.BlockSpec(
                    (group, tile_rows, model), lambda i, tile, used: (i, 0, 0)
                ),
            ),
            compiler_params=params(),
            cost_estimate=cost(0, 24 * capacity * tile_size),
            name="spread",
        )(
            from_tile,
            used,
            *[grads.reshape(-1, tile_rows, model)] * group,
        )
        reduced = lax.psum_scatter(in_slots, "dp", scatter_dimension=0, tiled=True).astype(f32)

        order = [(kind, i) for kind in (0, 1) for i in range(seq_count)]
        folds = len(order)
        pair_count = (lax.axis_size("dp") * parts).bit_length() - 1
        layer_out, input_grad, gain_grad = pl.pallas_call(
            after(functools.partial(lines_kernel, seq_count, seq_count, order, 2, 1), 10, 1),
            out_shape=[
                jax.ShapeDtypeStruct((total_rows, model), bf16),
                jax.ShapeDtypeStruct((share_rows, model), bf16),
                jax.ShapeDtypeStruct((2, model), f32),
            ],
            in_specs=[inside] * 3 + [anywhere] * 6 + [inside, anywhere],
            out_specs=[anywhere] * 2 + [inside],
            scratch_shapes=[
                pltpu.VMEM((folds, 3 * share, model), bf16),
                pltpu.VMEM((folds, 2 * share, model), bf16),
                pltpu.VMEM((folds, share, model), bf16),
                pltpu.VMEM((folds, window, model), bf16),
                pltpu.VMEM((seq_count, share, model), f32),
                pltpu.VMEM((seq_count, share, model), bf16),
                pltpu.VMEM((share_rows, model), bf16),
                pltpu.VMEM((seq_count, share, model), bf16),
                pltpu.VMEM((pair_count + 1, 8, model), f32),
                pltpu.VMEM((pair_count, 8, model), f32),
                dma((pair_count,)),
                dma((pair_count,)),
                dma((folds, 3)),
                dma((folds, 3)),
                dma((folds, 2)),
                dma((folds, 2)),
                dma((folds,)),
                dma((folds,)),
                dma((seq_count, 5)),
                dma((seq_count, 3)),
                dma((folds,)),
                dma((seq_count,)),
                dma((2,)),
                dma((1,)),
                dma,
                dma((seq_count,)),
                dma((seq_count,)),
            ],
            compiler_params=params(collective_id=2, has_side_effects=True),
            cost_estimate=cost(4 * share_rows * mask_rows * model, 60e6),
            name="lines",
        )(
            flat_rows,
            dr_m,
            norm_gains,
            tokens,
            dha,
            part,
            own,
            first_sums,
            second_sums,
            gains_part * even,
            in_slots,
        )
    else:
        w_outs = around(w_out)
        ffn_flat = ffn_all.reshape(3, -1)
        w_gate = ffn_flat[0].reshape(model, hidden)
        w_up = ffn_flat[1].reshape(model, hidden)
        w_down = ffn_flat[2].reshape(hidden, model)
        cols = min(256, hidden)
        col_block = pl.BlockSpec((model, cols), lambda c: (0, c))
        down_block = pl.BlockSpec((cols, model), lambda c: (c, 0))
        r_m, dhf_part, ffn_grad = pl.pallas_call(
            functools.partial(ffn_masked_kernel, parts),
            out_shape=[
                jax.ShapeDtypeStruct((mask_rows, model), f32),
                jax.ShapeDtypeStruct((mask_rows, model), bf16),
                jax.ShapeDtypeStruct((3, hidden, model), bf16),
            ],
            grid=(hidden // cols,),
            in_specs=[
                whole_spec((mask_rows, model)),
                whole_spec((mask_rows, model)),
                whole_spec((2, model)),
                col_block,
                col_block,
                down_block,
            ]
            + [whole_spec((mask_rows, width))] * parts
            + [whole_spec((width, model))] * parts,
            out_specs=[
                whole_spec((mask_rows, model)),
                whole_spec((mask_rows, model)),
                whole_spec((3, hidden, model)),
            ],
            scratch_shapes=[
                pltpu.VMEM((mask_rows, model), bf16),
                pltpu.VMEM((mask_rows, model), f32),
                pltpu.VMEM((cols // 128, model, 128), f32),
            ],
            compiler_params=params(),
            cost_estimate=cost(
                mask_rows * model * (18 * hidden + 2 * model), 20e6, mask_rows * hidden
            ),
            name="ffn_masked",
        )(x_m, cot, norm_gains, w_gate, w_up, w_down, *o_ms, *w_outs)

        for w in range(early, seq_count):
            o_own.append(attend_window(w, r_m))
        windows_o = [around(o) for o in o_own]

        share_m = mask_rows // parts
        dhf_mine = lax.dynamic_slice_in_dim(dhf_part, place * share_m, share_m, 0).astype(f32)
        for step in range(1, parts):
            send = lax.dynamic_slice_in_dim(
                dhf_part, lax.rem(place + step, parts) * share_m, share_m, 0
            )
            dhf_mine = dhf_mine + lax.ppermute(
                send, "tensor", [(i, (i + step) % parts) for i in range(parts)]
            ).astype(f32)
        dhf_all = around(dhf_mine.astype(bf16))
        dhf = jnp.zeros((mask_rows, model), bf16)
        for step, piece in enumerate(dhf_all):
            origin = lax.rem(place + parts - step, parts)
            dhf = lax.dynamic_update_slice_in_dim(dhf, piece, origin * share_m, 0)

        layer_out = None

        def ffn_window(w, before):
            return pl.pallas_call(
                after(functools.partial(ffn_kernel, parts), 6 + 2 * parts, 1),
                out_shape=[
                    jax.ShapeDtypeStruct((window, model), bf16),
                    jax.ShapeDtypeStruct((share, model), f32),
                ],
                grid_spec=pltpu.PrefetchScalarGridSpec(
                    num_scalar_prefetch=1,
                    grid=(hidden // cols,),
                    in_specs=[
                        pl.BlockSpec((window, model), lambda c, place_ref: (w, 0)),
                        whole_spec((2, model)),
                        pl.BlockSpec((model, cols), lambda c, place_ref: (0, c)),
                        pl.BlockSpec((model, cols), lambda c, place_ref: (0, c)),
                        pl.BlockSpec((cols, model), lambda c, place_ref: (c, 0)),
                    ]
                    + [whole_spec((window, width))] * parts
                    + [whole_spec((width, model))] * parts
                    + [UNREAD],
                    out_specs=[
                        whole_spec((window, model)),
                        whole_spec((share, model)),
                    ],
                    scratch_shapes=[
                        pltpu.VMEM((window, model), f32),
                        pltpu.VMEM((window, model), bf16),
                        pltpu.VMEM((window, model), f32),
                    ],
                ),
                compiler_params=params(),
                cost_estimate=cost(
                    window * model * (6 * hidden + 2 * model), 16e6, window * hidden
                ),
                name="ffn",
            )(
                place_ref,
                tokens,
                norm_gains,
                w_gate,
                w_up,
                w_down,
                *windows_o[w],
                *w_outs,
                before,
            )

        def place_window(w, part, own):
            terms = other_sums(part, share)
            total = own
            for term in terms:
                total = total + term.astype(f32)
            pieces = around(total.astype(bf16))
            return pl.pallas_call(
                after(place_kernel, 1 + parts, 0 if layer_out is None else 1),
                out_shape=jax.ShapeDtypeStruct((total_rows, model), bf16),
                grid_spec=pltpu.PrefetchScalarGridSpec(
                    num_scalar_prefetch=1,
                    grid=(1,),
                    in_specs=[whole_spec((share, model))] * parts
                    + [UNREAD] * (layer_out is not None),
                    out_specs=pl.BlockSpec((window, model), lambda i, place_ref: (w, 0)),
                ),
                input_output_aliases={} if layer_out is None else {1 + parts: 0},
                compiler_params=params(),
                cost_estimate=cost(0, 4 * window * model),
                name="place",
            )(place_ref, *pieces, *([] if layer_out is None else [layer_out]))

        parts_out = [ffn_window(0, o_own[-1])]

        cuts = seq_count if share_rows % (16 * seq_count) == 0 else 1
        cut_rows = share_rows // cuts
        dr_m, dha, attn_grad, gains_part = pl.pallas_call(
            after(attn_back_kernel, 16, 1),
            out_shape=[
                jax.ShapeDtypeStruct((mask_rows, model), f32),
                jax.ShapeDtypeStruct((cuts, parts, cut_rows, model), bf16),
                jax.ShapeDtypeStruct((4 * width, model), bf16),
                jax.ShapeDtypeStruct((2, model), f32),
            ],
            grid=(seq_count,),
            in_specs=[
                pl.BlockSpec((1, 1, count), lambda i: (i, 0, 0)),
                mask_model,
                mask_model,
                mask_model,
                whole_spec((2, model)),
                mask_head,
                mask_head,
                mask_head,
                mask_head,
                win_head,
                win_head,
                win_model,
                whole_spec((window, width)),
                whole_spec((window, width)),
                whole_spec((width, model)),
                whole_spec((model, 3 * width)),
                UNREAD,
            ],
            out_specs=[
                mask_model,
                whole_spec((cuts, parts, cut_rows, model)),
                whole_spec((4 * width, model)),
                whole_spec((2, model)),
            ],
            scratch_shapes=[
                pltpu.VMEM((model, 3 * width), f32),
                pltpu.VMEM((width, model), f32),
                pltpu.VMEM((2, model), f32),
                pltpu.VMEM((window, 3 * width), bf16),
                pltpu.VMEM((3 * width // 128, model, 128), f32),
            ],
            compiler_params=params(),
            cost_estimate=cost(
                12 * total_rows * model * width, 30e6, mask_rows * window * heads
            ),
            name="attn_back",
        )(
            rows[:, None, :],
            dhf,
            r_m,
            cot,
            norm_gains,
            o_m,
            q_m,
            cos_m,
            sin_m,
            k,
            v,
            tokens,
            cos,
            sin,
            w_out,
            w_qkv,
            parts_out[0][0],
        )

        for w in range(1, seq_count):
            parts_out.append(ffn_window(w, gains_part if w == 1 else parts_out[-1][0]))

        input_grad = None
        for cut in range(cuts):
            value = dha[cut].reshape(parts * cut_rows, model)
            terms = other_sums(value, cut_rows)
            before = [] if input_grad is None else [input_grad]
            input_grad = pl.pallas_call(
                after(
                    functools.partial(input_grad_kernel, (cut, cuts, len(terms))),
                    6 + len(terms),
                    len(before),
                ),
                out_shape=jax.ShapeDtypeStruct((share_rows, model), bf16),
                grid_spec=pltpu.PrefetchScalarGridSpec(
                    num_scalar_prefetch=1,
                    grid=(1,),
                    in_specs=[
                        whole_spec((1, mask_rows)),
                        whole_spec((mask_rows, model)),
                        whole_spec((2, model)),
                        pl.BlockSpec(
                            (cut_rows, model),
                            lambda i, place_ref, cut=cut: (place_ref[0] * cuts + cut, 0),
                        ),
                        pl.BlockSpec(
                            (1, 1, cut_rows, model),
                            lambda i, place_ref, cut=cut: (cut, place_ref[0], 0, 0),
                        ),
                    ]
                    + [whole_spec((cut_rows, model))] * len(terms)
                    + [UNREAD] * len(before),
                    out_specs=pl.BlockSpec((cut_rows, model), lambda i, place_ref, cut=cut: (cut, 0)),
                ),
                input_output_aliases={6 + len(terms): 0} if before else {},
                compiler_params=params(),
                cost_estimate=cost(4 * cut_rows * mask_rows * model, 6e6),
                name="input_grad",
            )(place_ref, flat_rows, dr_m, norm_gains, tokens, dha, *terms, *before)

        for w, outs in enumerate(parts_out):
            layer_out = place_window(w, *outs)

        gain_grad = small_total(gains_part * even)

        def total_tiles(tiles, before):
            piece = lax.psum_scatter(tiles, "dp", scatter_dimension=0, tiled=True)
            piece = pl.pallas_call(
                after(copy_kernel, 1, 1),
                out_shape=jax.ShapeDtypeStruct(piece.shape, bf16),
                in_specs=[pl.BlockSpec(memory_space=pltpu.VMEM), UNREAD],
                out_specs=pl.BlockSpec(memory_space=pltpu.VMEM),
                compiler_params=params(),
                name="copy",
            )(piece, before)
            return lax.all_gather(piece, "dp", axis=0, tiled=True)

        ffn_grads = total_tiles(ffn_grad.reshape(3 * hidden, model), parts_out[1][0])
        attn_grads = total_tiles(attn_grad, parts_out[-1][0])
        tiles = jnp.concatenate([attn_grads, ffn_grads], axis=0).reshape(-1, tile_rows, model)
        reduced = tiles[slot_tile].astype(f32)

    _, gain_moment, gain_new = adam_update(
        gain_grad, gain_first, gain_second, norm_gains, gain_rate, 0.0
    )

    first_new, second_new, param_new = adam_update(
        reduced, first_moment[0], second_moment[0], master[0], weight_rate, weight_decay
    )
    weight_grad = jnp.where(slot_used, reduced, 0.0)
    weight_first = jnp.where(slot_used, first_new, 0.0)
    weight_second = jnp.where(slot_used, second_new, 0.0)
    weight_master = jnp.where(slot_used, param_new, 0.0)
    weight_low = weight_master.astype(bf16)
    return (
        layer_out,
        input_grad,
        weight_grad[None],
        weight_first[None],
        weight_second[None],
        weight_master[None],
        weight_low[None],
        gain_grad,
        gain_moment,
        gain_new,
    )


def solution(mesh):
    return jax.shard_map(
        on_device,
        mesh=mesh,
        in_specs=(
            P("dp", None),
            P("dp", None),
            P("dp", None, None),
            P(),
            P(),
            P(),
            P("tensor", None),
            P("tensor", "dp", None, None),
            P("tensor", "dp", None, None),
            P("tensor", "dp", None, None),
        ),
        out_specs=(
            P("dp", None),
            P(("dp", "tensor"), None),
            P("tensor", "dp", None, None),
            P("tensor", "dp", None, None),
            P("tensor", "dp", None, None),
            P("tensor", "dp", None, None),
            P("tensor", "dp", None, None),
            P(),
            P(),
            P(),
        ),
        check_vma=False,
    )
```

```python
import functools

import jax
import jax.numpy as jnp
import numpy as np
from jax import lax
from jax.experimental import pallas as pl
from jax.experimental.pallas import tpu as pltpu
from jax.sharding import PartitionSpec as P

HEADS = 16
HD = 64
FF = 4096
STEP = 5

norm_eps = 1e-06
beta_one = 0.9
beta_two = 0.95
adam_eps = 1e-08
weight_rate = 0.05
gain_rate = 0.8
weight_decay = 0.1

score_scale = HD ** (-0.5)
f32 = jnp.float32
bf16 = jnp.bfloat16
VMEM_LIMIT = 60 * 1024 * 1024
NT = (((1,), (1,)), ((), ()))
TN = (((0,), (0,)), ((), ()))


def mm(left, right):
    return jnp.dot(left, right, preferred_element_type=f32)


def mm_nt(left, right):
    return lax.dot_general(left, right, NT, preferred_element_type=f32)


def mm_tn(left, right):
    return lax.dot_general(left, right, TN, preferred_element_type=f32)


def params(**kw):
    return pltpu.CompilerParams(vmem_limit_bytes=VMEM_LIMIT, **kw)


def cost(flops, nbytes, transcendentals=0):
    return pl.CostEstimate(
        flops=int(flops), bytes_accessed=int(nbytes), transcendentals=int(transcendentals)
    )


def whole_spec(shape):
    return pl.BlockSpec(shape, lambda *_: (0,) * len(shape))


def after(kernel, inputs, count):
    return lambda *refs: kernel(*refs[:inputs], *refs[inputs + count :])


UNREAD = pl.BlockSpec(memory_space=pl.ANY)


def rms_scale(values):
    return lax.rsqrt(jnp.mean(values * values, axis=-1, keepdims=True) + norm_eps)


def swap_halves(values):
    width = values.shape[1]
    lane = lax.broadcasted_iota(jnp.int32, values.shape, 1)
    return jnp.where(
        lane % HD < HD // 2,
        pltpu.roll(values, width - HD // 2, 1),
        pltpu.roll(values, HD // 2, 1),
    )


def cast_kernel(rank_ref, held_ref, slot_ref, tile_ref, low_ref, mine_ref):
    low_ref[...] = slot_ref[...].astype(bf16)
    tile = tile_ref[...].astype(bf16)
    held = held_ref[pl.program_id(0)] > 0
    mine_ref[...] = jnp.where(held, tile, jnp.zeros((), bf16))


def qkv_kernel(
    x_ref, gains_ref, tiles_ref, cos_ref, sin_ref, q_ref, k_ref, v_ref, w_ref, w_wide
):
    width = q_ref.shape[1]
    model = x_ref.shape[1]
    fold = model // width

    @pl.when(pl.program_id(0) == 0)
    def _():
        for block in range(3 * width // 128):
            part, lane = divmod(block * 128, width)
            for piece in range(fold):
                at = piece * width + lane
                w_wide[block, pl.ds(piece, width, stride=fold), :] = tiles_ref[
                    part * width : (part + 1) * width, at : at + 128
                ].astype(f32)
            w_ref[:, block * 128 : (block + 1) * 128] = w_wide[block].astype(bf16)

    x = x_ref[...].astype(f32)
    hidden = (x * rms_scale(x) * gains_ref[0:1, :]).astype(bf16)
    cos, sin = cos_ref[...], sin_ref[...]
    q = mm(hidden, w_ref[:, 0:width])
    q_ref[...] = (q * cos + swap_halves(q) * sin).astype(bf16)
    k = mm(hidden, w_ref[:, width : 2 * width])
    k_ref[...] = (k * cos + swap_halves(k) * sin).astype(bf16)
    v_ref[...] = mm(hidden, w_ref[:, 2 * width : 3 * width]).astype(bf16)


def attend(q, k, v):
    first = lax.broadcasted_iota(jnp.int32, q.shape, 1) < HD
    first_v = lax.broadcasted_iota(jnp.int32, v.shape, 1) < HD
    zero, one = jnp.zeros((), bf16), jnp.ones((), bf16)
    outs = []
    for head in range(2):
        q_head = jnp.where(first if head == 0 else ~first, q, zero)
        v_head = jnp.where(first_v if head == 0 else ~first_v, v, one)
        s = mm_nt(q_head, k)
        s = (s - jnp.max(s, axis=-1, keepdims=True)) * score_scale
        outs.append(mm(jnp.exp(s).astype(bf16), v_head))
    value = jnp.where(first, outs[0], outs[1])
    total = pltpu.roll(jnp.where(first, outs[1], outs[0]), HD, 1)
    return (value / total).astype(bf16)


def attend_kernel(q_ref, k_ref, v_ref, o_ref):
    o_ref[...] = attend(q_ref[...], k_ref[...], v_ref[...])


def attend_masked_kernel(rows_ref, x_ref, q_ref, k_ref, v_ref, o_ref, qm_ref, xm_ref):
    window = x_ref.shape[0]
    count = rows_ref.shape[1]
    pick = (
        lax.broadcasted_iota(jnp.int32, (count, window), 1) == rows_ref[0]
    ).astype(bf16)
    xm_ref[...] = mm(pick, x_ref[...]).astype(bf16)
    qm = mm(pick, q_ref[...]).astype(bf16)
    qm_ref[...] = qm
    for pair in range(q_ref.shape[1] // 128):
        lanes = slice(pair * 128, pair * 128 + 128)
        o_ref[:, lanes] = attend(qm[:, lanes], k_ref[:, lanes], v_ref[:, lanes])


def ffn_masked_kernel(
    parts, xm_ref, cot_ref, gains_ref, wg_ref, wu_ref, wd_ref, *refs
):
    o_refs, wo_refs = refs[:parts], refs[parts : 2 * parts]
    rm_ref, dhf_ref, grad_ref, hf_ref, acc_ref, wide_ref = refs[2 * parts :]
    step = pl.program_id(0)
    width = wg_ref.shape[1]
    cols = pl.ds(pl.multiple_of(step * width, width), width)
    hidden, model = grad_ref.shape[1:]
    fold = model // hidden

    def put(part, grad):
        if fold == 1:
            grad_ref[part, :, cols] = grad.astype(bf16)
            return
        for block in range(width // 128):
            wide_ref[block] = grad[:, block * 128 : (block + 1) * 128]
            for piece in range(fold):
                at = piece * hidden + step * width + block * 128
                at = pl.ds(pl.multiple_of(at, 128), 128)
                grad_ref[part, :, at] = wide_ref[
                    block, pl.ds(piece, hidden, stride=fold), :
                ].astype(bf16)

    @pl.when(step == 0)
    def _():
        r = xm_ref[...].astype(f32)
        for o_ref, wo_ref in zip(o_refs, wo_refs):
            r = r + mm(o_ref[...], wo_ref[...])
        rm_ref[...] = r
        hf_ref[...] = (r * rms_scale(r) * gains_ref[1:2, :]).astype(bf16)
        acc_ref[...] = jnp.zeros_like(acc_ref)

    hf, dy = hf_ref[...], cot_ref[...]
    wg, wu, wd = wg_ref[...], wu_ref[...], wd_ref[...]
    g, u = mm(hf, wg), mm(hf, wu)
    sig = jax.nn.sigmoid(g)
    act = (g * sig * u).astype(bf16)
    grad_ref[2, cols, :] = mm_tn(act, dy).astype(bf16)
    da = mm_nt(dy, wd)
    dg = (da * u * sig * (1.0 + g * (1.0 - sig))).astype(bf16)
    du = (da * g * sig).astype(bf16)
    put(0, mm_tn(hf, dg))
    put(1, mm_tn(hf, du))
    acc_ref[...] += mm_nt(dg, wg) + mm_nt(du, wu)

    @pl.when(step == pl.num_programs(0) - 1)
    def _():
        dhf_ref[...] = acc_ref[...].astype(bf16)


def ffn_kernel(parts, place_ref, x_ref, gains_ref, wg_ref, wu_ref, wd_ref, *refs):
    o_refs, wo_refs = refs[:parts], refs[parts : 2 * parts]
    part_ref, own_ref, r_ref, hf_ref, acc_ref = refs[2 * parts :]
    step = pl.program_id(0)

    @pl.when(step == 0)
    def _():
        r = x_ref[...].astype(f32)
        for o_ref, wo_ref in zip(o_refs, wo_refs):
            r = r + mm(o_ref[...], wo_ref[...])
        r_ref[...] = r
        hf_ref[...] = (r * rms_scale(r) * gains_ref[1:2, :]).astype(bf16)
        acc_ref[...] = jnp.zeros_like(acc_ref)

    hf = hf_ref[...]
    g, u = mm(hf, wg_ref[...]), mm(hf, wu_ref[...])
    act = (g * jax.nn.sigmoid(g) * u).astype(bf16)
    acc_ref[...] += mm(act, wd_ref[...])

    @pl.when(step == pl.num_programs(0) - 1)
    def _():
        share = own_ref.shape[0]
        part_ref[...] = acc_ref[...].astype(bf16)
        mine = pl.ds(pl.multiple_of(place_ref[0] * share, share), share)
        own_ref[...] = r_ref[mine, :] + acc_ref[mine, :]


def attn_back_kernel(
    rows_ref,
    dhf_ref,
    rm_ref,
    cot_ref,
    gains_ref,
    om_ref,
    qm_ref,
    cosm_ref,
    sinm_ref,
    k_ref,
    v_ref,
    x_ref,
    cos_ref,
    sin_ref,
    wo_ref,
    w_ref,
    drm_ref,
    dha_ref,
    gw_ref,
    gain_ref,
    gw_acc,
    go_acc,
    gain_acc,
    flow_ref,
    gw_wide,
):
    step = pl.program_id(0)

    @pl.when(step == 0)
    def _():
        gw_acc[...] = jnp.zeros_like(gw_acc)
        go_acc[...] = jnp.zeros_like(go_acc)
        gain_acc[...] = jnp.zeros_like(gain_acc)

    window, width = k_ref.shape
    count = rm_ref.shape[0]
    r = rm_ref[...]
    sf = rms_scale(r)
    nf = r * sf
    dhf = dhf_ref[...].astype(f32)
    dnf = dhf * gains_ref[1:2, :]
    dr = cot_ref[...].astype(f32) + sf * (
        dnf - nf * jnp.mean(dnf * nf, axis=-1, keepdims=True)
    )
    drm_ref[...] = dr
    gain_acc[1:2, :] += jnp.sum(dhf * nf, axis=0, keepdims=True)
    drb = dr.astype(bf16)
    go_acc[...] += mm_tn(om_ref[...], drb)
    dob = mm_nt(drb, wo_ref[...]).astype(bf16)

    first = lax.broadcasted_iota(jnp.int32, (count, 128), 1) < HD
    zero = jnp.zeros((), bf16)
    drq = []
    for pair in range(width // 128):
        lanes = slice(pair * 128, pair * 128 + 128)
        k, v = k_ref[:, lanes], v_ref[:, lanes]
        qm, do = qm_ref[:, lanes], dob[:, lanes]
        parts = []
        drk = dv = None
        for head in range(2):
            mine = first if head == 0 else ~first
            q_head = jnp.where(mine, qm, zero)
            do_head = jnp.where(mine, do, zero)
            s = mm_nt(k, q_head)
            s = jnp.exp((s - jnp.max(s, axis=0, keepdims=True)) * score_scale)
            att = s / jnp.sum(s, axis=0, keepdims=True)
            dpa = mm_nt(v, do_head)
            ds = att * (dpa - jnp.sum(dpa * att, axis=0, keepdims=True))
            ds = (ds * score_scale).astype(bf16)
            parts.append(mm_tn(ds, k))
            drk_head = mm(ds, q_head)
            dv_head = mm(att.astype(bf16), do_head)
            drk = drk_head if drk is None else drk + drk_head
            dv = dv_head if dv is None else dv + dv_head
        drq.append(jnp.where(first, parts[0], parts[1]))
        dk = drk * cos_ref[:, lanes] - swap_halves(drk) * sin_ref[:, lanes]
        flow_ref[:, width + pair * 128 : width + pair * 128 + 128] = dk.astype(bf16)
        flow_ref[:, 2 * width + pair * 128 : 2 * width + pair * 128 + 128] = dv.astype(
            bf16
        )
    spread = (
        lax.broadcasted_iota(jnp.int32, (window, count), 0) == rows_ref[0]
    ).astype(bf16)
    for pair in range(width // 128):
        lanes = slice(pair * 128, pair * 128 + 128)
        dq = drq[pair] * cosm_ref[:, lanes] - swap_halves(drq[pair]) * sinm_ref[:, lanes]
        flow_ref[:, lanes] = mm(spread, dq.astype(bf16)).astype(bf16)

    flow = flow_ref[...]
    x = x_ref[...].astype(f32)
    na = x * rms_scale(x)
    dha = mm_nt(flow, w_ref[...])
    gain_acc[0:1, :] += jnp.sum(dha * na, axis=0, keepdims=True)
    cuts, shares, rows = dha_ref.shape[:3]
    for piece in range(window // rows):
        block = step * (window // rows) + piece
        dha_ref[block % cuts, block // cuts] = dha[piece * rows : (piece + 1) * rows].astype(bf16)
    gw_acc[...] += mm_tn((na * gains_ref[0:1, :]).astype(bf16), flow)

    @pl.when(step == pl.num_programs(0) - 1)
    def _():
        fold = gw_acc.shape[0] // width
        for block in range(3 * width // 128):
            part, lane = divmod(block * 128, width)
            gw_wide[block] = gw_acc[:, block * 128 : (block + 1) * 128]
            for piece in range(fold):
                at = piece * width + lane
                gw_ref[part * width : (part + 1) * width, at : at + 128] = gw_wide[
                    block, pl.ds(piece, width, stride=fold), :
                ].astype(bf16)
        gw_ref[3 * width :, :] = go_acc[...].astype(bf16)
        gain_ref[...] = gain_acc[...]


def input_grad_kernel(
    cut, place_ref, rows_ref, drm_ref, gains_ref, x_ref, part_ref, *refs
):
    out_ref = refs[-1]
    block, count = x_ref.shape[0], drm_ref.shape[0]
    base = (place_ref[0] * cut[1] + cut[0]) * block
    spread = (
        lax.broadcasted_iota(jnp.int32, (block, count), 0) + base == rows_ref[...]
    ).astype(bf16)
    dr = drm_ref[...]
    high = dr.astype(bf16)
    low = (dr - high.astype(f32)).astype(bf16)
    dr = mm(spread, high) + mm(spread, low)
    x = x_ref[...].astype(f32)
    sa = rms_scale(x)
    na = x * sa
    dha = part_ref[0, 0].astype(f32)
    for ref in refs[: cut[2]]:
        dha = dha + ref[...].astype(f32)
    dna = dha * gains_ref[0:1, :]
    out = dr + sa * (dna - na * jnp.mean(dna * na, axis=-1, keepdims=True))
    out_ref[...] = out.astype(bf16)


def input_grad_rows(dha, x, dr, gain, spread):
    high = dr.astype(bf16)
    low = (dr - high.astype(f32)).astype(bf16)
    dr = mm(spread, high) + mm(spread, low)
    sa = rms_scale(x)
    na = x * sa
    dna = dha * gain
    return dr + sa * (dna - na * jnp.mean(dna * na, axis=-1, keepdims=True))


def remote(src, dst, send, recv, place):
    return pltpu.make_async_remote_copy(
        src_ref=src,
        dst_ref=dst,
        send_sem=send,
        recv_sem=recv,
        device_id={"tensor": place},
        device_id_type=pl.DeviceIdType.MESH,
    )


def greet_line(place, others=()):
    barrier = pltpu.get_barrier_semaphore()
    for axis, other in others:
        pl.semaphore_signal(
            barrier,
            inc=1,
            device_id={axis: other},
            device_id_type=pl.DeviceIdType.MESH,
        )
    for k in range(1, 4):
        pl.semaphore_signal(
            barrier,
            inc=1,
            device_id={"tensor": lax.rem(place + k, 4)},
            device_id_type=pl.DeviceIdType.MESH,
        )
    pl.semaphore_wait(barrier, 3 + len(others))


def sends(place, d, up):
    if up:
        return (place >= d - 1) & (place <= 2)
    return (place <= 4 - d) & (place >= 1)


def receives(place, d, up):
    return place >= d if up else place <= 3 - d


def each_way(place, d, rule, act):
    for up in (True, False):

        @pl.when(rule(place, d, up))
        def _():
            act(up)


def rows_ref(ref, index, share, count):
    return ref.at[pl.ds(pl.multiple_of(index * share, share), count * share), :]


def weights_kernel(
    rank_ref,
    held_ref,
    master_ref,
    low_ref,
    out_ref,
    mine,
    got,
    work,
    trade,
    h_send,
    h_recv,
    t_send,
    t_recv,
    f_send,
    f_recv,
    f_keep,
):
    me = lax.axis_index("dp")
    core = lax.rem(me, 2)
    tiles = mine.shape[0]
    half = tiles // 2

    def pair(bit):
        return me + bit - 2 * bit * lax.rem(me // bit, 2)

    def to(src, dst, send, recv, bit):
        return pltpu.make_async_remote_copy(
            src_ref=src,
            dst_ref=dst,
            send_sem=send,
            recv_sem=recv,
            device_id={"dp": pair(bit)},
            device_id_type=pl.DeviceIdType.MESH,
        )

    def share(first):
        return pl.ds(first * half, half)

    swap = to(mine.at[share(1 - core)], got, h_send, h_recv, 1)

    def move(stage, t):
        bit = (2, 4)[(stage + t // (half // 2)) % 2]
        return to(
            work.at[stage, t],
            trade.at[stage, t],
            t_send.at[stage, t],
            t_recv.at[stage, t],
            bit,
        )

    def final(t):
        return to(work.at[2, t], out_ref.at[core * half + t], f_send.at[t], f_recv.at[t], 1)

    def final_in(t):
        at = out_ref.at[(1 - core) * half + t]
        return to(at, at, f_send.at[t], f_recv.at[t], 1)

    def keep(t):
        return pltpu.make_async_copy(
            work.at[2, t], out_ref.at[core * half + t], f_keep.at[t]
        )

    barrier = pltpu.get_barrier_semaphore()
    for bit in (1, 2, 4):
        pl.semaphore_signal(
            barrier, inc=1, device_id={"dp": pair(bit)}, device_id_type=pl.DeviceIdType.MESH
        )
    for t in range(tiles):
        tile = master_ref[rank_ref[t]].astype(bf16)
        mine[t] = jnp.where(held_ref[t] > 0, tile, jnp.zeros((), bf16))
    pl.semaphore_wait(barrier, 3)
    swap.start()
    for n in range(low_ref.shape[0]):
        low_ref[n] = master_ref[n].astype(bf16)
    swap.wait_recv()
    turns = [t + n for t in range(half // 2) for n in (0, half // 2)]
    for t in turns:
        work[0, t] = mine[core * half + t] + got[t]
        move(0, t).start()
    for stage in (1, 2):
        for t in turns:
            move(stage - 1, t).wait_recv()
            work[stage, t] = work[stage - 1, t] + trade[stage - 1, t]
            if stage == 1:
                move(1, t).start()
            else:
                final(t).start()
                keep(t).start()
    for t in range(half):
        final_in(t).wait_recv()
    swap.wait_send()
    for t in range(half):
        keep(t).wait()
        final(t).wait_send()
        for stage in range(2):
            move(stage, t).wait_send()


def attend_all_kernel(
    windows,
    rows_in,
    gains_ref,
    tiles_ref,
    cos_ref,
    sin_ref,
    x_hbm,
    tiles_hbm,
    om_out,
    oa_out,
    ob_out,
    oc_out,
    wo_out,
    qm_ref,
    xm_ref,
    cosm_ref,
    sinm_ref,
    k_ref,
    v_ref,
    w_ref,
    q_ref,
    w_wide,
    om_own,
    o_own,
    x_ref,
    x_sem,
    own_sem,
    keep_sem,
    m_send,
    m_recv,
    o_send,
    o_recv,
    w_send,
    w_recv,
    c_send,
    c_recv,
):
    place = lax.axis_index("tensor")
    window = x_ref.shape[1]
    width = q_ref.shape[1]
    count = rows_in.shape[1]
    q_block = 256

    def load_x(w):
        return pltpu.make_async_copy(
            x_hbm.at[pl.ds(w * window, window), :], x_ref.at[w % 2], x_sem.at[w % 2]
        )

    def hop(kind, d, up):
        own, out, send, recv = (
            (om_own, om_out, m_send, m_recv) if kind == 0 else (o_own.at[0], oa_out, o_send, o_recv)
        )
        src, dst = (d - 1, d) if up else ((5 - d) % 4, 4 - d)
        n = 0 if up else 1
        return remote(
            own if d == 1 else out.at[src],
            out.at[dst],
            send.at[d - 1, n],
            recv.at[d - 1, n],
            lax.rem(place + (1 if up else 3), 4),
        )

    me = lax.axis_index("dp")
    core = lax.rem(me, 2)
    half = width // 2

    def half_of(ref, first):
        return ref.at[pl.ds(pl.multiple_of(first + core * half, half), half), :]

    def hop_w(d, up):
        src, dst = (d - 1, d) if up else ((5 - d) % 4, 4 - d)
        n = 0 if up else 1
        return remote(
            half_of(tiles_hbm, 3 * width) if d == 1 else half_of(wo_out.at[src - 1], 0),
            half_of(wo_out.at[dst - 1], 0),
            w_send.at[d - 1, n],
            w_recv.at[d - 1, n],
            lax.rem(place + (1 if up else 3), 4),
        )

    sibling = me + 1 - 2 * core

    def copy_w(n):
        return pltpu.make_async_remote_copy(
            src_ref=half_of(wo_out.at[n], 0),
            dst_ref=half_of(wo_out.at[n], 0),
            send_sem=c_send.at[n],
            recv_sem=c_recv.at[n],
            device_id={"dp": sibling},
            device_id_type=pl.DeviceIdType.MESH,
        )

    def copy_w_in(n):
        rows = pl.ds(pl.multiple_of((1 - core) * half, half), half)
        return pltpu.make_async_remote_copy(
            src_ref=wo_out.at[n].at[rows, :],
            dst_ref=wo_out.at[n].at[rows, :],
            send_sem=c_send.at[n],
            recv_sem=c_recv.at[n],
            device_id={"dp": sibling},
            device_id_type=pl.DeviceIdType.MESH,
        )

    def any_hop(kind, d, up):
        return hop_w(d, up) if kind == 2 else hop(kind, d, up)

    def hops(kind, d):
        each_way(place, d, sends, lambda up: any_hop(kind, d, up).start())

    def hops_in(kind, d):
        each_way(place, d, receives, lambda up: any_hop(kind, d, up).wait_recv())

    def store(w):
        to = (oa_out.at[0], ob_out, oc_out)[w]
        return pltpu.make_async_copy(o_own.at[w], to, own_sem.at[w])

    def attend_rows(w, first, last):
        for pair in range(width // 128):
            lanes = slice(pair * 128, pair * 128 + 128)
            keys = slice(w * window, (w + 1) * window)

            def block(i, carry):
                rows = pl.ds(pl.multiple_of(w * window + i * q_block, q_block), q_block)
                into = pl.ds(pl.multiple_of(i * q_block, q_block), q_block)
                o_own[w, into, lanes] = attend(
                    q_ref[rows, lanes], k_ref[keys, lanes], v_ref[keys, lanes]
                )
                return carry

            lax.fori_loop(first, last, block, 0)

    def picked(pick, table):
        high = table.astype(bf16)
        low = (table - high.astype(f32)).astype(bf16)
        return mm(pick, high) + mm(pick, low)

    def project(w):
        rows = window // 2

        def block(n, carry):
            here = pl.ds(pl.multiple_of(n * rows, rows), rows)
            at = pl.ds(pl.multiple_of(w * window + n * rows, rows), rows)
            x = x_ref[w % 2, here, :].astype(f32)
            hidden = (x * rms_scale(x) * gains_ref[0:1, :]).astype(bf16)
            cos, sin = cos_ref[here, :], sin_ref[here, :]
            q = mm(hidden, w_ref[:, 0:width])
            q_ref[at, :] = (q * cos + swap_halves(q) * sin).astype(bf16)
            k = mm(hidden, w_ref[:, width : 2 * width])
            k_ref[at, :] = (k * cos + swap_halves(k) * sin).astype(bf16)
            v_ref[at, :] = mm(hidden, w_ref[:, 2 * width : 3 * width]).astype(bf16)
            return carry

        load_x(w).wait()
        lax.fori_loop(0, 2, block, 0)
        at = slice(w * count, (w + 1) * count)
        pick = (
            lax.broadcasted_iota(jnp.int32, (count, window), 1) == rows_in[w]
        ).astype(bf16)
        xm_ref[at, :] = mm(pick, x_ref[w % 2]).astype(bf16)
        if w + 2 < windows:
            load_x(w + 2).start()
        cosm_ref[at, :] = picked(pick, cos_ref[...])
        sinm_ref[at, :] = picked(pick, sin_ref[...])
        qm_ref[at, :] = mm(pick, q_ref[w * window : (w + 1) * window, :]).astype(bf16)

    for w in range(2):
        load_x(w).start()
    greet_line(place, [("dp", sibling)])
    blocks = window // q_block
    hops(2, 1)
    fold = tiles_ref.shape[1] // width
    for block in range(3 * width // 128):
        part, lane = divmod(block * 128, width)
        for piece in range(fold):
            at = piece * width + lane
            w_wide[block, pl.ds(piece, width, stride=fold), :] = tiles_ref[
                part * width : (part + 1) * width, at : at + 128
            ].astype(f32)
        w_ref[:, block * 128 : (block + 1) * 128] = w_wide[block].astype(bf16)
    project(0)
    hops_in(2, 1)
    hops(2, 2)
    attend_rows(0, 0, blocks)
    hops(1, 1)
    store(0).start()
    hops_in(2, 2)
    hops(2, 3)
    project(1)
    project(2)
    hops_in(1, 1)
    hops(1, 2)
    for w in range(windows):
        keys = slice(w * window, (w + 1) * window)
        at = slice(w * count, (w + 1) * count)
        for pair in range(width // 128):
            lanes = slice(pair * 128, pair * 128 + 128)
            om_own[at, lanes] = attend(
                qm_ref[at, lanes], k_ref[keys, lanes], v_ref[keys, lanes]
            )
    hops(0, 1)
    keep = pltpu.make_async_copy(om_own, om_out.at[0], keep_sem)
    keep.start()
    attend_rows(1, 0, blocks // 2)
    hops_in(0, 1)
    hops(0, 2)
    attend_rows(1, blocks // 2, blocks)
    store(1).start()
    hops_in(0, 2)
    hops(0, 3)
    hops_in(1, 2)
    hops(1, 3)
    attend_rows(2, 0, blocks)
    store(2).start()
    hops_in(2, 3)
    for n in range(3):
        copy_w(n).start()
    keep.wait()
    for w in range(windows):
        store(w).wait()
    for kind in range(2):
        hops_in(kind, 3)
    for kind in range(3):
        for d in range(1, 4):
            each_way(place, d, sends, lambda up: any_hop(kind, d, up).wait_send())
    for n in range(3):
        copy_w(n).wait_send()
        copy_w_in(n).wait_recv()


def masked_attention_back(qm, do, k, v):
    first = lax.broadcasted_iota(jnp.int32, qm.shape, 1) < HD
    zero = jnp.zeros((), bf16)
    parts = []
    drk = dv = None
    for head in range(2):
        mine = first if head == 0 else ~first
        q_head = jnp.where(mine, qm, zero)
        do_head = jnp.where(mine, do, zero)
        s = mm_nt(k, q_head)
        s = jnp.exp((s - jnp.max(s, axis=0, keepdims=True)) * score_scale)
        att = s / jnp.sum(s, axis=0, keepdims=True)
        dpa = mm_nt(v, do_head)
        ds = att * (dpa - jnp.sum(dpa * att, axis=0, keepdims=True))
        ds = (ds * score_scale).astype(bf16)
        parts.append(mm_tn(ds, k))
        drk_head = mm(ds, q_head)
        dv_head = mm(att.astype(bf16), do_head)
        drk = drk_head if drk is None else drk + drk_head
        dv = dv_head if dv is None else dv + dv_head
    return jnp.where(first, parts[0], parts[1]), drk, dv


def middle_kernel(
    windows,
    rows_in,
    gains_ref,
    xm_ref,
    cot_ref,
    qm_ref,
    cosm_ref,
    sinm_ref,
    cos_ref,
    sin_ref,
    w_ref,
    ffn_ref,
    om_ref,
    oa_ref,
    wo_ref,
    wo_far,
    *refs,
):
    wg_ref, wu_ref, wd_ref = (ffn_ref.at[n] for n in range(3))
    om_refs, oa_refs = ([ref.at[n] for n in range(4)] for ref in (om_ref, oa_ref))
    wo_refs = [wo_ref] + [wo_far.at[n] for n in range(3)]
    x_hbm, k_hbm, v_hbm, o_one, o_two = refs[0:5]
    part_out, own_out, ra_out, rb_out, dha_out, grads_out, drm_ref, gain_ref = refs[5:13]
    (
        r_ref,
        hf_ref,
        acc_ref,
        p_ref,
        own_ref,
        obuf,
        x_ref,
        kv,
        flow_ref,
        gw_acc,
        gw_wide,
        go_acc,
        rm_ref,
        dpart,
        drecv,
        dall,
        bsum,
        b_load,
        b_send,
        b_recv,
        o_load,
        x_sem,
        kv_sem,
        grad_sem,
        p_sem,
        dha_sem,
        own_sem,
        a_send,
        a_recv,
        o_send,
        o_recv,
        d_send,
        d_recv,
        e_send,
        e_recv,
    ) = refs[13:]
    place = lax.axis_index("tensor")
    lower = place < 2
    outer = (place == 0) | (place == 3)
    inner = (place == 1) | (place == 2)
    window, model = x_ref.shape
    width = kv.shape[3]
    hidden = ffn_ref.shape[2]
    share = own_ref.shape[0]
    count = rm_ref.shape[0] // windows
    masked = rm_ref.shape[0]
    cols = 256
    chunks = hidden // cols

    def hop(g, d, up):
        src, dst = (d - 1, d) if up else ((5 - d) % 4, 4 - d)
        n = 0 if up else 1
        return remote(
            obuf.at[g, src],
            obuf.at[g, dst],
            o_send.at[g, d - 1, n],
            o_recv.at[g, d - 1, n],
            lax.rem(place + (1 if up else 3), 4),
        )

    def hops(g, d):
        each_way(place, d, sends, lambda up: hop(g, d, up).start())

    def hops_in(g, d):
        each_way(place, d, receives, lambda up: hop(g, d, up).wait_recv())

    def load_o(g):
        return pltpu.make_async_copy((o_one, o_two)[g], obuf.at[g, 0], o_load.at[g])

    def load_x(w):
        return pltpu.make_async_copy(
            x_hbm.at[pl.ds(w * window, window), :], x_ref, x_sem
        )

    def load_kv(w):
        return [
            pltpu.make_async_copy(
                hbm.at[pl.ds(w * window, window), :], kv.at[w % 2, n], kv_sem.at[w % 2, n]
            )
            for n, hbm in enumerate((k_hbm, v_hbm))
        ]

    def store_p(to):
        return pltpu.make_async_copy(p_ref, to, p_sem)

    def store_own(w):
        return pltpu.make_async_copy(own_ref, own_out.at[w], own_sem)

    def copy_a(w, i):
        return remote(
            rows_ref(part_out.at[w], jnp.where(lower, 3 - i, i), share, 1),
            rows_ref(ra_out.at[w], jnp.where(lower, 2 - i, i), share, 1),
            a_send.at[w, i],
            a_recv.at[w, i],
            jnp.where(lower, 1, 2),
        )

    def copy_d(k):
        to = lax.rem(place + k, 4)
        return remote(dpart.at[to], drecv.at[k - 1], d_send.at[k - 1], d_recv.at[k - 1], to)

    def copy_e(k, origin):
        to = lax.rem(place + k, 4)
        return remote(dall.at[origin], dall.at[origin], e_send.at[k - 1], e_recv.at[k - 1], to)

    for g in range(2):
        load_o(g).start()
    load_x(0).start()
    for copy in load_kv(0):
        copy.start()
    greet_line(place)
    load_o(0).wait()
    hops(0, 1)
    gain_att, gain_ffn = gains_ref[0:1, :], gains_ref[1:2, :]

    def grad_copies(c):
        side = (c % 2) * 2 * cols
        base = 4 * width
        at = pl.ds(c * cols, cols)
        below = window - 2 * cols + (c % 2) * cols
        return [
            pltpu.make_async_copy(
                p_ref.at[:, pl.ds(side, cols)],
                grads_out.at[pl.ds(base, model), at],
                grad_sem.at[c % 2, 0],
            ),
            pltpu.make_async_copy(
                p_ref.at[:, pl.ds(side + cols, cols)],
                grads_out.at[pl.ds(base + hidden, model), at],
                grad_sem.at[c % 2, 1],
            ),
            pltpu.make_async_copy(
                hf_ref.at[pl.ds(below, cols), :],
                grads_out.at[pl.ds(base + 2 * hidden + c * cols, cols), :],
                grad_sem.at[c % 2, 2],
            ),
        ]

    def masked_chunk(c):
        if c >= 2:
            for copy in grad_copies(c - 2):
                copy.wait()
        at = slice(c * cols, (c + 1) * cols)
        side = (c % 2) * 2 * cols
        below = window - 2 * cols + (c % 2) * cols
        hf, dy = hf_ref[0:masked, :], cot_ref[...]
        wg, wu, wd = wg_ref[:, at], wu_ref[:, at], wd_ref[at, :]
        g, u = mm(hf, wg), mm(hf, wu)
        sig = jax.nn.sigmoid(g)
        act = (g * sig * u).astype(bf16)
        hf_ref[below : below + cols, :] = mm_tn(act, dy).astype(bf16)
        da = mm_nt(dy, wd)
        dg = (da * u * sig * (1.0 + g * (1.0 - sig))).astype(bf16)
        du = (da * g * sig).astype(bf16)
        p_ref[:, side : side + cols] = mm_tn(hf, dg).astype(bf16)
        p_ref[:, side + cols : side + 2 * cols] = mm_tn(hf, du).astype(bf16)
        part = mm_nt(dg, wg) + mm_nt(du, wu)
        if c == 0:
            acc_ref[0:masked, :] = part
        else:
            acc_ref[0:masked, :] += part
        for copy in grad_copies(c):
            copy.start()

    def ffn(w, o_refs, next_x, between=None):
        half = window // 2

        def first(n, carry):
            rows = pl.ds(pl.multiple_of(n * half, half), half)
            r = x_ref[rows, :].astype(f32)
            for o, wo in zip(o_refs, wo_refs):
                r = r + mm(o[rows, :], wo[...])
            r_ref[rows, :] = r
            hf_ref[rows, :] = (r * rms_scale(r) * gain_ffn).astype(bf16)
            return carry

        lax.fori_loop(0, 2, first, 0)
        if next_x is not None:
            load_x(next_x).start()
        acc_ref[...] = jnp.zeros_like(acc_ref)

        def chunk(c, carry):
            at = pl.ds(pl.multiple_of(c * cols, cols), cols)
            hf = hf_ref[...]
            g, u = mm(hf, wg_ref[:, at]), mm(hf, wu_ref[:, at])
            act = (g * jax.nn.sigmoid(g) * u).astype(bf16)
            acc_ref[...] += mm(act, wd_ref[at, :])
            return carry

        if between is None:
            lax.fori_loop(0, chunks, chunk, 0)
        else:
            lax.fori_loop(0, chunks - 1, chunk, 0)
            between()
            lax.fori_loop(chunks - 1, chunks, chunk, 0)
        p_ref[...] = acc_ref[...].astype(bf16)
        store_p(part_out.at[w]).start()
        mine = pl.ds(pl.multiple_of(place * share, share), share)
        own_ref[...] = r_ref[mine, :] + acc_ref[mine, :]
        store_own(w).start()
        store_p(part_out.at[w]).wait()
        store_own(w).wait()

    def inward(w, blocks):
        @pl.when(outer)
        def _():
            for i in blocks:
                copy_a(w, i).start()

    def sum_dhf():
        for k in range(1, 4):
            copy_d(k).wait_recv()
        total = dpart[place].astype(f32)
        for k in range(3):
            total = total + drecv[k].astype(f32)
        dall[place] = total.astype(bf16)
        for k in range(1, 4):
            copy_e(k, place).start()

    r = xm_ref[...].astype(f32)
    for om, wo in zip(om_refs, wo_refs):
        r = r + mm(om[...], wo[...])
    rm_ref[...] = r
    hf_ref[0:masked, :] = (r * rms_scale(r) * gain_ffn).astype(bf16)
    for c in range(chunks // 2):
        masked_chunk(c)
    hops_in(0, 1)
    hops(0, 2)
    for c in range(chunks // 2, chunks):
        masked_chunk(c)
    block = model // 4
    for n in range(4):
        dpart[n] = acc_ref[0:masked, n * block : (n + 1) * block].astype(bf16)
    for k in range(1, 4):
        copy_d(k).start()
    hops_in(0, 2)
    hops(0, 3)
    for c in range(chunks - 2, chunks):
        for copy in grad_copies(c):
            copy.wait()

    load_o(1).wait()
    load_x(0).wait()
    ffn(0, oa_refs, 1)
    inward(0, (0,))
    hops_in(0, 3)
    hops(1, 1)
    load_x(1).wait()

    def meanwhile():
        sum_dhf()
        inward(0, (1, 2))

    ffn(1, [obuf.at[0, n] for n in range(4)], 0, meanwhile)
    inward(1, (0, 1, 2))
    hops_in(1, 1)
    hops(1, 2)
    hops_in(1, 2)
    hops(1, 3)

    def copy_b(w):
        return remote(
            bsum.at[w], rb_out.at[w], b_send.at[w], b_recv.at[w], jnp.where(lower, 2, 1)
        )

    def exchange_rows(w):
        @pl.when(inner)
        def _():
            for i in range(3):
                copy_a(w, i).wait_recv()
            rows = rows_ref(ra_out.at[w], jnp.where(lower, 1, 0), share, 2)
            mine = rows_ref(part_out.at[w], jnp.where(lower, 2, 0), share, 2)
            got = pltpu.make_async_copy(rows, bsum.at[w], b_load.at[0])
            add = pltpu.make_async_copy(mine, hf_ref.at[pl.ds(0, 2 * share), :], b_load.at[1])
            got.start()
            add.start()
            got.wait()
            add.wait()
            total = bsum[w].astype(f32) + hf_ref[0 : 2 * share, :].astype(f32)
            bsum[w] = total.astype(bf16)
            copy_b(w).start()

    for k in range(1, 4):
        copy_e(k, lax.rem(place + 4 - k, 4)).wait_recv()
    gw_acc[...] = jnp.zeros_like(gw_acc)
    go_acc[...] = jnp.zeros_like(go_acc)
    gain_ref[...] = jnp.zeros_like(gain_ref)
    def back_window(w, next_x):
        for copy in load_kv(w):
            copy.wait()
        if w + 1 < windows:
            for copy in load_kv(w + 1):
                copy.start()
        at = slice(w * count, (w + 1) * count)
        r = rm_ref[at, :]
        sf = rms_scale(r)
        nf = r * sf
        dhf = jnp.concatenate([dall[n, at, :] for n in range(4)], axis=1).astype(f32)
        dnf = dhf * gain_ffn
        dr = cot_ref[at, :].astype(f32) + sf * (
            dnf - nf * jnp.mean(dnf * nf, axis=-1, keepdims=True)
        )
        drm_ref[at, :] = dr
        gain_ref[1:2, :] += jnp.sum(dhf * nf, axis=0, keepdims=True)
        drb = dr.astype(bf16)
        go_acc[...] += mm_tn(om_refs[0][at, :], drb)
        dob = mm_nt(drb, wo_refs[0][...]).astype(bf16)
        spread = (
            lax.broadcasted_iota(jnp.int32, (window, count), 0) == rows_in[w]
        ).astype(bf16)
        for pair in range(width // 128):
            lanes = slice(pair * 128, pair * 128 + 128)
            drq, drk, dv = masked_attention_back(
                qm_ref[at, lanes], dob[:, lanes], kv[w % 2, 0, :, lanes], kv[w % 2, 1, :, lanes]
            )
            dk = drk * cos_ref[:, lanes] - swap_halves(drk) * sin_ref[:, lanes]
            dq = drq * cosm_ref[at, lanes] - swap_halves(drq) * sinm_ref[at, lanes]
            first = pair * 128
            flow_ref[:, first : first + 128] = mm(spread, dq.astype(bf16)).astype(bf16)
            flow_ref[:, width + first : width + first + 128] = dk.astype(bf16)
            flow_ref[:, 2 * width + first : 2 * width + first + 128] = dv.astype(bf16)
        load_x(w).wait()

        def back(n, carry):
            rows = pl.ds(pl.multiple_of(n * share, share), share)
            x = x_ref[rows, :].astype(f32)
            na = x * rms_scale(x)
            dha = mm_nt(flow_ref[rows, :], w_ref[...])
            gain_ref[0:1, :] += jnp.sum(dha * na, axis=0, keepdims=True)
            p_ref[rows, :] = dha.astype(bf16)
            hf_ref[rows, :] = (na * gain_att).astype(bf16)
            return carry

        lax.fori_loop(0, window // share, back, 0)
        for copy in dha_copies(dha_out, p_ref, dha_sem, w, windows, share):
            copy.start()
        if next_x is not None:
            load_x(next_x).start()
        gw_acc[...] += mm_tn(hf_ref[...], flow_ref[...])

    def dha_stored(w):
        for copy in dha_copies(dha_out, p_ref, dha_sem, w, windows, share):
            copy.wait()

    back_window(0, 1)
    dha_stored(0)
    back_window(1, 2)
    dha_stored(1)
    exchange_rows(0)
    back_window(2, None)
    dha_stored(2)
    hops_in(1, 3)
    ffn(2, [obuf.at[1, n] for n in range(4)], None)
    fold = model // width
    for block in range(3 * width // 128):
        part, lane = divmod(block * 128, width)
        gw_wide[...] = gw_acc[:, block * 128 : (block + 1) * 128]
        for piece in range(fold):
            at = piece * width + lane
            p_ref[part * width : (part + 1) * width, at : at + 128] = gw_wide[
                pl.ds(piece, width, stride=fold), :
            ].astype(bf16)
    p_ref[3 * width :, :] = go_acc[...].astype(bf16)
    store = store_p(grads_out.at[pl.ds(0, 4 * width), :])
    store.start()
    store.wait()

    @pl.when(outer)
    def _():
        for w in range(2):
            for i in range(3):
                copy_a(w, i).wait_send()

    @pl.when(inner)
    def _():
        for i in range(3):
            copy_a(1, i).wait_recv()
        copy_b(0).wait_send()
        copy_b(0).wait_recv()

    for k in range(1, 4):
        copy_d(k).wait_send()
        copy_e(k, place).wait_send()
    for g in range(2):
        for d in range(1, 4):
            each_way(place, d, sends, lambda up: hop(g, d, up).wait_send())


def dha_copies(dha_out, p_ref, sem, w, windows, share):
    copies = []
    per = p_ref.shape[0] // share
    for n in range(per):
        block = w * per + n
        copies.append(
            pltpu.make_async_copy(
                p_ref.at[pl.ds(n * share, share), :],
                dha_out.at[block % windows, pl.ds(block // windows * share, share), :],
                sem.at[n],
            )
        )
    return copies


def lines_kernel(
    cuts,
    windows,
    order,
    ready,
    traded,
    rows_in,
    drm_ref,
    gains_ref,
    x_ref,
    dha_ref,
    part_ref,
    own_in,
    ra_in,
    rb_in,
    gain_in,
    out_ref,
    grad_ref,
    gain_ref,
    ra,
    rb,
    rc,
    value,
    own,
    piece,
    x_rows,
    grad,
    gain_sum,
    gain_got,
    s_send,
    s_recv,
    a_send,
    a_recv,
    b_send,
    b_recv,
    c_send,
    c_recv,
    g_send,
    g_recv,
    v_sem,
    o_sem,
    r_sem,
    t_sem,
    x_sem,
    l_sem,
    i_sem,
):
    place = lax.axis_index("tensor")
    lower = place < 2
    outer = (place == 0) | (place == 3)
    inner = (place == 1) | (place == 2)
    share = rc.shape[1]
    folds = len(order)
    next_in = jnp.where(lower, 1, 2)
    inner_far = 3 - place
    outer_near = jnp.where(lower, 0, 3)
    outer_far = 3 - outer_near

    def block(ref, index):
        return rows_ref(ref, index, share, 1)

    def whole(f):
        kind, index = order[f]
        return part_ref.at[index] if kind == 0 else dha_ref.at[index]

    def copy_a(f, i):
        return remote(
            block(whole(f), jnp.where(lower, 3 - i, i)),
            block(ra.at[f], jnp.where(lower, 2 - i, i)),
            a_send.at[f, i],
            a_recv.at[f, i],
            next_in,
        )

    def copy_b(f, i):
        return remote(
            block(ra.at[f], jnp.where(lower, 2 - i, i)),
            block(rb.at[f], jnp.where(lower, 1 - i, i)),
            b_send.at[f, i],
            b_recv.at[f, i],
            jnp.where(lower, 2, 1),
        )

    def copy_c(f):
        src = block(rb.at[f], jnp.where(lower, 0, 1))
        return remote(src, rc.at[f], c_send.at[f], c_recv.at[f], outer_near)

    def load(f):
        return pltpu.make_async_copy(whole(f), value.at[f], v_sem.at[f])

    def load_own(w):
        return pltpu.make_async_copy(own_in.at[w], own.at[w], o_sem.at[w])

    def load_ra(f):
        return pltpu.make_async_copy(ra_in.at[order[f][1]], ra.at[f], r_sem.at[f])

    def load_rb(f):
        return pltpu.make_async_copy(rb_in.at[order[f][1]], rb.at[f], t_sem.at[f])

    def rows_of(w, origin):
        return pl.ds(pl.multiple_of((w * 4 + origin) * share, share), share)

    def pass_on(w, origin, way, n, target):
        rows = rows_of(w, origin)
        return remote(
            piece.at[w] if way < 2 else out_ref.at[rows, :],
            out_ref.at[rows, :],
            g_send.at[w, way],
            g_recv.at[w, n],
            target,
        )

    def got(w, n):
        origin = (
            jnp.where(outer, next_in, inner_far),
            jnp.where(outer, 3 - next_in, outer_near),
            jnp.where(outer, 3 - place, outer_far),
        )[n]
        rows = rows_of(w, origin)
        return remote(
            out_ref.at[rows, :], out_ref.at[rows, :], g_send.at[w, 0], g_recv.at[w, n], inner_far
        )

    def keep(w):
        return pltpu.make_async_copy(
            piece.at[w], out_ref.at[rows_of(w, place), :], l_sem.at[w]
        )

    def store(c):
        return pltpu.make_async_copy(
            grad.at[c], grad_ref.at[pl.ds(c * share, share), :], i_sem.at[c]
        )

    x_load = pltpu.make_async_copy(
        rows_ref(x_ref, place * cuts, share, cuts), x_rows, x_sem
    )

    for w in range(windows):
        load(w).start()
        load_own(w).start()
    for f in range(windows, folds):
        load(f).start()
    x_load.start()

    pairs = []
    for axis in ("dp", "tensor"):
        index, bit = lax.axis_index(axis), 1
        while bit < lax.axis_size(axis):
            pairs.append((axis, index + bit - 2 * bit * lax.rem(index // bit, 2)))
            bit *= 2

    def copy_s(t):
        axis, other = pairs[t]
        return pltpu.make_async_remote_copy(
            src_ref=gain_sum.at[t],
            dst_ref=gain_got.at[t],
            send_sem=s_send.at[t],
            recv_sem=s_recv.at[t],
            device_id={axis: other},
            device_id_type=pl.DeviceIdType.MESH,
        )

    def next_pair(t):
        if t > 0:
            copy_s(t - 1).wait_recv()
            gain_sum[t] = gain_sum[t - 1] + gain_got[t - 1]
        if t < len(pairs):
            copy_s(t).start()

    gain_sum[0] = jnp.zeros(gain_sum.shape[1:], f32)
    gain_sum[0, 0:2, :] = gain_in[...]

    def rows_at_(index):
        return pl.ds(pl.multiple_of(index * share, share), share)

    def finish(f, terms):
        kind, index = order[f]
        if kind == 0:
            load_own(index).wait()
            total = own[index]
        else:
            total = value[f, rows_at_(place), :].astype(f32)
        for term in terms:
            total = total + term.astype(f32)
        if kind == 0:
            piece[index] = total.astype(bf16)
            keep(index).start()
        else:
            first = place * (cuts * share) + index * share
            count = drm_ref.shape[0]
            spread = (
                lax.broadcasted_iota(jnp.int32, (share, count), 0) + first == rows_in[...]
            ).astype(bf16)
            x = x_rows[pl.ds(index * share, share), :].astype(f32)
            grad[index] = input_grad_rows(
                total, x, drm_ref[...], gains_ref[0:1, :], spread
            ).astype(bf16)
            store(index).start()

    greet_line(place, [pair for pair in pairs if pair[0] == "dp"])

    @pl.when(outer)
    def _():
        chunks = [(f, i) for f in range(ready, folds) for i in range(3)]

        def step(n):
            copy_a(*chunks[n]).wait_send()
            if n + 2 < len(chunks):
                copy_a(*chunks[n + 2]).start()

        def total(f):
            copy_c(f).wait_recv()
            if order[f][0] == 1:
                load(f).wait()
            finish(f, [rc[f]])
            if order[f][0] == 0:
                pass_on(f, place, 0, 1, next_in).start()

        for n in range(2):
            copy_a(*chunks[n]).start()
        next_pair(0)
        total(0)
        step(0)
        step(1)
        next_pair(1)
        total(1)
        step(2)
        step(3)
        step(4)
        next_pair(2)
        total(2)
        next_pair(3)
        step(5)
        step(6)
        x_load.wait()
        total(3)
        next_pair(4)
        for n in range(7, 12):
            step(n)
        total(4)
        next_pair(5)
        total(5)
        for w in range(windows):
            load(w).wait()
            pass_on(w, place, 0, 1, next_in).wait_send()
            for n in range(3):
                got(w, n).wait_recv()

    @pl.when(inner)
    def _():
        for f in range(ready):
            load_ra(f).start()
        for f in range(traded):
            load_rb(f).start()

        def give_b(f):
            load(f).wait()
            if f < ready:
                load_ra(f).wait()
            for i in range(2):
                if f >= ready:
                    copy_a(f, i).wait_recv()
                to = rows_at_(jnp.where(lower, 2 - i, i))
                mine = value[f, rows_at_(jnp.where(lower, 3 - i, i)), :]
                ra[f, to, :] = (ra[f, to, :].astype(f32) + mine.astype(f32)).astype(bf16)
                copy_b(f, i).start()

        def total(f):
            if f < traded:
                load(f).wait()
                load_ra(f).wait()
                load_rb(f).wait()
            else:
                came(f, 0)
            to = rows_at_(jnp.where(lower, 0, 1))
            mine = value[f, rows_at_(outer_near), :]
            rb[f, to, :] = (rb[f, to, :].astype(f32) + mine.astype(f32)).astype(bf16)
            copy_c(f).start()
            if f >= traded:
                came(f, 1)
            if f >= ready:
                copy_a(f, 2).wait_recv()
            near = rows_at_(jnp.where(lower, 0, 2))
            other = rows_at_(jnp.where(lower, 1, 0))
            finish(f, [ra[f, near, :], rb[f, other, :]])
            if order[f][0] == 0:
                pass_on(f, place, 0, 0, inner_far).start()
                pass_on(f, place, 1, 0, outer_near).start()

        def came(f, i):
            to = block(rb.at[f], jnp.where(lower, i, 1 - i))
            remote(to, to, b_send.at[f, i], b_recv.at[f, i], inner_far).wait_recv()

        def from_far_inner(w):
            got(w, 0).wait_recv()
            pass_on(w, inner_far, 2, 1, outer_near).start()

        def from_outer(w):
            got(w, 1).wait_recv()
            pass_on(w, outer_near, 3, 2, inner_far).start()

        def from_far_outer(w):
            got(w, 2).wait_recv()
            pass_on(w, outer_far, 4, 2, outer_near).start()

        next_pair(0)
        total(0)
        give_b(1)
        next_pair(1)
        from_far_inner(0)
        total(1)
        next_pair(2)
        give_b(2)
        from_outer(0)
        from_far_inner(1)
        total(2)
        next_pair(3)
        from_far_outer(0)
        from_far_inner(2)
        give_b(3)
        from_outer(1)
        from_far_outer(1)
        x_load.wait()
        total(3)
        next_pair(4)
        from_outer(2)
        give_b(4)
        from_far_outer(2)
        total(4)
        give_b(5)
        total(5)
        next_pair(5)
        for f in range(folds):
            copy_c(f).wait_send()
            for i in range(2):
                if f >= traded:
                    copy_b(f, i).wait_send()
        for w in range(windows):
            pass_on(w, place, 0, 0, inner_far).wait_send()
            pass_on(w, place, 1, 0, outer_near).wait_send()
            pass_on(w, inner_far, 2, 1, outer_near).wait_send()
            pass_on(w, outer_near, 3, 2, inner_far).wait_send()
            pass_on(w, outer_far, 4, 2, outer_near).wait_send()

    gain_ref[...] = gain_sum[len(pairs), 0:2, :]
    for t in range(len(pairs)):
        copy_s(t).wait_send()
    for w in range(windows):
        keep(w).wait()
    for c in range(cuts):
        store(c).wait()


def place_kernel(place_ref, *refs):
    out_ref = refs[-1]
    parts = lax.axis_size("tensor")
    share = refs[0].shape[0]
    for step in range(parts):
        origin = lax.rem(place_ref[0] + parts - step, parts)
        out_ref[pl.ds(pl.multiple_of(origin * share, share), share), :] = refs[step][...]


def spread_kernel(tile_ref, used_ref, *refs):
    out_ref = refs[-1]
    step = pl.program_id(0)
    per = len(refs) - 1
    for n in range(per):
        used = used_ref[step * per + n] > 0

        @pl.when(used)
        def _():
            out_ref[n] = refs[n][0]

        @pl.when(jnp.logical_not(used))
        def _():
            out_ref[n] = jnp.zeros(out_ref.shape[1:], bf16)


def copy_kernel(in_ref, out_ref):
    out_ref[...] = in_ref[...]


def collect_kernel(slot_ref, *refs):
    out_ref = refs[-1]
    for index, ref in enumerate(refs[:-1]):
        out_ref[index] = ref[0]


def exchange(value, axis, bit):
    size = lax.axis_size(axis)
    return lax.ppermute(value, axis, [(i, i ^ bit) for i in range(size)])


def dp_total(value):
    size = lax.axis_size("dp")
    value = value + exchange(value, "dp", 1)
    bits = []
    bit = 2
    while bit < size:
        bits.append(bit)
        bit *= 2
    core = lax.axis_index("dp") % 2
    half = value.shape[0] // 2
    mine = lax.dynamic_slice_in_dim(value, core * half, half, 0)
    cut = half // 2
    low, high = mine[:cut], mine[cut:]
    for bit_low, bit_high in zip(bits, bits[::-1]):
        low = low + exchange(low, "dp", bit_low)
        high = high + exchange(high, "dp", bit_high)
    mine = jnp.concatenate([low, high], axis=0)
    other = exchange(mine, "dp", 1)
    return jnp.where(
        core == 0,
        jnp.concatenate([mine, other], axis=0),
        jnp.concatenate([other, mine], axis=0),
    )


def around(value):
    size = lax.axis_size("tensor")
    return [value] + [
        lax.ppermute(value, "tensor", [(i, (i + k) % size) for i in range(size)])
        for k in range(1, size)
    ]


def rows_at(value, index, share, count):
    return lax.dynamic_slice_in_dim(value, index * share, count * share, 0)


def other_sums(value, share):
    place = lax.axis_index("tensor")
    total = lax.psum_scatter(value, "tensor", scatter_dimension=0, tiled=True)
    own = rows_at(value, place, share, 1).astype(f32)
    return (total.astype(f32) - own,)


def small_total(value):
    for axis in ("dp", "tensor"):
        bit = 1
        while bit < lax.axis_size(axis):
            value = value + exchange(value, axis, bit)
            bit *= 2
    return value


def slot_ranks(owner_row):
    count_all = owner_row.shape[0]
    tile_order = jnp.arange(count_all, dtype=jnp.int32)
    earlier = (owner_row[:, None] == owner_row[None, :]) & (
        tile_order[None, :] < tile_order[:, None]
    )
    return jnp.sum(earlier.astype(jnp.int32), axis=1)


def adam_update(grad_now, first_old, second_old, param_old, rate, decay):
    first_new = beta_one * first_old + (1.0 - beta_one) * grad_now
    second_new = beta_two * second_old + (1.0 - beta_two) * grad_now * grad_now
    first_hat = first_new / (1.0 - beta_one**STEP)
    second_hat = second_new / (1.0 - beta_two**STEP)
    param_new = param_old - rate * (
        first_hat / (jnp.sqrt(second_hat) + adam_eps) + decay * param_old
    )
    return (first_new, second_new, param_new)


def head_tables(positions, heads, lib):
    frequency = lib.exp(
        -lib.log(lib.float32(10000.0))
        * (2.0 * lib.arange(HD // 2, dtype=lib.float32) / HD).astype(lib.float32)
    )
    angles = positions.astype(lib.float32)[..., None] * frequency
    cos, sin = lib.cos(angles), lib.sin(angles)
    cos = lib.concatenate([cos, cos], axis=-1)
    sin = lib.concatenate([-sin, sin], axis=-1)
    reps = (1,) * (cos.ndim - 1) + (heads,)
    return lib.tile(cos, reps), lib.tile(sin, reps)


def on_device(
    tokens,
    masked_rows,
    cotangent,
    norm_gains,
    gain_first,
    gain_second,
    owners,
    master,
    first_moment,
    second_moment,
):
    seq_count, mask_count = masked_rows.shape
    total_rows, model = tokens.shape
    window = total_rows // seq_count
    parts = lax.axis_size("tensor")
    place = lax.axis_index("tensor")
    owner_self = lax.axis_index("dp")
    heads = HEADS // parts
    width = heads * HD
    hidden = FF // parts
    capacity, tile_rows = master.shape[1:3]
    tile_size = tile_rows * model
    attn_tiles = 4 * model * width // tile_size
    ffn_tiles = 3 * model * hidden // tile_size
    count = -(-mask_count // 16) * 16
    place_ref = place.astype(jnp.int32).reshape(1)

    owner_row = owners[0]
    slot_rank = slot_ranks(owner_row)
    slot_index = owner_row * capacity + slot_rank
    slot_match = (owner_row[None, :] == owner_self) & (
        slot_rank[None, :] == jnp.arange(capacity, dtype=jnp.int32)[:, None]
    )
    slot_used = jnp.any(slot_match, axis=1)[:, None, None]
    slot_tile = jnp.argmax(slot_match, axis=1)

    mask_rows = seq_count * count
    share = window // parts
    share_rows = total_rows // parts
    dp_size = lax.axis_size("dp")
    lines = dp_size == 8 and attn_tiles == 8 and parts == 4 and seq_count == 3 and hidden == model and mask_rows <= window // 2
    anywhere = pl.BlockSpec(memory_space=pl.ANY)
    inside = pl.BlockSpec(memory_space=pltpu.VMEM)
    dma = pltpu.SemaphoreType.DMA

    tile_block = (1, tile_rows, model)
    if lines:
        small = pl.BlockSpec(memory_space=pltpu.SMEM)
        half_tiles = attn_tiles // 2
        low_slots, attn_sums = pl.pallas_call(
            weights_kernel,
            out_shape=[
                jax.ShapeDtypeStruct((capacity, tile_rows, model), bf16),
                jax.ShapeDtypeStruct((attn_tiles, tile_rows, model), bf16),
            ],
            in_specs=[small, small, inside],
            out_specs=[inside, anywhere],
            scratch_shapes=[
                pltpu.VMEM((attn_tiles, tile_rows, model), bf16),
                pltpu.VMEM((half_tiles, tile_rows, model), bf16),
                pltpu.VMEM((3, half_tiles, tile_rows, model), bf16),
                pltpu.VMEM((2, half_tiles, tile_rows, model), bf16),
                dma,
                dma,
                dma((2, half_tiles)),
                dma((2, half_tiles)),
                dma((half_tiles,)),
                dma((half_tiles,)),
                dma((half_tiles,)),
            ],
            compiler_params=params(collective_id=4, has_side_effects=True),
            cost_estimate=cost(0, 12e6),
            name="weights",
        )(
            slot_rank[:attn_tiles],
            (owner_row[:attn_tiles] == owner_self).astype(jnp.int32),
            master[0],
        )
        attn_flat = attn_sums.reshape(4 * width, model)
    else:
        grid_size = max(capacity, attn_tiles)
        low_slots, attn_mine = pl.pallas_call(
            cast_kernel,
            out_shape=[
                jax.ShapeDtypeStruct((capacity, tile_rows, model), bf16),
                jax.ShapeDtypeStruct((attn_tiles, tile_rows, model), bf16),
            ],
            grid_spec=pltpu.PrefetchScalarGridSpec(
                num_scalar_prefetch=2,
                grid=(grid_size,),
                in_specs=[
                    pl.BlockSpec(
                        tile_block, lambda i, rank, held: (jnp.minimum(i, capacity - 1), 0, 0)
                    ),
                    pl.BlockSpec(
                        tile_block,
                        lambda i, rank, held: (rank[jnp.minimum(i, attn_tiles - 1)], 0, 0),
                    ),
                ],
                out_specs=[
                    pl.BlockSpec(
                        tile_block, lambda i, rank, held: (jnp.minimum(i, capacity - 1), 0, 0)
                    ),
                    pl.BlockSpec(
                        tile_block, lambda i, rank, held: (jnp.minimum(i, attn_tiles - 1), 0, 0)
                    ),
                ],
            ),
            compiler_params=params(),
            cost_estimate=cost(0, 12 * capacity * tile_size),
            name="cast",
        )(
            slot_rank,
            jnp.pad(
                (owner_row[:attn_tiles] == owner_self).astype(jnp.int32),
                (0, grid_size - attn_tiles),
                mode="edge",
            ),
            master[0],
            master[0],
        )
        attn_flat = dp_total(attn_mine).reshape(4 * width, model)
    w_out = attn_flat[3 * width :]
    every_slot = lax.all_gather(low_slots, "dp", axis=0, tiled=True)

    cos, sin = map(jnp.asarray, head_tables(np.arange(window), heads, np))
    rows = jnp.pad(masked_rows, ((0, 0), (0, count - mask_count)), constant_values=-1)
    cot = jnp.pad(cotangent, ((0, 0), (0, count - mask_count), (0, 0)))
    cot = cot.reshape(seq_count * count, model)

    win_model = pl.BlockSpec((window, model), lambda i: (i, 0))
    win_head = pl.BlockSpec((window, width), lambda i: (i, 0))
    mask_model = pl.BlockSpec((count, model), lambda i: (i, 0))
    mask_head = pl.BlockSpec((count, width), lambda i: (i, 0))
    if lines:
        (
            o_m,
            o_first,
            o_second,
            o_third,
            w_far,
            q_m,
            x_m,
            cos_m,
            sin_m,
            k,
            v,
            w_qkv,
        ) = pl.pallas_call(
            functools.partial(attend_all_kernel, seq_count),
            out_shape=[
                jax.ShapeDtypeStruct((4, mask_rows, width), bf16),
                jax.ShapeDtypeStruct((4, window, width), bf16),
                jax.ShapeDtypeStruct((window, width), bf16),
                jax.ShapeDtypeStruct((window, width), bf16),
                jax.ShapeDtypeStruct((3, width, model), bf16),
                jax.ShapeDtypeStruct((mask_rows, width), bf16),
                jax.ShapeDtypeStruct((mask_rows, model), bf16),
                jax.ShapeDtypeStruct((mask_rows, width), f32),
                jax.ShapeDtypeStruct((mask_rows, width), f32),
                jax.ShapeDtypeStruct((total_rows, width), bf16),
                jax.ShapeDtypeStruct((total_rows, width), bf16),
                jax.ShapeDtypeStruct((model, 3 * width), bf16),
            ],
            in_specs=[inside] * 5 + [anywhere] * 2,
            out_specs=[anywhere] * 5 + [inside] * 7,
            scratch_shapes=[
                pltpu.VMEM((total_rows, width), bf16),
                pltpu.VMEM((3 * width // 128, model, 128), f32),
                pltpu.VMEM((mask_rows, width), bf16),
                pltpu.VMEM((seq_count, window, width), bf16),
                pltpu.VMEM((2, window, model), bf16),
                dma((2,)),
                dma((seq_count,)),
                dma,
                dma((3, 2)),
                dma((3, 2)),
                dma((3, 2)),
                dma((3, 2)),
                dma((3, 2)),
                dma((3, 2)),
                dma((3,)),
                dma((3,)),
            ],
            compiler_params=params(collective_id=3, has_side_effects=True),
            cost_estimate=cost(4e10, 20e6),
            name="attend_all",
        )(rows[:, :, None], norm_gains, attn_flat, cos, sin, tokens, attn_flat)
        before_tiles = o_third
    else:
        block = min(512, window)
        per_window = window // block
        row_block = pl.BlockSpec((block, model), lambda i: (i, 0))
        head_block = pl.BlockSpec((block, width), lambda i: (i, 0))
        table_block = pl.BlockSpec((block, width), lambda i: (i % per_window, 0))
        q, k, v, w_qkv = pl.pallas_call(
            qkv_kernel,
            out_shape=[jax.ShapeDtypeStruct((total_rows, width), bf16)] * 3
            + [jax.ShapeDtypeStruct((model, 3 * width), bf16)],
            grid=(total_rows // block,),
            in_specs=[
                row_block,
                whole_spec((2, model)),
                whole_spec((3 * width, model)),
                table_block,
                table_block,
            ],
            out_specs=[head_block] * 3 + [whole_spec((model, 3 * width))],
            scratch_shapes=[pltpu.VMEM((3 * width // 128, model, 128), f32)],
            compiler_params=params(),
            cost_estimate=cost(6 * total_rows * model * width, 2 * total_rows * model * 2),
            name="qkv",
        )(tokens, norm_gains, attn_flat, cos, sin)

        o_m, q_m, x_m = pl.pallas_call(
            attend_masked_kernel,
            out_shape=[
                jax.ShapeDtypeStruct((seq_count * count, width), bf16),
                jax.ShapeDtypeStruct((seq_count * count, width), bf16),
                jax.ShapeDtypeStruct((seq_count * count, model), bf16),
            ],
            grid=(seq_count,),
            in_specs=[
                pl.BlockSpec((1, count, 1), lambda i: (i, 0, 0)),
                win_model,
                win_head,
                win_head,
                win_head,
            ],
            out_specs=[mask_head, mask_head, mask_model],
            compiler_params=params(),
            cost_estimate=cost(
                seq_count * count * window * (2 * model + 8 * width), 9e6, seq_count * count * window * heads
            ),
            name="attend_masked",
        )(rows[:, :, None], tokens, q, k, v)
        o_ms = around(o_m)

        q_block = min(256, window)

        def attend_window(w, before):
            return pl.pallas_call(
                after(attend_kernel, 3, 1),
                out_shape=jax.ShapeDtypeStruct((window, width), bf16),
                grid=(width // 128, window // q_block),
                in_specs=[
                    pl.BlockSpec((q_block, 128), lambda p, i: (w * (window // q_block) + i, p)),
                    pl.BlockSpec((window, 128), lambda p, i: (w, p)),
                    pl.BlockSpec((window, 128), lambda p, i: (w, p)),
                    UNREAD,
                ],
                out_specs=pl.BlockSpec((q_block, 128), lambda p, i: (i, p)),
                compiler_params=params(),
                cost_estimate=cost(
                    16 * window * window * width, 4 * window * width * 2, window * window * heads
                ),
                name="attend",
            )(q, k, v, before)

        early = max(seq_count - 1, 1)
        o_own = []
        for w in range(early):
            o_own.append(attend_window(w, o_own[-1] if o_own else o_m))
        before_tiles = o_own[-1]
        cos_m, sin_m = (
            table.reshape(mask_rows, width) for table in head_tables(rows, heads, jnp)
        )

    group = 4
    ffn_all = pl.pallas_call(
        after(collect_kernel, 1 + group, 1),
        out_shape=jax.ShapeDtypeStruct((ffn_tiles, tile_rows, model), bf16),
        grid_spec=pltpu.PrefetchScalarGridSpec(
            num_scalar_prefetch=1,
            grid=(ffn_tiles // group,),
            in_specs=[
                pl.BlockSpec(
                    tile_block,
                    lambda i, slot, n=n: (slot[attn_tiles + i * group + n], 0, 0),
                )
                for n in range(group)
            ]
            + [UNREAD],
            out_specs=pl.BlockSpec((group, tile_rows, model), lambda i, slot: (i, 0, 0)),
        ),
        compiler_params=params(),
        cost_estimate=cost(0, 4 * ffn_tiles * tile_size),
        name="collect",
    )(slot_index, *[every_slot] * group, before_tiles)
    even = jnp.array([[1.0], [1.0 / parts]], f32)
    flat_rows = jnp.where(
        rows >= 0, rows + window * jnp.arange(seq_count, dtype=jnp.int32)[:, None], -1
    ).reshape(1, mask_rows)
    if lines:
        grad_rows = 4 * width + 3 * hidden
        part, own, first_sums, second_sums, dha, grads, dr_m, gains_part = pl.pallas_call(
            functools.partial(middle_kernel, seq_count),
            out_shape=[
                jax.ShapeDtypeStruct((seq_count, window, model), bf16),
                jax.ShapeDtypeStruct((seq_count, share, model), f32),
                jax.ShapeDtypeStruct((2, 3 * share, model), bf16),
                jax.ShapeDtypeStruct((1, 2 * share, model), bf16),
                jax.ShapeDtypeStruct((seq_count, window, model), bf16),
                jax.ShapeDtypeStruct((grad_rows, model), bf16),
                jax.ShapeDtypeStruct((mask_rows, model), f32),
                jax.ShapeDtypeStruct((2, model), f32),
            ],
            in_specs=[inside] * 15 + [anywhere] * 5,
            out_specs=[anywhere] * 6 + [inside] * 2,
            scratch_shapes=[
                pltpu.VMEM((window, model), f32),
                pltpu.VMEM((window, model), bf16),
                pltpu.VMEM((window, model), f32),
                pltpu.VMEM((window, model), bf16),
                pltpu.VMEM((share, model), f32),
                pltpu.VMEM((2, 4, window, width), bf16),
                pltpu.VMEM((window, model), bf16),
                pltpu.VMEM((2, 2, window, width), bf16),
                pltpu.VMEM((window, 3 * width), bf16),
                pltpu.VMEM((model, 3 * width), f32),
                pltpu.VMEM((model, 128), f32),
                pltpu.VMEM((width, model), f32),
                pltpu.VMEM((mask_rows, model), f32),
                pltpu.VMEM((4, mask_rows, model // 4), bf16),
                pltpu.VMEM((3, mask_rows, model // 4), bf16),
                pltpu.VMEM((4, mask_rows, model // 4), bf16),
                pltpu.VMEM((1, 2 * share, model), bf16),
                dma((2,)),
                dma((1,)),
                dma((1,)),
                dma((2,)),
                dma,
                dma((2, 2)),
                dma((2, 3)),
                dma,
                dma((window // share,)),
                dma,
                dma((2, 3)),
                dma((2, 3)),
                dma((2, 3, 2)),
                dma((2, 3, 2)),
                dma((3,)),
                dma((3,)),
                dma((3,)),
                dma((3,)),
            ],
            compiler_params=params(collective_id=1, has_side_effects=True),
            cost_estimate=cost(1e11, 100e6),
            name="middle",
        )(
            rows[:, None, :],
            norm_gains,
            x_m,
            cot,
            q_m,
            cos_m,
            sin_m,
            cos,
            sin,
            w_qkv,
            ffn_all.reshape(3, model, hidden),
            o_m,
            o_first,
            w_out,
            w_far,
            tokens,
            k,
            v,
            o_second,
            o_third,
        )

        group = 8
        slots = lax.axis_size("dp") * capacity
        slot_hit = slot_index[None, :] == jnp.arange(slots, dtype=jnp.int32)[:, None]
        used = jnp.any(slot_hit, axis=1).astype(jnp.int32)
        tile_count = slot_index.shape[0]
        held_at = jnp.arange(slots, dtype=jnp.int32) // group * tile_count
        held_at = held_at + jnp.argmax(slot_hit, axis=1).astype(jnp.int32)
        held_at = jnp.where(used > 0, held_at, 0).reshape(-1, group)
        from_tile = lax.rem(lax.cummax(held_at, axis=0), tile_count).reshape(-1)
        in_slots = pl.pallas_call(
            spread_kernel,
            out_shape=jax.ShapeDtypeStruct((slots, tile_rows, model), bf16),
            grid_spec=pltpu.PrefetchScalarGridSpec(
                num_scalar_prefetch=2,
                grid=(slots // group,),
                in_specs=[
                    pl.BlockSpec(
                        tile_block, lambda i, tile, used, n=n: (tile[i * group + n], 0, 0)
                    )
                    for n in range(group)
                ],
                out_specs=pl.BlockSpec(
                    (group, tile_rows, model), lambda i, tile, used: (i, 0, 0)
                ),
            ),
            compiler_params=params(),
            cost_estimate=cost(0, 24 * capacity * tile_size),
            name="spread",
        )(
            from_tile,
            used,
            *[grads.reshape(-1, tile_rows, model)] * group,
        )
        reduced = lax.psum_scatter(in_slots, "dp", scatter_dimension=0, tiled=True).astype(f32)

        order = [(kind, i) for kind in (0, 1) for i in range(seq_count)]
        folds = len(order)
        pair_count = (lax.axis_size("dp") * parts).bit_length() - 1
        layer_out, input_grad, gain_grad = pl.pallas_call(
            after(functools.partial(lines_kernel, seq_count, seq_count, order, 2, 1), 10, 1),
            out_shape=[
                jax.ShapeDtypeStruct((total_rows, model), bf16),
                jax.ShapeDtypeStruct((share_rows, model), bf16),
                jax.ShapeDtypeStruct((2, model), f32),
            ],
            in_specs=[inside] * 3 + [anywhere] * 6 + [inside, anywhere],
            out_specs=[anywhere] * 2 + [inside],
            scratch_shapes=[
                pltpu.VMEM((folds, 3 * share, model), bf16),
                pltpu.VMEM((folds, 2 * share, model), bf16),
                pltpu.VMEM((folds, share, model), bf16),
                pltpu.VMEM((folds, window, model), bf16),
                pltpu.VMEM((seq_count, share, model), f32),
                pltpu.VMEM((seq_count, share, model), bf16),
                pltpu.VMEM((share_rows, model), bf16),
                pltpu.VMEM((seq_count, share, model), bf16),
                pltpu.VMEM((pair_count + 1, 8, model), f32),
                pltpu.VMEM((pair_count, 8, model), f32),
                dma((pair_count,)),
                dma((pair_count,)),
                dma((folds, 3)),
                dma((folds, 3)),
                dma((folds, 2)),
                dma((folds, 2)),
                dma((folds,)),
                dma((folds,)),
                dma((seq_count, 5)),
                dma((seq_count, 3)),
                dma((folds,)),
                dma((seq_count,)),
                dma((2,)),
                dma((1,)),
                dma,
                dma((seq_count,)),
                dma((seq_count,)),
            ],
            compiler_params=params(collective_id=2, has_side_effects=True),
            cost_estimate=cost(4 * share_rows * mask_rows * model, 60e6),
            name="lines",
        )(
            flat_rows,
            dr_m,
            norm_gains,
            tokens,
            dha,
            part,
            own,
            first_sums,
            second_sums,
            gains_part * even,
            in_slots,
        )
    else:
        w_outs = around(w_out)
        ffn_flat = ffn_all.reshape(3, -1)
        w_gate = ffn_flat[0].reshape(model, hidden)
        w_up = ffn_flat[1].reshape(model, hidden)
        w_down = ffn_flat[2].reshape(hidden, model)
        cols = min(256, hidden)
        col_block = pl.BlockSpec((model, cols), lambda c: (0, c))
        down_block = pl.BlockSpec((cols, model), lambda c: (c, 0))
        r_m, dhf_part, ffn_grad = pl.pallas_call(
            functools.partial(ffn_masked_kernel, parts),
            out_shape=[
                jax.ShapeDtypeStruct((mask_rows, model), f32),
                jax.ShapeDtypeStruct((mask_rows, model), bf16),
                jax.ShapeDtypeStruct((3, hidden, model), bf16),
            ],
            grid=(hidden // cols,),
            in_specs=[
                whole_spec((mask_rows, model)),
                whole_spec((mask_rows, model)),
                whole_spec((2, model)),
                col_block,
                col_block,
                down_block,
            ]
            + [whole_spec((mask_rows, width))] * parts
            + [whole_spec((width, model))] * parts,
            out_specs=[
                whole_spec((mask_rows, model)),
                whole_spec((mask_rows, model)),
                whole_spec((3, hidden, model)),
            ],
            scratch_shapes=[
                pltpu.VMEM((mask_rows, model), bf16),
                pltpu.VMEM((mask_rows, model), f32),
                pltpu.VMEM((cols // 128, model, 128), f32),
            ],
            compiler_params=params(),
            cost_estimate=cost(
                mask_rows * model * (18 * hidden + 2 * model), 20e6, mask_rows * hidden
            ),
            name="ffn_masked",
        )(x_m, cot, norm_gains, w_gate, w_up, w_down, *o_ms, *w_outs)

        for w in range(early, seq_count):
            o_own.append(attend_window(w, r_m))
        windows_o = [around(o) for o in o_own]

        share_m = mask_rows // parts
        dhf_mine = lax.dynamic_slice_in_dim(dhf_part, place * share_m, share_m, 0).astype(f32)
        for step in range(1, parts):
            send = lax.dynamic_slice_in_dim(
                dhf_part, lax.rem(place + step, parts) * share_m, share_m, 0
            )
            dhf_mine = dhf_mine + lax.ppermute(
                send, "tensor", [(i, (i + step) % parts) for i in range(parts)]
            ).astype(f32)
        dhf_all = around(dhf_mine.astype(bf16))
        dhf = jnp.zeros((mask_rows, model), bf16)
        for step, piece in enumerate(dhf_all):
            origin = lax.rem(place + parts - step, parts)
            dhf = lax.dynamic_update_slice_in_dim(dhf, piece, origin * share_m, 0)

        layer_out = None

        def ffn_window(w, before):
            return pl.pallas_call(
                after(functools.partial(ffn_kernel, parts), 6 + 2 * parts, 1),
                out_shape=[
                    jax.ShapeDtypeStruct((window, model), bf16),
                    jax.ShapeDtypeStruct((share, model), f32),
                ],
                grid_spec=pltpu.PrefetchScalarGridSpec(
                    num_scalar_prefetch=1,
                    grid=(hidden // cols,),
                    in_specs=[
                        pl.BlockSpec((window, model), lambda c, place_ref: (w, 0)),
                        whole_spec((2, model)),
                        pl.BlockSpec((model, cols), lambda c, place_ref: (0, c)),
                        pl.BlockSpec((model, cols), lambda c, place_ref: (0, c)),
                        pl.BlockSpec((cols, model), lambda c, place_ref: (c, 0)),
                    ]
                    + [whole_spec((window, width))] * parts
                    + [whole_spec((width, model))] * parts
                    + [UNREAD],
                    out_specs=[
                        whole_spec((window, model)),
                        whole_spec((share, model)),
                    ],
                    scratch_shapes=[
                        pltpu.VMEM((window, model), f32),
                        pltpu.VMEM((window, model), bf16),
                        pltpu.VMEM((window, model), f32),
                    ],
                ),
                compiler_params=params(),
                cost_estimate=cost(
                    window * model * (6 * hidden + 2 * model), 16e6, window * hidden
                ),
                name="ffn",
            )(
                place_ref,
                tokens,
                norm_gains,
                w_gate,
                w_up,
                w_down,
                *windows_o[w],
                *w_outs,
                before,
            )

        def place_window(w, part, own):
            terms = other_sums(part, share)
            total = own
            for term in terms:
                total = total + term.astype(f32)
            pieces = around(total.astype(bf16))
            return pl.pallas_call(
                after(place_kernel, 1 + parts, 0 if layer_out is None else 1),
                out_shape=jax.ShapeDtypeStruct((total_rows, model), bf16),
                grid_spec=pltpu.PrefetchScalarGridSpec(
                    num_scalar_prefetch=1,
                    grid=(1,),
                    in_specs=[whole_spec((share, model))] * parts
                    + [UNREAD] * (layer_out is not None),
                    out_specs=pl.BlockSpec((window, model), lambda i, place_ref: (w, 0)),
                ),
                input_output_aliases={} if layer_out is None else {1 + parts: 0},
                compiler_params=params(),
                cost_estimate=cost(0, 4 * window * model),
                name="place",
            )(place_ref, *pieces, *([] if layer_out is None else [layer_out]))

        parts_out = [ffn_window(0, o_own[-1])]

        cuts = seq_count if share_rows % (16 * seq_count) == 0 else 1
        cut_rows = share_rows // cuts
        dr_m, dha, attn_grad, gains_part = pl.pallas_call(
            after(attn_back_kernel, 16, 1),
            out_shape=[
                jax.ShapeDtypeStruct((mask_rows, model), f32),
                jax.ShapeDtypeStruct((cuts, parts, cut_rows, model), bf16),
                jax.ShapeDtypeStruct((4 * width, model), bf16),
                jax.ShapeDtypeStruct((2, model), f32),
            ],
            grid=(seq_count,),
            in_specs=[
                pl.BlockSpec((1, 1, count), lambda i: (i, 0, 0)),
                mask_model,
                mask_model,
                mask_model,
                whole_spec((2, model)),
                mask_head,
                mask_head,
                mask_head,
                mask_head,
                win_head,
                win_head,
                win_model,
                whole_spec((window, width)),
                whole_spec((window, width)),
                whole_spec((width, model)),
                whole_spec((model, 3 * width)),
                UNREAD,
            ],
            out_specs=[
                mask_model,
                whole_spec((cuts, parts, cut_rows, model)),
                whole_spec((4 * width, model)),
                whole_spec((2, model)),
            ],
            scratch_shapes=[
                pltpu.VMEM((model, 3 * width), f32),
                pltpu.VMEM((width, model), f32),
                pltpu.VMEM((2, model), f32),
                pltpu.VMEM((window, 3 * width), bf16),
                pltpu.VMEM((3 * width // 128, model, 128), f32),
            ],
            compiler_params=params(),
            cost_estimate=cost(
                12 * total_rows * model * width, 30e6, mask_rows * window * heads
            ),
            name="attn_back",
        )(
            rows[:, None, :],
            dhf,
            r_m,
            cot,
            norm_gains,
            o_m,
            q_m,
            cos_m,
            sin_m,
            k,
            v,
            tokens,
            cos,
            sin,
            w_out,
            w_qkv,
            parts_out[0][0],
        )

        for w in range(1, seq_count):
            parts_out.append(ffn_window(w, gains_part if w == 1 else parts_out[-1][0]))

        input_grad = None
        for cut in range(cuts):
            value = dha[cut].reshape(parts * cut_rows, model)
            terms = other_sums(value, cut_rows)
            before = [] if input_grad is None else [input_grad]
            input_grad = pl.pallas_call(
                after(
                    functools.partial(input_grad_kernel, (cut, cuts, len(terms))),
                    6 + len(terms),
                    len(before),
                ),
                out_shape=jax.ShapeDtypeStruct((share_rows, model), bf16),
                grid_spec=pltpu.PrefetchScalarGridSpec(
                    num_scalar_prefetch=1,
                    grid=(1,),
                    in_specs=[
                        whole_spec((1, mask_rows)),
                        whole_spec((mask_rows, model)),
                        whole_spec((2, model)),
                        pl.BlockSpec(
                            (cut_rows, model),
                            lambda i, place_ref, cut=cut: (place_ref[0] * cuts + cut, 0),
                        ),
                        pl.BlockSpec(
                            (1, 1, cut_rows, model),
                            lambda i, place_ref, cut=cut: (cut, place_ref[0], 0, 0),
                        ),
                    ]
                    + [whole_spec((cut_rows, model))] * len(terms)
                    + [UNREAD] * len(before),
                    out_specs=pl.BlockSpec((cut_rows, model), lambda i, place_ref, cut=cut: (cut, 0)),
                ),
                input_output_aliases={6 + len(terms): 0} if before else {},
                compiler_params=params(),
                cost_estimate=cost(4 * cut_rows * mask_rows * model, 6e6),
                name="input_grad",
            )(place_ref, flat_rows, dr_m, norm_gains, tokens, dha, *terms, *before)

        for w, outs in enumerate(parts_out):
            layer_out = place_window(w, *outs)

        gain_grad = small_total(gains_part * even)

        def total_tiles(tiles, before):
            piece = lax.psum_scatter(tiles, "dp", scatter_dimension=0, tiled=True)
            piece = pl.pallas_call(
                after(copy_kernel, 1, 1),
                out_shape=jax.ShapeDtypeStruct(piece.shape, bf16),
                in_specs=[pl.BlockSpec(memory_space=pltpu.VMEM), UNREAD],
                out_specs=pl.BlockSpec(memory_space=pltpu.VMEM),
                compiler_params=params(),
                name="copy",
            )(piece, before)
            return lax.all_gather(piece, "dp", axis=0, tiled=True)

        ffn_grads = total_tiles(ffn_grad.reshape(3 * hidden, model), parts_out[1][0])
        attn_grads = total_tiles(attn_grad, parts_out[-1][0])
        tiles = jnp.concatenate([attn_grads, ffn_grads], axis=0).reshape(-1, tile_rows, model)
        reduced = tiles[slot_tile].astype(f32)

    _, gain_moment, gain_new = adam_update(
        gain_grad, gain_first, gain_second, norm_gains, gain_rate, 0.0
    )

    first_new, second_new, param_new = adam_update(
        reduced, first_moment[0], second_moment[0], master[0], weight_rate, weight_decay
    )
    weight_grad = jnp.where(slot_used, reduced, 0.0)
    weight_first = jnp.where(slot_used, first_new, 0.0)
    weight_second = jnp.where(slot_used, second_new, 0.0)
    weight_master = jnp.where(slot_used, param_new, 0.0)
    weight_low = weight_master.astype(bf16)
    return (
        layer_out,
        input_grad,
        weight_grad[None],
        weight_first[None],
        weight_second[None],
        weight_master[None],
        weight_low[None],
        gain_grad,
        gain_moment,
        gain_new,
    )


def solution(mesh):
    return jax.shard_map(
        on_device,
        mesh=mesh,
        in_specs=(
            P("dp", None),
            P("dp", None),
            P("dp", None, None),
            P(),
            P(),
            P(),
            P("tensor", None),
            P("tensor", "dp", None, None),
            P("tensor", "dp", None, None),
            P("tensor", "dp", None, None),
        ),
        out_specs=(
            P("dp", None),
            P(("dp", "tensor"), None),
            P("tensor", "dp", None, None),
            P("tensor", "dp", None, None),
            P("tensor", "dp", None, None),
            P("tensor", "dp", None, None),
            P("tensor", "dp", None, None),
            P(),
            P(),
            P(),
        ),
        check_vma=False,
    )
```
